32 devices in a mesh: dp: 8 (over z, x), col: 4 (over y, core).
Axes of the slice: x: 2, y: 2, z: 4, core: 2. Of those that a mesh axis runs over, the one named last changes fastest.
Arguments:
- features: bfloat16 [100, 262144], P('col', 'dp'), may hold values from -6 to 6
- neighbors_one: int32 [5, 65536], P(None, 'dp'), may hold values from 0 to 32767, as said below
- present_one: int32 [5, 65536], P(None, 'dp'), may hold values 0 or 1
- neighbors_two: int32 [10, 16384], P(None, 'dp'), may hold values from 0 to 8191, as said below
- present_two: int32 [10, 16384], P(None, 'dp'), may hold values 0 or 1
- neighbors_three: int32 [15, 4096], P(None, 'dp'), may hold values from 0 to 2047, as said below
- present_three: int32 [15, 4096], P(None, 'dp'), may hold values 0 or 1
- labels: int32 [4096], P('dp'), may hold values from 0 to 46
- seed_weight: int32 [4096], P('dp'), may hold values from 0 to 1, as said below
- serve_rows: int32 [64, 8], P('dp'), may hold values from 0 to 511
- take_seed: int32 [64, 8], P('dp'), may hold values from 0 to 511
- fetch_live: int32 [64], P('dp'), may hold values from 0 to 8, as said below
- weight_one: float32 [2, 100, 256], P(None, 'col'), may hold values from -0.4375 to 0.4375
- weight_two: float32 [2, 256, 256], P(None, 'col'), may hold values from -4 to 4
- weight_three: float32 [2, 256, 47], P(None, 'col'), may hold values from -4 to 4
- hidden_bias: float32 [2, 256], P(None, 'col'), may hold values from -0.5 to 0.5
- head_bias: float32 [47], replicated, may hold values from -1 to 1
- first_one: float32 [2, 100, 256], P(None, 'col'), may hold values from -0.21875 to 0.21875
- first_two: float32 [2, 256, 256], P(None, 'col'), may hold values from -0.21875 to 0.21875
- first_three: float32 [2, 256, 47], P(None, 'col'), may hold values from -0.21875 to 0.21875
- first_hidden: float32 [2, 256], P(None, 'col'), may hold values from -0.75 to 0.75
- first_head: float32 [47], replicated, may hold values from -6 to 6
- second_one: float32 [2, 100, 256], P(None, 'col'), may hold values from 0.0001024 to 0.0004096
- second_two: float32 [2, 256, 256], P(None, 'col'), may hold values from 0.0001024 to 0.0004096
- second_three: float32 [2, 256, 47], P(None, 'col'), may hold values from 0.0001024 to 0.0004096
- second_hidden: float32 [2, 256], P(None, 'col'), may hold values from 0.0016384 to 0.0065536
- second_head: float32 [47], replicated, may hold values from 0.08192 to 0.32768
Outputs:
- new_weight_one: float32 [2, 100, 256], P(None, 'col')
- new_weight_two: float32 [2, 256, 256], P(None, 'col')
- new_weight_three: float32 [2, 256, 47], P(None, 'col')
- new_hidden_bias: float32 [2, 256], P(None, 'col')
- new_head_bias: float32 [47], replicated
- moment_one: float32 [2, 100, 256], P(None, 'col')
- moment_two: float32 [2, 256, 256], P(None, 'col')
- moment_three: float32 [2, 256, 47], P(None, 'col')
- moment_hidden: float32 [2, 256], P(None, 'col')
- moment_head: float32 [47], replicated
- square_one: float32 [2, 100, 256], P(None, 'col')
- square_two: float32 [2, 256, 256], P(None, 'col')
- square_three: float32 [2, 256, 47], P(None, 'col')
- square_hidden: float32 [2, 256], P(None, 'col')
- square_head: float32 [47], replicated
- layer_norms: float32 [2, 5], replicated
- loss_sum: float32 [], replicated
- seed_count: float32 [], replicated
The draws below stay inside these ranges and needn't reach their ends.
Inputs may be any that keep to these rules, and one draw needn't show every extreme that they name: `seed_weight`: share of counted seeds rises from about a third on block 0 to all seeds on the last block. `fetch_live`: some owners serve all 8 slots to every block; the others a quarter to a half of them. `neighbors_one`: A node at row i of its block has its neighbors at rows of at least 4 i - 64 and below 4 i + 64 of the set below, within that block's rows. `neighbors_two`: A node at row i of its block has its neighbors at rows of at least 4 i - 64 and below 4 i + 64 of the set below, within that block's rows. `neighbors_three`: A seed at row i of its block has its neighbors at rows of at least 4 i - 64 and below 4 i + 64 of the set below, within that block's rows.
All inputs are finite; a program needn't handle non-finite values. No bound on the sum of `present_one` or of `present_two` or of `present_three` on one device may be relied on, other than what follows from the above.
Results may differ from the reference program's by a relative error of at most 0.012.
The reference program's roundings to bfloat16 on the way (of `inputs`) count: a program that leaves them out, or rounds other values in their place, can miss the bound.
Values may be sent and summed in bfloat16 or wider, within the bound.
No kernel may reach another device: no remote copies, remote signals or barrier semaphores. Data moves between devices by JAX's collectives and lax.ppermute only.
A program may use at most 64 MiB of HBM per device.

```python
import math
import jax
import jax.numpy as jnp
from jax import lax

F_IN = 100
HIDDEN_SIZE = 256
CLASSES = 47
SEEDS_DEV = 512
FAN_ONE = 5
FAN_TWO = 10
FAN_THREE = 15
REACH = 64
SLOTS = 8
STEP = 5
MID_DEV = 2048
LOW_DEV = 8192
BASE_DEV = 32768
SEEDS = 4096
MID_ROWS = 16384
LOW_ROWS = 65536
BASE_ROWS = 262144
N_DP = 8


def local_links(key, fanout, rows_all, rows_dev, below):
    offsets = jax.random.randint(key, (fanout, rows_all), -REACH, REACH)
    center = 4 * (jnp.arange(rows_all) % rows_dev)
    return jnp.clip(center[None, :] + offsets, 0, below - 1).astype(jnp.int32)


def draw_neighbors_one(key, part):
    key = jax.random.fold_in(key, 31)
    return local_links(key, FAN_ONE, LOW_ROWS, LOW_DEV, BASE_DEV)


def draw_neighbors_two(key, part):
    key = jax.random.fold_in(key, 37)
    return local_links(key, FAN_TWO, MID_ROWS, MID_DEV, LOW_DEV)


def draw_neighbors_three(key, part):
    key = jax.random.fold_in(key, 41)
    return local_links(key, FAN_THREE, SEEDS, SEEDS_DEV, MID_DEV)


def draw_seed_weight(key, part):
    key = jax.random.fold_in(key, 11)
    spread_top = max(N_DP - 1, 1)
    block_of = jnp.arange(SEEDS) // SEEDS_DEV
    ticket = jax.random.randint(key, (SEEDS,), 0, 3 * spread_top)
    return (ticket < spread_top + 2 * block_of).astype(jnp.int32)


def draw_fetch_live(key, part):
    key = jax.random.fold_in(key, 23)
    key_hot, key_forced, key_drawn = jax.random.split(key, 3)
    favored = jax.random.randint(key_hot, (N_DP,), 0, 4) == 0
    forced = jnp.arange(N_DP) == jax.random.randint(key_forced, (), 0, N_DP)
    favored = favored | forced
    drawn = jax.random.randint(key_drawn, (N_DP * N_DP,), SLOTS // 4, SLOTS // 2 + 1)
    owner_of = jnp.arange(N_DP * N_DP) % N_DP
    return jnp.where(favored[owner_of], SLOTS, drawn).astype(jnp.int32)


def touch_ends(values, own_key, low, largest):
    longest = values.shape.index(max(values.shape))
    spots = []
    for shift in (0, 1):
        where = [jax.random.randint(jax.random.fold_in(own_key, axis), (), 0, length) for axis, length in enumerate(values.shape)]
        where[longest] = (where[longest] + shift) % values.shape[longest]
        spots.append(tuple(where))
    return values.at[spots[0]].set(low).at[spots[1]].set(largest)


def shard_levels(rng, shape, cuts, smallest, largest):
    def one(axis_at, shards_of):
        steps = jax.random.uniform(jax.random.fold_in(jax.random.fold_in(rng, 6), axis_at), (shards_of,), jnp.float32, smallest / len(cuts), largest / len(cuts))
        return jnp.repeat(jnp.exp(steps), shape[axis_at] // shards_of).reshape((-1,) + (1,) * (len(shape) - axis_at - 1))

    level = one(*cuts[0])
    for cut in cuts[1:]:
        level = level * one(*cut)
    return level


def centred(stream_key, shape, deviation, most, pieces=(), kind=jnp.bfloat16):
    values = deviation * jax.random.normal(stream_key, shape, jnp.float32)
    if pieces:
        values = values * shard_levels(stream_key, shape, pieces, -0.22, 0.18)
    return jnp.clip(values, -most, most).astype(kind)


def setup_inputs(seed: int = 0) -> dict:
    splits = jax.random.split(jax.random.key(seed), 28)
    return {
        "features": centred(splits[0], (F_IN, BASE_ROWS), 1.0, 6.0, ((0, 4), (1, 8))),
        "neighbors_one": draw_neighbors_one(jax.random.fold_in(splits[27], 71), 0),
        "present_one": touch_ends((jax.random.randint(splits[2], (FAN_ONE, LOW_ROWS), 0, 3) < 2).astype(jnp.int32), jax.random.fold_in(splits[2], 1), 0, 1),
        "neighbors_two": draw_neighbors_two(jax.random.fold_in(splits[27], 71), 0),
        "present_two": touch_ends((jax.random.randint(splits[4], (FAN_TWO, MID_ROWS), 0, 3) < 2).astype(jnp.int32), jax.random.fold_in(splits[4], 1), 0, 1),
        "neighbors_three": draw_neighbors_three(jax.random.fold_in(splits[27], 71), 0),
        "present_three": touch_ends((jax.random.randint(splits[6], (FAN_THREE, SEEDS), 0, 3) < 2).astype(jnp.int32), jax.random.fold_in(splits[6], 1), 0, 1),
        "labels": touch_ends(jax.random.randint(splits[7], (SEEDS,), 0, CLASSES), jax.random.fold_in(splits[7], 1), 0, CLASSES - 1).astype(jnp.int32),
        "seed_weight": draw_seed_weight(jax.random.fold_in(splits[27], 71), 0),
        "serve_rows": touch_ends(jax.random.randint(splits[9], (N_DP * N_DP, SLOTS), 0, SEEDS_DEV), jax.random.fold_in(splits[9], 1), 0, SEEDS_DEV - 1).astype(jnp.int32),
        "take_seed": touch_ends(jax.random.randint(splits[10], (N_DP * N_DP, SLOTS), 0, SEEDS_DEV), jax.random.fold_in(splits[10], 1), 0, SEEDS_DEV - 1).astype(jnp.int32),
        "fetch_live": draw_fetch_live(jax.random.fold_in(splits[27], 71), 0),
        "weight_one": centred(splits[12], (2, F_IN, HIDDEN_SIZE), (2 * F_IN) ** -0.5, 0.4375, ((1, 4),), jnp.float32),
        "weight_two": centred(splits[13], (2, HIDDEN_SIZE, HIDDEN_SIZE), 2 ** -0.5, 4.0, ((1, 4),), jnp.float32),
        "weight_three": centred(splits[14], (2, HIDDEN_SIZE, CLASSES), 2 ** -0.5, 4.0, ((1, 4),), jnp.float32),
        "hidden_bias": jnp.clip(jax.random.uniform(splits[15], (2, HIDDEN_SIZE), jnp.float32, -0.5, 0.5) * shard_levels(splits[15], (2, HIDDEN_SIZE), ((1, 4),), -0.4, 0.0), -0.5, 0.5),
        "head_bias": jnp.clip(jax.random.uniform(splits[16], (CLASSES,), jnp.float32, -1.0, 1.0), -1.0, 1.0),
        "first_one": centred(splits[17], (2, F_IN, HIDDEN_SIZE), (0.0006 * SEEDS ** 0.5), 0.21875, ((1, 4),), jnp.float32),
        "first_two": centred(splits[18], (2, HIDDEN_SIZE, HIDDEN_SIZE), (0.0006 * SEEDS ** 0.5), 0.21875, ((1, 4),), jnp.float32),
        "first_three": centred(splits[19], (2, HIDDEN_SIZE, CLASSES), (0.0006 * SEEDS ** 0.5), 0.21875, ((1, 4),), jnp.float32),
        "first_hidden": centred(splits[20], (2, HIDDEN_SIZE), (0.002 * SEEDS ** 0.5), 0.75, ((1, 4),), jnp.float32),
        "first_head": centred(splits[21], (CLASSES,), (0.015 * SEEDS ** 0.5), 6.0, (), jnp.float32),
        "second_one": jnp.clip(jnp.exp(math.log(0.0004096) - 1.3862944 * jax.random.uniform(splits[22], (2, F_IN, HIDDEN_SIZE), jnp.float32) ** shard_levels(splits[22], (2, F_IN, HIDDEN_SIZE), ((1, 4),), -0.2, 0.2)), 0.0001024, 0.0004096),
        "second_two": jnp.clip(jnp.exp(math.log(0.0004096) - 1.3862944 * jax.random.uniform(splits[23], (2, HIDDEN_SIZE, HIDDEN_SIZE), jnp.float32) ** shard_levels(splits[23], (2, HIDDEN_SIZE, HIDDEN_SIZE), ((1, 4),), -0.2, 0.2)), 0.0001024, 0.0004096),
        "second_three": jnp.clip(jnp.exp(math.log(0.0004096) - 1.3862944 * jax.random.uniform(splits[24], (2, HIDDEN_SIZE, CLASSES), jnp.float32) ** shard_levels(splits[24], (2, HIDDEN_SIZE, CLASSES), ((1, 4),), -0.2, 0.2)), 0.0001024, 0.0004096),
        "second_hidden": jnp.clip(jnp.exp(math.log(0.0065536) - 1.3862944 * jax.random.uniform(splits[25], (2, HIDDEN_SIZE), jnp.float32) ** shard_levels(splits[25], (2, HIDDEN_SIZE), ((1, 4),), -0.2, 0.2)), 0.0016384, 0.0065536),
        "second_head": jnp.clip(jnp.exp(jax.random.uniform(splits[26], (CLASSES,), jnp.float32, math.log(0.08192), math.log(0.32768))), 0.08192, 0.32768),
    }


DIST_WEIGHT = 1.0
ROW_EPS = 1e-06
LEARN_RATE = 0.5
BETA_ONE = 0.9
BETA_TWO = 0.999
ADAM_EPS = 1e-06
DECAY_RATE = 0.01

@jax.custom_vjp
def low(v):
    return lax.optimization_barrier(v.astype(jnp.bfloat16)).astype(jnp.float32)

@jax.custom_vjp
def low_back(v):
    return v

def low_keep(v):
    return (low(v), None)

def low_pass(kept, grad):
    return (grad,)

def back_keep(v):
    return (v, None)

def back_low(kept, grad):
    return (low(grad),)
low.defvjp(low_keep, low_pass)
low_back.defvjp(back_keep, back_low)

def take_rows(table, picks):
    return jax.vmap(lambda block, chosen: block[chosen])(table, picks)

def layer_apply(states, neighbor, present, weight, bias, final_layer):
    rows = neighbor.shape[1]
    valid = present.astype(jnp.float32)
    totals = jnp.maximum(lax.optimization_barrier(jnp.sum(valid, 2)), 1.0)
    gathered = take_rows(states, neighbor)
    average = lax.optimization_barrier(jnp.sum(gathered * valid[..., None], 2)) / totals[..., None]
    inputs = low(jnp.stack([states[:, :rows], average], 2))
    result = jnp.einsum('bnsk,skd->bnd', inputs, low(weight), precision=lax.Precision.HIGHEST) + bias
    result = low_back(result)
    if final_layer:
        return result
    active = jax.nn.silu(result)
    return active * lax.rsqrt(lax.optimization_barrier(jnp.sum(active * active, -1, keepdims=True)) + ROW_EPS)

def forward(params, features, wiring, labels, weighting, serve, take, alive):
    weight_one, weight_two, weight_three, hidden_bias, head_bias = params
    states = layer_apply(features, wiring[0], wiring[1], weight_one, hidden_bias[0], False)
    states = layer_apply(states, wiring[2], wiring[3], weight_two, hidden_bias[1], False)
    logits = layer_apply(states, wiring[4], wiring[5], weight_three, head_bias, True)
    lse = jax.nn.logsumexp(logits, -1)
    target = jnp.take_along_axis(logits, labels[..., None], -1)[..., 0]
    ce_total = jnp.sum(weighting * (lse - target))
    embed = states[:, :SEEDS_DEV]
    fetched = low_back(jnp.swapaxes(take_rows(low(embed), serve), 0, 1))
    local_rows = take_rows(embed, take)
    differ = local_rows - fetched
    return ce_total + DIST_WEIGHT * jnp.sum(alive[..., None] * differ * differ)

def lamb(weight, grad, first, second):
    first_new = BETA_ONE * first + (1.0 - BETA_ONE) * grad
    second_new = BETA_TWO * second + (1.0 - BETA_TWO) * grad * grad
    update = first_new / (1.0 - BETA_ONE ** STEP) / (jnp.sqrt(second_new / (1.0 - BETA_TWO ** STEP)) + ADAM_EPS) + DECAY_RATE * weight
    weight_norm = jnp.sqrt(jnp.sum(weight * weight))
    update_norm = jnp.sqrt(jnp.sum(update * update))
    return (weight - LEARN_RATE * (weight_norm / update_norm) * update, first_new, second_new, weight_norm, update_norm)

def reference(features, neighbors_one, present_one, neighbors_two, present_two, neighbors_three, present_three, labels, seed_weight, serve_rows, take_seed, fetch_live, weight_one, weight_two, weight_three, hidden_bias, head_bias, first_one, first_two, first_three, first_hidden, first_head, second_one, second_two, second_three, second_hidden, second_head):

    def blocks(array):
        return array.reshape((N_DP, -1) + array.shape[1:])
    wiring = tuple((blocks(item.T) for item in (neighbors_one, present_one, neighbors_two, present_two, neighbors_three, present_three)))
    weighting = blocks(seed_weight).astype(jnp.float32)
    serve = serve_rows.reshape(N_DP, N_DP, -1)
    take = take_seed.reshape(N_DP, N_DP, -1)
    slots = take.shape[2]
    alive = (jnp.arange(slots)[None, None, :] < fetch_live.reshape(N_DP, N_DP)[..., None]).astype(jnp.float32)
    params = (weight_one, weight_two, weight_three, hidden_bias, head_bias)
    feats = blocks(features.T).astype(jnp.float32)
    total, pullback = jax.vjp(lambda p: forward(p, feats, wiring, blocks(labels), weighting, serve, take, alive), params)
    grads = pullback(jnp.float32(1.0))[0]
    firsts = (first_one, first_two, first_three, first_hidden, first_head)
    seconds = (second_one, second_two, second_three, second_hidden, second_head)
    results = [lamb(params[i], grads[i], firsts[i], seconds[i]) for i in range(5)]
    norms = jnp.stack([jnp.stack([item[3] for item in results]), jnp.stack([item[4] for item in results])])
    return (results[0][0], results[1][0], results[2][0], results[3][0], results[4][0], results[0][1], results[1][1], results[2][1], results[3][1], results[4][1], results[0][2], results[1][2], results[2][2], results[3][2], results[4][2], norms, total, jnp.sum(weighting))
```

```python
import functools

import jax
import jax.numpy as jnp
from jax import lax
from jax.experimental import pallas as pl
from jax.experimental.pallas import tpu as pltpu
from jax.sharding import PartitionSpec as P

REACH = 64
STEP = 5
DIST_WEIGHT = 1.0
ROW_EPS = 1e-06
LEARN_RATE = 0.5
BETA_ONE = 0.9
BETA_TWO = 0.999
ADAM_EPS = 1e-06
DECAY_RATE = 0.01

BF = jnp.bfloat16
F32 = jnp.float32
LANES = 128
WINDOW = 768
SENTINEL = 4.0
PARAMS = pltpu.CompilerParams(vmem_limit_bytes=56 * 2**20)


class Sizes:
    def __init__(self, features, neighbors_one, neighbors_two, neighbors_three, weight_two, weight_three, serve_rows):
        self.feat = features.shape[0]
        self.hold = -(-self.feat // 16) * 16
        self.base = features.shape[1]
        self.low = neighbors_one.shape[1]
        self.mid = neighbors_two.shape[1]
        self.seeds = neighbors_three.shape[1]
        self.hid = weight_two.shape[2]
        self.group = weight_two.shape[1]
        self.classes = weight_three.shape[2]
        self.head = -(-self.classes // 16) * 16
        self.own = self.seeds // 4
        self.n_b = 4 * self.own + 2 * LANES
        self.n_a = 16 * self.own + 6 * LANES
        self.n_low = self.n_a + self.n_b + self.own
        self.n_mid = self.n_b + self.own
        self.slots = serve_rows.shape[0] * serve_rows.shape[1]
        self.slot = serve_rows.shape[1]
        self.dp = serve_rows.shape[0]
        self.w_lanes = self.hid + 2 * self.hid + 2 * LANES + LANES
        self.rows_one = 2 * 2 * self.hold
        self.rows_two = 4 * self.group
        self.misc = self.rows_one + self.rows_two + self.head
        self.pay = self.misc + 16

    def a_start(self, part):
        return jnp.clip(16 * self.own * part - 3 * LANES, 0, self.low - self.n_a)

    def b_start(self, part):
        return jnp.maximum(4 * self.own * part - LANES, 0)

    def b_columns(self, part, tile):
        return pl.ds(aligned(jnp.minimum(self.b_start(part) + LANES * tile, self.mid - LANES)), LANES)


def dot(a, b, over):
    return lax.dot_general(a, b, (((over[0],), (over[1],)), ((), ())), preferred_element_type=F32)


def two_parts(value):
    high = value.astype(BF)
    return high, (value - high.astype(F32)).astype(BF)


def three_parts(value):
    high = value.astype(BF).astype(F32)
    rest = value - high
    middle = rest.astype(BF).astype(F32)
    return high, middle, (rest - middle).astype(BF).astype(F32)


def aligned(value):
    return pl.multiple_of(value, LANES)


def sigmoid(value):
    return 1.0 / (1.0 + jnp.exp(-value))


def mean_kernel(sz, feat_ref, nbr_ref, pres_ref, out_ref):
    spare = jnp.zeros((sz.hold - sz.feat, LANES), F32)
    last = sz.base // LANES - 6

    def tile(step, carry):
        lane = aligned(step * LANES)
        valid = pres_ref[:, pl.ds(lane, LANES)].astype(F32)
        counts = jnp.maximum(jnp.sum(valid, 0, keepdims=True), 1.0)
        first = jnp.clip(4 * step - 1, 0, last)
        local = nbr_ref[:, pl.ds(lane, LANES)] - first * LANES
        piece = local >> 7
        spot = local & 127
        sources = [
            jnp.concatenate([feat_ref[:, pl.ds(aligned((first + j) * LANES), LANES)].astype(F32), spare], 0)
            for j in range(6)
        ]
        totals = [jnp.zeros((8, LANES), F32) for _ in range(sz.hold // 8)]
        for slot in range(nbr_ref.shape[0]):
            spots = jnp.broadcast_to(spot[slot : slot + 1], (8, LANES))
            pieces = jnp.broadcast_to(piece[slot : slot + 1], (8, LANES))
            marks = jnp.broadcast_to(valid[slot : slot + 1], (8, LANES))
            for h in range(sz.hold // 8):
                taken = None
                for j in range(6):
                    found = jnp.take_along_axis(
                        sources[j][8 * h : 8 * h + 8], spots, axis=1, mode="promise_in_bounds"
                    )
                    taken = found if j == 0 else jnp.where(pieces == j, found, taken)
                totals[h] = totals[h] + taken * marks
        average = jnp.concatenate(totals, 0) / counts
        own = jnp.concatenate([feat_ref[:, pl.ds(lane, LANES)].astype(F32), spare], 0)
        out_ref[:, pl.ds(lane, LANES)] = jnp.concatenate([own, average], 0).astype(BF)
        return carry

    lax.fori_loop(0, sz.low // LANES, tile, 0, unroll=4)


def layer_one_means(sz, features, neighbors, present):
    return pl.pallas_call(
        functools.partial(mean_kernel, sz),
        out_shape=jax.ShapeDtypeStruct((2 * sz.hold, sz.low), BF),
        compiler_params=PARAMS,
    )(features, neighbors, present)


def window_counts(local, rows):
    spots = lax.broadcasted_iota(jnp.int32, (rows, LANES), 0)
    counts = jnp.zeros((rows, LANES), F32)
    for slot in range(local.shape[0]):
        counts = counts + jnp.where(local[slot : slot + 1] == spots, 1.0, 0.0)
    return counts.astype(BF)


def slot_totals(present):
    return jnp.maximum(jnp.sum(present.astype(F32), 0, keepdims=True), 1.0)


def a_window(sz, part, tile):
    first = 4 * sz.b_start(part) + 4 * LANES * tile - LANES - sz.a_start(part)
    return aligned(jnp.clip(first, 0, sz.n_a - WINDOW))


def head_weight(sz, part, messages, low_ref):
    lane = sz.n_low + 3 * sz.hid
    for r in range(4):
        row = pl.multiple_of(2 * sz.group * (part ^ r), 2 * sz.group)
        low_ref[pl.ds(row, 2 * sz.group), :] = jnp.concatenate(
            [messages[r][:, lane + LANES * s : lane + LANES * s + LANES] for s in range(2)], 0
        )


def second_weight(sz, part, messages, low_ref):
    lane = sz.n_low + sz.hid
    for r in range(4):
        row = pl.multiple_of(2 * sz.group * (part ^ r), 2 * sz.group)
        low_ref[pl.ds(row, 2 * sz.group), :] = jnp.concatenate(
            [messages[r][:, lane + sz.hid * s : lane + sz.hid * s + sz.hid] for s in range(2)], 0
        )


def transposed(value):
    return value.astype(F32).T.astype(BF)


def forward_kernel(
    sz, m0, m1, m2, m3, nbr2, pres2, nbr3, pres3, info,
    result1, scale1, inputs2, result2, scale2, inputs3, counts2, counts3, sent,
    x_ref, high1, low1, w2_ref, bias_ref,
):
    part = lax.axis_index("col")
    messages = (m0, m1, m2, m3)
    n_a, n_b, own, hid, group = sz.n_a, sz.n_b, sz.own, sz.hid, sz.group
    for r in range(4):
        x_ref[2 * sz.hold * r : 2 * sz.hold * (r + 1), :] = messages[r][:, : sz.n_low]
        lane = sz.n_low + 3 * hid + 2 * LANES
        tail = messages[r][:, lane : lane + LANES].astype(F32)
        for layer in range(2):
            column = tail[:, 3 * layer : 3 * layer + 1] + tail[:, 3 * layer + 1 : 3 * layer + 2]
            column = column + tail[:, 3 * layer + 2 : 3 * layer + 3]
            row = pl.multiple_of(group * (part ^ r), group)
            bias_ref[pl.ds(row, group), LANES * layer : LANES * layer + LANES] = jnp.broadcast_to(column, (group, LANES))
    weight1 = transposed(
        jnp.concatenate([m[:, sz.n_low : sz.n_low + hid] for m in messages], 0)
    )
    second_weight(sz, part, messages, w2_ref)
    weight2 = transposed(w2_ref[...])

    def first_layer(lane):
        result = dot(weight1, x_ref[:, pl.ds(lane, LANES)], (1, 0)) + bias_ref[:, :LANES]
        active = result * sigmoid(result)
        scale = lax.rsqrt(jnp.sum(active * active, 0, keepdims=True) + ROW_EPS)
        result1[:, pl.ds(lane, LANES)] = result
        scale1[:, pl.ds(lane, LANES)] = scale
        high, low = two_parts(active * scale)
        high1[:, pl.ds(lane, LANES)] = high
        low1[:, pl.ds(lane, LANES)] = low

    def first_step(step, carry):
        first_layer(aligned(step * LANES))
        return carry

    lax.fori_loop(0, sz.n_low // LANES, first_step, 0)

    def second_inputs(lane, self_lane, window, local, totals, tile):
        counts = window_counts(local, WINDOW)
        counts2[WINDOW * tile : WINDOW * (tile + 1), :] = counts
        average = dot(high1[:, pl.ds(window, WINDOW)], counts, (1, 0))
        average = (average + dot(low1[:, pl.ds(window, WINDOW)], counts, (1, 0))) / totals
        average = average.astype(BF)
        for c in range(4):
            inputs2[2 * group * c : 2 * group * c + group, lane : lane + LANES] = high1[
                group * c : group * (c + 1), self_lane : self_lane + LANES
            ]
            inputs2[2 * group * c + group : 2 * group * (c + 1), lane : lane + LANES] = average[
                group * c : group * (c + 1)
            ]

    b_start = sz.b_start(part)
    for tile in range(n_b // LANES):
        columns = sz.b_columns(part, tile)
        window = a_window(sz, part, tile)
        marks = pres2[:, columns]
        local = jnp.where(marks > 0, nbr2[:, columns] - (sz.a_start(part) + window), -1)
        second_inputs(LANES * tile, n_a + LANES * tile, window, local, slot_totals(marks), tile)
    for tile in range(own // LANES):
        columns = pl.ds(aligned(own * part + LANES * tile), LANES)
        marks = pres2[:, columns]
        local = jnp.where(marks > 0, nbr2[:, columns] - b_start, -1)
        second_inputs(n_b + LANES * tile, n_a + n_b + LANES * tile, n_a, local, slot_totals(marks), n_b // LANES + tile)

    result = dot(weight2, inputs2[...], (1, 0)) + bias_ref[:, LANES : LANES + 1]
    active = result * sigmoid(result)
    scale = lax.rsqrt(jnp.sum(active * active, 0, keepdims=True) + ROW_EPS)
    result2[...] = result
    scale2[...] = scale
    high2, low2 = two_parts(active * scale)
    columns = pl.ds(aligned(own * part), own)
    marks = pres3[:, columns]
    local = jnp.where(marks > 0, nbr3[:, columns] - b_start, -1)
    counts = window_counts(local, n_b)
    counts3[...] = counts
    average = dot(high2[:, :n_b], counts, (1, 0)) + dot(low2[:, :n_b], counts, (1, 0))
    average = (average / slot_totals(marks)).astype(BF)
    embed_high, embed_low = high2[:, n_b:], low2[:, n_b:]
    for c in range(4):
        inputs3[2 * group * c : 2 * group * c + group, :] = embed_high[group * c : group * (c + 1)]
        inputs3[2 * group * c + group : 2 * group * (c + 1), :] = average[group * c : group * (c + 1)]
    spots = lax.broadcasted_iota(jnp.int32, (sz.slots, own), 1) + own * part
    serve = jnp.where(info[:, 0:1] == spots, 1.0, 0.0).astype(BF)
    take = jnp.where(info[:, 1:2] == spots, 1.0, 0.0)
    owned = jnp.sum(take, 1, keepdims=True)
    take = take.astype(BF)
    sent[:, :hid] = dot(serve, embed_high, (1, 1)).astype(BF)
    local_high = dot(take, embed_high, (1, 1))
    dead = (lax.broadcasted_iota(jnp.int32, (sz.slots, hid), 1) == 0) & ((owned > 0.5) & (info[:, 2:3] == 0))
    sent[:, hid : 2 * hid] = jnp.where(dead, SENTINEL, local_high).astype(BF)
    sent[:, 2 * hid :] = dot(take, embed_low, (1, 1)).astype(BF)


def forward(sz, messages, nbr2, pres2, nbr3, pres3, info):
    tiles = sz.n_mid // LANES
    shape = jax.ShapeDtypeStruct
    return pl.pallas_call(
        functools.partial(forward_kernel, sz),
        out_shape=(
            shape((sz.hid, sz.n_low), F32),
            shape((1, sz.n_low), F32),
            shape((2 * sz.hid, sz.n_mid), BF),
            shape((sz.hid, sz.n_mid), F32),
            shape((1, sz.n_mid), F32),
            shape((2 * sz.hid, sz.own), BF),
            shape((WINDOW * tiles, LANES), BF),
            shape((sz.n_b, sz.own), BF),
            shape((sz.slots, 3 * sz.hid), BF),
        ),
        scratch_shapes=[
            pltpu.VMEM((8 * sz.hold, sz.n_low), BF),
            pltpu.VMEM((sz.hid, sz.n_low), BF),
            pltpu.VMEM((sz.hid, sz.n_low), BF),
            pltpu.VMEM((2 * sz.hid, sz.hid), BF),
            pltpu.VMEM((sz.hid, 2 * LANES), F32),
        ],
        compiler_params=PARAMS,
    )(*messages, nbr2, pres2, nbr3, pres3, info)


def norm_backward(grad, result, scale):
    gate = sigmoid(result)
    active = result * gate
    inner = jnp.sum(grad * active, 0, keepdims=True)
    grad_active = scale * grad - active * (scale * scale * scale * inner)
    return (grad_active * gate * (1.0 + result * (1.0 - gate))).astype(BF)


def backward_kernel(
    sz, m0, m1, m2, m3, pres2, pres3, info, labels, weighting, head_bias,
    result1, scale1, inputs2, result2, scale2, inputs3, counts2, counts3, sent, received,
    keep, send,
    x_ref, w2_ref, w3_ref, grad_a, grad_bc, grad_mid, low_grad1, g2_ref, g3_ref, gb_ref,
):
    part = lax.axis_index("col")
    messages = (m0, m1, m2, m3)
    n_a, n_b, own, hid, group = sz.n_a, sz.n_b, sz.own, sz.hid, sz.group
    for r in range(4):
        x_ref[2 * sz.hold * r : 2 * sz.hold * (r + 1), :] = messages[r][:, : sz.n_low]
    second_weight(sz, part, messages, w2_ref)
    head_weight(sz, part, messages, w3_ref)

    columns = pl.ds(aligned(own * part), own)
    classes = lax.broadcasted_iota(jnp.int32, (sz.head, own), 0)
    logits = dot(transposed(w3_ref[...])[: sz.head], inputs3[...], (1, 0)) + head_bias[...]
    logits = jnp.where(classes < sz.classes, logits, -1e30)
    highest = jnp.max(logits, 0, keepdims=True)
    expo = jnp.exp(logits - highest)
    totals = jnp.sum(expo, 0, keepdims=True)
    onehot = jnp.where(classes == labels[:, columns], 1.0, 0.0)
    weights = weighting[:, columns].astype(F32)
    target = jnp.sum(jnp.where(classes == labels[:, columns], logits, 0.0), 0, keepdims=True)
    ce_total = jnp.sum(weights * (highest + jnp.log(totals) - target))
    seed_count = jnp.sum(weights)
    grad_logits = (weights * (expo / totals - onehot)).astype(BF)
    g3_ref[...] = dot(grad_logits, inputs3[...], (1, 1))
    grad_inputs3 = dot(w3_ref[:, : sz.head], grad_logits, (1, 0))
    pieces = [grad_inputs3[group * c : group * (c + 1)] for c in range(8)]
    scaled = jnp.concatenate(pieces[1::2], 0) / slot_totals(pres3[:, columns])
    high, low = two_parts(scaled)
    grad_mid[:, :n_b] = dot(high, counts3[...], (1, 1)) + dot(low, counts3[...], (1, 1))
    grad_embed = jnp.concatenate(pieces[0::2], 0)

    spots = lax.broadcasted_iota(jnp.int32, (sz.slots, own), 1) + own * part
    serve = jnp.where(info[:, 0:1] == spots, 1.0, 0.0)
    take = jnp.where(info[:, 1:2] == spots, 1.0, 0.0)
    served = jnp.sum(serve, 1, keepdims=True)
    taken = jnp.sum(take, 1, keepdims=True)
    alive = info[:, 2:3].astype(F32)
    arrived = received[...].astype(F32).reshape(sz.dp, 4, sz.slot, 3 * hid)
    arrived = jnp.sum(arrived, 1).reshape(sz.slots, 3 * hid)
    fetched = arrived[:, :hid]
    theirs = arrived[:, hid : 2 * hid]
    alive_there = jnp.where(theirs[:, 0:1] < 0.5 * SENTINEL, 1.0, 0.0)
    theirs = theirs + arrived[:, 2 * hid :]
    mine = sent[...].astype(F32)
    differ = (mine[:, hid : 2 * hid] + mine[:, 2 * hid :] - fetched)
    mask = (taken > 0.5) & (alive > 0.5)
    differ = jnp.where(mask, differ, 0.0)
    dist_total = DIST_WEIGHT * jnp.sum(differ * differ)
    local_high, local_low = two_parts(2.0 * DIST_WEIGHT * differ)
    back = jnp.where((served > 0.5) & (alive_there > 0.5), theirs - mine[:, :hid], 0.0)
    back = (-2.0 * DIST_WEIGHT * back).astype(BF)
    take = take.astype(BF)
    serve = serve.astype(BF)
    grad_embed = grad_embed + dot(local_high, take, (0, 0)) + dot(local_low, take, (0, 0))
    grad_embed = grad_embed + dot(back, serve, (0, 0))
    grad_mid[:, n_b:] = grad_embed

    low_grad2 = norm_backward(grad_mid[...], result2[...], scale2[...])
    g2_ref[...] = dot(inputs2[...], low_grad2, (1, 1))
    ones = jnp.ones((16, sz.n_mid), BF)
    gb_ref[:, hid : 2 * hid] = dot(ones, low_grad2, (1, 1))
    grad_a[...] = jnp.zeros_like(grad_a)
    tiles_b = n_b // LANES
    for tile in range(sz.n_mid // LANES):
        lane = LANES * tile
        in_b = tile < tiles_b
        columns = sz.b_columns(part, tile) if in_b else pl.ds(aligned(own * part + lane - n_b), LANES)
        marks = pres2[:, columns]
        grad_inputs = dot(w2_ref[...], low_grad2[:, lane : lane + LANES], (1, 0))
        pieces = [grad_inputs[group * c : group * (c + 1)] for c in range(8)]
        high, low = two_parts(jnp.concatenate(pieces[1::2], 0) / slot_totals(marks))
        counts = counts2[WINDOW * tile : WINDOW * (tile + 1), :]
        spread = dot(high, counts, (1, 1)) + dot(low, counts, (1, 1))
        grad_bc[:, lane : lane + LANES] = jnp.concatenate(pieces[0::2], 0)
        if in_b:
            window = pl.ds(a_window(sz, part, tile), WINDOW)
            grad_a[:, window] = grad_a[:, window] + spread
        else:
            grad_bc[:, :n_b] = grad_bc[:, :n_b] + spread

    def first_back(grad, lane):
        low_grad1[:, pl.ds(lane, LANES)] = norm_backward(
            grad, result1[:, pl.ds(lane, LANES)], scale1[:, pl.ds(lane, LANES)]
        )

    def step_a(step, carry):
        lane = aligned(step * LANES)
        first_back(grad_a[:, pl.ds(lane, LANES)], lane)
        return carry

    def step_bc(step, carry):
        lane = aligned(step * LANES)
        first_back(grad_bc[:, pl.ds(lane, LANES)], aligned(n_a + lane))
        return carry

    lax.fori_loop(0, n_a // LANES, step_a, 0)
    lax.fori_loop(0, sz.n_mid // LANES, step_bc, 0)
    g1 = dot(x_ref[...], low_grad1[...], (1, 1))
    ones = jnp.ones((16, sz.n_low), BF)
    gb_ref[:, :hid] = dot(ones, low_grad1[...], (1, 1))
    head_row = dot(jnp.ones((16, own), BF), grad_logits, (1, 1))
    head_row = jnp.concatenate([head_row, jnp.zeros((16, LANES - sz.head), F32)], 1)
    lane_at = lax.broadcasted_iota(jnp.int32, (16, LANES), 1)
    row_at = lax.broadcasted_iota(jnp.int32, (16, LANES), 0)
    sums = three_parts(
        jnp.where(lane_at == 0, ce_total + dist_total, jnp.where(lane_at == 1, seed_count, 0.0))
    )
    for r in range(4):
        target_ref = (keep, send)[r % 2]
        base = sz.pay * (r // 2)
        shard = part ^ r
        rows1 = g1[2 * sz.hold * r : 2 * sz.hold * (r + 1)]
        rows2 = g2_ref[pl.ds(pl.multiple_of(2 * group * shard, 2 * group), 2 * group), :]
        at = base
        for rows in (rows1, rows2):
            for half in range(hid // LANES):
                piece = rows[:, LANES * half : LANES * (half + 1)]
                target_ref[at : at + piece.shape[0], :] = piece.astype(BF)
                at += piece.shape[0]
        target_ref[at : at + sz.head, :] = g3_ref[:, pl.ds(aligned(2 * group * shard), LANES)].astype(BF)
        at += sz.head
        odd = (shard % 2) == 1
        block = aligned((shard // 2) * LANES)
        one = gb_ref[:, pl.ds(block, LANES)]
        two = gb_ref[:, pl.ds(aligned(hid + block), LANES)]
        one = jnp.where(odd, pltpu.roll(one, group, 1), one)
        two = jnp.where(odd, two, pltpu.roll(two, group, 1))
        bias_row = jnp.where(lane_at < group, one, two)
        misc = jnp.where(row_at == 0, bias_row, jnp.where(row_at == 1, head_row, 0.0))
        for i in range(3):
            misc = jnp.where(row_at == 2 + i, sums[i], misc)
        target_ref[at : at + 16, :] = misc.astype(BF)


def backward(sz, messages, pres2, pres3, info, labels, weighting, head_bias, saved, received):
    shape = jax.ShapeDtypeStruct
    return pl.pallas_call(
        functools.partial(backward_kernel, sz),
        out_shape=(shape((2 * sz.pay, LANES), BF), shape((2 * sz.pay, LANES), BF)),
        scratch_shapes=[
            pltpu.VMEM((8 * sz.hold, sz.n_low), BF),
            pltpu.VMEM((2 * sz.hid, sz.hid), BF),
            pltpu.VMEM((2 * sz.hid, LANES), BF),
            pltpu.VMEM((sz.hid, sz.n_a), F32),
            pltpu.VMEM((sz.hid, sz.n_mid), F32),
            pltpu.VMEM((sz.hid, sz.n_mid), F32),
            pltpu.VMEM((sz.hid, sz.n_low), BF),
            pltpu.VMEM((2 * sz.hid, sz.hid), F32),
            pltpu.VMEM((sz.head, 2 * sz.hid), F32),
            pltpu.VMEM((16, 2 * sz.hid), F32),
        ],
        compiler_params=PARAMS,
    )(*messages, pres2, pres3, info, labels, weighting, head_bias, *saved, received)


def add_kernel(sz, own, other, out):
    for i in range(own.shape[0] // sz.pay):
        at = sz.pay * i
        rows = slice(at, at + sz.misc)
        out[rows, :] = (own[rows, :].astype(F32) + other[rows, :].astype(F32)).astype(out.dtype)
        rows = slice(at + sz.misc, at + sz.pay)
        total = own[rows, :].astype(F32) + other[rows, :].astype(F32)
        parts = three_parts(total[2:3] + total[3:4] + total[4:5])
        row_at = lax.broadcasted_iota(jnp.int32, total.shape, 0)
        for j in range(3):
            total = jnp.where(row_at == 2 + j, parts[j], total)
        out[rows, :] = total.astype(out.dtype)


def add_pay(sz, own, other, kind):
    return pl.pallas_call(
        functools.partial(add_kernel, sz),
        out_shape=jax.ShapeDtypeStruct(own.shape, kind),
        compiler_params=PARAMS,
    )(own, other)


def unpacked(sz, grad):
    def wide(at, rows):
        return jnp.concatenate([grad[at : at + rows, :], grad[at + rows : at + 2 * rows, :]], 1)

    one = wide(0, 2 * sz.hold)
    two = wide(sz.rows_one, 2 * sz.group)
    at = sz.rows_one + sz.rows_two
    three = grad[at : at + sz.head, :].T
    misc = grad[sz.misc : sz.misc + 8, :]
    hidden = jnp.concatenate([misc[0:1, : sz.group], misc[0:1, sz.group : 2 * sz.group]], 0)
    return (
        [one[s * sz.hold : s * sz.hold + sz.feat] for s in range(2)],
        [two[s * sz.group : (s + 1) * sz.group] for s in range(2)],
        [three[s * sz.group : (s + 1) * sz.group, : sz.classes] for s in range(2)],
        [hidden],
        [misc[1:2, : sz.classes]],
        misc,
    )


def lamb_kernel(sz, grad, w1, w2, w3, wh, wb, f1, f2, f3, fh, fb, s1, s2, s3, sh, sb, *outs):
    params = (w1, w2, w3, wh, wb)
    firsts = (f1, f2, f3, fh, fb)
    seconds = (s1, s2, s3, sh, sb)
    moments, squares, updates = outs[:5], outs[5:10], outs[10:15]
    sums_ref, totals_ref = outs[15], outs[16]
    grads = unpacked(sz, grad)
    lane_at = lax.broadcasted_iota(jnp.int32, (8, LANES), 1)
    row_at = lax.broadcasted_iota(jnp.int32, (8, LANES), 0)
    sums = jnp.zeros((8, LANES), F32)
    for i in range(5):
        weight_sum = jnp.zeros((1, 1), F32)
        update_sum = jnp.zeros((1, 1), F32)
        for s in range(len(grads[i])):
            at = (s,) if i < 3 else (Ellipsis,)
            g = grads[i][s]
            w = params[i][at]
            m = BETA_ONE * firsts[i][at] + (1.0 - BETA_ONE) * g
            v = BETA_TWO * seconds[i][at] + (1.0 - BETA_TWO) * g * g
            u = (m / (1.0 - BETA_ONE**STEP)) / (jnp.sqrt(v / (1.0 - BETA_TWO**STEP)) + ADAM_EPS) + DECAY_RATE * w
            moments[i][at] = m
            squares[i][at] = v
            updates[i][at] = u
            weight_sum = weight_sum + jnp.sum(jnp.sum(w * w, 0, keepdims=True), 1, keepdims=True)
            update_sum = update_sum + jnp.sum(jnp.sum(u * u, 0, keepdims=True), 1, keepdims=True)
        if i == 4:
            weight_sum = 0.25 * weight_sum
            update_sum = 0.25 * update_sum
        sums = jnp.where((lane_at == i) & (row_at == 0), weight_sum, sums)
        sums = jnp.where((lane_at == i) & (row_at == 1), update_sum, sums)
    sums_ref[...] = sums
    misc = grads[5]
    totals_ref[...] = jnp.broadcast_to(misc[2:3] + misc[3:4] + misc[4:5], (8, LANES))


def lamb(sz, grad, params, firsts, seconds):
    shape = jax.ShapeDtypeStruct
    like = [shape(item.shape, F32) for item in params]
    return pl.pallas_call(
        functools.partial(lamb_kernel, sz),
        out_shape=tuple(like * 3 + [shape((8, LANES), F32)] * 2),
        compiler_params=PARAMS,
    )(grad, *params, *firsts, *seconds)


def step_kernel(own, other, w1, w2, w3, wh, wb, u1, u2, u3, uh, ub, n1, n2, n3, nh, nb, norms_ref):
    norms = jnp.sqrt(own[...] + other[...])
    norms_ref[...] = norms[0:2, 0:5]
    for i, (w, u, n) in enumerate(
        ((w1, u1, n1), (w2, u2, n2), (w3, u3, n3), (wh, uh, nh), (wb, ub, nb))
    ):
        ratio = LEARN_RATE * (norms[0:1, i : i + 1] / norms[1:2, i : i + 1])
        for s in range(w.shape[0] if i < 3 else 1):
            at = (s,) if i < 3 else (Ellipsis,)
            n[at] = w[at] - ratio * u[at]


def take_step(own, other, params, updates):
    shape = jax.ShapeDtypeStruct
    return pl.pallas_call(
        step_kernel,
        out_shape=tuple([shape(item.shape, F32) for item in params] + [shape((2, 5), F32)]),
        compiler_params=PARAMS,
    )(own, other, *params, *updates)


def swap(value, axis, count, bit):
    return lax.ppermute(value, axis, [(i, i ^ bit) for i in range(count)])


def weight_message(sz, w1, w2, w3, hidden_bias):
    one = jnp.pad(w1, ((0, 0), (0, sz.hold - sz.feat), (0, 0))).reshape(2 * sz.hold, sz.hid)
    two = jnp.concatenate([w2[0], w2[1]], 1)
    three = jnp.pad(w3, ((0, 0), (0, 0), (0, LANES - sz.classes)))
    three = jnp.concatenate([three[0], three[1]], 1)
    high = lax.reduce_precision(hidden_bias, 8, 7)
    middle = lax.reduce_precision(hidden_bias - high, 8, 7)
    bias = jnp.stack([high, middle, hidden_bias - high - middle], 1).reshape(6, sz.group).T
    bias = jnp.pad(bias, ((0, 0), (0, LANES - 6)))
    return jnp.concatenate([one, two, three, bias], 1).astype(BF)


def shards(
    features, neighbors_one, present_one, neighbors_two, present_two, neighbors_three, present_three,
    labels, seed_weight, serve_rows, take_seed, fetch_live,
    weight_one, weight_two, weight_three, hidden_bias, head_bias,
    first_one, first_two, first_three, first_hidden, first_head,
    second_one, second_two, second_three, second_hidden, second_head,
):
    sz = Sizes(features, neighbors_one, neighbors_two, neighbors_three, weight_two, weight_three, serve_rows)
    part = lax.axis_index("col")
    mixed = layer_one_means(sz, features, neighbors_one, present_one)
    weights = weight_message(sz, weight_one, weight_two, weight_three, hidden_bias)

    def message(target):
        return jnp.concatenate(
            [
                lax.dynamic_slice_in_dim(mixed, sz.a_start(target), sz.n_a, 1),
                lax.dynamic_slice_in_dim(mixed, sz.b_start(target), sz.n_b, 1),
                lax.dynamic_slice_in_dim(mixed, sz.own * target, sz.own, 1),
                weights,
            ],
            1,
        )

    messages = [message(part)]
    for r in range(1, 4):
        messages.append(swap(message(part ^ r), "col", 4, r))
    alive = jnp.arange(sz.slot, dtype=jnp.int32)[None, :] < fetch_live[:, None]
    info = jnp.stack([serve_rows.reshape(-1), take_seed.reshape(-1), alive.astype(jnp.int32).reshape(-1)], 1)
    saved = forward(sz, messages, neighbors_two, present_two, neighbors_three, present_three, info)
    sent = jnp.broadcast_to(saved[-1].reshape(sz.dp, 1, sz.slot, 3 * sz.hid), (sz.dp, 4, sz.slot, 3 * sz.hid))
    received = lax.all_to_all(
        sent.reshape(4 * sz.slots, 3 * sz.hid), ("dp", "col"), split_axis=0, concat_axis=0, tiled=True
    )
    bias_column = jnp.pad(head_bias, (0, sz.head - sz.classes))[:, None]
    keep, send = backward(
        sz, messages, present_two, present_three, info, labels[None, :], seed_weight[None, :], bias_column, saved, received
    )
    total = add_pay(sz, keep, swap(send, "col", 4, 1), BF)
    grad = add_pay(sz, total[: sz.pay], swap(total[sz.pay :], "col", 4, 2), BF)
    bit = 1
    while bit < sz.dp:
        grad = add_pay(sz, grad, swap(grad, "dp", sz.dp, bit), BF if 2 * bit < sz.dp else F32)
        bit *= 2
    params = (weight_one, weight_two, weight_three, hidden_bias, head_bias[None, :])
    firsts = (first_one, first_two, first_three, first_hidden, first_head[None, :])
    seconds = (second_one, second_two, second_three, second_hidden, second_head[None, :])
    outs = lamb(sz, grad, params, firsts, seconds)
    moments, squares, updates = outs[:5], outs[5:10], outs[10:15]
    sums, totals = outs[15], outs[16]
    pair = sums + swap(sums, "col", 4, 1)
    fresh = take_step(pair, swap(pair, "col", 4, 2), params, updates)
    return (
        *fresh[:4],
        fresh[4][0],
        *moments[:4],
        moments[4][0],
        *squares[:4],
        squares[4][0],
        fresh[5],
        totals[0, 0],
        totals[0, 1],
    )


def solution(mesh):
    wide = P(None, "col", None)
    tree = [wide, wide, wide, P(None, "col"), P()]
    return jax.shard_map(
        shards,
        mesh=mesh,
        in_specs=(
            P("col", "dp"),
            *[P(None, "dp")] * 6,
            P("dp"),
            P("dp"),
            P("dp", None),
            P("dp", None),
            P("dp"),
            *tree,
            *tree,
            *tree,
        ),
        out_specs=(*tree, *tree, *tree, P(), P(), P()),
        check_vma=False,
    )
```

```python
import functools

import jax
import jax.numpy as jnp
from jax import lax
from jax.experimental import pallas as pl
from jax.experimental.pallas import tpu as pltpu
from jax.sharding import PartitionSpec as P

REACH = 64
STEP = 5
DIST_WEIGHT = 1.0
ROW_EPS = 1e-06
LEARN_RATE = 0.5
BETA_ONE = 0.9
BETA_TWO = 0.999
ADAM_EPS = 1e-06
DECAY_RATE = 0.01

BF = jnp.bfloat16
F32 = jnp.float32
LANES = 128
WINDOW = 768
SENTINEL = 4.0
MIB = 2**20
LOSS_BITS = 14
FIRST_MIB = 8
MEAN_MIB = 8
SEEDS_MIB = 16
REST_MIB = 28
BACK_MIB = 12


def cost(micros):
    return pl.CostEstimate(flops=int(micros * 10**9), bytes_accessed=1, transcendentals=0)


def call(kernel, outs, scratch, mib, *args, far_in=(), far_out=(), copies=0, micros=1):
    near = pl.BlockSpec(memory_space=pltpu.VMEM)
    far = pl.BlockSpec(memory_space=pltpu.HBM)
    scratch = [pltpu.VMEM(shape, kind) for shape, kind in scratch]
    args = [pltpu.with_memory_space_constraint(a, pltpu.HBM) if i in far_in else a for i, a in enumerate(args)]
    return pl.pallas_call(
        kernel,
        in_specs=[far if i in far_in else near for i in range(len(args))],
        out_specs=tuple(far if i in far_out else near for i in range(len(outs))),
        out_shape=tuple(
            pltpu.HBM(shape, kind) if i in far_out else jax.ShapeDtypeStruct(shape, kind)
            for i, (shape, kind) in enumerate(outs)
        ),
        scratch_shapes=scratch + ([pltpu.SemaphoreType.DMA((copies,))] if copies else []),
        compiler_params=pltpu.CompilerParams(vmem_limit_bytes=mib * MIB),
        cost_estimate=cost(micros),
    )(*args)


def start_copies(pairs, sems, first=0):
    copies = [pltpu.make_async_copy(src, dst, sems.at[first + i]) for i, (src, dst) in enumerate(pairs)]
    for copy in copies:
        copy.start()
    return copies


def wait_all(copies):
    for copy in copies:
        copy.wait()


class Sizes:
    def __init__(self, features, neighbors_one, neighbors_two, neighbors_three, weight_two, weight_three, serve_rows):
        self.feat = features.shape[0]
        self.main = self.feat - 1
        self.hold = 32
        self.base = features.shape[1]
        self.low = neighbors_one.shape[1]
        self.mid = neighbors_two.shape[1]
        self.seeds = neighbors_three.shape[1]
        self.hid = weight_two.shape[2]
        self.group = weight_two.shape[1]
        self.classes = weight_three.shape[2]
        self.head = -(-self.classes // 16) * 16
        self.own = self.seeds // 4
        self.n_b = 4 * self.own + 2 * LANES
        self.n_a = 16 * self.own + 6 * LANES
        self.n_mid = self.n_b + self.own
        self.n_low = self.n_a + self.n_mid
        self.tiles_b = self.n_b // LANES
        self.tiles_mid = self.n_mid // LANES
        self.tiles_low = self.n_low // LANES
        self.slots = serve_rows.shape[0] * serve_rows.shape[1]
        self.slot = serve_rows.shape[1]
        self.dp = serve_rows.shape[0]
        self.rows_one = 2 * 2 * self.hold
        self.rows_two = 4 * self.group
        self.at_three = self.rows_one + self.rows_two
        self.misc = self.at_three + self.head
        self.pay = self.misc + 16
        self.blocks = -(-self.pay // self.main)
        self.message_a = self.pair_lanes(self.n_a)
        self.message_b = self.pair_lanes(self.n_mid)
        self.full_b = self.message_b + LANES * self.blocks
        self.tiles_b_all = 16 * self.own // LANES + 1
        self.count_rows = WINDOW + 16
        hid, at = self.hid, self.n_mid
        places = {}
        for name, lanes in (
            ("turned1", hid), ("turned2", 2 * hid), ("weight2", 2 * hid), ("weight3", 2 * LANES), ("turned3", 2 * hid),
            ("states", self.n_b), ("embed", 2 * self.own), ("inputs2", 2 * self.own),
        ):
            places[name] = at
            at += lanes
        self.low_lanes = at
        at = 0
        for name, lanes in (("result1", self.n_mid), ("result2", self.own), ("bias", 2 * LANES)):
            places[name] = at
            at += lanes
        self.high_lanes = at
        at = 0
        for name, lanes in (("g1", hid), ("g2", 2 * hid), ("g3", 2 * hid), ("grad_b", self.n_b), ("grad_embed", self.own)):
            places[name] = at
            at += lanes
        self.part_lanes = at
        self.at = places

    def pair_lanes(self, lanes):
        return 2 * lanes + LANES * -(-2 * lanes // LANES // self.main)

    def a_start(self, part):
        return jnp.clip(16 * self.own * part - 3 * LANES, 0, self.low - self.n_a)

    def b_start(self, part):
        return jnp.maximum(4 * self.own * part - LANES, 0)

    def b_columns(self, part, tile):
        return pl.ds(aligned(jnp.minimum(self.b_start(part) + LANES * tile, self.mid - LANES)), LANES)

    def mid_columns(self, part, tile):
        if tile < self.tiles_b:
            return self.b_columns(part, tile)
        return pl.ds(aligned(self.own * part + LANES * (tile - self.tiles_b)), LANES)

    def ranges(self, part):
        return (
            (self.a_start(part), 0, self.n_a),
            (self.b_start(part), self.n_a, self.n_b),
            (self.own * part, self.n_a + self.n_b, self.own),
        )


def dot(a, b, over):
    return lax.dot_general(a, b, (((over[0],), (over[1],)), ((), ())), preferred_element_type=F32)


def two_parts(value):
    high = value.astype(BF)
    return high, (value - high.astype(F32)).astype(BF)


def three_parts(value):
    high = value.astype(BF).astype(F32)
    rest = value - high
    middle = rest.astype(BF).astype(F32)
    return high, middle, (rest - middle).astype(BF).astype(F32)


def aligned(value):
    return pl.multiple_of(value, LANES)


def sigmoid(value):
    return 1.0 / (1.0 + jnp.exp(-value))


def unpack_tile(sz, message, tail, tile):
    spare = jnp.zeros((sz.hold - sz.feat, LANES), F32)
    main = message[:, LANES * tile : LANES * (tile + 1)].astype(F32)
    return jnp.concatenate([main, tail[tile : tile + 1, :], spare], 0).astype(BF)


def mean_tiles(sz, tiles, feat_ref, nbr_ref, pres_ref, mean_ref, tail_ref, base_ref, code_ref, count_ref):
    last = feat_ref.shape[1] // LANES - 6
    slots = nbr_ref.shape[0]
    base_ref[...] = jnp.zeros_like(base_ref)
    if tiles % 8:
        code_ref[...] = jnp.full_like(code_ref, -1)
        count_ref[...] = jnp.ones_like(count_ref)
    for tile in range(feat_ref.shape[1] // LANES):
        row = feat_ref[:, LANES * tile : LANES * (tile + 1)].astype(F32)
        base_ref[8 + tile : 9 + tile, :] = row[sz.main : sz.feat]

    def one_tile(step, carry):
        lane = aligned(step * LANES)
        present = pres_ref[:, pl.ds(lane, LANES)]
        valid = present.astype(F32)
        counts = jnp.maximum(jnp.sum(valid, 0, keepdims=True), 1.0)
        first = jnp.clip(4 * step - 1, 0, last)
        links = nbr_ref[:, pl.ds(lane, LANES)]
        code = jnp.where(present > 0, links, -1)
        count_ref[pl.ds(step, 1), :] = counts
        for slot in range(slots):
            code_ref[slot, pl.ds(step, 1), :] = code[slot : slot + 1]
        local = links - first * LANES
        piece = local >> 7
        spot = local & 127
        sources = [
            feat_ref[:, pl.ds(aligned((first + j) * LANES), LANES)].astype(F32) for j in range(6)
        ]
        totals = [jnp.zeros((8, LANES), F32) for _ in range(sz.main // 8)]
        for slot in range(slots):
            spots = jnp.broadcast_to(spot[slot : slot + 1], (8, LANES))
            pieces = jnp.broadcast_to(piece[slot : slot + 1], (8, LANES))
            marks = jnp.broadcast_to(valid[slot : slot + 1], (8, LANES))
            for h in range(sz.main // 8):
                taken = None
                for j in range(6):
                    found = jnp.take_along_axis(
                        sources[j][8 * h : 8 * h + 8], spots, axis=1, mode="promise_in_bounds"
                    )
                    taken = found if j == 0 else jnp.where(pieces == j, found, taken)
                totals[h] = totals[h] + taken * marks
        mean_ref[:, pl.ds(lane, LANES)] = (jnp.concatenate(totals, 0) / counts).astype(BF)
        return carry

    lax.fori_loop(0, tiles // 4 * 4, one_tile, 0, unroll=4)
    for step in range(tiles // 4 * 4, tiles):
        one_tile(step, 0)
    sub = lax.broadcasted_iota(jnp.int32, (8, LANES), 0)

    for block in range(-(-tiles // 8)):
        total = jnp.zeros((8, LANES), F32)
        for slot in range(slots):
            code = code_ref[slot, 8 * block : 8 * (block + 1), :]
            piece = (code >> 7) - (4 * (8 * block + sub) - 1)
            taken = None
            for j in range(6):
                source = base_ref[pl.ds(8 + 32 * block - 1 + j, 8, stride=4), :]
                found = jnp.take_along_axis(source, code & 127, axis=1, mode="promise_in_bounds")
                taken = found if j == 0 else jnp.where(piece == j, found, taken)
            total = total + jnp.where(code >= 0, taken, 0.0)
        tail_ref[8 * block : 8 * (block + 1), :] = total / count_ref[8 * block : 8 * (block + 1), :]


def pack_pair(sz, ranges, feat_ref, base_ref, mean_ref, tail_ref, turn_ref, out_ref):
    turn_ref[...] = jnp.zeros_like(turn_ref)
    base = ranges[0][1]
    lanes = sum(count for _, _, count in ranges)
    tiles = lanes // LANES
    for first, at, count in ranges:
        at = at - base
        source = pl.ds(aligned(first), count)
        out_ref[:, at : at + count] = feat_ref[: sz.main, source]
        out_ref[:, lanes + at : lanes + at + count] = mean_ref[: sz.main, source]
        at, rows = at // LANES, count // LANES
        turn_ref[at : at + rows, :] = base_ref[pl.ds(8 + first // LANES, rows), :]
        turn_ref[tiles + at : tiles + at + rows, :] = tail_ref[pl.ds(first // LANES, rows), :]
    for block in range(-(-2 * tiles // sz.main)):
        at = 2 * lanes + LANES * block
        out_ref[:, at : at + LANES] = turn_ref[sz.main * block : sz.main * (block + 1), :].astype(BF)


def own_pair(sz, ranges, feat_ref, mean_ref, tail_ref, own_ref):
    spare = jnp.zeros((sz.hold - sz.feat, LANES), F32)
    base = ranges[0][1]
    for start, at, count in ranges:
        for tile in range(count // LANES):
            lanes = pl.ds(aligned(start + LANES * tile), LANES)
            out_lanes = slice(at - base + LANES * tile, at - base + LANES * (tile + 1))
            own = [feat_ref[:, lanes].astype(F32), spare]
            own_ref[: sz.hold, out_lanes] = jnp.concatenate(own, 0).astype(BF)
            tail = tail_ref[pl.ds(start // LANES + tile, 1), :]
            average = [mean_ref[:, lanes].astype(F32), tail, spare]
            own_ref[sz.hold :, out_lanes] = jnp.concatenate(average, 0).astype(BF)


def mean_scratch(sz, tiles, slots):
    return [
        ((sz.main, LANES * tiles), BF),
        ((-(-tiles // 8) * 8, LANES), F32),
        ((2 * sz.main, LANES), F32),
        ((4 * -(-tiles // 8) * 8 + 16, LANES), F32),
        ((slots, -(-tiles // 8) * 8, LANES), jnp.int32),
        ((-(-tiles // 8) * 8, LANES), F32),
    ]


def unpack_pair(sz, message, r, lanes, turn_ref, out_ref):
    tiles = lanes // LANES
    for block in range(-(-2 * tiles // sz.main)):
        at = 2 * lanes + LANES * block
        turn_ref[sz.main * block : sz.main * (block + 1), :] = message[:, at : at + LANES].astype(F32)
    tail = turn_ref[...]
    for tile in range(2 * tiles):
        row = sz.hold * (r if tile < tiles else 4 + r)
        at = LANES * (tile % tiles)
        out_ref[row : row + sz.hold, at : at + LANES] = unpack_tile(sz, message, tail, tile)


def first_kernel(
    sz, features, neighbors, present, w1_in, w2_in, w3_in, wh_in, own_b, packed, m1, m2, m3,
    feat_ref, nbr_ref, pres_ref, w1, w2, w3, wh, own_ref,
    mean_ref, tail_ref, turn_ref, base_ref, code_ref, count_ref, one_ref, three_ref, pack, sems,
):
    part = lax.axis_index("col")
    rows = pl.ds(0, nbr_ref.shape[1])
    copies = start_copies(
        (
            (features.at[:, pl.ds(0, feat_ref.shape[1])], feat_ref),
            (neighbors.at[:, rows], nbr_ref),
            (present.at[:, rows], pres_ref),
            (w1_in, w1),
            (w2_in, w2),
            (w3_in, w3),
            (wh_in, wh),
        ),
        sems,
    )
    wait_all(copies[:3])
    mean_tiles(sz, sz.tiles_b_all, feat_ref, nbr_ref, pres_ref, mean_ref, tail_ref, base_ref, code_ref, count_ref)
    wait_all(copies[3:])
    one_ref[...] = jnp.zeros_like(one_ref)
    three_ref[...] = jnp.zeros_like(three_ref)
    for s in range(2):
        for f in range(sz.feat):
            one_ref[s * sz.hold + f : s * sz.hold + f + 1, :] = w1[f, s : s + 1, :]
        for c in range(sz.classes):
            three_ref[c : c + 1, s * sz.group : (s + 1) * sz.group] = w3[c, s : s + 1, :]
    at = 0
    for half in range(sz.hid // LANES):
        pack[at : at + 2 * sz.hold, :] = one_ref[:, LANES * half : LANES * (half + 1)]
        at += 2 * sz.hold
    for half in range(sz.hid // LANES):
        for s in range(2):
            pack[at : at + sz.group, :] = w2[s, :, LANES * half : LANES * (half + 1)]
            at += sz.group
    pack[at : at + sz.head, :] = three_ref[...]
    row = jnp.concatenate([wh[0:1, :], wh[1:2, :]], 1)
    row_at = lax.broadcasted_iota(jnp.int32, (16, LANES), 0)
    misc = jnp.zeros((16, LANES), F32)
    for i, piece in enumerate(three_parts(row)):
        misc = jnp.where(row_at == i, piece, misc)
    pack[sz.misc : sz.pay, :] = misc
    pack[sz.pay :, :] = jnp.zeros((sz.main * sz.blocks - sz.pay, LANES), F32)
    store = start_copies(((pack, packed),), sems, 7)
    for block in range(sz.blocks):
        at = sz.message_b + LANES * block
        piece = pack[sz.main * block : sz.main * (block + 1), :].astype(BF)
        m1[:, at : at + LANES] = piece
        m2[:, at : at + LANES] = piece
    own_pair(sz, sz.ranges(part)[1:], feat_ref, mean_ref, tail_ref, own_ref)
    store += start_copies(((own_ref, own_b),), sems, 8)
    for r, out in ((1, m1), (2, m2), (3, m3)):
        pack_pair(sz, sz.ranges(part ^ r)[1:], feat_ref, base_ref, mean_ref, tail_ref, turn_ref, out)
    wait_all(store)


def first_messages(sz, features, neighbors, present, w1, w2, w3, hidden):
    rows = LANES * sz.tiles_b_all
    bases = min(4 * rows + LANES, sz.base)
    slots = neighbors.shape[0]
    return call(
        functools.partial(first_kernel, sz),
        [
            ((2 * sz.hold, sz.n_mid), BF),
            ((sz.main * sz.blocks, LANES), F32),
            ((sz.main, sz.full_b), BF),
            ((sz.main, sz.full_b), BF),
            ((sz.main, sz.message_b), BF),
        ],
        [
            ((sz.feat, bases), BF),
            ((slots, rows), jnp.int32),
            ((slots, rows), jnp.int32),
            (w1.shape, F32),
            (w2.shape, F32),
            (w3.shape, F32),
            (hidden.shape, F32),
            ((2 * sz.hold, sz.n_mid), BF),
            *mean_scratch(sz, sz.tiles_b_all, slots),
            ((2 * sz.hold, sz.hid), F32),
            ((sz.head, LANES), F32),
            ((sz.main * sz.blocks, LANES), F32),
        ],
        FIRST_MIB,
        features,
        neighbors,
        present,
        w1,
        w2,
        w3,
        hidden,
        far_in=range(7),
        far_out=(0, 1),
        copies=9,
        micros=4,
    )


def mean_kernel(
    sz, feat_ref, nbr_ref, pres_ref, own_a, a1, a2, a3,
    mean_ref, tail_ref, turn_ref, base_ref, code_ref, count_ref, own_ref, sems,
):
    part = lax.axis_index("col")
    tiles = sz.low // LANES
    mean_tiles(sz, tiles, feat_ref, nbr_ref, pres_ref, mean_ref, tail_ref, base_ref, code_ref, count_ref)
    own_pair(sz, sz.ranges(part)[:1], feat_ref, mean_ref, tail_ref, own_ref)
    store = start_copies(((own_ref, own_a),), sems)
    for r, out in ((1, a1), (2, a2), (3, a3)):
        pack_pair(sz, sz.ranges(part ^ r)[:1], feat_ref, base_ref, mean_ref, tail_ref, turn_ref, out)
    wait_all(store)


def mean_messages(sz, features, neighbors, present):
    return call(
        functools.partial(mean_kernel, sz),
        [((2 * sz.hold, sz.n_a), BF)] + [((sz.main, sz.message_a), BF)] * 3,
        mean_scratch(sz, sz.low // LANES, neighbors.shape[0]) + [((2 * sz.hold, sz.n_a), BF)],
        MEAN_MIB,
        features,
        neighbors,
        present,
        far_out=(0,),
        copies=1,
        micros=6,
    )


def window_counts(local, rows):
    spots = lax.broadcasted_iota(jnp.int32, (256, LANES), 0).astype(F32).astype(BF)
    blocks = []
    for first in range(0, rows, 256):
        place = local - first
        place = jnp.where((place >= 0) & (place < 256), place, -1).astype(F32)
        counts = jnp.zeros((256, LANES), BF)
        for slot in range(local.shape[0]):
            row = jnp.broadcast_to(place[slot : slot + 1], (16, LANES)).astype(BF)
            row = jnp.concatenate([row] * 16, 0)
            counts = counts + jnp.where(row == spots, jnp.bfloat16(1.0), jnp.bfloat16(0.0))
        blocks.append(counts)
    return jnp.concatenate(blocks, 0)


def slot_totals(present):
    return jnp.maximum(jnp.sum(present.astype(F32), 0, keepdims=True), 1.0)


def a_window(sz, part, tile):
    first = 4 * sz.b_start(part) + 4 * LANES * tile - LANES - sz.a_start(part)
    return aligned(jnp.clip(first, 0, sz.n_a - WINDOW))


def counts_kernel(sz, nbr2, pres2, nbr3, pres3, out, counts, sems):
    part = lax.axis_index("col")
    stores = []
    for tile in range(sz.tiles_mid + sz.own // LANES):
        start = sz.b_start(part)
        links, valid, slot = (nbr2, pres2, tile) if tile < sz.tiles_mid else (nbr3, pres3, tile - sz.tiles_mid)
        if tile < sz.tiles_mid:
            columns = sz.mid_columns(part, tile)
        else:
            columns = pl.ds(aligned(sz.own * part + LANES * slot), LANES)
        if tile < sz.tiles_b:
            start = sz.a_start(part) + a_window(sz, part, tile)
        at = sz.count_rows * tile
        marks = valid[:, columns]
        local = jnp.where(marks > 0, links[:, columns] - start, -1)
        counts[at : at + WINDOW, :] = window_counts(local, WINDOW)
        counts[at + WINDOW : at + sz.count_rows, :] = jnp.broadcast_to(slot_totals(marks), (16, LANES)).astype(BF)
        rows = pl.ds(at, sz.count_rows)
        stores += start_copies(((counts.at[rows, :], out.at[rows, :]),), sems, tile)
    wait_all(stores)


def make_counts(sz, nbr2, pres2, nbr3, pres3):
    tiles = sz.tiles_mid + sz.own // LANES
    shape = (sz.count_rows * tiles, LANES)
    return call(
        functools.partial(counts_kernel, sz),
        [(shape, BF)],
        [(shape, BF)],
        6,
        nbr2,
        pres2,
        nbr3,
        pres3,
        far_out=(0,),
        copies=tiles,
        micros=4,
    )[0]


def tile_counts(sz, counts, tile):
    at = sz.count_rows * tile
    totals = counts[at + WINDOW : at + WINDOW + 16, :].astype(F32)[0:1]
    return counts[at : at + WINDOW, :], totals


def first_layer(weight, inputs, bias):
    result = dot(weight, inputs, (1, 0)) + bias
    active = result * sigmoid(result)
    scale = lax.rsqrt(jnp.sum(active * active, 0, keepdims=True) + ROW_EPS)
    return result, scale, active * scale


def join_inputs(sz, own, average):
    pieces = []
    for c in range(4):
        pieces.append(own[sz.group * c : sz.group * (c + 1)])
        pieces.append(average[sz.group * c : sz.group * (c + 1)])
    return jnp.concatenate(pieces, 0)


def norm_backward(grad, result, scale):
    gate = sigmoid(result)
    active = result * gate
    inner = jnp.sum(grad * active, 0, keepdims=True)
    grad_active = scale * grad - active * (scale * scale * scale * inner)
    return (grad_active * gate * (1.0 + result * (1.0 - gate))).astype(BF)


def split_inputs(sz, grad):
    pieces = [grad[sz.group * c : sz.group * (c + 1)] for c in range(8)]
    return jnp.concatenate(pieces[0::2], 0), jnp.concatenate(pieces[1::2], 0)


def row_sums(grad):
    return dot(jnp.ones((16, grad.shape[1]), BF), grad, (1, 1))


def spread(sz, scaled, counts):
    high, low = two_parts(scaled)
    total = dot(jnp.concatenate([high, low], 0), counts, (1, 1))
    return total[: sz.hid] + total[sz.hid :]


def halves(ref, at, lanes):
    return jnp.concatenate([ref[:, at : at + lanes], ref[:, at + lanes : at + 2 * lanes]], 0)


def store_halves(ref, at, lanes, value):
    rows = value.shape[0] // 2
    ref[:rows, at : at + lanes] = value[:rows]
    ref[:rows, at + lanes : at + 2 * lanes] = value[rows:]


def seed_picks(sz, info, part):
    spots = lax.broadcasted_iota(jnp.int32, (sz.slots, sz.own), 1) + sz.own * part
    serve = jnp.where(info[:, 0:1] == spots, 1.0, 0.0)
    take = jnp.where(info[:, 1:2] == spots, 1.0, 0.0)
    return serve, take, jnp.sum(serve, 1, keepdims=True), jnp.sum(take, 1, keepdims=True)


def seeds_kernel(
    sz, own_b, packed, s1, s2, s3, passed, counts, info_in,
    low_out, high_out, sent,
    xb, pack, m1, m2, m3, p3, window_ref, info, low, high, turn_ref, w1_ref, w2_ref, states, sems,
):
    part = lax.axis_index("col")
    own, hid, n_b, group, hold, at = sz.own, sz.hid, sz.n_b, sz.group, sz.hold, sz.at
    n_mid = sz.n_mid
    copies = start_copies(
        (
            (packed, pack),
            (passed.at[:, pl.ds(sz.message_b, LANES * sz.blocks)], p3),
            (s1, m1),
            (s2, m2),
            (s3, m3),
            (own_b, xb),
            (counts.at[pl.ds(sz.count_rows * sz.tiles_b, sz.count_rows * (own // LANES)), :], window_ref),
            (info_in, info),
        ),
        sems,
    )
    wait_all(copies[:4])
    for r, (message, first_lane) in enumerate(((None, 0), (m1, sz.message_b), (m2, sz.message_b), (p3, 0))):
        for block in range(sz.blocks if r else 0):
            first = first_lane + LANES * block
            pack[sz.main * block : sz.main * (block + 1), :] = message[:, first : first + LANES].astype(F32)
        shard = part ^ r
        for half in range(hid // LANES):
            lanes = slice(LANES * half, LANES * (half + 1))
            for s in range(2):
                first = 2 * hold * half + hold * s
                w1_ref[4 * hold * s + hold * r : 4 * hold * s + hold * (r + 1), lanes] = pack[first : first + hold, :]
            first = sz.rows_one + 2 * group * half
            row = pl.multiple_of(2 * group * shard, 2 * group)
            w2_ref[pl.ds(row, 2 * group), lanes] = pack[first : first + 2 * group, :]
        low[: sz.head, pl.ds(aligned(at["turned3"] + 2 * group * shard), LANES)] = pack[sz.at_three : sz.misc, :].astype(BF)
        misc = pack[sz.misc : sz.misc + 8, :]
        column = jnp.broadcast_to(misc[0:1] + misc[1:2] + misc[2:3], (LANES, LANES)).T
        row = pl.multiple_of(group * shard, group)
        for layer in range(2):
            lanes = slice(at["bias"] + LANES * layer, at["bias"] + LANES * (layer + 1))
            high[pl.ds(row, group), lanes] = column[group * layer : group * (layer + 1)]
    turned1 = w1_ref[...].T.astype(BF)
    turned2 = w2_ref[...].T.astype(BF)
    low[:, at["turned1"] : at["turned1"] + hid] = turned1
    low[:, at["turned2"] : at["turned2"] + 2 * hid] = turned2
    store_halves(low, at["weight2"], hid, w2_ref[...].astype(BF))
    weight3 = low[: sz.head, at["turned3"] : at["turned3"] + 2 * hid].astype(F32).T
    weight3 = jnp.concatenate([weight3, jnp.zeros((2 * hid, LANES - sz.head), F32)], 1)
    store_halves(low, at["weight3"], LANES, weight3.astype(BF))

    def piece(lanes, count):
        return (low.at[:, pl.ds(lanes, count)], low_out.at[:, pl.ds(lanes, count)])

    stores = start_copies((piece(n_mid, at["states"] - n_mid),), sems, 8)
    wait_all(copies[4:])
    low[:hold, :n_mid] = xb[:hold, :]
    low[4 * hold : 5 * hold, :n_mid] = xb[hold:, :]
    for r, message in ((1, m1), (2, m2), (3, m3)):
        unpack_pair(sz, message, r, n_mid, turn_ref, low)
    stores += start_copies((piece(0, n_mid),), sems, 9)
    bias1 = high[:hid, at["bias"] : at["bias"] + LANES]
    bias2 = high[:hid, at["bias"] + LANES : at["bias"] + 2 * LANES]
    for tile in range(sz.tiles_mid):
        lanes = slice(LANES * tile, LANES * (tile + 1))
        result, scale, state = first_layer(turned1, low[:, lanes], bias1)
        high[:hid, lanes] = result
        high[hid:, lanes] = jnp.broadcast_to(scale, (8, LANES))
        upper, lower = two_parts(state)
        states[:hid, lanes] = upper
        states[hid:, lanes] = lower
    low[:, at["states"] : at["states"] + n_b] = states[:hid, :n_b]
    for tile in range(own // LANES):
        window, totals = tile_counts(sz, window_ref, tile)
        total = dot(states[:, :n_b], window, (1, 0))
        average = ((total[:hid] + total[hid:]) / totals).astype(BF)
        x = join_inputs(sz, states[:hid, n_b + LANES * tile : n_b + LANES * (tile + 1)], average)
        first = at["inputs2"] + LANES * tile
        low[:, first : first + LANES] = x[:hid]
        low[:, first + own : first + own + LANES] = x[hid:]
        result, scale, state = first_layer(turned2, x, bias2)
        first = at["result2"] + LANES * tile
        high[:hid, first : first + LANES] = result
        high[hid:, first : first + LANES] = jnp.broadcast_to(scale, (8, LANES))
        upper, lower = two_parts(state)
        first = at["embed"] + LANES * tile
        low[:, first : first + LANES] = upper
        low[:, first + own : first + own + LANES] = lower
    tail = (piece(at["states"], sz.low_lanes - at["states"]), (high, high_out))
    stores += start_copies(tail, sems, 10)
    serve, take, _, owned = seed_picks(sz, info, part)
    value = sent_rows(sz, low, at["embed"], serve, take)
    dead = (owned > 0.5) & (info[:, 2:3] == 0)
    lane_at = lax.broadcasted_iota(jnp.int32, (sz.slots, 3 * hid), 1)
    value = jnp.where((lane_at == hid) & dead, SENTINEL, value)
    value = value.reshape(sz.dp, 1, sz.slot, 3 * hid)
    value = jnp.broadcast_to(value, (sz.dp, 4, sz.slot, 3 * hid))
    sent[...] = value.reshape(4 * sz.slots, 3 * hid).astype(BF)
    wait_all(stores)


def sent_rows(sz, low, at, serve, take):
    embed_high = low[:, at : at + sz.own]
    embed_low = low[:, at + sz.own : at + 2 * sz.own]
    take = take.astype(BF)
    return jnp.concatenate(
        [dot(serve.astype(BF), embed_high, (1, 1)), dot(take, embed_high, (1, 1)), dot(take, embed_low, (1, 1))], 1
    )


def seeds_forward(sz, messages, counts, info):
    hid = sz.hid
    tail = (sz.main, LANES * sz.blocks)
    return call(
        functools.partial(seeds_kernel, sz),
        [
            ((hid, sz.low_lanes), BF),
            ((hid + 8, sz.high_lanes), F32),
            ((4 * sz.slots, 3 * hid), BF),
        ],
        [
            ((2 * sz.hold, sz.n_mid), BF),
            ((sz.main * sz.blocks, LANES), F32),
            ((sz.main, sz.full_b), BF),
            ((sz.main, sz.full_b), BF),
            ((sz.main, sz.message_b), BF),
            (tail, BF),
            ((sz.count_rows * (sz.own // LANES), LANES), BF),
            (info.shape, jnp.int32),
            ((hid, sz.low_lanes), BF),
            ((hid + 8, sz.high_lanes), F32),
            ((2 * sz.main, LANES), F32),
            ((8 * sz.hold, hid), F32),
            ((2 * hid, hid), F32),
            ((2 * hid, sz.n_mid), BF),
        ],
        SEEDS_MIB,
        *messages,
        counts,
        info,
        far_in=range(8),
        micros=4,
        far_out=(0, 1),
        copies=12,
    )


def rest_kernel(
    sz, low_in, high_in, counts_in, own_a, v1, v2, v3, labels_in, weighting_in, head_in, part_out,
    labels, weighting, head_bias, low, xa, bias, counts, xo, a1, a2, a3, turn_ref,
    states, states2, result1, scale1, inputs2, result2, scale2, grad_a, low_grad, part_ref, sems,
):
    part = lax.axis_index("col")
    own, hid, n_a, n_b, hold = sz.own, sz.hid, sz.n_a, sz.n_b, sz.hold
    at = dict(sz.at)
    for name in ("turned1", "turned2", "weight2", "weight3", "turned3", "states", "embed"):
        at[name] -= sz.n_mid
    lanes = at["embed"] + own
    copies = start_copies(
        (
            (own_a, xo),
            (v1, a1),
            (v2, a2),
            (v3, a3),
            (low_in.at[:, pl.ds(sz.n_mid, hid)], low.at[:, pl.ds(0, hid)]),
            (high_in.at[:, pl.ds(sz.at["bias"], 2 * LANES)], bias),
            (low_in.at[:, pl.ds(sz.n_mid + hid, lanes - hid)], low.at[:, pl.ds(hid, lanes - hid)]),
            (counts_in, counts),
            (labels_in, labels),
            (weighting_in, weighting),
            (head_in, head_bias),
        ),
        sems,
    )
    wait_all(copies[:4])
    xa[:hold, :] = xo[:hold, :]
    xa[4 * hold : 5 * hold, :] = xo[hold:, :]
    for r, message in ((1, a1), (2, a2), (3, a3)):
        unpack_pair(sz, message, r, n_a, turn_ref, xa)
    wait_all(copies[4:6])
    turned1 = low[:, at["turned1"] : at["turned1"] + hid]
    bias1 = bias[:hid, :LANES]
    bias2 = bias[:hid, LANES:]

    def forward_step(index, carry):
        lanes = pl.ds(aligned(index * LANES), LANES)
        result, scale, state = first_layer(turned1, xa[:, lanes], bias1)
        result1[:, lanes] = result
        scale1[:, lanes] = scale
        upper, lower = two_parts(state)
        states[:hid, lanes] = upper
        states[hid:, lanes] = lower
        return carry

    lax.fori_loop(0, n_a // LANES, forward_step, 0, unroll=2)
    wait_all(copies[6:])
    turned2 = low[:, at["turned2"] : at["turned2"] + 2 * hid]
    for tile in range(sz.tiles_b):
        lanes = slice(LANES * tile, LANES * (tile + 1))
        window, totals = tile_counts(sz, counts, tile)
        total = dot(states[:, pl.ds(a_window(sz, part, tile), WINDOW)], window, (1, 0))
        average = ((total[:hid] + total[hid:]) / totals).astype(BF)
        x = join_inputs(sz, low[:, at["states"] + LANES * tile : at["states"] + LANES * (tile + 1)], average)
        inputs2[:, lanes] = x
        result, scale, state = first_layer(turned2, x, bias2)
        result2[:, lanes] = result
        scale2[:, lanes] = scale
        upper, lower = two_parts(state)
        states2[:hid, lanes] = upper
        states2[hid:, lanes] = lower
    counts3, totals3 = tile_counts(sz, counts, sz.tiles_mid)
    total = dot(states2[...], counts3, (1, 0))
    average = ((total[:hid] + total[hid:]) / totals3).astype(BF)
    inputs3 = join_inputs(sz, low[:, at["embed"] : at["embed"] + own], average)

    columns = pl.ds(aligned(own * part), own)
    classes = lax.broadcasted_iota(jnp.int32, (sz.head, own), 0)
    head_row = jnp.concatenate([head_bias[...], jnp.zeros((1, LANES - sz.classes), F32)], 1)
    head_column = jnp.broadcast_to(head_row, (LANES, LANES)).T[: sz.head]
    logits = dot(low[: sz.head, at["turned3"] : at["turned3"] + 2 * hid], inputs3, (1, 0)) + head_column
    logits = jnp.where(classes < sz.classes, logits, -1e30)
    highest = jnp.max(logits, 0, keepdims=True)
    expo = jnp.exp(logits - highest)
    totals = jnp.sum(expo, 0, keepdims=True)
    hit = classes == labels[:, columns]
    weights = weighting[:, columns].astype(F32)
    target = jnp.sum(jnp.where(hit, logits, 0.0), 0, keepdims=True)
    ce_total = jnp.sum(weights * (highest + jnp.log(totals) - target), 1, keepdims=True)
    seed_count = jnp.sum(weights, 1, keepdims=True)
    grad_logits = (weights * (expo / totals - jnp.where(hit, 1.0, 0.0))).astype(BF)
    g3 = at["g3"]
    part_ref[: sz.head, g3 : g3 + 2 * hid] = dot(grad_logits, inputs3, (1, 1))
    head_sums = jnp.concatenate([row_sums(grad_logits), jnp.zeros((16, LANES - sz.head), F32)], 1)
    part_ref[sz.head + 16 : sz.head + 32, g3 : g3 + LANES] = head_sums
    lane_at = lax.broadcasted_iota(jnp.int32, (16, LANES), 1)
    sums = jnp.where(lane_at == 0, ce_total, jnp.where(lane_at == 1, seed_count, 0.0))
    part_ref[sz.head + 16 : sz.head + 32, g3 + LANES : g3 + 2 * LANES] = sums
    own_part, average_part = split_inputs(sz, dot(halves(low, at["weight3"], LANES)[:, : sz.head], grad_logits, (1, 0)))
    part_ref[:hid, at["grad_embed"] : at["grad_embed"] + own] = own_part
    grad_mid = spread(sz, average_part / totals3, counts3)
    low_grad2 = norm_backward(grad_mid, result2[...], scale2[...])
    g2 = dot(inputs2[...], low_grad2, (1, 1))
    part_ref[:hid, at["g2"] : at["g2"] + hid] = g2[:hid]
    part_ref[:hid, at["g2"] + hid : at["g2"] + 2 * hid] = g2[hid:]
    part_ref[sz.head : sz.head + 16, g3 + hid : g3 + 2 * hid] = row_sums(low_grad2)
    weight2 = halves(low, at["weight2"], hid)
    grad_a[...] = jnp.zeros_like(grad_a)
    for tile in range(sz.tiles_b):
        lanes = slice(LANES * tile, LANES * (tile + 1))
        own_part, average_part = split_inputs(sz, dot(weight2, low_grad2[:, lanes], (1, 0)))
        part_ref[:hid, at["grad_b"] + LANES * tile : at["grad_b"] + LANES * (tile + 1)] = own_part
        window, totals = tile_counts(sz, counts, tile)
        lanes = pl.ds(a_window(sz, part, tile), WINDOW)
        grad_a[:, lanes] = grad_a[:, lanes] + spread(sz, average_part / totals, window)

    rows = pl.ds(0, hid + 8)
    split = at["g2"]
    stores = start_copies(
        (
            (part_ref.at[rows, pl.ds(split, hid * 2)], part_out.at[rows, pl.ds(split, hid * 2)]),
            (
                part_ref.at[rows, pl.ds(at["grad_b"], n_b + own)],
                part_out.at[rows, pl.ds(at["grad_b"], n_b + own)],
            ),
        ),
        sems,
        11,
    )

    def backward_step(index, carry):
        lanes = pl.ds(aligned(index * LANES), LANES)
        low_grad[:, lanes] = norm_backward(grad_a[:, lanes], result1[:, lanes], scale1[:, lanes])
        return carry

    lax.fori_loop(0, n_a // LANES, backward_step, 0, unroll=2)
    part_ref[:hid, at["g1"] : at["g1"] + hid] = dot(xa[...], low_grad[...], (1, 1))
    part_ref[sz.head : sz.head + 16, g3 : g3 + hid] = row_sums(low_grad[...])
    stores += start_copies(
        (
            (part_ref.at[rows, pl.ds(0, hid)], part_out.at[rows, pl.ds(0, hid)]),
            (part_ref.at[rows, pl.ds(g3, 2 * hid)], part_out.at[rows, pl.ds(g3, 2 * hid)]),
        ),
        sems,
        13,
    )
    wait_all(stores)


def rest_step(sz, low, high, counts, means, labels, weighting, head_bias):
    hid = sz.hid
    return call(
        functools.partial(rest_kernel, sz),
        [((hid + 8, sz.part_lanes), F32)],
        [
            (labels.shape, jnp.int32),
            (weighting.shape, jnp.int32),
            (head_bias.shape, F32),
            ((hid, sz.at["embed"] + sz.own - sz.n_mid), BF),
            ((hid, sz.n_a), BF),
            ((hid + 8, 2 * LANES), F32),
            (counts.shape, BF),
            ((2 * sz.hold, sz.n_a), BF),
            ((sz.main, sz.message_a), BF),
            ((sz.main, sz.message_a), BF),
            ((sz.main, sz.message_a), BF),
            ((2 * sz.main, LANES), F32),
            ((2 * hid, sz.n_a), BF),
            ((2 * hid, sz.n_b), BF),
            ((hid, sz.n_a), F32),
            ((1, sz.n_a), F32),
            ((2 * hid, sz.n_b), BF),
            ((hid, sz.n_b), F32),
            ((1, sz.n_b), F32),
            ((hid, sz.n_a), F32),
            ((hid, sz.n_a), BF),
            ((hid + 8, sz.part_lanes), F32),
        ],
        REST_MIB,
        low,
        high,
        counts,
        *means,
        labels,
        weighting,
        head_bias,
        far_in=range(10),
        micros=14,
        far_out=(0,),
        copies=15,
    )[0]


def seeds_back_kernel(
    sz, info_in, received, low_in, high_in, counts_in, part_in, keep0, keep1, send,
    info, x_ref, weight_ref, low, high, window_ref, partial, g1_ref, g2_ref, gb_ref, sems,
):
    part = lax.axis_index("col")
    own, hid, group, n_b, n_mid = sz.own, sz.hid, sz.group, sz.n_b, sz.n_mid
    at = dict(sz.at)
    at["inputs2"] -= at["embed"]
    split = at["grad_b"]
    copies = start_copies(
        (
            (info_in, info),
            (low_in.at[:, pl.ds(at["embed"], 4 * own)], low),
            (part_in.at[:, pl.ds(split, n_b + own)], partial.at[:, pl.ds(split, n_b + own)]),
            (high_in, high),
            (low_in.at[:, pl.ds(at["weight2"], 2 * hid)], weight_ref),
            (counts_in.at[pl.ds(sz.count_rows * sz.tiles_b, sz.count_rows * (own // LANES)), :], window_ref),
            (part_in.at[:, pl.ds(0, split)], partial.at[:, pl.ds(0, split)]),
            (low_in.at[:, pl.ds(0, n_mid)], x_ref),
        ),
        sems,
    )
    arrived = received[...].astype(F32).reshape(sz.dp, 4, sz.slot, 3 * hid)
    arrived = jnp.sum(arrived, 1).reshape(sz.slots, 3 * hid)
    at["embed"] = 0
    wait_all(copies[:2])
    serve, take, served, taken = seed_picks(sz, info, part)
    mine = sent_rows(sz, low, 0, serve, take)
    theirs = arrived[:, hid : 2 * hid]
    alive_there = theirs[:, 0:1] < 0.5 * SENTINEL
    theirs = theirs + arrived[:, 2 * hid :]
    differ = mine[:, hid : 2 * hid] + mine[:, 2 * hid :] - arrived[:, :hid]
    differ = jnp.where((taken > 0.5) & (info[:, 2:3] > 0), differ, 0.0)
    dist_total = DIST_WEIGHT * jnp.sum(jnp.sum(differ * differ, 0, keepdims=True), 1, keepdims=True)
    local_high, local_low = two_parts(2.0 * DIST_WEIGHT * differ)
    back = jnp.where((served > 0.5) & alive_there, theirs - mine[:, :hid], 0.0)
    back = (-2.0 * DIST_WEIGHT * back).astype(BF)
    take = take.astype(BF)
    serve = serve.astype(BF)
    wait_all(copies[2:])
    grad = partial[:hid, at["grad_embed"] : at["grad_embed"] + own]
    grad = grad + dot(local_high, take, (0, 0)) + dot(local_low, take, (0, 0)) + dot(back, serve, (0, 0))
    lanes = slice(at["result2"], at["result2"] + own)
    low_grad2 = norm_backward(grad, high[:hid, lanes], high[hid:, lanes][0:1])
    added = dot(halves(low, at["inputs2"], own), low_grad2, (1, 1))
    for half in range(2):
        lanes = slice(at["g2"] + hid * half, at["g2"] + hid * (half + 1))
        g2_ref[hid * half : hid * (half + 1), :] = partial[:hid, lanes] + added[hid * half : hid * (half + 1)]
    g3 = at["g3"]
    sums = partial[sz.head : sz.head + 16, g3 : g3 + 2 * hid]
    gb_ref[:, hid:] = sums[:, hid:] + row_sums(low_grad2)
    weight2 = halves(weight_ref, 0, hid)
    own_part, average_part = split_inputs(sz, dot(weight2, low_grad2, (1, 0)))
    total_b = partial[:hid, at["grad_b"] : at["grad_b"] + n_b]
    for tile in range(own // LANES):
        window, totals = tile_counts(sz, window_ref, tile)
        total_b = total_b + spread(sz, average_part[:, LANES * tile : LANES * (tile + 1)] / totals, window)
    low_grad = jnp.concatenate(
        [
            norm_backward(total_b, high[:hid, :n_b], high[hid:, :n_b][0:1]),
            norm_backward(own_part, high[:hid, n_b:n_mid], high[hid:, n_b:n_mid][0:1]),
        ],
        1,
    )
    half = 4 * sz.hold
    g1_ref[...] = partial[:hid, at["g1"] : at["g1"] + hid] + dot(x_ref[...], low_grad, (1, 1))
    gb_ref[:, :hid] = sums[:, :hid] + row_sums(low_grad)
    head_row = partial[sz.head + 16 : sz.head + 32, g3 : g3 + LANES]
    totals = partial[sz.head + 16 : sz.head + 32, g3 + LANES : g3 + 2 * LANES]
    lane_at = lax.broadcasted_iota(jnp.int32, (16, LANES), 1)
    row_at = lax.broadcasted_iota(jnp.int32, (16, LANES), 0)
    fixed = ((totals[0:1, 0:1] + dist_total) * float(2**LOSS_BITS) + 0.5).astype(jnp.int32)
    count = totals[0:1, 1:2].astype(jnp.int32)
    whole = jnp.where(lane_at < 32, fixed, count)
    bits = (lax.shift_right_logical(whole, lane_at & 31) & 1).astype(F32)
    bits = jnp.where(lane_at < 64, bits, 0.0)
    for r, (target_ref, base) in enumerate(((keep0, 0), (send, 0), (keep1, 0), (send, sz.pay))):
        shard = part ^ r
        block2 = pl.ds(pl.multiple_of(2 * group * shard, 2 * group), 2 * group)
        row = base
        for h in range(hid // LANES):
            lanes = slice(LANES * h, LANES * (h + 1))
            for s in range(2):
                rows = slice(half * s + sz.hold * r, half * s + sz.hold * (r + 1))
                target_ref[row : row + sz.hold, :] = g1_ref[rows, lanes].astype(BF)
                row += sz.hold
        for h in range(hid // LANES):
            target_ref[row : row + 2 * group, :] = g2_ref[block2, LANES * h : LANES * (h + 1)].astype(BF)
            row += 2 * group
        third = partial[: sz.head, pl.ds(aligned(g3 + 2 * group * shard), LANES)]
        target_ref[row : row + sz.head, :] = third.astype(BF)
        row += sz.head
        odd = (shard % 2) == 1
        block = aligned((shard // 2) * LANES)
        one = gb_ref[:, pl.ds(block, LANES)]
        two = gb_ref[:, pl.ds(aligned(hid + block), LANES)]
        one = jnp.where(odd, pltpu.roll(one, group, 1), one)
        two = jnp.where(odd, two, pltpu.roll(two, group, 1))
        bias_row = jnp.where(lane_at < group, one, two)
        misc = jnp.where(row_at == 0, bias_row, jnp.where(row_at == 1, head_row, jnp.where(row_at == 2, bits, 0.0)))
        target_ref[row : row + 16, :] = misc.astype(BF)


def seeds_backward(sz, info, received, low, high, counts, partial):
    hid = sz.hid
    return call(
        functools.partial(seeds_back_kernel, sz),
        [((sz.pay, LANES), BF), ((sz.pay, LANES), BF), ((2 * sz.pay, LANES), BF)],
        [
            (info.shape, jnp.int32),
            ((hid, sz.n_mid), BF),
            ((hid, 2 * hid), BF),
            ((hid, 4 * sz.own), BF),
            ((hid + 8, sz.high_lanes), F32),
            ((sz.count_rows * (sz.own // LANES), LANES), BF),
            ((hid + 8, sz.part_lanes), F32),
            ((8 * sz.hold, hid), F32),
            ((2 * hid, hid), F32),
            ((16, 2 * hid), F32),
        ],
        BACK_MIB,
        info,
        received,
        low,
        high,
        counts,
        partial,
        far_in=(0, 2, 3, 4, 5),
        micros=3,
        copies=8,
    )


def lamb_kernel(sz, grad, w1, w2, w3, wh, wb, f1, f2, f3, fh, fb, s1, s2, s3, sh, sb, *rest):
    params = (w1, w2, w3, wh, wb)
    firsts = (f1, f2, f3, fh, fb)
    seconds = (s1, s2, s3, sh, sb)
    moments, squares, updates = rest[:5], rest[5:10], rest[10:15]
    sums_ref, totals_ref, one_ref, three_ref = rest[15:]
    group, hold = sz.group, sz.hold

    def wide(at, rows):
        return jnp.concatenate([grad[at : at + rows, :], grad[at + rows : at + 2 * rows, :]], 1)

    one = wide(0, 2 * hold)
    three = grad[sz.at_three : sz.misc, :]
    turned = pltpu.roll(three, group, 1)
    for f in range(sz.feat):
        one_ref[f, 0:1, :] = one[f : f + 1]
        one_ref[f, 1:2, :] = one[hold + f : hold + f + 1]
    for c in range(sz.classes):
        three_ref[c, 0:1, :] = three[c : c + 1, :group]
        three_ref[c, 1:2, :] = turned[c : c + 1, :group]
    misc = grad[sz.misc : sz.misc + 8, :]
    hidden = jnp.concatenate([misc[0:1, :group], misc[0:1, group : 2 * group]], 0)
    two = wide(sz.rows_one, 2 * group).reshape(2, group, sz.hid)
    grads = (one_ref[...], two, three_ref[...], hidden, misc[1:2, : sz.classes])
    lane_at = lax.broadcasted_iota(jnp.int32, (8, LANES), 1)
    row_at = lax.broadcasted_iota(jnp.int32, (8, LANES), 0)
    sums = jnp.zeros((8, LANES), F32)
    for i in range(5):
        g = grads[i]
        w = params[i][...]
        m = BETA_ONE * firsts[i][...] + (1.0 - BETA_ONE) * g
        v = BETA_TWO * seconds[i][...] + (1.0 - BETA_TWO) * g * g
        u = (m / (1.0 - BETA_ONE**STEP)) / (jnp.sqrt(v / (1.0 - BETA_TWO**STEP)) + ADAM_EPS) + DECAY_RATE * w
        moments[i][...] = m
        squares[i][...] = v
        updates[i][...] = u
        for row, item in ((0, w), (1, u)):
            item = item * item
            if i < 3:
                item = jnp.sum(item, 0)
            total = jnp.sum(jnp.sum(item, 0, keepdims=True), 1, keepdims=True)
            if i == 4:
                total = 0.25 * total
            sums = jnp.where((lane_at == i) & (row_at == row), total, sums)
    sums_ref[...] = sums
    power = (1 << (lane_at & 15)).astype(F32)
    power = jnp.where((lane_at & 31) < 16, power, power * float(2**16))
    bits = jnp.broadcast_to(misc[2:3], (8, LANES)) * power
    loss = jnp.sum(jnp.where(lane_at < 32, bits, 0.0), 1, keepdims=True) * float(2.0**-LOSS_BITS)
    count = jnp.sum(jnp.where((lane_at >= 32) & (lane_at < 64), bits, 0.0), 1, keepdims=True)
    totals_ref[...] = jnp.where(lane_at == 0, loss, count)


def lamb(sz, grad, params, firsts, seconds):
    like = [(item.shape, F32) for item in params]
    return call(
        functools.partial(lamb_kernel, sz),
        like * 3 + [((8, LANES), F32)] * 2,
        [(params[0].shape, F32), (params[2].shape, F32)],
        6,
        grad,
        *params,
        *firsts,
        *seconds,
    )


def step_kernel(own, other, w1, w2, w3, wh, wb, u1, u2, u3, uh, ub, n1, n2, n3, nh, nb, norms_ref):
    norms = jnp.sqrt(own[...] + other[...])
    norms_ref[...] = norms[0:2, 0:5]
    for i, (w, u, n) in enumerate(
        ((w1, u1, n1), (w2, u2, n2), (w3, u3, n3), (wh, uh, nh), (wb, ub, nb))
    ):
        ratio = LEARN_RATE * (norms[0:1, i : i + 1] / norms[1:2, i : i + 1])
        n[...] = w[...] - ratio * u[...]


def take_step(own, other, params, updates):
    return call(
        step_kernel,
        [(item.shape, F32) for item in params] + [((2, 5), F32)],
        [],
        3,
        own,
        other,
        *params,
        *updates,
    )


def swap(value, axis, count, bit):
    return lax.ppermute(value, axis, [(i, i ^ bit) for i in range(count)])


def merged(own, other):
    return lax.reduce_precision(own.astype(F32) + other.astype(F32), 8, 7)


def shards(
    features, neighbors_one, present_one, neighbors_two, present_two, neighbors_three, present_three,
    labels, seed_weight, serve_rows, take_seed, fetch_live,
    weight_one, weight_two, weight_three, hidden_bias, head_bias,
    first_one, first_two, first_three, first_hidden, first_head,
    second_one, second_two, second_three, second_hidden, second_head,
):
    sz = Sizes(features, neighbors_one, neighbors_two, neighbors_three, weight_two, weight_three, serve_rows)

    def tree(one, two, three, hidden, head):
        return (one.transpose(1, 0, 2), two, three.transpose(2, 0, 1), hidden, head[None, :])

    def back(one, two, three, hidden, head):
        return (one.transpose(1, 0, 2), two, three.transpose(1, 2, 0), hidden, head[0])

    params = tree(weight_one, weight_two, weight_three, hidden_bias, head_bias)
    firsts = tree(first_one, first_two, first_three, first_hidden, first_head)
    seconds = tree(second_one, second_two, second_three, second_hidden, second_head)

    own_b, packed, *sent = first_messages(sz, features, neighbors_one, present_one, *params[:4])
    s1, s2, s3 = [swap(sent[r - 1], "col", 4, r) for r in (1, 2, 3)]
    own_a, *means = mean_messages(sz, features, neighbors_one, present_one)
    s1, *means = lax.optimization_barrier((s1, *means))
    means = [swap(means[r - 1], "col", 4, r) for r in (1, 2, 3)]
    neighbors_two, s2 = lax.optimization_barrier((neighbors_two, s2))
    counts = make_counts(sz, neighbors_two, present_two, neighbors_three, present_three)
    later, _ = lax.optimization_barrier((s2, own_a))
    passed = swap(later, "col", 4, 1)
    alive = jnp.arange(sz.slot, dtype=jnp.int32)[None, :] < fetch_live[:, None]
    info = jnp.stack([serve_rows.reshape(-1), take_seed.reshape(-1), alive.astype(jnp.int32).reshape(-1)], 1)
    low, high, rows = seeds_forward(sz, (own_b, packed, s1, s2, s3, passed), counts, info)
    received = lax.all_to_all(rows, ("dp", "col"), split_axis=0, concat_axis=0, tiled=True)
    partial = rest_step(sz, low, high, counts, (own_a, *means), labels[None, :], seed_weight[None, :], head_bias[None, :])
    keep0, keep1, send = seeds_backward(sz, info, received, low, high, counts, partial)
    other = swap(send, "col", 4, 1)
    grad = merged(keep0, other[: sz.pay])
    grad = merged(grad, swap(merged(keep1, other[sz.pay :]).astype(BF), "col", 4, 2))
    bit = 1
    while bit < sz.dp:
        grad = merged(grad, swap(grad.astype(BF), "dp", sz.dp, bit))
        bit *= 2
    outs = lamb(sz, grad, params, firsts, seconds)
    moments, squares, updates = outs[:5], outs[5:10], outs[10:15]
    sums, totals = outs[15], outs[16]
    pair = sums + swap(sums, "col", 4, 1)
    fresh = take_step(pair, swap(pair, "col", 4, 2), params, updates)
    return (*back(*fresh[:5]), *back(*moments), *back(*squares), fresh[5], totals[0, 0], totals[0, 1])


def solution(mesh):
    wide = P(None, "col", None)
    tree = [wide, wide, wide, P(None, "col"), P()]
    return jax.shard_map(
        shards,
        mesh=mesh,
        in_specs=(
            P("col", "dp"),
            *[P(None, "dp")] * 6,
            P("dp"),
            P("dp"),
            P("dp", None),
            P("dp", None),
            P("dp"),
            *tree,
            *tree,
            *tree,
        ),
        out_specs=(*tree, *tree, *tree, P(), P(), P()),
        check_vma=False,
    )
```

```python
import functools

import jax
import jax.numpy as jnp
from jax import lax
from jax.experimental import pallas as pl
from jax.experimental.pallas import tpu as pltpu
from jax.sharding import PartitionSpec as P

REACH = 64
STEP = 5
DIST_WEIGHT = 1.0
ROW_EPS = 1e-06
LEARN_RATE = 0.5
BETA_ONE = 0.9
BETA_TWO = 0.999
ADAM_EPS = 1e-06
DECAY_RATE = 0.01

BF = jnp.bfloat16
F32 = jnp.float32
LANES = 128
WINDOW = 768
SENTINEL = 4.0
MIB = 2**20
LOSS_BITS = 14
EARLY = 6
FIRST_MIB = 8
MEAN_MIB = 8
SEEDS_MIB = 16
REST_MIB = 28
BACK_MIB = 12


def cost(micros):
    return pl.CostEstimate(flops=int(micros * 10**9), bytes_accessed=1, transcendentals=0)


def call(kernel, outs, scratch, mib, *args, far_in=(), far_out=(), copies=0, micros=1, loose=(), name=None):
    near = pl.BlockSpec(memory_space=pltpu.VMEM)
    far = pl.BlockSpec(memory_space=pltpu.HBM)
    free = pl.BlockSpec(memory_space=pl.ANY)
    scratch = [pltpu.VMEM(shape, kind) for shape, kind in scratch]
    args = [pltpu.with_memory_space_constraint(a, pltpu.HBM) if i in far_in else a for i, a in enumerate(args)]
    return pl.pallas_call(
        kernel,
        in_specs=[free if i in loose else far if i in far_in else near for i in range(len(args))],
        out_specs=tuple(far if i in far_out else near for i in range(len(outs))),
        out_shape=tuple(
            pltpu.HBM(shape, kind) if i in far_out else jax.ShapeDtypeStruct(shape, kind)
            for i, (shape, kind) in enumerate(outs)
        ),
        scratch_shapes=scratch + ([pltpu.SemaphoreType.DMA((copies,))] if copies else []),
        compiler_params=pltpu.CompilerParams(vmem_limit_bytes=mib * MIB),
        cost_estimate=cost(micros),
        name=name,
    )(*args)


def start_copies(pairs, sems, first=0):
    copies = [pltpu.make_async_copy(src, dst, sems.at[first + i]) for i, (src, dst) in enumerate(pairs)]
    for copy in copies:
        copy.start()
    return copies


def wait_all(copies):
    for copy in copies:
        copy.wait()


class Sizes:
    def __init__(self, features, neighbors_one, neighbors_two, neighbors_three, weight_two, weight_three, serve_rows):
        self.feat = features.shape[0]
        self.main = self.feat - 1
        self.hold = 32
        self.base = features.shape[1]
        self.low = neighbors_one.shape[1]
        self.mid = neighbors_two.shape[1]
        self.seeds = neighbors_three.shape[1]
        self.hid = weight_two.shape[2]
        self.group = weight_two.shape[1]
        self.classes = weight_three.shape[2]
        self.head = -(-self.classes // 16) * 16
        self.own = self.seeds // 4
        self.n_b = 4 * self.own + 2 * LANES
        self.n_a = 16 * self.own + 6 * LANES
        self.n_mid = self.n_b + self.own
        self.n_low = self.n_a + self.n_mid
        self.tiles_b = self.n_b // LANES
        self.tiles_mid = self.n_mid // LANES
        self.tiles_low = self.n_low // LANES
        self.slots = serve_rows.shape[0] * serve_rows.shape[1]
        self.slot = serve_rows.shape[1]
        self.dp = serve_rows.shape[0]
        self.rows_one = 2 * 2 * self.hold
        self.rows_two = 4 * self.group
        self.at_three = self.rows_one + self.rows_two
        self.misc = self.at_three + self.head
        self.pay = self.misc + 16
        self.blocks = -(-self.pay // self.main)
        self.early = EARLY * LANES
        self.message_a = self.pair_lanes(self.n_a, self.n_a - self.early)
        self.message_b = self.pair_lanes(self.n_mid, self.n_mid + self.early)
        self.full_b = self.message_b + LANES * self.blocks
        self.tiles_b_all = 16 * self.own // LANES + 1
        self.count_rows = WINDOW + 16
        hid, at = self.hid, self.n_mid
        places = {}
        for name, lanes in (
            ("turned1", hid), ("turned2", 2 * hid), ("weight2", 2 * hid), ("weight3", 2 * LANES), ("turned3", 2 * hid),
            ("states", self.n_b), ("embed", 2 * self.own), ("inputs2", 2 * self.own),
        ):
            places[name] = at
            at += lanes
        self.low_lanes = at
        at = 0
        for name, lanes in (("result1", self.n_mid), ("result2", self.own), ("bias", 2 * LANES)):
            places[name] = at
            at += lanes
        self.high_lanes = at
        at = 0
        for name, lanes in (("g1", hid), ("g2", 2 * hid), ("g3", 2 * hid), ("grad_b", self.n_b), ("grad_embed", self.own)):
            places[name] = at
            at += lanes
        self.part_lanes = at
        self.at = places

    def pair_lanes(self, means, own):
        lanes = means + own
        return lanes + LANES * -(-lanes // LANES // self.main)

    def first_ranges(self, part):
        a, b, c = self.ranges(part)
        b = (b[0], 0, b[2])
        c = (c[0], b[2], c[2])
        return [b, c, (a[0], self.n_mid, self.early)], [b, c]

    def second_ranges(self, part):
        first = self.a_start(part)
        return [(first + self.early, 0, self.n_a - self.early)], [(first, 0, self.n_a)]

    def a_start(self, part):
        return jnp.clip(16 * self.own * part - 3 * LANES, 0, self.low - self.n_a)

    def b_start(self, part):
        return jnp.maximum(4 * self.own * part - LANES, 0)

    def b_columns(self, part, tile):
        return pl.ds(aligned(jnp.minimum(self.b_start(part) + LANES * tile, self.mid - LANES)), LANES)

    def mid_columns(self, part, tile):
        if tile < self.tiles_b:
            return self.b_columns(part, tile)
        return pl.ds(aligned(self.own * part + LANES * (tile - self.tiles_b)), LANES)

    def ranges(self, part):
        return (
            (self.a_start(part), 0, self.n_a),
            (self.b_start(part), self.n_a, self.n_b),
            (self.own * part, self.n_a + self.n_b, self.own),
        )


def dot(a, b, over):
    return lax.dot_general(a, b, (((over[0],), (over[1],)), ((), ())), preferred_element_type=F32)


def two_parts(value):
    high = value.astype(BF)
    return high, (value - high.astype(F32)).astype(BF)


def three_parts(value):
    high = value.astype(BF).astype(F32)
    rest = value - high
    middle = rest.astype(BF).astype(F32)
    return high, middle, (rest - middle).astype(BF).astype(F32)


def aligned(value):
    return pl.multiple_of(value, LANES)


def sigmoid(value):
    return 0.5 * jnp.tanh(0.5 * value) + 0.5


def unpack_tile(sz, message, tail, tile):
    spare = jnp.zeros((sz.hold - sz.feat, LANES), F32)
    main = message[:, LANES * tile : LANES * (tile + 1)].astype(F32)
    return jnp.concatenate([main, tail[tile : tile + 1, :], spare], 0).astype(BF)


def mean_tiles(sz, begin, tiles, feat_ref, nbr_ref, pres_ref, mean_ref, tail_ref, base_ref, code_ref, count_ref):
    last = feat_ref.shape[1] // LANES - 6
    slots = nbr_ref.shape[0]
    base_ref[...] = jnp.zeros_like(base_ref)
    if begin % 8 or tiles % 8:
        code_ref[...] = jnp.full_like(code_ref, -1)
        count_ref[...] = jnp.ones_like(count_ref)
    for tile in range(feat_ref.shape[1] // LANES):
        row = feat_ref[:, LANES * tile : LANES * (tile + 1)].astype(F32)
        base_ref[8 + tile : 9 + tile, :] = row[sz.main : sz.feat]

    def one_tile(step, carry):
        lane = aligned(step * LANES)
        present = pres_ref[:, pl.ds(lane, LANES)]
        valid = present.astype(F32)
        counts = jnp.maximum(jnp.sum(valid, 0, keepdims=True), 1.0)
        first = jnp.clip(4 * step - 1, 0, last)
        links = nbr_ref[:, pl.ds(lane, LANES)]
        code = jnp.where(present > 0, links, -1)
        count_ref[pl.ds(step, 1), :] = counts
        for slot in range(slots):
            code_ref[slot, pl.ds(step, 1), :] = code[slot : slot + 1]
        local = links - first * LANES
        piece = local >> 7
        spot = local & 127
        sources = [
            feat_ref[:, pl.ds(aligned((first + j) * LANES), LANES)].astype(F32) for j in range(6)
        ]
        totals = [jnp.zeros((8, LANES), F32) for _ in range(sz.main // 8)]
        for slot in range(slots):
            spots = jnp.broadcast_to(spot[slot : slot + 1], (8, LANES))
            pieces = jnp.broadcast_to(piece[slot : slot + 1], (8, LANES))
            marks = jnp.broadcast_to(valid[slot : slot + 1], (8, LANES))
            for h in range(sz.main // 8):
                taken = None
                for j in range(6):
                    found = jnp.take_along_axis(
                        sources[j][8 * h : 8 * h + 8], spots, axis=1, mode="promise_in_bounds"
                    )
                    taken = found if j == 0 else jnp.where(pieces == j, found, taken)
                totals[h] = totals[h] + taken * marks
        mean_ref[:, pl.ds(lane, LANES)] = (jnp.concatenate(totals, 0) / counts).astype(BF)
        return carry

    even = begin + (tiles - begin) // 4 * 4
    lax.fori_loop(begin, even, one_tile, 0, unroll=4)
    for step in range(even, tiles):
        one_tile(step, 0)
    sub = lax.broadcasted_iota(jnp.int32, (8, LANES), 0)

    for block in range(begin // 8, -(-tiles // 8)):
        total = jnp.zeros((8, LANES), F32)
        for slot in range(slots):
            code = code_ref[slot, 8 * block : 8 * (block + 1), :]
            piece = (code >> 7) - (4 * (8 * block + sub) - 1)
            taken = None
            for j in range(6):
                source = base_ref[pl.ds(8 + 32 * block - 1 + j, 8, stride=4), :]
                found = jnp.take_along_axis(source, code & 127, axis=1, mode="promise_in_bounds")
                taken = found if j == 0 else jnp.where(piece == j, found, taken)
            total = total + jnp.where(code >= 0, taken, 0.0)
        tail_ref[8 * block : 8 * (block + 1), :] = total / count_ref[8 * block : 8 * (block + 1), :]


def pack_pair(sz, ranges, feat_ref, base_ref, mean_ref, tail_ref, turn_ref, out_ref):
    turn_ref[...] = jnp.zeros_like(turn_ref)
    lanes = 0
    for source_ref, rows_ref, shift, group in zip((feat_ref, mean_ref), (base_ref, tail_ref), (8, 0), ranges):
        for first, at, count in group:
            at = at + lanes
            out_ref[:, at : at + count] = source_ref[: sz.main, pl.ds(aligned(first), count)]
            at, rows = at // LANES, count // LANES
            turn_ref[at : at + rows, :] = rows_ref[pl.ds(shift + first // LANES, rows), :]
        lanes += sum(count for _, _, count in group)
    for block in range(-(-lanes // LANES // sz.main)):
        at = lanes + LANES * block
        out_ref[:, at : at + LANES] = turn_ref[sz.main * block : sz.main * (block + 1), :].astype(BF)


def own_pair(sz, ranges, feat_ref, mean_ref, tail_ref, own_ref):
    spare = jnp.zeros((sz.hold - sz.feat, LANES), F32)
    base = ranges[0][1]
    for start, at, count in ranges:
        for tile in range(count // LANES):
            lanes = pl.ds(aligned(start + LANES * tile), LANES)
            out_lanes = slice(at - base + LANES * tile, at - base + LANES * (tile + 1))
            own = [feat_ref[:, lanes].astype(F32), spare]
            own_ref[: sz.hold, out_lanes] = jnp.concatenate(own, 0).astype(BF)
            tail = tail_ref[pl.ds(start // LANES + tile, 1), :]
            average = [mean_ref[:, lanes].astype(F32), tail, spare]
            own_ref[sz.hold :, out_lanes] = jnp.concatenate(average, 0).astype(BF)


def mean_scratch(sz, tiles, slots):
    return [
        ((sz.main, LANES * tiles), BF),
        ((-(-tiles // 8) * 8, LANES), F32),
        ((2 * sz.main, LANES), F32),
        ((4 * -(-tiles // 8) * 8 + 16, LANES), F32),
        ((slots, -(-tiles // 8) * 8, LANES), jnp.int32),
        ((-(-tiles // 8) * 8, LANES), F32),
    ]


def unpack_tails(sz, message, lanes, turn_ref):
    for block in range(-(-lanes // LANES // sz.main)):
        at = lanes + LANES * block
        turn_ref[sz.main * block : sz.main * (block + 1), :] = message[:, at : at + LANES].astype(F32)
    return turn_ref[...]


def unpack_tiles(sz, message, tail, first, tiles, row, at, out_ref):
    for tile in range(tiles):
        lane = at + LANES * tile
        out_ref[row : row + sz.hold, lane : lane + LANES] = unpack_tile(sz, message, tail, first + tile)


def first_kernel(
    sz, features, neighbors, present, w1_in, w2_in, w3_in, wh_in, own_b, packed, mean_out, tail_out, m1, m2, m3,
    feat_ref, nbr_ref, pres_ref, w1, w2, w3, wh, own_ref,
    mean_ref, tail_ref, turn_ref, base_ref, code_ref, count_ref, one_ref, three_ref, pack, sems,
):
    part = lax.axis_index("col")
    rows = pl.ds(0, nbr_ref.shape[1])
    weights = start_copies(((w1_in, w1), (w2_in, w2), (w3_in, w3), (wh_in, wh)), sems)
    copies = start_copies(
        (
            (features.at[:, pl.ds(0, feat_ref.shape[1])], feat_ref),
            (neighbors.at[:, rows], nbr_ref),
            (present.at[:, rows], pres_ref),
        ),
        sems,
        4,
    )
    wait_all(weights)
    one_ref[...] = jnp.zeros_like(one_ref)
    three_ref[...] = jnp.zeros_like(three_ref)
    for s in range(2):
        for f in range(sz.feat):
            one_ref[s * sz.hold + f : s * sz.hold + f + 1, :] = w1[f, s : s + 1, :]
        for c in range(sz.classes):
            three_ref[c : c + 1, s * sz.group : (s + 1) * sz.group] = w3[c, s : s + 1, :]
    at = 0
    for half in range(sz.hid // LANES):
        pack[at : at + 2 * sz.hold, :] = one_ref[:, LANES * half : LANES * (half + 1)]
        at += 2 * sz.hold
    for half in range(sz.hid // LANES):
        for s in range(2):
            pack[at : at + sz.group, :] = w2[s, :, LANES * half : LANES * (half + 1)]
            at += sz.group
    pack[at : at + sz.head, :] = three_ref[...]
    row = jnp.concatenate([wh[0:1, :], wh[1:2, :]], 1)
    row_at = lax.broadcasted_iota(jnp.int32, (16, LANES), 0)
    misc = jnp.zeros((16, LANES), F32)
    for i, piece in enumerate(three_parts(row)):
        misc = jnp.where(row_at == i, piece, misc)
    pack[sz.misc : sz.pay, :] = misc
    pack[sz.pay :, :] = jnp.zeros((sz.main * sz.blocks - sz.pay, LANES), F32)
    store = start_copies(((pack, packed),), sems, 7)
    for block in range(sz.blocks):
        at = sz.message_b + LANES * block
        piece = pack[sz.main * block : sz.main * (block + 1), :].astype(BF)
        m1[:, at : at + LANES] = piece
        m2[:, at : at + LANES] = piece
    wait_all(copies)
    mean_tiles(sz, 0, sz.tiles_b_all, feat_ref, nbr_ref, pres_ref, mean_ref, tail_ref, base_ref, code_ref, count_ref)
    store += start_copies(((mean_ref, mean_out), (tail_ref, tail_out)), sems, 9)
    own_pair(sz, sz.ranges(part)[1:], feat_ref, mean_ref, tail_ref, own_ref)
    store += start_copies(((own_ref, own_b),), sems, 8)
    for r, out in ((1, m1), (2, m2), (3, m3)):
        pack_pair(sz, sz.first_ranges(part ^ r), feat_ref, base_ref, mean_ref, tail_ref, turn_ref, out)
    wait_all(store)


def first_messages(sz, features, neighbors, present, w1, w2, w3, hidden):
    rows = LANES * sz.tiles_b_all
    bases = min(4 * rows + LANES, sz.base)
    slots = neighbors.shape[0]
    return call(
        functools.partial(first_kernel, sz),
        [
            ((2 * sz.hold, sz.n_mid), BF),
            ((sz.main * sz.blocks, LANES), F32),
            ((sz.main, rows), BF),
            ((-(-sz.tiles_b_all // 8) * 8, LANES), F32),
            ((sz.main, sz.full_b), BF),
            ((sz.main, sz.full_b), BF),
            ((sz.main, sz.message_b), BF),
        ],
        [
            ((sz.feat, bases), BF),
            ((slots, rows), jnp.int32),
            ((slots, rows), jnp.int32),
            (w1.shape, F32),
            (w2.shape, F32),
            (w3.shape, F32),
            (hidden.shape, F32),
            ((2 * sz.hold, sz.n_mid), BF),
            *mean_scratch(sz, sz.tiles_b_all, slots),
            ((2 * sz.hold, sz.hid), F32),
            ((sz.head, LANES), F32),
            ((sz.main * sz.blocks, LANES), F32),
        ],
        FIRST_MIB,
        features,
        neighbors,
        present,
        w1,
        w2,
        w3,
        hidden,
        far_in=range(7),
        far_out=(0, 1, 2, 3),
        copies=11,
        micros=4,
    )


def mean_kernel(
    sz, feat_ref, nbr_ref, pres_ref, mean_in, tail_in, nbr2, pres2, nbr3, pres3, own_a, counts_out, a1, a2, a3,
    mean_ref, tail_ref, turn_ref, base_ref, code_ref, count_ref, own_ref, kept_ref, counts, sems,
):
    part = lax.axis_index("col")
    tiles = sz.low // LANES
    begin = sz.tiles_b_all
    loads = start_copies(((mean_in, mean_ref.at[:, pl.ds(0, LANES * begin)]), (tail_in, kept_ref)), sems, 1)
    fill_counts(sz, part, nbr2, pres2, nbr3, pres3, counts)
    store = start_copies(((counts, counts_out),), sems, 3)
    mean_tiles(sz, begin, tiles, feat_ref, nbr_ref, pres_ref, mean_ref, tail_ref, base_ref, code_ref, count_ref)
    wait_all(loads)
    tail_ref[:begin, :] = kept_ref[:begin, :]
    own_pair(sz, sz.ranges(part)[:1], feat_ref, mean_ref, tail_ref, own_ref)
    store += start_copies(((own_ref, own_a),), sems)
    for r, out in ((1, a1), (2, a2), (3, a3)):
        pack_pair(sz, sz.second_ranges(part ^ r), feat_ref, base_ref, mean_ref, tail_ref, turn_ref, out)
    wait_all(store)


def mean_messages(sz, features, neighbors, present, mean, tail, links):
    counts = (sz.count_rows * (sz.tiles_b + sz.own // LANES), LANES)
    return call(
        functools.partial(mean_kernel, sz),
        [((2 * sz.hold, sz.n_a), BF), (counts, BF)] + [((sz.main, sz.message_a), BF)] * 3,
        mean_scratch(sz, sz.low // LANES, neighbors.shape[0]) + [((2 * sz.hold, sz.n_a), BF), (tail.shape, F32), (counts, BF)],
        MEAN_MIB,
        features,
        neighbors,
        present,
        mean,
        tail,
        *links,
        far_in=(3, 4),
        far_out=(0, 1),
        copies=4,
        micros=6,
    )


def window_counts(local, rows):
    spots = lax.broadcasted_iota(jnp.int32, (256, LANES), 0).astype(F32).astype(BF)
    blocks = []
    for first in range(0, rows, 256):
        place = local - first
        place = jnp.where((place >= 0) & (place < 256), place, -1).astype(F32)
        counts = jnp.zeros((256, LANES), BF)
        for slot in range(local.shape[0]):
            row = jnp.broadcast_to(place[slot : slot + 1], (16, LANES)).astype(BF)
            row = jnp.concatenate([row] * 16, 0)
            counts = counts + jnp.where(row == spots, jnp.bfloat16(1.0), jnp.bfloat16(0.0))
        blocks.append(counts)
    return jnp.concatenate(blocks, 0)


def slot_totals(present):
    return jnp.maximum(jnp.sum(present.astype(F32), 0, keepdims=True), 1.0)


def a_window(sz, part, tile):
    first = 4 * sz.b_start(part) + 4 * LANES * tile - LANES - sz.a_start(part)
    return aligned(jnp.clip(first, 0, sz.n_a - WINDOW))


def counts_tile(sz, links, marks, start, at, counts):
    local = jnp.where(marks > 0, links - start, -1)
    counts[at : at + WINDOW, :] = window_counts(local, WINDOW)
    counts[at + WINDOW : at + sz.count_rows, :] = jnp.broadcast_to(slot_totals(marks), (16, LANES)).astype(BF)


def fill_counts(sz, part, nbr2, pres2, nbr3, pres3, counts):
    for tile in range(sz.tiles_b):
        columns = sz.b_columns(part, tile)
        start = sz.a_start(part) + a_window(sz, part, tile)
        counts_tile(sz, nbr2[:, columns], pres2[:, columns], start, sz.count_rows * tile, counts)
    for tile in range(sz.own // LANES):
        columns = pl.ds(aligned(sz.own * part + LANES * tile), LANES)
        at = sz.count_rows * (sz.tiles_b + tile)
        counts_tile(sz, nbr3[:, columns], pres3[:, columns], sz.b_start(part), at, counts)


def tile_counts(sz, counts, tile):
    at = sz.count_rows * tile
    totals = counts[at + WINDOW : at + WINDOW + 16, :].astype(F32)[0:1]
    return counts[at : at + WINDOW, :], totals


def activate(result):
    active = result * sigmoid(result)
    scale = lax.rsqrt(jnp.sum(active * active, 0, keepdims=True) + ROW_EPS)
    return result, scale, active * scale


def first_layer(weight, inputs, bias):
    result = dot(weight, inputs, (1, 0)) + bias
    active = result * sigmoid(result)
    scale = lax.rsqrt(jnp.sum(active * active, 0, keepdims=True) + ROW_EPS)
    return result, scale, active * scale


def join_inputs(sz, own, average):
    pieces = []
    for c in range(4):
        pieces.append(own[sz.group * c : sz.group * (c + 1)])
        pieces.append(average[sz.group * c : sz.group * (c + 1)])
    return jnp.concatenate(pieces, 0)


def norm_backward(grad, result, scale):
    gate = sigmoid(result)
    active = result * gate
    inner = jnp.sum(grad * active, 0, keepdims=True)
    grad_active = scale * grad - active * (scale * scale * scale * inner)
    return (grad_active * gate * (1.0 + result * (1.0 - gate))).astype(BF)


def split_inputs(sz, grad):
    pieces = [grad[sz.group * c : sz.group * (c + 1)] for c in range(8)]
    return jnp.concatenate(pieces[0::2], 0), jnp.concatenate(pieces[1::2], 0)


def row_sums(grad):
    return dot(jnp.ones((16, grad.shape[1]), BF), grad, (1, 1))


def spread(sz, scaled, counts):
    high, low = two_parts(scaled)
    total = dot(jnp.concatenate([high, low], 0), counts, (1, 1))
    return total[: sz.hid] + total[sz.hid :]


def halves(ref, at, lanes):
    return jnp.concatenate([ref[:, at : at + lanes], ref[:, at + lanes : at + 2 * lanes]], 0)


def store_halves(ref, at, lanes, value):
    rows = value.shape[0] // 2
    ref[:rows, at : at + lanes] = value[:rows]
    ref[:rows, at + lanes : at + 2 * lanes] = value[rows:]


def slot_column(table):
    rows, slots = table.shape
    wide = jnp.broadcast_to(table.astype(F32)[:, None, :], (rows, slots, slots))
    hit = lax.broadcasted_iota(jnp.int32, wide.shape, 1) == lax.broadcasted_iota(jnp.int32, wide.shape, 2)
    return jnp.sum(jnp.where(hit, wide, 0.0), 2, keepdims=True).reshape(rows * slots, 1)


def alive_column(sz, live):
    shape = (sz.dp, sz.dp)
    hit = lax.broadcasted_iota(jnp.int32, shape, 0) == lax.broadcasted_iota(jnp.int32, shape, 1)
    counts = jnp.sum(jnp.where(hit, jnp.broadcast_to(live.astype(F32), shape), 0.0), 1, keepdims=True)
    slot = lax.broadcasted_iota(jnp.int32, (sz.dp, sz.slot), 1).astype(F32)
    return slot_column(jnp.where(slot < counts, 1.0, 0.0))


def seed_picks(sz, serve_rows, take_rows, part):
    spots = (lax.broadcasted_iota(jnp.int32, (sz.slots, sz.own), 1) + sz.own * part).astype(F32)
    serve = jnp.where(slot_column(serve_rows) == spots, 1.0, 0.0)
    take = jnp.where(slot_column(take_rows) == spots, 1.0, 0.0)
    return serve, take, jnp.sum(serve, 1, keepdims=True), jnp.sum(take, 1, keepdims=True)


def seeds_kernel(
    sz, own_b, packed, s1, s2, s3, passed, nbr2_in, pres2_in, serve_in, take_in, live_in,
    low_out, high_out, window_out, sent,
    xb, pack, m1, m2, m3, p3, nbr2, pres2, window_ref, serve_rows, take_rows, live_rows, low, high, turn_ref, w1_ref, w2_ref, states, sems,
):
    part = lax.axis_index("col")
    own, hid, n_b, group, hold, at = sz.own, sz.hid, sz.n_b, sz.group, sz.hold, sz.at
    n_mid = sz.n_mid
    copies = start_copies(
        (
            (packed, pack),
            (passed.at[:, pl.ds(sz.message_b, LANES * sz.blocks)], p3),
            (s1, m1),
            (s2, m2),
            (s3, m3),
            (own_b, xb),
            (nbr2_in.at[:, pl.ds(aligned(own * part), own)], nbr2),
            (pres2_in.at[:, pl.ds(aligned(own * part), own)], pres2),
            (serve_in, serve_rows),
            (take_in, take_rows),
            (live_in, live_rows),
        ),
        sems,
    )
    wait_all(copies[:4])
    for r, (message, first_lane) in enumerate(((None, 0), (m1, sz.message_b), (m2, sz.message_b), (p3, 0))):
        for block in range(sz.blocks if r else 0):
            first = first_lane + LANES * block
            pack[sz.main * block : sz.main * (block + 1), :] = message[:, first : first + LANES].astype(F32)
        shard = part ^ r
        for half in range(hid // LANES):
            lanes = slice(LANES * half, LANES * (half + 1))
            for s in range(2):
                first = 2 * hold * half + hold * s
                w1_ref[4 * hold * s + hold * r : 4 * hold * s + hold * (r + 1), lanes] = pack[first : first + hold, :]
            first = sz.rows_one + 2 * group * half
            row = pl.multiple_of(2 * group * shard, 2 * group)
            w2_ref[pl.ds(row, 2 * group), lanes] = pack[first : first + 2 * group, :]
        low[: sz.head, pl.ds(aligned(at["turned3"] + 2 * group * shard), LANES)] = pack[sz.at_three : sz.misc, :].astype(BF)
        misc = pack[sz.misc : sz.misc + 8, :]
        column = jnp.broadcast_to(misc[0:1] + misc[1:2] + misc[2:3], (LANES, LANES)).T
        row = pl.multiple_of(group * shard, group)
        for layer in range(2):
            lanes = slice(at["bias"] + LANES * layer, at["bias"] + LANES * (layer + 1))
            high[pl.ds(row, group), lanes] = column[group * layer : group * (layer + 1)]
    turned1 = w1_ref[...].T.astype(BF)
    turned2 = w2_ref[...].T.astype(BF)
    low[:, at["turned1"] : at["turned1"] + hid] = turned1
    low[:, at["turned2"] : at["turned2"] + 2 * hid] = turned2
    store_halves(low, at["weight2"], hid, w2_ref[...].astype(BF))
    weight3 = low[: sz.head, at["turned3"] : at["turned3"] + 2 * hid].astype(F32).T
    weight3 = jnp.concatenate([weight3, jnp.zeros((2 * hid, LANES - sz.head), F32)], 1)
    store_halves(low, at["weight3"], LANES, weight3.astype(BF))

    def piece(lanes, count):
        return (low.at[:, pl.ds(lanes, count)], low_out.at[:, pl.ds(lanes, count)])

    stores = start_copies((piece(n_mid, at["states"] - n_mid),), sems, 11)
    wait_all(copies[4:])
    for tile in range(own // LANES):
        lanes = slice(LANES * tile, LANES * (tile + 1))
        counts_tile(sz, nbr2[:, lanes], pres2[:, lanes], sz.b_start(part), sz.count_rows * tile, window_ref)
    stores += start_copies(((window_ref, window_out),), sems, 18)
    low[:hold, :n_mid] = xb[:hold, :]
    low[4 * hold : 5 * hold, :n_mid] = xb[hold:, :]
    for r, message in ((1, m1), (2, m2), (3, m3)):
        tail = unpack_tails(sz, message, 2 * n_mid + sz.early, turn_ref)
        unpack_tiles(sz, message, tail, 0, sz.tiles_mid, hold * r, 0, low)
        first = (n_mid + sz.early) // LANES
        unpack_tiles(sz, message, tail, first, sz.tiles_mid, hold * (4 + r), 0, low)
    stores += start_copies((piece(0, n_mid),), sems, 12)
    bias1 = high[:hid, at["bias"] : at["bias"] + LANES]
    bias2 = high[:hid, at["bias"] + LANES : at["bias"] + 2 * LANES]
    high[:hid, :n_mid] = dot(turned1, low[:, :n_mid], (1, 0))
    for tile in range(sz.tiles_mid):
        lanes = slice(LANES * tile, LANES * (tile + 1))
        result, scale, state = activate(high[:hid, lanes] + bias1)
        high[:hid, lanes] = result
        high[hid:, lanes] = jnp.broadcast_to(scale, (8, LANES))
        upper, lower = two_parts(state)
        states[:hid, lanes] = upper
        states[hid:, lanes] = lower
    low[:, at["states"] : at["states"] + n_b] = states[:hid, :n_b]
    rows = pl.ds(0, hid + 8)
    others = pl.ds(at["bias"], 2 * LANES)
    stores += start_copies(
        (
            piece(at["states"], n_b),
            (high.at[rows, pl.ds(0, n_mid)], high_out.at[rows, pl.ds(0, n_mid)]),
            (high.at[rows, others], high_out.at[rows, others]),
        ),
        sems,
        13,
    )
    for tile in range(own // LANES):
        window, totals = tile_counts(sz, window_ref, tile)
        total = dot(states[:, :n_b], window, (1, 0))
        average = ((total[:hid] + total[hid:]) / totals).astype(BF)
        x = join_inputs(sz, states[:hid, n_b + LANES * tile : n_b + LANES * (tile + 1)], average)
        first = at["inputs2"] + LANES * tile
        low[:, first : first + LANES] = x[:hid]
        low[:, first + own : first + own + LANES] = x[hid:]
        result, scale, state = first_layer(turned2, x, bias2)
        first = at["result2"] + LANES * tile
        high[:hid, first : first + LANES] = result
        high[hid:, first : first + LANES] = jnp.broadcast_to(scale, (8, LANES))
        upper, lower = two_parts(state)
        first = at["embed"] + LANES * tile
        low[:, first : first + LANES] = upper
        low[:, first + own : first + own + LANES] = lower
    last = pl.ds(at["result2"], own)
    tail = (piece(at["embed"], sz.low_lanes - at["embed"]), (high.at[rows, last], high_out.at[rows, last]))
    stores += start_copies(tail, sems, 16)
    serve, take, _, owned = seed_picks(sz, serve_rows[...], take_rows[...], part)
    value = sent_rows(sz, low, at["embed"], serve, take)
    dead = (owned > 0.5) & (alive_column(sz, live_rows[...]) < 0.5)
    lane_at = lax.broadcasted_iota(jnp.int32, (sz.slots, 3 * hid), 1)
    value = jnp.where((lane_at == hid) & dead, SENTINEL, value)
    value = value.reshape(sz.dp, 1, sz.slot, 3 * hid)
    value = jnp.broadcast_to(value, (sz.dp, 4, sz.slot, 3 * hid))
    sent[...] = value.reshape(4 * sz.slots, 3 * hid).astype(BF)
    wait_all(stores)


def sent_rows(sz, low, at, serve, take):
    embed_high = low[:, at : at + sz.own]
    embed_low = low[:, at + sz.own : at + 2 * sz.own]
    take = take.astype(BF)
    return jnp.concatenate(
        [dot(serve.astype(BF), embed_high, (1, 1)), dot(take, embed_high, (1, 1)), dot(take, embed_low, (1, 1))], 1
    )


def seeds_forward(sz, messages, nbr2, pres2, tables):
    hid = sz.hid
    tail = (sz.main, LANES * sz.blocks)
    return call(
        functools.partial(seeds_kernel, sz),
        [
            ((hid, sz.low_lanes), BF),
            ((hid + 8, sz.high_lanes), F32),
            ((sz.count_rows * (sz.own // LANES), LANES), BF),
            ((4 * sz.slots, 3 * hid), BF),
        ],
        [
            ((2 * sz.hold, sz.n_mid), BF),
            ((sz.main * sz.blocks, LANES), F32),
            ((sz.main, sz.full_b), BF),
            ((sz.main, sz.full_b), BF),
            ((sz.main, sz.message_b), BF),
            (tail, BF),
            ((nbr2.shape[0], sz.own), jnp.int32),
            ((nbr2.shape[0], sz.own), jnp.int32),
            ((sz.count_rows * (sz.own // LANES), LANES), BF),
            *[(item.shape, jnp.int32) for item in tables],
            ((hid, sz.low_lanes), BF),
            ((hid + 8, sz.high_lanes), F32),
            ((2 * sz.main, LANES), F32),
            ((8 * sz.hold, hid), F32),
            ((2 * hid, hid), F32),
            ((2 * hid, sz.n_mid), BF),
        ],
        SEEDS_MIB,
        *messages,
        nbr2,
        pres2,
        *tables,
        far_in=(0, 1, 6, 7, 8, 9, 10),
        loose=(2, 3, 4, 5),
        micros=4,
        far_out=(0, 1, 2),
        copies=19,
    )


def rest_kernel(
    sz, low_in, high_in, counts_in, own_a, a1, a2, a3, e1, e2, e3, labels_in, weighting_in, head_in, part_out,
    labels, weighting, head_bias, low, xa, bias, counts, xo, c1, c2, c3, turn_ref,
    states, states2, result1, scale1, inputs2, result2, scale2, grad_a, low_grad, part_ref, sems,
):
    part = lax.axis_index("col")
    own, hid, n_a, n_b, hold = sz.own, sz.hid, sz.n_a, sz.n_b, sz.hold
    at = dict(sz.at)
    for name in ("turned1", "turned2", "weight2", "weight3", "turned3", "states", "embed"):
        at[name] -= sz.n_mid
    lanes = at["embed"] + own
    copies = start_copies(
        (
            (own_a, xo),
            *[(e.at[:, pl.ds(sz.n_mid, sz.early)], c.at[:, pl.ds(0, sz.early)]) for e, c in ((e1, c1), (e2, c2), (e3, c3))],
            *[
                (e.at[:, pl.ds(2 * sz.n_mid + sz.early, LANES)], c.at[:, pl.ds(sz.early, LANES)])
                for e, c in ((e1, c1), (e2, c2), (e3, c3))
            ],
            (low_in.at[:, pl.ds(sz.n_mid, hid)], low.at[:, pl.ds(0, hid)]),
            (high_in.at[:, pl.ds(sz.at["bias"], 2 * LANES)], bias),
            (low_in.at[:, pl.ds(sz.n_mid + hid, lanes - hid)], low.at[:, pl.ds(hid, lanes - hid)]),
            (counts_in, counts),
            (labels_in, labels),
            (weighting_in, weighting),
            (head_in, head_bias),
        ),
        sems,
    )
    late = (n_a - sz.early) // LANES
    for r, message in ((1, a1), (2, a2), (3, a3)):
        tail = unpack_tails(sz, message, 2 * n_a - sz.early, turn_ref)
        unpack_tiles(sz, message, tail, 0, late, hold * r, sz.early, xa)
        unpack_tiles(sz, message, tail, late, n_a // LANES, hold * (4 + r), 0, xa)
    wait_all(copies[:7])
    for r, before in ((1, c1), (2, c2), (3, c3)):
        tail = before[:, sz.early :].astype(F32)[sz.tiles_mid : sz.tiles_mid + EARLY]
        unpack_tiles(sz, before, tail, 0, EARLY, hold * r, 0, xa)
    xa[:hold, :] = xo[:hold, :]
    xa[4 * hold : 5 * hold, :] = xo[hold:, :]
    wait_all(copies[7:9])
    turned1 = low[:, at["turned1"] : at["turned1"] + hid]
    bias1 = bias[:hid, :LANES]
    bias2 = bias[:hid, LANES:]

    result1[...] = dot(turned1, xa[...], (1, 0))

    def forward_step(index, carry):
        lanes = pl.ds(aligned(index * LANES), LANES)
        result, scale, state = activate(result1[:, lanes] + bias1)
        result1[:, lanes] = result
        scale1[:, lanes] = scale
        upper, lower = two_parts(state)
        states[:hid, lanes] = upper
        states[hid:, lanes] = lower
        return carry

    lax.fori_loop(0, n_a // LANES, forward_step, 0, unroll=2)
    wait_all(copies[9:])
    turned2 = low[:, at["turned2"] : at["turned2"] + 2 * hid]
    for tile in range(sz.tiles_b):
        lanes = slice(LANES * tile, LANES * (tile + 1))
        window, totals = tile_counts(sz, counts, tile)
        total = dot(states[:, pl.ds(a_window(sz, part, tile), WINDOW)], window, (1, 0))
        average = ((total[:hid] + total[hid:]) / totals).astype(BF)
        inputs2[:, lanes] = join_inputs(sz, low[:, at["states"] + LANES * tile : at["states"] + LANES * (tile + 1)], average)
    result2[...] = dot(turned2, inputs2[...], (1, 0))
    for tile in range(sz.tiles_b):
        lanes = slice(LANES * tile, LANES * (tile + 1))
        result, scale, state = activate(result2[:, lanes] + bias2)
        result2[:, lanes] = result
        scale2[:, lanes] = scale
        upper, lower = two_parts(state)
        states2[:hid, lanes] = upper
        states2[hid:, lanes] = lower
    counts3, totals3 = tile_counts(sz, counts, sz.tiles_b)
    total = dot(states2[...], counts3, (1, 0))
    average = ((total[:hid] + total[hid:]) / totals3).astype(BF)
    inputs3 = join_inputs(sz, low[:, at["embed"] : at["embed"] + own], average)

    columns = pl.ds(aligned(own * part), own)
    classes = lax.broadcasted_iota(jnp.int32, (sz.head, own), 0)
    head_row = jnp.concatenate([head_bias[...], jnp.zeros((1, LANES - sz.classes), F32)], 1)
    head_column = jnp.broadcast_to(head_row, (LANES, LANES)).T[: sz.head]
    logits = dot(low[: sz.head, at["turned3"] : at["turned3"] + 2 * hid], inputs3, (1, 0)) + head_column
    logits = jnp.where(classes < sz.classes, logits, -1e30)
    highest = jnp.max(logits, 0, keepdims=True)
    expo = jnp.exp(logits - highest)
    totals = jnp.sum(expo, 0, keepdims=True)
    hit = classes == labels[:, columns]
    weights = weighting[:, columns].astype(F32)
    target = jnp.sum(jnp.where(hit, logits, 0.0), 0, keepdims=True)
    ce_total = jnp.sum(weights * (highest + jnp.log(totals) - target), 1, keepdims=True)
    seed_count = jnp.sum(weights, 1, keepdims=True)
    grad_logits = (weights * (expo / totals - jnp.where(hit, 1.0, 0.0))).astype(BF)
    g3 = at["g3"]
    part_ref[: sz.head, g3 : g3 + 2 * hid] = dot(grad_logits, inputs3, (1, 1))
    head_sums = jnp.concatenate([row_sums(grad_logits), jnp.zeros((16, LANES - sz.head), F32)], 1)
    part_ref[sz.head + 16 : sz.head + 32, g3 : g3 + LANES] = head_sums
    lane_at = lax.broadcasted_iota(jnp.int32, (16, LANES), 1)
    sums = jnp.where(lane_at == 0, ce_total, jnp.where(lane_at == 1, seed_count, 0.0))
    part_ref[sz.head + 16 : sz.head + 32, g3 + LANES : g3 + 2 * LANES] = sums
    own_part, average_part = split_inputs(sz, dot(halves(low, at["weight3"], LANES)[:, : sz.head], grad_logits, (1, 0)))
    part_ref[:hid, at["grad_embed"] : at["grad_embed"] + own] = own_part
    grad_mid = spread(sz, average_part / totals3, counts3)
    low_grad2 = norm_backward(grad_mid, result2[...], scale2[...])
    g2 = dot(inputs2[...], low_grad2, (1, 1))
    part_ref[:hid, at["g2"] : at["g2"] + hid] = g2[:hid]
    part_ref[:hid, at["g2"] + hid : at["g2"] + 2 * hid] = g2[hid:]
    part_ref[sz.head : sz.head + 16, g3 + hid : g3 + 2 * hid] = row_sums(low_grad2)
    weight2 = halves(low, at["weight2"], hid)
    grad_a[...] = jnp.zeros_like(grad_a)
    own_part, average_part = split_inputs(sz, dot(weight2, low_grad2, (1, 0)))
    part_ref[:hid, at["grad_b"] : at["grad_b"] + n_b] = own_part
    for tile in range(sz.tiles_b):
        window, totals = tile_counts(sz, counts, tile)
        lanes = pl.ds(a_window(sz, part, tile), WINDOW)
        grad_a[:, lanes] = grad_a[:, lanes] + spread(sz, average_part[:, LANES * tile : LANES * (tile + 1)] / totals, window)
    rows, few = pl.ds(0, hid + 8), pl.ds(0, sz.head + 32)
    split = at["g2"]
    stores = start_copies(
        (
            (part_ref.at[rows, pl.ds(split, hid * 2)], part_out.at[rows, pl.ds(split, hid * 2)]),
            (
                part_ref.at[rows, pl.ds(at["grad_b"], n_b + own)],
                part_out.at[rows, pl.ds(at["grad_b"], n_b + own)],
            ),
        ),
        sems,
        14,
    )

    def backward_step(index, carry):
        lanes = pl.ds(aligned(index * LANES), LANES)
        low_grad[:, lanes] = norm_backward(grad_a[:, lanes], result1[:, lanes], scale1[:, lanes])
        return carry

    lax.fori_loop(0, n_a // LANES, backward_step, 0, unroll=2)
    part_ref[:hid, at["g1"] : at["g1"] + hid] = dot(xa[...], low_grad[...], (1, 1))
    part_ref[sz.head : sz.head + 16, g3 : g3 + hid] = row_sums(low_grad[...])
    stores += start_copies(
        (
            (part_ref.at[rows, pl.ds(0, hid)], part_out.at[rows, pl.ds(0, hid)]),
            (part_ref.at[few, pl.ds(g3, 2 * hid)], part_out.at[few, pl.ds(g3, 2 * hid)]),
        ),
        sems,
        16,
    )
    wait_all(stores)


def rest_step(sz, low, high, counts, means, labels, weighting, head_bias):
    hid = sz.hid
    return call(
        functools.partial(rest_kernel, sz),
        [((hid + 8, sz.part_lanes), F32)],
        [
            (labels.shape, jnp.int32),
            (weighting.shape, jnp.int32),
            (head_bias.shape, F32),
            ((hid, sz.at["embed"] + sz.own - sz.n_mid), BF),
            ((hid, sz.n_a), BF),
            ((hid + 8, 2 * LANES), F32),
            (counts.shape, BF),
            ((2 * sz.hold, sz.n_a), BF),
            *[((sz.main, sz.early + LANES), BF)] * 3,
            ((2 * sz.main, LANES), F32),
            ((2 * hid, sz.n_a), BF),
            ((2 * hid, sz.n_b), BF),
            ((hid, sz.n_a), F32),
            ((1, sz.n_a), F32),
            ((2 * hid, sz.n_b), BF),
            ((hid, sz.n_b), F32),
            ((1, sz.n_b), F32),
            ((hid, sz.n_a), F32),
            ((hid, sz.n_a), BF),
            ((hid + 8, sz.part_lanes), F32),
        ],
        REST_MIB,
        low,
        high,
        counts,
        *means,
        labels,
        weighting,
        head_bias,
        far_in=(0, 1, 2, 3, 10, 11, 12),
        loose=(7, 8, 9),
        micros=14,
        far_out=(0,),
        copies=18,
    )[0]


def seeds_back_kernel(
    sz, serve_in, take_in, live_in, received, low_in, high_in, counts_in, part_in, keep0, keep1, send,
    serve_rows, take_rows, live_rows, x_ref, weight_ref, low, high, window_ref, partial, g1_ref, g2_ref, gb_ref, sems,
):
    part = lax.axis_index("col")
    own, hid, group, n_b, n_mid = sz.own, sz.hid, sz.group, sz.n_b, sz.n_mid
    at = dict(sz.at)
    at["inputs2"] -= at["embed"]
    split = at["grad_b"]
    few = pl.ds(0, sz.head + 32)
    lanes = pl.ds(at["result2"], own)
    copies = start_copies(
        (
            (serve_in, serve_rows),
            (take_in, take_rows),
            (live_in, live_rows),
            (low_in.at[:, pl.ds(at["embed"], 4 * own)], low),
            (part_in.at[:, pl.ds(split + n_b, own)], partial.at[:, pl.ds(split + n_b, own)]),
            (high_in.at[:, lanes], high.at[:, lanes]),
            (low_in.at[:, pl.ds(at["weight2"], 2 * hid)], weight_ref),
            (counts_in.at[pl.ds(0, sz.count_rows * (own // LANES)), :], window_ref),
            (part_in.at[:, pl.ds(split, n_b)], partial.at[:, pl.ds(split, n_b)]),
            (high_in.at[:, pl.ds(0, n_mid)], high.at[:, pl.ds(0, n_mid)]),
            (low_in.at[:, pl.ds(0, n_mid)], x_ref),
            (part_in.at[:, pl.ds(0, at["g3"])], partial.at[:, pl.ds(0, at["g3"])]),
            (part_in.at[few, pl.ds(at["g3"], 2 * hid)], partial.at[few, pl.ds(at["g3"], 2 * hid)]),
        ),
        sems,
    )
    arrived = received[...].astype(F32).reshape(sz.dp, 4, sz.slot, 3 * hid)
    arrived = jnp.sum(arrived, 1).reshape(sz.slots, 3 * hid)
    at["embed"] = 0
    wait_all(copies[:4])
    serve, take, served, taken = seed_picks(sz, serve_rows[...], take_rows[...], part)
    mine = sent_rows(sz, low, 0, serve, take)
    theirs = arrived[:, hid : 2 * hid]
    alive_there = theirs[:, 0:1] < 0.5 * SENTINEL
    theirs = theirs + arrived[:, 2 * hid :]
    differ = mine[:, hid : 2 * hid] + mine[:, 2 * hid :] - arrived[:, :hid]
    differ = jnp.where((taken > 0.5) & (alive_column(sz, live_rows[...]) > 0.5), differ, 0.0)
    dist_total = DIST_WEIGHT * jnp.sum(jnp.sum(differ * differ, 0, keepdims=True), 1, keepdims=True)
    local_high, local_low = two_parts(2.0 * DIST_WEIGHT * differ)
    back = jnp.where((served > 0.5) & alive_there, theirs - mine[:, :hid], 0.0)
    back = (-2.0 * DIST_WEIGHT * back).astype(BF)
    take = take.astype(BF)
    serve = serve.astype(BF)
    wait_all(copies[4:6])
    grad = partial[:hid, at["grad_embed"] : at["grad_embed"] + own]
    grad = grad + dot(local_high, take, (0, 0)) + dot(local_low, take, (0, 0)) + dot(back, serve, (0, 0))
    lanes = slice(at["result2"], at["result2"] + own)
    low_grad2 = norm_backward(grad, high[:hid, lanes], high[hid:, lanes][0:1])
    wait_all(copies[6:9])
    weight2 = halves(weight_ref, 0, hid)
    own_part, average_part = split_inputs(sz, dot(weight2, low_grad2, (1, 0)))
    total_b = partial[:hid, at["grad_b"] : at["grad_b"] + n_b]
    for tile in range(own // LANES):
        window, totals = tile_counts(sz, window_ref, tile)
        total_b = total_b + spread(sz, average_part[:, LANES * tile : LANES * (tile + 1)] / totals, window)
    wait_all(copies[9:10])
    low_grad = jnp.concatenate(
        [
            norm_backward(total_b, high[:hid, :n_b], high[hid:, :n_b][0:1]),
            norm_backward(own_part, high[:hid, n_b:n_mid], high[hid:, n_b:n_mid][0:1]),
        ],
        1,
    )
    wait_all(copies[10:])
    added = dot(halves(low, at["inputs2"], own), low_grad2, (1, 1))
    for half in range(2):
        lanes = slice(at["g2"] + hid * half, at["g2"] + hid * (half + 1))
        g2_ref[hid * half : hid * (half + 1), :] = partial[:hid, lanes] + added[hid * half : hid * (half + 1)]
    g3 = at["g3"]
    sums = partial[sz.head : sz.head + 16, g3 : g3 + 2 * hid]
    gb_ref[:, hid:] = sums[:, hid:] + row_sums(low_grad2)
    half = 4 * sz.hold
    g1_ref[...] = partial[:hid, at["g1"] : at["g1"] + hid] + dot(x_ref[...], low_grad, (1, 1))
    gb_ref[:, :hid] = sums[:, :hid] + row_sums(low_grad)
    head_row = partial[sz.head + 16 : sz.head + 32, g3 : g3 + LANES]
    totals = partial[sz.head + 16 : sz.head + 32, g3 + LANES : g3 + 2 * LANES]
    lane_at = lax.broadcasted_iota(jnp.int32, (16, LANES), 1)
    row_at = lax.broadcasted_iota(jnp.int32, (16, LANES), 0)
    fixed = ((totals[0:1, 0:1] + dist_total) * float(2**LOSS_BITS) + 0.5).astype(jnp.int32)
    count = totals[0:1, 1:2].astype(jnp.int32)
    whole = jnp.where(lane_at < 32, fixed, count)
    bits = (lax.shift_right_logical(whole, lane_at & 31) & 1).astype(F32)
    bits = jnp.where(lane_at < 64, bits, 0.0)
    for r, (target_ref, base) in enumerate(((keep0, 0), (send, 0), (keep1, 0), (send, sz.pay))):
        shard = part ^ r
        block2 = pl.ds(pl.multiple_of(2 * group * shard, 2 * group), 2 * group)
        row = base
        for h in range(hid // LANES):
            lanes = slice(LANES * h, LANES * (h + 1))
            for s in range(2):
                rows = slice(half * s + sz.hold * r, half * s + sz.hold * (r + 1))
                target_ref[row : row + sz.hold, :] = g1_ref[rows, lanes].astype(BF)
                row += sz.hold
        for h in range(hid // LANES):
            target_ref[row : row + 2 * group, :] = g2_ref[block2, LANES * h : LANES * (h + 1)].astype(BF)
            row += 2 * group
        third = partial[: sz.head, pl.ds(aligned(g3 + 2 * group * shard), LANES)]
        target_ref[row : row + sz.head, :] = third.astype(BF)
        row += sz.head
        odd = (shard % 2) == 1
        block = aligned((shard // 2) * LANES)
        one = gb_ref[:, pl.ds(block, LANES)]
        two = gb_ref[:, pl.ds(aligned(hid + block), LANES)]
        one = jnp.where(odd, pltpu.roll(one, group, 1), one)
        two = jnp.where(odd, two, pltpu.roll(two, group, 1))
        bias_row = jnp.where(lane_at < group, one, two)
        misc = jnp.where(row_at == 0, bias_row, jnp.where(row_at == 1, head_row, jnp.where(row_at == 2, bits, 0.0)))
        target_ref[row : row + 16, :] = misc.astype(BF)


def seeds_backward(sz, tables, received, low, high, counts, partial):
    hid = sz.hid
    return call(
        functools.partial(seeds_back_kernel, sz),
        [((sz.pay, LANES), BF), ((sz.pay, LANES), BF), ((2 * sz.pay, LANES), BF)],
        [
            *[(item.shape, jnp.int32) for item in tables],
            ((hid, sz.n_mid), BF),
            ((hid, 2 * hid), BF),
            ((hid, 4 * sz.own), BF),
            ((hid + 8, sz.high_lanes), F32),
            ((sz.count_rows * (sz.own // LANES), LANES), BF),
            ((hid + 8, sz.part_lanes), F32),
            ((8 * sz.hold, hid), F32),
            ((2 * hid, hid), F32),
            ((16, 2 * hid), F32),
        ],
        BACK_MIB,
        *tables,
        received,
        low,
        high,
        counts,
        partial,
        far_in=(0, 1, 2, 4, 5, 6, 7),
        micros=3,
        copies=13,
    )


def lamb_kernel(sz, grad, w1, w2, w3, wh, wb, f1, f2, f3, fh, fb, s1, s2, s3, sh, sb, *rest):
    params = (w1, w2, w3, wh, wb)
    firsts = (f1, f2, f3, fh, fb)
    seconds = (s1, s2, s3, sh, sb)
    moments, squares, updates = rest[:5], rest[5:10], rest[10:15]
    sums_ref, totals_ref, one_ref, three_ref = rest[15:]
    group, hold = sz.group, sz.hold

    def wide(at, rows):
        return jnp.concatenate([grad[at : at + rows, :], grad[at + rows : at + 2 * rows, :]], 1)

    one = wide(0, 2 * hold)
    three = grad[sz.at_three : sz.misc, :]
    turned = pltpu.roll(three, group, 1)
    for f in range(sz.feat):
        one_ref[f, 0:1, :] = one[f : f + 1]
        one_ref[f, 1:2, :] = one[hold + f : hold + f + 1]
    for c in range(sz.classes):
        three_ref[c, 0:1, :] = three[c : c + 1, :group]
        three_ref[c, 1:2, :] = turned[c : c + 1, :group]
    misc = grad[sz.misc : sz.misc + 8, :]
    hidden = jnp.concatenate([misc[0:1, :group], misc[0:1, group : 2 * group]], 0)
    two = wide(sz.rows_one, 2 * group).reshape(2, group, sz.hid)
    grads = (one_ref[...], two, three_ref[...], hidden, misc[1:2, : sz.classes])
    lane_at = lax.broadcasted_iota(jnp.int32, (8, LANES), 1)
    row_at = lax.broadcasted_iota(jnp.int32, (8, LANES), 0)
    sums = jnp.zeros((8, LANES), F32)
    for i in range(5):
        g = grads[i]
        w = params[i][...]
        m = BETA_ONE * firsts[i][...] + (1.0 - BETA_ONE) * g
        v = BETA_TWO * seconds[i][...] + (1.0 - BETA_TWO) * g * g
        u = (m / (1.0 - BETA_ONE**STEP)) / (jnp.sqrt(v / (1.0 - BETA_TWO**STEP)) + ADAM_EPS) + DECAY_RATE * w
        moments[i][...] = m
        squares[i][...] = v
        updates[i][...] = u
        for row, item in ((0, w), (1, u)):
            item = item * item
            if i < 3:
                item = jnp.sum(item, 0)
            total = jnp.sum(jnp.sum(item, 0, keepdims=True), 1, keepdims=True)
            if i == 4:
                total = 0.25 * total
            sums = jnp.where((lane_at == i) & (row_at == row), total, sums)
    sums_ref[...] = sums
    power = (1 << (lane_at & 15)).astype(F32)
    power = jnp.where((lane_at & 31) < 16, power, power * float(2**16))
    bits = jnp.broadcast_to(misc[2:3], (8, LANES)) * power
    loss = jnp.sum(jnp.where(lane_at < 32, bits, 0.0), 1, keepdims=True) * float(2.0**-LOSS_BITS)
    count = jnp.sum(jnp.where((lane_at >= 32) & (lane_at < 64), bits, 0.0), 1, keepdims=True)
    totals_ref[...] = jnp.where(lane_at == 0, loss, count)


def lamb(sz, grad, params, firsts, seconds):
    like = [(item.shape, F32) for item in params]
    return call(
        functools.partial(lamb_kernel, sz),
        like * 3 + [((8, LANES), F32)] * 2,
        [(params[0].shape, F32), (params[2].shape, F32)],
        6,
        grad,
        *params,
        *firsts,
        *seconds,
    )


def step_kernel(own, core, far, across, w1, w2, w3, wh, wb, u1, u2, u3, uh, ub, n1, n2, n3, nh, nb, norms_ref):
    norms = jnp.sqrt((own[...] + core[...]) + (far[...] + across[...]))
    norms_ref[...] = norms[0:2, 0:5]
    for i, (w, u, n) in enumerate(
        ((w1, u1, n1), (w2, u2, n2), (w3, u3, n3), (wh, uh, nh), (wb, ub, nb))
    ):
        ratio = LEARN_RATE * (norms[0:1, i : i + 1] / norms[1:2, i : i + 1])
        n[...] = w[...] - ratio * u[...]


def take_step(sums, params, updates):
    return call(
        step_kernel,
        [(item.shape, F32) for item in params] + [((2, 5), F32)],
        [],
        3,
        *sums,
        *params,
        *updates,
    )


def swap(value, axis, count, bit):
    return lax.ppermute(value, axis, [(i, i ^ bit) for i in range(count)])


def merged(own, other):
    return lax.reduce_precision(own.astype(F32) + other.astype(F32), 8, 7)


def shards(
    features, neighbors_one, present_one, neighbors_two, present_two, neighbors_three, present_three,
    labels, seed_weight, serve_rows, take_seed, fetch_live,
    weight_one, weight_two, weight_three, hidden_bias, head_bias,
    first_one, first_two, first_three, first_hidden, first_head,
    second_one, second_two, second_three, second_hidden, second_head,
):
    sz = Sizes(features, neighbors_one, neighbors_two, neighbors_three, weight_two, weight_three, serve_rows)

    def tree(one, two, three, hidden, head):
        return (one.transpose(1, 0, 2), two, three.transpose(2, 0, 1), hidden, head[None, :])

    def back(one, two, three, hidden, head):
        return (one.transpose(1, 0, 2), two, three.transpose(1, 2, 0), hidden, head[0])

    params = tree(weight_one, weight_two, weight_three, hidden_bias, head_bias)
    firsts = tree(first_one, first_two, first_three, first_hidden, first_head)
    seconds = tree(second_one, second_two, second_three, second_hidden, second_head)

    own_b, packed, mean, tail, *sent = first_messages(sz, features, neighbors_one, present_one, *params[:4])
    s1, s2, s3 = [swap(sent[r - 1], "col", 4, r) for r in (1, 2, 3)]
    links = (neighbors_two, present_two, neighbors_three, present_three)
    own_a, counts, *means = mean_messages(sz, features, neighbors_one, present_one, mean, tail, links)
    s1, *means = lax.optimization_barrier((s1, *means))
    means = [swap(means[r - 1], "col", 4, r) for r in (1, 2, 3)]
    later, s3, counts = lax.optimization_barrier((s2, s3, counts))
    passed = swap(later, "col", 4, 1)
    tables = (serve_rows, take_seed, fetch_live[None, :])
    low, high, window, rows = seeds_forward(
        sz, (own_b, packed, s1, s2, s3, passed), neighbors_two, present_two, tables
    )
    received = lax.all_to_all(rows, ("dp", "col"), split_axis=0, concat_axis=0, tiled=True)
    partial = rest_step(sz, low, high, counts, (own_a, *means, s1, s2, s3), labels[None, :], seed_weight[None, :], head_bias[None, :])
    keep0, keep1, send = seeds_backward(sz, tables, received, low, high, window, partial)
    other = swap(send, "col", 4, 1)
    own = merged(keep0, other[: sz.pay]).astype(BF)
    far = merged(keep1, other[sz.pay :]).astype(BF)
    pair = [[(d, c), (d ^ 1, c ^ 2)] for d in range(sz.dp) for c in range(4)]
    pair = [(a * 4 + b, c * 4 + d) for (a, b), (c, d) in pair]
    near = (swap(far, "col", 4, 2), swap(own, "dp", sz.dp, 1), lax.ppermute(far, ("dp", "col"), pair))
    near = [item.astype(F32) for item in (own, *near)]
    grad = lax.reduce_precision((near[0] + near[1]) + (near[2] + near[3]), 8, 7)
    bit = 2
    while bit < sz.dp:
        grad = merged(grad, swap(grad.astype(BF), "dp", sz.dp, bit))
        bit *= 2
    outs = lamb(sz, grad, params, firsts, seconds)
    moments, squares, updates = outs[:5], outs[5:10], outs[10:15]
    sums, totals = outs[15], outs[16]
    fresh = take_step([sums] + [swap(sums, "col", 4, r) for r in (1, 2, 3)], params, updates)
    return (*back(*fresh[:5]), *back(*moments), *back(*squares), fresh[5], totals[0, 0], totals[0, 1])


def solution(mesh):
    wide = P(None, "col", None)
    tree = [wide, wide, wide, P(None, "col"), P()]
    return jax.shard_map(
        shards,
        mesh=mesh,
        in_specs=(
            P("col", "dp"),
            *[P(None, "dp")] * 6,
            P("dp"),
            P("dp"),
            P("dp", None),
            P("dp", None),
            P("dp"),
            *tree,
            *tree,
            *tree,
        ),
        out_specs=(*tree, *tree, *tree, P(), P(), P()),
        check_vma=False,
    )
```

```python
import functools

import jax
import jax.numpy as jnp
from jax import lax
from jax.experimental import pallas as pl
from jax.experimental.pallas import tpu as pltpu
from jax.sharding import PartitionSpec as P

REACH = 64
STEP = 5
DIST_WEIGHT = 1.0
ROW_EPS = 1e-06
LEARN_RATE = 0.5
BETA_ONE = 0.9
BETA_TWO = 0.999
ADAM_EPS = 1e-06
DECAY_RATE = 0.01

BF = jnp.bfloat16
F32 = jnp.float32
LANES = 128
WINDOW = 768
SENTINEL = 4.0
MIB = 2**20
LOSS_BITS = 14
EARLY = 6
FIRST_MIB = 8
MEAN_MIB = 8
SEEDS_MIB = 16
REST_MIB = 28
BACK_MIB = 12


def cost(micros):
    return pl.CostEstimate(flops=int(micros * 10**9), bytes_accessed=1, transcendentals=0)


def call(kernel, outs, scratch, mib, *args, far_in=(), far_out=(), copies=0, micros=1, loose=(), name=None):
    near = pl.BlockSpec(memory_space=pltpu.VMEM)
    far = pl.BlockSpec(memory_space=pltpu.HBM)
    free = pl.BlockSpec(memory_space=pl.ANY)
    scratch = [pltpu.VMEM(shape, kind) for shape, kind in scratch]
    args = [pltpu.with_memory_space_constraint(a, pltpu.HBM) if i in far_in else a for i, a in enumerate(args)]
    return pl.pallas_call(
        kernel,
        in_specs=[free if i in loose else far if i in far_in else near for i in range(len(args))],
        out_specs=tuple(far if i in far_out else near for i in range(len(outs))),
        out_shape=tuple(
            pltpu.HBM(shape, kind) if i in far_out else jax.ShapeDtypeStruct(shape, kind)
            for i, (shape, kind) in enumerate(outs)
        ),
        scratch_shapes=scratch + ([pltpu.SemaphoreType.DMA((copies,))] if copies else []),
        compiler_params=pltpu.CompilerParams(vmem_limit_bytes=mib * MIB),
        cost_estimate=cost(micros),
        name=name,
    )(*args)


def start_copies(pairs, sems, first=0):
    copies = [pltpu.make_async_copy(src, dst, sems.at[first + i]) for i, (src, dst) in enumerate(pairs)]
    for copy in copies:
        copy.start()
    return copies


def wait_all(copies):
    for copy in copies:
        copy.wait()


class Sizes:
    def __init__(self, features, neighbors_one, neighbors_two, neighbors_three, weight_two, weight_three, serve_rows):
        self.feat = features.shape[0]
        self.main = self.feat - 1
        self.hold = 32
        self.base = features.shape[1]
        self.low = neighbors_one.shape[1]
        self.mid = neighbors_two.shape[1]
        self.seeds = neighbors_three.shape[1]
        self.hid = weight_two.shape[2]
        self.group = weight_two.shape[1]
        self.classes = weight_three.shape[2]
        self.head = -(-self.classes // 16) * 16
        self.own = self.seeds // 4
        self.n_b = 4 * self.own + 2 * LANES
        self.n_a = 16 * self.own + 6 * LANES
        self.n_mid = self.n_b + self.own
        self.n_low = self.n_a + self.n_mid
        self.tiles_b = self.n_b // LANES
        self.tiles_mid = self.n_mid // LANES
        self.tiles_low = self.n_low // LANES
        self.slots = serve_rows.shape[0] * serve_rows.shape[1]
        self.slot = serve_rows.shape[1]
        self.dp = serve_rows.shape[0]
        self.rows_one = 2 * 2 * self.hold
        self.rows_two = 4 * self.group
        self.at_three = self.rows_one + self.rows_two
        self.misc = self.at_three + self.head
        self.pay = self.misc + 16
        self.blocks = -(-self.pay // self.main)
        self.early = EARLY * LANES
        self.message_a = self.pair_lanes(self.n_a, self.n_a - self.early)
        self.message_b = self.pair_lanes(self.n_mid, self.n_mid + self.early)
        self.full_b = self.message_b + LANES * self.blocks
        self.tiles_b_all = 16 * self.own // LANES + 1
        self.count_rows = WINDOW + 16
        hid, at = self.hid, self.n_mid
        places = {}
        for name, lanes in (
            ("turned1", hid), ("turned2", 2 * hid), ("weight2", 2 * hid), ("weight3", 2 * LANES), ("turned3", 2 * hid),
            ("states", self.n_b), ("embed", 2 * self.own), ("inputs2", 2 * self.own),
        ):
            places[name] = at
            at += lanes
        self.low_lanes = at
        at = 0
        for name, lanes in (("result1", self.n_mid), ("result2", self.own), ("bias", 2 * LANES)):
            places[name] = at
            at += lanes
        self.high_lanes = at
        at = 0
        for name, lanes in (("g1", hid), ("g2", 2 * hid), ("g3", 2 * hid), ("grad_b", self.n_b), ("grad_embed", self.own)):
            places[name] = at
            at += lanes
        self.part_lanes = at
        self.at = places

    def pair_lanes(self, means, own):
        lanes = means + own
        return lanes + LANES * -(-lanes // LANES // self.main)

    def first_ranges(self, part):
        a, b, c = self.ranges(part)
        b = (b[0], 0, b[2])
        c = (c[0], b[2], c[2])
        return [b, c, (a[0], self.n_mid, self.early)], [b, c]

    def second_ranges(self, part):
        first = self.a_start(part)
        return [(first + self.early, 0, self.n_a - self.early)], [(first, 0, self.n_a)]

    def a_start(self, part):
        return jnp.clip(16 * self.own * part - 3 * LANES, 0, self.low - self.n_a)

    def b_start(self, part):
        return jnp.maximum(4 * self.own * part - LANES, 0)

    def b_columns(self, part, tile):
        return pl.ds(aligned(jnp.minimum(self.b_start(part) + LANES * tile, self.mid - LANES)), LANES)

    def mid_columns(self, part, tile):
        if tile < self.tiles_b:
            return self.b_columns(part, tile)
        return pl.ds(aligned(self.own * part + LANES * (tile - self.tiles_b)), LANES)

    def ranges(self, part):
        return (
            (self.a_start(part), 0, self.n_a),
            (self.b_start(part), self.n_a, self.n_b),
            (self.own * part, self.n_a + self.n_b, self.own),
        )


def dot(a, b, over):
    return lax.dot_general(a, b, (((over[0],), (over[1],)), ((), ())), preferred_element_type=F32)


def two_parts(value):
    high = value.astype(BF)
    return high, (value - high.astype(F32)).astype(BF)


def three_parts(value):
    high = value.astype(BF).astype(F32)
    rest = value - high
    middle = rest.astype(BF).astype(F32)
    return high, middle, (rest - middle).astype(BF).astype(F32)


def aligned(value):
    return pl.multiple_of(value, LANES)


def sigmoid(value):
    return 0.5 * jnp.tanh(0.5 * value) + 0.5


def unpack_tile(sz, message, tail, tile):
    spare = jnp.zeros((sz.hold - sz.feat, LANES), F32)
    main = message[:, LANES * tile : LANES * (tile + 1)].astype(F32)
    return jnp.concatenate([main, tail[tile : tile + 1, :], spare], 0).astype(BF)


def mean_tiles(sz, begin, tiles, feat_ref, nbr_ref, pres_ref, mean_ref, tail_ref, base_ref, code_ref, count_ref):
    last = feat_ref.shape[1] // LANES - 6
    slots = nbr_ref.shape[0]
    base_ref[...] = jnp.zeros_like(base_ref)
    if begin % 8 or tiles % 8:
        code_ref[...] = jnp.full_like(code_ref, -1)
        count_ref[...] = jnp.ones_like(count_ref)
    for tile in range(feat_ref.shape[1] // LANES):
        row = feat_ref[:, LANES * tile : LANES * (tile + 1)].astype(F32)
        base_ref[8 + tile : 9 + tile, :] = row[sz.main : sz.feat]

    def one_tile(step, carry):
        lane = aligned(step * LANES)
        present = pres_ref[:, pl.ds(lane, LANES)]
        valid = present.astype(F32)
        counts = jnp.maximum(jnp.sum(valid, 0, keepdims=True), 1.0)
        first = jnp.clip(4 * step - 1, 0, last)
        links = nbr_ref[:, pl.ds(lane, LANES)]
        code = jnp.where(present > 0, links, -1)
        count_ref[pl.ds(step, 1), :] = counts
        for slot in range(slots):
            code_ref[slot, pl.ds(step, 1), :] = code[slot : slot + 1]
        local = links - first * LANES
        piece = local >> 7
        spot = local & 127
        sources = [
            feat_ref[:, pl.ds(aligned((first + j) * LANES), LANES)].astype(F32) for j in range(6)
        ]
        totals = [jnp.zeros((8, LANES), F32) for _ in range(sz.main // 8)]
        for slot in range(slots):
            spots = jnp.broadcast_to(spot[slot : slot + 1], (8, LANES))
            pieces = jnp.broadcast_to(piece[slot : slot + 1], (8, LANES))
            marks = jnp.broadcast_to(valid[slot : slot + 1], (8, LANES))
            for h in range(sz.main // 8):
                taken = None
                for j in range(6):
                    found = jnp.take_along_axis(
                        sources[j][8 * h : 8 * h + 8], spots, axis=1, mode="promise_in_bounds"
                    )
                    taken = found if j == 0 else jnp.where(pieces == j, found, taken)
                totals[h] = totals[h] + taken * marks
        mean_ref[:, pl.ds(lane, LANES)] = (jnp.concatenate(totals, 0) / counts).astype(BF)
        return carry

    even = begin + (tiles - begin) // 4 * 4
    lax.fori_loop(begin, even, one_tile, 0, unroll=4)
    for step in range(even, tiles):
        one_tile(step, 0)
    sub = lax.broadcasted_iota(jnp.int32, (8, LANES), 0)

    for block in range(begin // 8, -(-tiles // 8)):
        total = jnp.zeros((8, LANES), F32)
        for slot in range(slots):
            code = code_ref[slot, 8 * block : 8 * (block + 1), :]
            piece = (code >> 7) - (4 * (8 * block + sub) - 1)
            taken = None
            for j in range(6):
                source = base_ref[pl.ds(8 + 32 * block - 1 + j, 8, stride=4), :]
                found = jnp.take_along_axis(source, code & 127, axis=1, mode="promise_in_bounds")
                taken = found if j == 0 else jnp.where(piece == j, found, taken)
            total = total + jnp.where(code >= 0, taken, 0.0)
        tail_ref[8 * block : 8 * (block + 1), :] = total / count_ref[8 * block : 8 * (block + 1), :]


def pack_pair(sz, ranges, feat_ref, base_ref, mean_ref, tail_ref, turn_ref, out_ref):
    turn_ref[...] = jnp.zeros_like(turn_ref)
    lanes = 0
    for source_ref, rows_ref, shift, group in zip((feat_ref, mean_ref), (base_ref, tail_ref), (8, 0), ranges):
        for first, at, count in group:
            at = at + lanes
            out_ref[:, at : at + count] = source_ref[: sz.main, pl.ds(aligned(first), count)]
            at, rows = at // LANES, count // LANES
            turn_ref[at : at + rows, :] = rows_ref[pl.ds(shift + first // LANES, rows), :]
        lanes += sum(count for _, _, count in group)
    for block in range(-(-lanes // LANES // sz.main)):
        at = lanes + LANES * block
        out_ref[:, at : at + LANES] = turn_ref[sz.main * block : sz.main * (block + 1), :].astype(BF)


def own_pair(sz, ranges, feat_ref, mean_ref, tail_ref, own_ref):
    spare = jnp.zeros((sz.hold - sz.feat, LANES), F32)
    base = ranges[0][1]
    for start, at, count in ranges:
        for tile in range(count // LANES):
            lanes = pl.ds(aligned(start + LANES * tile), LANES)
            out_lanes = slice(at - base + LANES * tile, at - base + LANES * (tile + 1))
            own = [feat_ref[:, lanes].astype(F32), spare]
            own_ref[: sz.hold, out_lanes] = jnp.concatenate(own, 0).astype(BF)
            tail = tail_ref[pl.ds(start // LANES + tile, 1), :]
            average = [mean_ref[:, lanes].astype(F32), tail, spare]
            own_ref[sz.hold :, out_lanes] = jnp.concatenate(average, 0).astype(BF)


def mean_scratch(sz, tiles, slots):
    return [
        ((sz.main, LANES * tiles), BF),
        ((-(-tiles // 8) * 8, LANES), F32),
        ((2 * sz.main, LANES), F32),
        ((4 * -(-tiles // 8) * 8 + 16, LANES), F32),
        ((slots, -(-tiles // 8) * 8, LANES), jnp.int32),
        ((-(-tiles // 8) * 8, LANES), F32),
    ]


def unpack_tails(sz, message, lanes, turn_ref):
    for block in range(-(-lanes // LANES // sz.main)):
        at = lanes + LANES * block
        turn_ref[sz.main * block : sz.main * (block + 1), :] = message[:, at : at + LANES].astype(F32)
    return turn_ref[...]


def unpack_tiles(sz, message, tail, first, tiles, row, at, out_ref):
    for tile in range(tiles):
        lane = at + LANES * tile
        out_ref[row : row + sz.hold, lane : lane + LANES] = unpack_tile(sz, message, tail, first + tile)


def first_kernel(
    sz, features, neighbors, present, w1_in, w2_in, w3_in, wh_in, own_b, packed, mean_out, tail_out, m1, m2, m3,
    feat_ref, nbr_ref, pres_ref, w1, w2, w3, wh, own_ref,
    mean_ref, tail_ref, turn_ref, base_ref, code_ref, count_ref, one_ref, three_ref, pack, sems,
):
    part = lax.axis_index("col")
    rows = pl.ds(0, nbr_ref.shape[1])
    weights = start_copies(((w1_in, w1), (w2_in, w2), (w3_in, w3), (wh_in, wh)), sems)
    copies = start_copies(
        (
            (features.at[:, pl.ds(0, feat_ref.shape[1])], feat_ref),
            (neighbors.at[:, rows], nbr_ref),
            (present.at[:, rows], pres_ref),
        ),
        sems,
        4,
    )
    wait_all(weights)
    one_ref[...] = jnp.zeros_like(one_ref)
    three_ref[...] = jnp.zeros_like(three_ref)
    for s in range(2):
        for f in range(sz.feat):
            one_ref[s * sz.hold + f : s * sz.hold + f + 1, :] = w1[f, s : s + 1, :]
        for c in range(sz.classes):
            three_ref[c : c + 1, s * sz.group : (s + 1) * sz.group] = w3[c, s : s + 1, :]
    at = 0
    for half in range(sz.hid // LANES):
        pack[at : at + 2 * sz.hold, :] = one_ref[:, LANES * half : LANES * (half + 1)]
        at += 2 * sz.hold
    for half in range(sz.hid // LANES):
        for s in range(2):
            pack[at : at + sz.group, :] = w2[s, :, LANES * half : LANES * (half + 1)]
            at += sz.group
    pack[at : at + sz.head, :] = three_ref[...]
    row = jnp.concatenate([wh[0:1, :], wh[1:2, :]], 1)
    row_at = lax.broadcasted_iota(jnp.int32, (16, LANES), 0)
    misc = jnp.zeros((16, LANES), F32)
    for i, piece in enumerate(three_parts(row)):
        misc = jnp.where(row_at == i, piece, misc)
    pack[sz.misc : sz.pay, :] = misc
    pack[sz.pay :, :] = jnp.zeros((sz.main * sz.blocks - sz.pay, LANES), F32)
    store = start_copies(((pack, packed),), sems, 7)
    for block in range(sz.blocks):
        at = sz.message_b + LANES * block
        piece = pack[sz.main * block : sz.main * (block + 1), :].astype(BF)
        m1[:, at : at + LANES] = piece
        m2[:, at : at + LANES] = piece
    wait_all(copies)
    mean_tiles(sz, 0, sz.tiles_b_all, feat_ref, nbr_ref, pres_ref, mean_ref, tail_ref, base_ref, code_ref, count_ref)
    store += start_copies(((mean_ref, mean_out), (tail_ref, tail_out)), sems, 9)
    own_pair(sz, sz.ranges(part)[1:], feat_ref, mean_ref, tail_ref, own_ref)
    store += start_copies(((own_ref, own_b),), sems, 8)
    for r, out in ((1, m1), (2, m2), (3, m3)):
        pack_pair(sz, sz.first_ranges(part ^ r), feat_ref, base_ref, mean_ref, tail_ref, turn_ref, out)
    wait_all(store)


def first_messages(sz, features, neighbors, present, w1, w2, w3, hidden):
    rows = LANES * sz.tiles_b_all
    bases = min(4 * rows + LANES, sz.base)
    slots = neighbors.shape[0]
    return call(
        functools.partial(first_kernel, sz),
        [
            ((2 * sz.hold, sz.n_mid), BF),
            ((sz.main * sz.blocks, LANES), F32),
            ((sz.main, rows), BF),
            ((-(-sz.tiles_b_all // 8) * 8, LANES), F32),
            ((sz.main, sz.full_b), BF),
            ((sz.main, sz.full_b), BF),
            ((sz.main, sz.message_b), BF),
        ],
        [
            ((sz.feat, bases), BF),
            ((slots, rows), jnp.int32),
            ((slots, rows), jnp.int32),
            (w1.shape, F32),
            (w2.shape, F32),
            (w3.shape, F32),
            (hidden.shape, F32),
            ((2 * sz.hold, sz.n_mid), BF),
            *mean_scratch(sz, sz.tiles_b_all, slots),
            ((2 * sz.hold, sz.hid), F32),
            ((sz.head, LANES), F32),
            ((sz.main * sz.blocks, LANES), F32),
        ],
        FIRST_MIB,
        features,
        neighbors,
        present,
        w1,
        w2,
        w3,
        hidden,
        far_in=range(7),
        far_out=(0, 1, 2, 3),
        copies=11,
        micros=4,
    )


def mean_kernel(
    sz, feat_ref, nbr_ref, pres_ref, mean_in, tail_in, nbr2, pres2, nbr3, pres3, own_a, counts_out, a1, a2, a3,
    mean_ref, tail_ref, turn_ref, base_ref, code_ref, count_ref, own_ref, kept_ref, counts, sems,
):
    part = lax.axis_index("col")
    tiles = sz.low // LANES
    begin = sz.tiles_b_all
    loads = start_copies(((mean_in, mean_ref.at[:, pl.ds(0, LANES * begin)]), (tail_in, kept_ref)), sems, 1)
    fill_counts(sz, part, nbr2, pres2, nbr3, pres3, counts)
    store = start_copies(((counts, counts_out),), sems, 3)
    mean_tiles(sz, begin, tiles, feat_ref, nbr_ref, pres_ref, mean_ref, tail_ref, base_ref, code_ref, count_ref)
    wait_all(loads)
    tail_ref[:begin, :] = kept_ref[:begin, :]
    own_pair(sz, sz.ranges(part)[:1], feat_ref, mean_ref, tail_ref, own_ref)
    store += start_copies(((own_ref, own_a),), sems)
    for r, out in ((1, a1), (2, a2), (3, a3)):
        pack_pair(sz, sz.second_ranges(part ^ r), feat_ref, base_ref, mean_ref, tail_ref, turn_ref, out)
    wait_all(store)


def mean_messages(sz, features, neighbors, present, mean, tail, links):
    counts = (sz.count_rows * (sz.tiles_b + sz.own // LANES), LANES)
    return call(
        functools.partial(mean_kernel, sz),
        [((2 * sz.hold, sz.n_a), BF), (counts, BF)] + [((sz.main, sz.message_a), BF)] * 3,
        mean_scratch(sz, sz.low // LANES, neighbors.shape[0]) + [((2 * sz.hold, sz.n_a), BF), (tail.shape, F32), (counts, BF)],
        MEAN_MIB,
        features,
        neighbors,
        present,
        mean,
        tail,
        *links,
        far_in=(3, 4),
        far_out=(0, 1),
        copies=4,
        micros=6,
    )


def window_counts(local, rows):
    spots = lax.broadcasted_iota(jnp.int32, (256, LANES), 0).astype(F32).astype(BF)
    blocks = []
    for first in range(0, rows, 256):
        place = local - first
        place = jnp.where((place >= 0) & (place < 256), place, -1).astype(F32)
        counts = jnp.zeros((256, LANES), BF)
        for slot in range(local.shape[0]):
            row = jnp.broadcast_to(place[slot : slot + 1], (16, LANES)).astype(BF)
            row = jnp.concatenate([row] * 16, 0)
            counts = counts + jnp.where(row == spots, jnp.bfloat16(1.0), jnp.bfloat16(0.0))
        blocks.append(counts)
    return jnp.concatenate(blocks, 0)


def slot_totals(present):
    return jnp.maximum(jnp.sum(present.astype(F32), 0, keepdims=True), 1.0)


def a_window(sz, part, tile):
    first = 4 * sz.b_start(part) + 4 * LANES * tile - LANES - sz.a_start(part)
    return aligned(jnp.clip(first, 0, sz.n_a - WINDOW))


def counts_tile(sz, links, marks, start, at, counts):
    local = jnp.where(marks > 0, links - start, -1)
    counts[at : at + WINDOW, :] = window_counts(local, WINDOW)
    counts[at + WINDOW : at + sz.count_rows, :] = jnp.broadcast_to(slot_totals(marks), (16, LANES)).astype(BF)


def fill_counts(sz, part, nbr2, pres2, nbr3, pres3, counts):
    for tile in range(sz.tiles_b):
        columns = sz.b_columns(part, tile)
        start = sz.a_start(part) + a_window(sz, part, tile)
        counts_tile(sz, nbr2[:, columns], pres2[:, columns], start, sz.count_rows * tile, counts)
    for tile in range(sz.own // LANES):
        columns = pl.ds(aligned(sz.own * part + LANES * tile), LANES)
        at = sz.count_rows * (sz.tiles_b + tile)
        counts_tile(sz, nbr3[:, columns], pres3[:, columns], sz.b_start(part), at, counts)


def tile_counts(sz, counts, tile):
    at = sz.count_rows * tile
    totals = counts[at + WINDOW : at + WINDOW + 16, :].astype(F32)[0:1]
    return counts[at : at + WINDOW, :], totals


def activate(result):
    active = result * sigmoid(result)
    scale = lax.rsqrt(jnp.sum(active * active, 0, keepdims=True) + ROW_EPS)
    return result, scale, active * scale


def first_layer(weight, inputs, bias):
    result = dot(weight, inputs, (1, 0)) + bias
    active = result * sigmoid(result)
    scale = lax.rsqrt(jnp.sum(active * active, 0, keepdims=True) + ROW_EPS)
    return result, scale, active * scale


def join_inputs(sz, own, average):
    pieces = []
    for c in range(4):
        pieces.append(own[sz.group * c : sz.group * (c + 1)])
        pieces.append(average[sz.group * c : sz.group * (c + 1)])
    return jnp.concatenate(pieces, 0)


def norm_backward(grad, result, scale):
    gate = sigmoid(result)
    active = result * gate
    inner = jnp.sum(grad * active, 0, keepdims=True)
    grad_active = scale * grad - active * (scale * scale * scale * inner)
    return (grad_active * gate * (1.0 + result * (1.0 - gate))).astype(BF)


def split_inputs(sz, grad):
    pieces = [grad[sz.group * c : sz.group * (c + 1)] for c in range(8)]
    return jnp.concatenate(pieces[0::2], 0), jnp.concatenate(pieces[1::2], 0)


def row_sums(grad):
    return dot(jnp.ones((16, grad.shape[1]), BF), grad, (1, 1))


def spread(sz, scaled, counts):
    return dot(scaled.astype(BF), counts, (1, 1))


def halves(ref, at, lanes):
    return jnp.concatenate([ref[:, at : at + lanes], ref[:, at + lanes : at + 2 * lanes]], 0)


def store_halves(ref, at, lanes, value):
    rows = value.shape[0] // 2
    ref[:rows, at : at + lanes] = value[:rows]
    ref[:rows, at + lanes : at + 2 * lanes] = value[rows:]


def slot_column(table):
    rows, slots = table.shape
    wide = jnp.broadcast_to(table.astype(F32)[:, None, :], (rows, slots, slots))
    hit = lax.broadcasted_iota(jnp.int32, wide.shape, 1) == lax.broadcasted_iota(jnp.int32, wide.shape, 2)
    return jnp.sum(jnp.where(hit, wide, 0.0), 2, keepdims=True).reshape(rows * slots, 1)


def alive_column(sz, live):
    shape = (sz.dp, sz.dp)
    hit = lax.broadcasted_iota(jnp.int32, shape, 0) == lax.broadcasted_iota(jnp.int32, shape, 1)
    counts = jnp.sum(jnp.where(hit, jnp.broadcast_to(live.astype(F32), shape), 0.0), 1, keepdims=True)
    slot = lax.broadcasted_iota(jnp.int32, (sz.dp, sz.slot), 1).astype(F32)
    return slot_column(jnp.where(slot < counts, 1.0, 0.0))


def seed_picks(sz, serve_rows, take_rows, part):
    spots = (lax.broadcasted_iota(jnp.int32, (sz.slots, sz.own), 1) + sz.own * part).astype(F32)
    serve = jnp.where(slot_column(serve_rows) == spots, 1.0, 0.0)
    take = jnp.where(slot_column(take_rows) == spots, 1.0, 0.0)
    return serve, take, jnp.sum(serve, 1, keepdims=True), jnp.sum(take, 1, keepdims=True)


def seeds_kernel(
    sz, own_b, packed, s1, s2, s3, passed, nbr2_in, pres2_in, serve_in, take_in, live_in,
    low_out, high_out, window_out, sent,
    xb, pack, m1, m2, m3, p3, nbr2, pres2, window_ref, serve_rows, take_rows, live_rows, low, high, turn_ref, w1_ref, w2_ref, states, sems,
):
    part = lax.axis_index("col")
    own, hid, n_b, group, hold, at = sz.own, sz.hid, sz.n_b, sz.group, sz.hold, sz.at
    n_mid = sz.n_mid
    copies = start_copies(
        (
            (packed, pack),
            (passed.at[:, pl.ds(sz.message_b, LANES * sz.blocks)], p3),
            (s1, m1),
            (s2, m2),
            (s3, m3),
            (own_b, xb),
            (nbr2_in.at[:, pl.ds(aligned(own * part), own)], nbr2),
            (pres2_in.at[:, pl.ds(aligned(own * part), own)], pres2),
            (serve_in, serve_rows),
            (take_in, take_rows),
            (live_in, live_rows),
        ),
        sems,
    )
    wait_all(copies[:4])
    for r, (message, first_lane) in enumerate(((None, 0), (m1, sz.message_b), (m2, sz.message_b), (p3, 0))):
        for block in range(sz.blocks if r else 0):
            first = first_lane + LANES * block
            pack[sz.main * block : sz.main * (block + 1), :] = message[:, first : first + LANES].astype(F32)
        shard = part ^ r
        for half in range(hid // LANES):
            lanes = slice(LANES * half, LANES * (half + 1))
            for s in range(2):
                first = 2 * hold * half + hold * s
                w1_ref[4 * hold * s + hold * r : 4 * hold * s + hold * (r + 1), lanes] = pack[first : first + hold, :]
            first = sz.rows_one + 2 * group * half
            row = pl.multiple_of(2 * group * shard, 2 * group)
            w2_ref[pl.ds(row, 2 * group), lanes] = pack[first : first + 2 * group, :]
        low[: sz.head, pl.ds(aligned(at["turned3"] + 2 * group * shard), LANES)] = pack[sz.at_three : sz.misc, :].astype(BF)
        misc = pack[sz.misc : sz.misc + 8, :]
        column = jnp.broadcast_to(misc[0:1] + misc[1:2] + misc[2:3], (LANES, LANES)).T
        row = pl.multiple_of(group * shard, group)
        for layer in range(2):
            lanes = slice(at["bias"] + LANES * layer, at["bias"] + LANES * (layer + 1))
            high[pl.ds(row, group), lanes] = column[group * layer : group * (layer + 1)]
    turned1 = w1_ref[...].T.astype(BF)
    turned2 = w2_ref[...].T.astype(BF)
    low[:, at["turned1"] : at["turned1"] + hid] = turned1
    low[:, at["turned2"] : at["turned2"] + 2 * hid] = turned2
    store_halves(low, at["weight2"], hid, w2_ref[...].astype(BF))
    weight3 = low[: sz.head, at["turned3"] : at["turned3"] + 2 * hid].astype(F32).T
    weight3 = jnp.concatenate([weight3, jnp.zeros((2 * hid, LANES - sz.head), F32)], 1)
    store_halves(low, at["weight3"], LANES, weight3.astype(BF))

    def piece(lanes, count):
        return (low.at[:, pl.ds(lanes, count)], low_out.at[:, pl.ds(lanes, count)])

    stores = start_copies((piece(n_mid, at["states"] - n_mid),), sems, 11)
    wait_all(copies[4:])
    for tile in range(own // LANES):
        lanes = slice(LANES * tile, LANES * (tile + 1))
        counts_tile(sz, nbr2[:, lanes], pres2[:, lanes], sz.b_start(part), sz.count_rows * tile, window_ref)
    stores += start_copies(((window_ref, window_out),), sems, 18)
    low[:hold, :n_mid] = xb[:hold, :]
    low[4 * hold : 5 * hold, :n_mid] = xb[hold:, :]
    for r, message in ((1, m1), (2, m2), (3, m3)):
        tail = unpack_tails(sz, message, 2 * n_mid + sz.early, turn_ref)
        unpack_tiles(sz, message, tail, 0, sz.tiles_mid, hold * r, 0, low)
        first = (n_mid + sz.early) // LANES
        unpack_tiles(sz, message, tail, first, sz.tiles_mid, hold * (4 + r), 0, low)
    stores += start_copies((piece(0, n_mid),), sems, 12)
    bias1 = high[:hid, at["bias"] : at["bias"] + LANES]
    bias2 = high[:hid, at["bias"] + LANES : at["bias"] + 2 * LANES]
    high[:hid, :n_mid] = dot(turned1, low[:, :n_mid], (1, 0))
    for tile in range(sz.tiles_mid):
        lanes = slice(LANES * tile, LANES * (tile + 1))
        result, scale, state = activate(high[:hid, lanes] + bias1)
        high[:hid, lanes] = result
        high[hid:, lanes] = jnp.broadcast_to(scale, (8, LANES))
        upper, lower = two_parts(state)
        states[:hid, lanes] = upper
        states[hid:, lanes] = lower
    low[:, at["states"] : at["states"] + n_b] = states[:hid, :n_b]
    rows = pl.ds(0, hid + 8)
    others = pl.ds(at["bias"], 2 * LANES)
    stores += start_copies(
        (
            piece(at["states"], n_b),
            (high.at[rows, pl.ds(0, n_mid)], high_out.at[rows, pl.ds(0, n_mid)]),
            (high.at[rows, others], high_out.at[rows, others]),
        ),
        sems,
        13,
    )
    for tile in range(own // LANES):
        window, totals = tile_counts(sz, window_ref, tile)
        total = dot(states[:, :n_b], window, (1, 0))
        average = ((total[:hid] + total[hid:]) / totals).astype(BF)
        x = join_inputs(sz, states[:hid, n_b + LANES * tile : n_b + LANES * (tile + 1)], average)
        first = at["inputs2"] + LANES * tile
        low[:, first : first + LANES] = x[:hid]
        low[:, first + own : first + own + LANES] = x[hid:]
        result, scale, state = first_layer(turned2, x, bias2)
        first = at["result2"] + LANES * tile
        high[:hid, first : first + LANES] = result
        high[hid:, first : first + LANES] = jnp.broadcast_to(scale, (8, LANES))
        upper, lower = two_parts(state)
        first = at["embed"] + LANES * tile
        low[:, first : first + LANES] = upper
        low[:, first + own : first + own + LANES] = lower
    last = pl.ds(at["result2"], own)
    tail = (piece(at["embed"], sz.low_lanes - at["embed"]), (high.at[rows, last], high_out.at[rows, last]))
    stores += start_copies(tail, sems, 16)
    serve, take, _, owned = seed_picks(sz, serve_rows[...], take_rows[...], part)
    embed_high = low[:, at["embed"] : at["embed"] + own]
    served = dot(serve.astype(BF), embed_high, (1, 1))
    taken = dot(take.astype(BF), embed_high, (1, 1))
    dead = (owned > 0.5) & (alive_column(sz, live_rows[...]) < 0.5)
    first = lax.broadcasted_iota(jnp.int32, (sz.slots, hid), 1) == 0
    value = jnp.concatenate([served, jnp.where(first & dead, SENTINEL, taken)], 1)
    value = value.reshape(sz.dp, 1, sz.slot, 2 * hid)
    value = jnp.broadcast_to(value, (sz.dp, 4, sz.slot, 2 * hid))
    sent[...] = value.reshape(4 * sz.slots, 2 * hid).astype(BF)
    wait_all(stores)


def sent_rows(sz, low, at, serve, take):
    embed_high = low[:, at : at + sz.own]
    embed_low = low[:, at + sz.own : at + 2 * sz.own]
    take = take.astype(BF)
    return jnp.concatenate(
        [dot(serve.astype(BF), embed_high, (1, 1)), dot(take, embed_high, (1, 1)), dot(take, embed_low, (1, 1))], 1
    )


def seeds_forward(sz, messages, nbr2, pres2, tables):
    hid = sz.hid
    tail = (sz.main, LANES * sz.blocks)
    return call(
        functools.partial(seeds_kernel, sz),
        [
            ((hid, sz.low_lanes), BF),
            ((hid + 8, sz.high_lanes), F32),
            ((sz.count_rows * (sz.own // LANES), LANES), BF),
            ((4 * sz.slots, 2 * hid), BF),
        ],
        [
            ((2 * sz.hold, sz.n_mid), BF),
            ((sz.main * sz.blocks, LANES), F32),
            ((sz.main, sz.full_b), BF),
            ((sz.main, sz.full_b), BF),
            ((sz.main, sz.message_b), BF),
            (tail, BF),
            ((nbr2.shape[0], sz.own), jnp.int32),
            ((nbr2.shape[0], sz.own), jnp.int32),
            ((sz.count_rows * (sz.own // LANES), LANES), BF),
            *[(item.shape, jnp.int32) for item in tables],
            ((hid, sz.low_lanes), BF),
            ((hid + 8, sz.high_lanes), F32),
            ((2 * sz.main, LANES), F32),
            ((8 * sz.hold, hid), F32),
            ((2 * hid, hid), F32),
            ((2 * hid, sz.n_mid), BF),
        ],
        SEEDS_MIB,
        *messages,
        nbr2,
        pres2,
        *tables,
        far_in=(0, 1, 6, 7, 8, 9, 10),
        loose=(2, 3, 4, 5),
        micros=4,
        far_out=(0, 1, 2),
        copies=19,
    )


def rest_kernel(
    sz, low_in, high_in, counts_in, own_a, a1, a2, a3, e1, e2, e3, labels_in, weighting_in, head_in, part_out,
    labels, weighting, head_bias, low, xa, bias, counts, xo, c1, c2, c3, turn_ref,
    states, states2, result1, scale1, inputs2, result2, scale2, grad_a, low_grad, part_ref, sems,
):
    part = lax.axis_index("col")
    own, hid, n_a, n_b, hold = sz.own, sz.hid, sz.n_a, sz.n_b, sz.hold
    at = dict(sz.at)
    for name in ("turned1", "turned2", "weight2", "weight3", "turned3", "states", "embed"):
        at[name] -= sz.n_mid
    lanes = at["embed"] + own
    copies = start_copies(
        (
            (own_a, xo),
            *[(e.at[:, pl.ds(sz.n_mid, sz.early)], c.at[:, pl.ds(0, sz.early)]) for e, c in ((e1, c1), (e2, c2), (e3, c3))],
            *[
                (e.at[:, pl.ds(2 * sz.n_mid + sz.early, LANES)], c.at[:, pl.ds(sz.early, LANES)])
                for e, c in ((e1, c1), (e2, c2), (e3, c3))
            ],
            (low_in.at[:, pl.ds(sz.n_mid, hid)], low.at[:, pl.ds(0, hid)]),
            (high_in.at[:, pl.ds(sz.at["bias"], 2 * LANES)], bias),
            (low_in.at[:, pl.ds(sz.n_mid + hid, lanes - hid)], low.at[:, pl.ds(hid, lanes - hid)]),
            (counts_in, counts),
            (labels_in, labels),
            (weighting_in, weighting),
            (head_in, head_bias),
        ),
        sems,
    )
    late = (n_a - sz.early) // LANES
    for r, message in ((1, a1), (2, a2), (3, a3)):
        tail = unpack_tails(sz, message, 2 * n_a - sz.early, turn_ref)
        unpack_tiles(sz, message, tail, 0, late, hold * r, sz.early, xa)
        unpack_tiles(sz, message, tail, late, n_a // LANES, hold * (4 + r), 0, xa)
    wait_all(copies[:7])
    for r, before in ((1, c1), (2, c2), (3, c3)):
        tail = before[:, sz.early :].astype(F32)[sz.tiles_mid : sz.tiles_mid + EARLY]
        unpack_tiles(sz, before, tail, 0, EARLY, hold * r, 0, xa)
    xa[:hold, :] = xo[:hold, :]
    xa[4 * hold : 5 * hold, :] = xo[hold:, :]
    wait_all(copies[7:9])
    turned1 = low[:, at["turned1"] : at["turned1"] + hid]
    bias1 = bias[:hid, :LANES]
    bias2 = bias[:hid, LANES:]

    result1[...] = dot(turned1, xa[...], (1, 0))

    def forward_step(index, carry):
        lanes = pl.ds(aligned(index * LANES), LANES)
        result, scale, state = activate(result1[:, lanes] + bias1)
        result1[:, lanes] = result
        scale1[:, lanes] = scale
        upper, lower = two_parts(state)
        states[:hid, lanes] = upper
        states[hid:, lanes] = lower
        return carry

    lax.fori_loop(0, n_a // LANES, forward_step, 0, unroll=2)
    wait_all(copies[9:])
    turned2 = low[:, at["turned2"] : at["turned2"] + 2 * hid]
    for tile in range(sz.tiles_b):
        lanes = slice(LANES * tile, LANES * (tile + 1))
        window, totals = tile_counts(sz, counts, tile)
        total = dot(states[:, pl.ds(a_window(sz, part, tile), WINDOW)], window, (1, 0))
        average = ((total[:hid] + total[hid:]) / totals).astype(BF)
        inputs2[:, lanes] = join_inputs(sz, low[:, at["states"] + LANES * tile : at["states"] + LANES * (tile + 1)], average)
    result2[...] = dot(turned2, inputs2[...], (1, 0))
    for tile in range(sz.tiles_b):
        lanes = slice(LANES * tile, LANES * (tile + 1))
        result, scale, state = activate(result2[:, lanes] + bias2)
        result2[:, lanes] = result
        scale2[:, lanes] = scale
        upper, lower = two_parts(state)
        states2[:hid, lanes] = upper
        states2[hid:, lanes] = lower
    counts3, totals3 = tile_counts(sz, counts, sz.tiles_b)
    total = dot(states2[...], counts3, (1, 0))
    average = ((total[:hid] + total[hid:]) / totals3).astype(BF)
    inputs3 = join_inputs(sz, low[:, at["embed"] : at["embed"] + own], average)

    columns = pl.ds(aligned(own * part), own)
    classes = lax.broadcasted_iota(jnp.int32, (sz.head, own), 0)
    head_row = jnp.concatenate([head_bias[...], jnp.zeros((1, LANES - sz.classes), F32)], 1)
    head_column = jnp.broadcast_to(head_row, (LANES, LANES)).T[: sz.head]
    logits = dot(low[: sz.head, at["turned3"] : at["turned3"] + 2 * hid], inputs3, (1, 0)) + head_column
    logits = jnp.where(classes < sz.classes, logits, -1e30)
    highest = jnp.max(logits, 0, keepdims=True)
    expo = jnp.exp(logits - highest)
    totals = jnp.sum(expo, 0, keepdims=True)
    hit = classes == labels[:, columns]
    weights = weighting[:, columns].astype(F32)
    target = jnp.sum(jnp.where(hit, logits, 0.0), 0, keepdims=True)
    ce_total = jnp.sum(weights * (highest + jnp.log(totals) - target), 1, keepdims=True)
    seed_count = jnp.sum(weights, 1, keepdims=True)
    grad_logits = (weights * (expo / totals - jnp.where(hit, 1.0, 0.0))).astype(BF)
    g3 = at["g3"]
    part_ref[: sz.head, g3 : g3 + 2 * hid] = dot(grad_logits, inputs3, (1, 1))
    head_sums = jnp.concatenate([row_sums(grad_logits), jnp.zeros((16, LANES - sz.head), F32)], 1)
    part_ref[sz.head + 16 : sz.head + 32, g3 : g3 + LANES] = head_sums
    lane_at = lax.broadcasted_iota(jnp.int32, (16, LANES), 1)
    sums = jnp.where(lane_at == 0, ce_total, jnp.where(lane_at == 1, seed_count, 0.0))
    part_ref[sz.head + 16 : sz.head + 32, g3 + LANES : g3 + 2 * LANES] = sums
    own_part, average_part = split_inputs(sz, dot(halves(low, at["weight3"], LANES)[:, : sz.head], grad_logits, (1, 0)))
    part_ref[:hid, at["grad_embed"] : at["grad_embed"] + own] = own_part
    grad_mid = spread(sz, average_part / totals3, counts3)
    low_grad2 = norm_backward(grad_mid, result2[...], scale2[...])
    g2 = dot(inputs2[...], low_grad2, (1, 1))
    part_ref[:hid, at["g2"] : at["g2"] + hid] = g2[:hid]
    part_ref[:hid, at["g2"] + hid : at["g2"] + 2 * hid] = g2[hid:]
    part_ref[sz.head : sz.head + 16, g3 + hid : g3 + 2 * hid] = row_sums(low_grad2)
    weight2 = halves(low, at["weight2"], hid)
    grad_a[...] = jnp.zeros_like(grad_a)
    own_part, average_part = split_inputs(sz, dot(weight2, low_grad2, (1, 0)))
    part_ref[:hid, at["grad_b"] : at["grad_b"] + n_b] = own_part
    for tile in range(sz.tiles_b):
        window, totals = tile_counts(sz, counts, tile)
        lanes = pl.ds(a_window(sz, part, tile), WINDOW)
        grad_a[:, lanes] = grad_a[:, lanes] + spread(sz, average_part[:, LANES * tile : LANES * (tile + 1)] / totals, window)
    rows, few = pl.ds(0, hid + 8), pl.ds(0, sz.head + 32)
    split = at["g2"]
    stores = start_copies(
        (
            (part_ref.at[rows, pl.ds(split, hid * 2)], part_out.at[rows, pl.ds(split, hid * 2)]),
            (
                part_ref.at[rows, pl.ds(at["grad_b"], n_b + own)],
                part_out.at[rows, pl.ds(at["grad_b"], n_b + own)],
            ),
        ),
        sems,
        14,
    )

    def backward_step(index, carry):
        lanes = pl.ds(aligned(index * LANES), LANES)
        low_grad[:, lanes] = norm_backward(grad_a[:, lanes], result1[:, lanes], scale1[:, lanes])
        return carry

    lax.fori_loop(0, n_a // LANES, backward_step, 0, unroll=2)
    part_ref[:hid, at["g1"] : at["g1"] + hid] = dot(xa[...], low_grad[...], (1, 1))
    part_ref[sz.head : sz.head + 16, g3 : g3 + hid] = row_sums(low_grad[...])
    stores += start_copies(
        (
            (part_ref.at[rows, pl.ds(0, hid)], part_out.at[rows, pl.ds(0, hid)]),
            (part_ref.at[few, pl.ds(g3, 2 * hid)], part_out.at[few, pl.ds(g3, 2 * hid)]),
        ),
        sems,
        16,
    )
    wait_all(stores)


def rest_step(sz, low, high, counts, means, labels, weighting, head_bias):
    hid = sz.hid
    return call(
        functools.partial(rest_kernel, sz),
        [((hid + 8, sz.part_lanes), F32)],
        [
            (labels.shape, jnp.int32),
            (weighting.shape, jnp.int32),
            (head_bias.shape, F32),
            ((hid, sz.at["embed"] + sz.own - sz.n_mid), BF),
            ((hid, sz.n_a), BF),
            ((hid + 8, 2 * LANES), F32),
            (counts.shape, BF),
            ((2 * sz.hold, sz.n_a), BF),
            *[((sz.main, sz.early + LANES), BF)] * 3,
            ((2 * sz.main, LANES), F32),
            ((2 * hid, sz.n_a), BF),
            ((2 * hid, sz.n_b), BF),
            ((hid, sz.n_a), F32),
            ((1, sz.n_a), F32),
            ((2 * hid, sz.n_b), BF),
            ((hid, sz.n_b), F32),
            ((1, sz.n_b), F32),
            ((hid, sz.n_a), F32),
            ((hid, sz.n_a), BF),
            ((hid + 8, sz.part_lanes), F32),
        ],
        REST_MIB,
        low,
        high,
        counts,
        *means,
        labels,
        weighting,
        head_bias,
        far_in=(0, 1, 2, 3, 10, 11, 12),
        loose=(7, 8, 9),
        micros=14,
        far_out=(0,),
        copies=18,
    )[0]


def seeds_back_kernel(
    sz, serve_in, take_in, live_in, received, low_in, high_in, counts_in, part_in, keep0, keep1, send,
    serve_rows, take_rows, live_rows, x_ref, weight_ref, low, high, window_ref, partial, g1_ref, g2_ref, gb_ref, sems,
):
    part = lax.axis_index("col")
    own, hid, group, n_b, n_mid = sz.own, sz.hid, sz.group, sz.n_b, sz.n_mid
    at = dict(sz.at)
    at["inputs2"] -= at["embed"]
    split = at["grad_b"]
    few = pl.ds(0, sz.head + 32)
    lanes = pl.ds(at["result2"], own)
    copies = start_copies(
        (
            (serve_in, serve_rows),
            (take_in, take_rows),
            (live_in, live_rows),
            (low_in.at[:, pl.ds(at["embed"], 4 * own)], low),
            (part_in.at[:, pl.ds(split + n_b, own)], partial.at[:, pl.ds(split + n_b, own)]),
            (high_in.at[:, lanes], high.at[:, lanes]),
            (low_in.at[:, pl.ds(at["weight2"], 2 * hid)], weight_ref),
            (counts_in.at[pl.ds(0, sz.count_rows * (own // LANES)), :], window_ref),
            (part_in.at[:, pl.ds(split, n_b)], partial.at[:, pl.ds(split, n_b)]),
            (high_in.at[:, pl.ds(0, n_mid)], high.at[:, pl.ds(0, n_mid)]),
            (low_in.at[:, pl.ds(0, n_mid)], x_ref),
            (part_in.at[:, pl.ds(0, at["g3"])], partial.at[:, pl.ds(0, at["g3"])]),
            (part_in.at[few, pl.ds(at["g3"], 2 * hid)], partial.at[few, pl.ds(at["g3"], 2 * hid)]),
        ),
        sems,
    )
    arrived = received[...].astype(F32).reshape(sz.dp, 4, sz.slot, 2 * hid)
    arrived = jnp.sum(arrived, 1).reshape(sz.slots, 2 * hid)
    at["embed"] = 0
    wait_all(copies[:4])
    serve, take, served, taken = seed_picks(sz, serve_rows[...], take_rows[...], part)
    mine = sent_rows(sz, low, 0, serve, take)
    theirs = arrived[:, hid:]
    alive_there = theirs[:, 0:1] < 0.5 * SENTINEL
    differ = mine[:, hid : 2 * hid] + mine[:, 2 * hid :] - arrived[:, :hid]
    differ = jnp.where((taken > 0.5) & (alive_column(sz, live_rows[...]) > 0.5), differ, 0.0)
    dist_total = DIST_WEIGHT * jnp.sum(jnp.sum(differ * differ, 0, keepdims=True), 1, keepdims=True)
    local_high, local_low = two_parts(2.0 * DIST_WEIGHT * differ)
    back = jnp.where((served > 0.5) & alive_there, theirs - mine[:, :hid], 0.0)
    back = (-2.0 * DIST_WEIGHT * back).astype(BF)
    take = take.astype(BF)
    serve = serve.astype(BF)
    wait_all(copies[4:6])
    grad = partial[:hid, at["grad_embed"] : at["grad_embed"] + own]
    grad = grad + dot(local_high, take, (0, 0)) + dot(local_low, take, (0, 0)) + dot(back, serve, (0, 0))
    lanes = slice(at["result2"], at["result2"] + own)
    low_grad2 = norm_backward(grad, high[:hid, lanes], high[hid:, lanes][0:1])
    wait_all(copies[6:9])
    weight2 = halves(weight_ref, 0, hid)
    own_part, average_part = split_inputs(sz, dot(weight2, low_grad2, (1, 0)))
    total_b = partial[:hid, at["grad_b"] : at["grad_b"] + n_b]
    for tile in range(own // LANES):
        window, totals = tile_counts(sz, window_ref, tile)
        total_b = total_b + spread(sz, average_part[:, LANES * tile : LANES * (tile + 1)] / totals, window)
    wait_all(copies[9:10])
    low_grad = jnp.concatenate(
        [
            norm_backward(total_b, high[:hid, :n_b], high[hid:, :n_b][0:1]),
            norm_backward(own_part, high[:hid, n_b:n_mid], high[hid:, n_b:n_mid][0:1]),
        ],
        1,
    )
    wait_all(copies[10:])
    added = dot(halves(low, at["inputs2"], own), low_grad2, (1, 1))
    for half in range(2):
        lanes = slice(at["g2"] + hid * half, at["g2"] + hid * (half + 1))
        g2_ref[hid * half : hid * (half + 1), :] = partial[:hid, lanes] + added[hid * half : hid * (half + 1)]
    g3 = at["g3"]
    sums = partial[sz.head : sz.head + 16, g3 : g3 + 2 * hid]
    gb_ref[:, hid:] = sums[:, hid:] + row_sums(low_grad2)
    half = 4 * sz.hold
    g1_ref[...] = partial[:hid, at["g1"] : at["g1"] + hid] + dot(x_ref[...], low_grad, (1, 1))
    gb_ref[:, :hid] = sums[:, :hid] + row_sums(low_grad)
    head_row = partial[sz.head + 16 : sz.head + 32, g3 : g3 + LANES]
    totals = partial[sz.head + 16 : sz.head + 32, g3 + LANES : g3 + 2 * LANES]
    lane_at = lax.broadcasted_iota(jnp.int32, (16, LANES), 1)
    row_at = lax.broadcasted_iota(jnp.int32, (16, LANES), 0)
    fixed = ((totals[0:1, 0:1] + dist_total) * float(2**LOSS_BITS) + 0.5).astype(jnp.int32)
    count = totals[0:1, 1:2].astype(jnp.int32)
    whole = jnp.where(lane_at < 32, fixed, count)
    bits = (lax.shift_right_logical(whole, lane_at & 31) & 1).astype(F32)
    bits = jnp.where(lane_at < 64, bits, 0.0)
    for r, (target_ref, base) in enumerate(((keep0, 0), (send, 0), (keep1, 0), (send, sz.pay))):
        shard = part ^ r
        block2 = pl.ds(pl.multiple_of(2 * group * shard, 2 * group), 2 * group)
        row = base
        for h in range(hid // LANES):
            lanes = slice(LANES * h, LANES * (h + 1))
            for s in range(2):
                rows = slice(half * s + sz.hold * r, half * s + sz.hold * (r + 1))
                target_ref[row : row + sz.hold, :] = g1_ref[rows, lanes].astype(BF)
                row += sz.hold
        for h in range(hid // LANES):
            target_ref[row : row + 2 * group, :] = g2_ref[block2, LANES * h : LANES * (h + 1)].astype(BF)
            row += 2 * group
        third = partial[: sz.head, pl.ds(aligned(g3 + 2 * group * shard), LANES)]
        target_ref[row : row + sz.head, :] = third.astype(BF)
        row += sz.head
        odd = (shard % 2) == 1
        block = aligned((shard // 2) * LANES)
        one = gb_ref[:, pl.ds(block, LANES)]
        two = gb_ref[:, pl.ds(aligned(hid + block), LANES)]
        one = jnp.where(odd, pltpu.roll(one, group, 1), one)
        two = jnp.where(odd, two, pltpu.roll(two, group, 1))
        bias_row = jnp.where(lane_at < group, one, two)
        misc = jnp.where(row_at == 0, bias_row, jnp.where(row_at == 1, head_row, jnp.where(row_at == 2, bits, 0.0)))
        target_ref[row : row + 16, :] = misc.astype(BF)


def seeds_backward(sz, tables, received, low, high, counts, partial):
    hid = sz.hid
    return call(
        functools.partial(seeds_back_kernel, sz),
        [((sz.pay, LANES), BF), ((sz.pay, LANES), BF), ((2 * sz.pay, LANES), BF)],
        [
            *[(item.shape, jnp.int32) for item in tables],
            ((hid, sz.n_mid), BF),
            ((hid, 2 * hid), BF),
            ((hid, 4 * sz.own), BF),
            ((hid + 8, sz.high_lanes), F32),
            ((sz.count_rows * (sz.own // LANES), LANES), BF),
            ((hid + 8, sz.part_lanes), F32),
            ((8 * sz.hold, hid), F32),
            ((2 * hid, hid), F32),
            ((16, 2 * hid), F32),
        ],
        BACK_MIB,
        *tables,
        received,
        low,
        high,
        counts,
        partial,
        far_in=(0, 1, 2, 4, 5, 6, 7),
        micros=3,
        copies=13,
    )


def lamb_kernel(sz, grad, w1, w2, w3, wh, wb, f1, f2, f3, fh, fb, s1, s2, s3, sh, sb, *rest):
    params = (w1, w2, w3, wh, wb)
    firsts = (f1, f2, f3, fh, fb)
    seconds = (s1, s2, s3, sh, sb)
    moments, squares, updates = rest[:5], rest[5:10], rest[10:15]
    sums_ref, totals_ref, one_ref, three_ref = rest[15:]
    group, hold = sz.group, sz.hold

    def wide(at, rows):
        return jnp.concatenate([grad[at : at + rows, :], grad[at + rows : at + 2 * rows, :]], 1)

    one = wide(0, 2 * hold)
    three = grad[sz.at_three : sz.misc, :]
    turned = pltpu.roll(three, group, 1)
    for f in range(sz.feat):
        one_ref[f, 0:1, :] = one[f : f + 1]
        one_ref[f, 1:2, :] = one[hold + f : hold + f + 1]
    for c in range(sz.classes):
        three_ref[c, 0:1, :] = three[c : c + 1, :group]
        three_ref[c, 1:2, :] = turned[c : c + 1, :group]
    misc = grad[sz.misc : sz.misc + 8, :]
    hidden = jnp.concatenate([misc[0:1, :group], misc[0:1, group : 2 * group]], 0)
    two = wide(sz.rows_one, 2 * group).reshape(2, group, sz.hid)
    grads = (one_ref[...], two, three_ref[...], hidden, misc[1:2, : sz.classes])
    lane_at = lax.broadcasted_iota(jnp.int32, (8, LANES), 1)
    row_at = lax.broadcasted_iota(jnp.int32, (8, LANES), 0)
    sums = jnp.zeros((8, LANES), F32)
    for i in range(5):
        g = grads[i]
        w = params[i][...]
        m = BETA_ONE * firsts[i][...] + (1.0 - BETA_ONE) * g
        v = BETA_TWO * seconds[i][...] + (1.0 - BETA_TWO) * g * g
        u = (m / (1.0 - BETA_ONE**STEP)) / (jnp.sqrt(v / (1.0 - BETA_TWO**STEP)) + ADAM_EPS) + DECAY_RATE * w
        moments[i][...] = m
        squares[i][...] = v
        updates[i][...] = u
        for row, item in ((0, w), (1, u)):
            item = item * item
            if i < 3:
                item = jnp.sum(item, 0)
            total = jnp.sum(jnp.sum(item, 0, keepdims=True), 1, keepdims=True)
            if i == 4:
                total = 0.25 * total
            sums = jnp.where((lane_at == i) & (row_at == row), total, sums)
    sums_ref[...] = sums
    power = (1 << (lane_at & 15)).astype(F32)
    power = jnp.where((lane_at & 31) < 16, power, power * float(2**16))
    bits = jnp.broadcast_to(misc[2:3], (8, LANES)) * power
    loss = jnp.sum(jnp.where(lane_at < 32, bits, 0.0), 1, keepdims=True) * float(2.0**-LOSS_BITS)
    count = jnp.sum(jnp.where((lane_at >= 32) & (lane_at < 64), bits, 0.0), 1, keepdims=True)
    totals_ref[...] = jnp.where(lane_at == 0, loss, count)


def lamb(sz, grad, params, firsts, seconds):
    like = [(item.shape, F32) for item in params]
    return call(
        functools.partial(lamb_kernel, sz),
        like * 3 + [((8, LANES), F32)] * 2,
        [(params[0].shape, F32), (params[2].shape, F32)],
        6,
        grad,
        *params,
        *firsts,
        *seconds,
    )


def step_kernel(own, far, w1, w2, w3, wh, wb, u1, u2, u3, uh, ub, n1, n2, n3, nh, nb, norms_ref):
    norms = jnp.sqrt(own[...] + far[...])
    norms_ref[...] = norms[0:2, 0:5]
    for i, (w, u, n) in enumerate(
        ((w1, u1, n1), (w2, u2, n2), (w3, u3, n3), (wh, uh, nh), (wb, ub, nb))
    ):
        ratio = LEARN_RATE * (norms[0:1, i : i + 1] / norms[1:2, i : i + 1])
        n[...] = w[...] - ratio * u[...]


def take_step(sums, params, updates):
    return call(
        step_kernel,
        [(item.shape, F32) for item in params] + [((2, 5), F32)],
        [],
        3,
        *sums,
        *params,
        *updates,
    )


def swap(value, axis, count, bit):
    return lax.ppermute(value, axis, [(i, i ^ bit) for i in range(count)])


def merged(own, other):
    return lax.reduce_precision(own.astype(F32) + other.astype(F32), 8, 7)


def shards(
    features, neighbors_one, present_one, neighbors_two, present_two, neighbors_three, present_three,
    labels, seed_weight, serve_rows, take_seed, fetch_live,
    weight_one, weight_two, weight_three, hidden_bias, head_bias,
    first_one, first_two, first_three, first_hidden, first_head,
    second_one, second_two, second_three, second_hidden, second_head,
):
    sz = Sizes(features, neighbors_one, neighbors_two, neighbors_three, weight_two, weight_three, serve_rows)

    def tree(one, two, three, hidden, head):
        return (one.transpose(1, 0, 2), two, three.transpose(2, 0, 1), hidden, head[None, :])

    def back(one, two, three, hidden, head):
        return (one.transpose(1, 0, 2), two, three.transpose(1, 2, 0), hidden, head[0])

    params = tree(weight_one, weight_two, weight_three, hidden_bias, head_bias)
    firsts = tree(first_one, first_two, first_three, first_hidden, first_head)
    seconds = tree(second_one, second_two, second_three, second_hidden, second_head)

    own_b, packed, mean, tail, *sent = first_messages(sz, features, neighbors_one, present_one, *params[:4])
    s1, s2, s3 = [swap(sent[r - 1], "col", 4, r) for r in (1, 2, 3)]
    links = (neighbors_two, present_two, neighbors_three, present_three)
    own_a, counts, *means = mean_messages(sz, features, neighbors_one, present_one, mean, tail, links)
    s1, *means = lax.optimization_barrier((s1, *means))
    means = [swap(means[r - 1], "col", 4, r) for r in (1, 2, 3)]
    later, s3, counts = lax.optimization_barrier((s2, s3, counts))
    passed = swap(later, "col", 4, 1)
    tables = (serve_rows, take_seed, fetch_live[None, :])
    low, high, window, rows = seeds_forward(
        sz, (own_b, packed, s1, s2, s3, passed), neighbors_two, present_two, tables
    )
    received = lax.all_to_all(rows, ("dp", "col"), split_axis=0, concat_axis=0, tiled=True)
    partial = rest_step(sz, low, high, counts, (own_a, *means, s1, s2, s3), labels[None, :], seed_weight[None, :], head_bias[None, :])
    keep0, keep1, send = seeds_backward(sz, tables, received, low, high, window, partial)
    other = swap(send, "col", 4, 1)
    own = merged(keep0, other[: sz.pay]).astype(BF)
    far = merged(keep1, other[sz.pay :]).astype(BF)
    pair = [[(d, c), (d ^ 1, c ^ 2)] for d in range(sz.dp) for c in range(4)]
    pair = [(a * 4 + b, c * 4 + d) for (a, b), (c, d) in pair]
    near = (swap(far, "col", 4, 2), swap(own, "dp", sz.dp, 1), lax.ppermute(far, ("dp", "col"), pair))
    near = [item.astype(F32) for item in (own, *near)]
    grad = lax.reduce_precision((near[0] + near[1]) + (near[2] + near[3]), 8, 7)
    bit = 2
    while bit < sz.dp:
        grad = merged(grad, swap(grad.astype(BF), "dp", sz.dp, bit))
        bit *= 2
    outs = lamb(sz, grad, params, firsts, seconds)
    moments, squares, updates = outs[:5], outs[5:10], outs[10:15]
    sums, totals = outs[15], outs[16]
    pair = sums + swap(sums, "col", 4, 1)
    fresh = take_step([pair, swap(pair, "col", 4, 2)], params, updates)
    return (*back(*fresh[:5]), *back(*moments), *back(*squares), fresh[5], totals[0, 0], totals[0, 1])


def solution(mesh):
    wide = P(None, "col", None)
    tree = [wide, wide, wide, P(None, "col"), P()]
    return jax.shard_map(
        shards,
        mesh=mesh,
        in_specs=(
            P("col", "dp"),
            *[P(None, "dp")] * 6,
            P("dp"),
            P("dp"),
            P("dp", None),
            P("dp", None),
            P("dp"),
            *tree,
            *tree,
            *tree,
        ),
        out_specs=(*tree, *tree, *tree, P(), P(), P()),
        check_vma=False,
    )
```

```python
import functools

import jax
import jax.numpy as jnp
from jax import lax
from jax.experimental import pallas as pl
from jax.experimental.pallas import tpu as pltpu
from jax.sharding import PartitionSpec as P

REACH = 64
STEP = 5
DIST_WEIGHT = 1.0
ROW_EPS = 1e-06
LEARN_RATE = 0.5
BETA_ONE = 0.9
BETA_TWO = 0.999
ADAM_EPS = 1e-06
DECAY_RATE = 0.01

BF = jnp.bfloat16
F32 = jnp.float32
LANES = 128
WINDOW = 640
HALF = 64
FRONT = 320
SENTINEL = 4.0
MIB = 2**20
LOSS_BITS = 14
EARLY = 4
FIRST_MIB = 8
MEAN_MIB = 8
SEEDS_MIB = 16
REST_MIB = 28
BACK_MIB = 12


def cost(micros):
    return pl.CostEstimate(flops=int(micros * 10**9), bytes_accessed=1, transcendentals=0)


def call(kernel, outs, scratch, mib, *args, far_in=(), far_out=(), copies=0, micros=1, loose=(), name=None):
    near = pl.BlockSpec(memory_space=pltpu.VMEM)
    far = pl.BlockSpec(memory_space=pltpu.HBM)
    free = pl.BlockSpec(memory_space=pl.ANY)
    scratch = [pltpu.VMEM(shape, kind) for shape, kind in scratch]
    args = [pltpu.with_memory_space_constraint(a, pltpu.HBM) if i in far_in else a for i, a in enumerate(args)]
    return pl.pallas_call(
        kernel,
        in_specs=[free if i in loose else far if i in far_in else near for i in range(len(args))],
        out_specs=tuple(far if i in far_out else near for i in range(len(outs))),
        out_shape=tuple(
            pltpu.HBM(shape, kind) if i in far_out else jax.ShapeDtypeStruct(shape, kind)
            for i, (shape, kind) in enumerate(outs)
        ),
        scratch_shapes=scratch + ([pltpu.SemaphoreType.DMA((copies,))] if copies else []),
        compiler_params=pltpu.CompilerParams(vmem_limit_bytes=mib * MIB),
        cost_estimate=cost(micros),
        name=name,
    )(*args)


def start_copies(pairs, sems, first=0):
    copies = [pltpu.make_async_copy(src, dst, sems.at[first + i]) for i, (src, dst) in enumerate(pairs)]
    for copy in copies:
        copy.start()
    return copies


def wait_all(copies):
    for copy in copies:
        copy.wait()


class Sizes:
    def __init__(self, features, neighbors_one, neighbors_two, neighbors_three, weight_two, weight_three, serve_rows):
        self.feat = features.shape[0]
        self.main = self.feat - 1
        self.hold = 32
        self.base = features.shape[1]
        self.low = neighbors_one.shape[1]
        self.mid = neighbors_two.shape[1]
        self.seeds = neighbors_three.shape[1]
        self.hid = weight_two.shape[2]
        self.group = weight_two.shape[1]
        self.classes = weight_three.shape[2]
        self.head = -(-self.classes // 16) * 16
        self.own = self.seeds // 4
        self.n_b = 4 * self.own + LANES
        self.n_a = 16 * self.own + 5 * LANES
        self.n_mid = self.n_b + self.own
        self.n_low = self.n_a + self.n_mid
        self.tiles_b = self.n_b // LANES
        self.tiles_mid = self.n_mid // LANES
        self.tiles_low = self.n_low // LANES
        self.slots = serve_rows.shape[0] * serve_rows.shape[1]
        self.slot = serve_rows.shape[1]
        self.dp = serve_rows.shape[0]
        self.rows_one = 2 * 2 * self.hold
        self.rows_two = 4 * self.group
        self.at_three = self.rows_one + self.rows_two
        self.misc = self.at_three + self.head
        self.pay = self.misc + 16
        self.blocks = -(-self.pay // self.main)
        self.early = EARLY * LANES
        self.message_a = self.pair_lanes(self.n_a, self.n_a - self.early)
        self.message_b = self.pair_lanes(self.n_mid, self.n_mid + self.early)
        self.full_b = self.message_b + LANES * self.blocks
        self.tiles_b_all = 16 * self.own // LANES + 1
        self.tiles_all = self.low // LANES + 8
        self.count_rows = WINDOW + 16
        hid, at = self.hid, self.n_mid
        places = {}
        for name, lanes in (
            ("turned1", hid), ("turned2", 2 * hid), ("weight2", 2 * hid), ("weight3", 2 * LANES), ("turned3", 2 * hid),
            ("states", self.n_b), ("embed", 2 * self.own), ("inputs2", 2 * self.own),
        ):
            places[name] = at
            at += lanes
        self.low_lanes = at
        at = 0
        for name, lanes in (("result1", self.n_mid), ("result2", self.own), ("bias", 2 * LANES)):
            places[name] = at
            at += lanes
        self.high_lanes = at
        at = 0
        for name, lanes in (("g1", hid), ("g2", 2 * hid), ("g3", 2 * hid), ("grad_b", self.n_b), ("grad_embed", self.own)):
            places[name] = at
            at += lanes
        self.part_lanes = at
        self.at = places

    def pair_lanes(self, means, own):
        lanes = means + own
        return lanes + LANES * -(-lanes // LANES // self.main)

    def first_ranges(self, part):
        a, b, c = self.ranges(part)
        b = (b[0], 0, b[2])
        c = (c[0], b[2], c[2])
        return [b, c, (a[0], self.n_mid, self.early)], [b, c]

    def second_ranges(self, part):
        first = 16 * self.own * part
        return [(first + self.early, 0, self.n_a - self.early)], [(first, 0, self.n_a)]

    def a_row(self, part):
        return 16 * self.own * part - FRONT

    def b_row(self, part):
        return 4 * self.own * part - HALF

    def seed_window(self):
        rows = self.count_rows * (self.own // LANES)
        return pl.ds(self.count_rows * self.tiles_b + rows, rows)

    def ranges(self, part):
        return (
            (16 * self.own * part, 0, self.n_a),
            (self.b_row(part) + FRONT, self.n_a, self.n_b),
            (self.own * part + FRONT, self.n_a + self.n_b, self.own),
        )


def dot(a, b, over):
    return lax.dot_general(a, b, (((over[0],), (over[1],)), ((), ())), preferred_element_type=F32)


def two_parts(value):
    high = value.astype(BF)
    return high, (value - high.astype(F32)).astype(BF)


def three_parts(value):
    high = value.astype(BF).astype(F32)
    rest = value - high
    middle = rest.astype(BF).astype(F32)
    return high, middle, (rest - middle).astype(BF).astype(F32)


def aligned(value):
    return pl.multiple_of(value, LANES)


def sigmoid(value):
    return 0.5 * jnp.tanh(0.5 * value) + 0.5


def unpack_tile(sz, message, tail, tile):
    spare = jnp.zeros((sz.hold - sz.feat, LANES), F32)
    main = message[:, LANES * tile : LANES * (tile + 1)].astype(F32)
    return jnp.concatenate([main, tail[tile : tile + 1, :], spare], 0).astype(BF)


def half_tiles(left, right):
    lane = lax.broadcasted_iota(jnp.int32, left.shape, 1)
    return jnp.where(lane < HALF, pltpu.roll(left, HALF, 1), pltpu.roll(right, HALF, 1))


def half_columns(ref, tile, tiles, spare):
    if isinstance(tile, int):
        left, right = max(tile - 1, 0), min(tile, tiles - 1)
        left, right = [ref[:, LANES * i : LANES * (i + 1)] for i in (left, right)]
        left = left if tile > 0 else jnp.full_like(left, spare)
        right = right if tile < tiles else jnp.full_like(right, spare)
        return half_tiles(left, right)
    left = ref[:, pl.ds(aligned(jnp.maximum(tile - 1, 0) * LANES), LANES)]
    right = ref[:, pl.ds(aligned(jnp.minimum(tile, tiles - 1) * LANES), LANES)]
    left = jnp.where(tile > 0, left, spare)
    right = jnp.where(tile < tiles, right, spare)
    return half_tiles(left, right)


def take_tile(ref, rows, first, half):
    if not half:
        return ref[:rows, pl.ds(aligned(first), LANES)].astype(F32)
    first = first - HALF
    left = ref[:rows, pl.ds(aligned(first), LANES)].astype(F32)
    return half_tiles(left, ref[:rows, pl.ds(aligned(first + LANES), LANES)].astype(F32))


def take_tail(ref, first, half):
    if not half:
        return ref[pl.ds(first // LANES, 1), :]
    row = (first - HALF) // LANES
    return half_tiles(ref[pl.ds(row, 1), :], ref[pl.ds(row + 1, 1), :])


def fill_own(sz, feat_ref, self_ref, self_tail, places):
    spare = jnp.zeros((sz.hold - sz.feat, LANES), F32)
    zeros = jnp.zeros((sz.feat, LANES), BF)
    count = min(sz.low, feat_ref.shape[1]) // LANES
    lane = lax.broadcasted_iota(jnp.int32, (sz.feat, LANES), 1)
    shift = FRONT // LANES
    before = zeros
    for place in range(places):
        tile = place - shift
        after = zeros
        if tile >= 0 and tile < count:
            after = pltpu.roll(feat_ref[:, LANES * tile : LANES * (tile + 1)], HALF, 1)
        value = jnp.where(lane < HALF, before.astype(F32), after.astype(F32))
        self_tail[place : place + 1, :] = value[sz.main : sz.feat]
        self_ref[:, LANES * place : LANES * (place + 1)] = jnp.concatenate([value, spare], 0).astype(BF)
        before = after


def mean_tiles(sz, begin, tiles, feat_ref, nbr_ref, pres_ref, links_ref, present_ref, mean_ref, tail_ref, base_ref, code_ref, count_ref):
    last = feat_ref.shape[1] // LANES - 6
    slots = nbr_ref.shape[0]
    base_ref[...] = jnp.zeros_like(base_ref)
    if begin % 8 or tiles % 8:
        code_ref[...] = jnp.full_like(code_ref, -1)
        count_ref[...] = jnp.ones_like(count_ref)
    for tile in range(feat_ref.shape[1] // LANES):
        row = feat_ref[:, LANES * tile : LANES * (tile + 1)].astype(F32)
        base_ref[8 + tile : 9 + tile, :] = row[sz.main : sz.feat]

    for table, shifted in ((nbr_ref, links_ref), (pres_ref, present_ref)):
        count = table.shape[1] // LANES
        for tile in range(begin, tiles):
            shifted[:, LANES * tile : LANES * (tile + 1)] = half_columns(table, tile, count, 0)

    def one_tile(step, carry):
        lanes = pl.ds(aligned(step * LANES), LANES)
        present = present_ref[:, lanes]
        valid = present.astype(F32)
        counts = jnp.maximum(jnp.sum(valid, 0, keepdims=True), 1.0)
        first = jnp.clip(4 * step - 3, 0, last)
        links = links_ref[:, lanes]
        code = jnp.where(present > 0, links, -1)
        count_ref[pl.ds(step, 1), :] = counts
        for slot in range(slots):
            code_ref[slot, pl.ds(step, 1), :] = code[slot : slot + 1]
        local = links - first * LANES
        piece = local >> 7
        spot = local & 127
        sources = [
            feat_ref[:, pl.ds(aligned((first + j) * LANES), LANES)].astype(F32) for j in range(6)
        ]
        totals = [jnp.zeros((8, LANES), F32) for _ in range(sz.main // 8)]
        for slot in range(slots):
            spots = jnp.broadcast_to(spot[slot : slot + 1], (8, LANES))
            pieces = jnp.broadcast_to(piece[slot : slot + 1], (8, LANES))
            marks = jnp.broadcast_to(valid[slot : slot + 1], (8, LANES))
            for h in range(sz.main // 8):
                taken = None
                for j in range(6):
                    found = jnp.take_along_axis(
                        sources[j][8 * h : 8 * h + 8], spots, axis=1, mode="promise_in_bounds"
                    )
                    taken = found if j == 0 else jnp.where(pieces == j, found, taken)
                totals[h] = totals[h] + taken * marks
        mean_ref[:, pl.ds(aligned((step + 2) * LANES), LANES)] = (jnp.concatenate(totals, 0) / counts).astype(BF)
        return carry

    even = begin + (tiles - begin) // 4 * 4
    lax.fori_loop(begin, even, one_tile, 0, unroll=4)
    for step in range(even, tiles):
        one_tile(step, 0)
    sub = lax.broadcasted_iota(jnp.int32, (8, LANES), 0)

    for block in range(begin // 8, -(-tiles // 8)):
        total = jnp.zeros((8, LANES), F32)
        for slot in range(slots):
            code = code_ref[slot, 8 * block : 8 * (block + 1), :]
            piece = (code >> 7) - (4 * (8 * block + sub) - 3)
            taken = None
            for j in range(6):
                source = base_ref[pl.ds(8 + 32 * block - 3 + j, 8, stride=4), :]
                found = jnp.take_along_axis(source, code & 127, axis=1, mode="promise_in_bounds")
                taken = found if j == 0 else jnp.where(piece == j, found, taken)
            total = total + jnp.where(code >= 0, taken, 0.0)
        tail_ref[8 * block + 2 : 8 * block + 10, :] = total / count_ref[8 * block : 8 * (block + 1), :]


def pack_pair(sz, ranges, self_ref, self_tail, mean_ref, tail_ref, turn_ref, out_ref):
    turn_ref[...] = jnp.zeros_like(turn_ref)
    lanes = 0
    for source_ref, rows_ref, group in zip((self_ref, mean_ref), (self_tail, tail_ref), ranges):
        for i, (first, at, count) in enumerate(group):
            at = at + lanes
            if i != 1:
                out_ref[:, at : at + count] = source_ref[: sz.main, pl.ds(aligned(first), count)]
                turn_ref[at // LANES : (at + count) // LANES, :] = rows_ref[pl.ds(first // LANES, count // LANES), :]
                continue
            for tile in range(count // LANES):
                place = first + LANES * tile
                piece = take_tile(source_ref, sz.main, place, True)
                out_ref[:, at + LANES * tile : at + LANES * (tile + 1)] = piece.astype(BF)
                turn_ref[at // LANES + tile : at // LANES + tile + 1, :] = take_tail(rows_ref, place, True)
        lanes += sum(count for _, _, count in group)
    for block in range(-(-lanes // LANES // sz.main)):
        at = lanes + LANES * block
        out_ref[:, at : at + LANES] = turn_ref[sz.main * block : sz.main * (block + 1), :].astype(BF)


def own_pair(sz, ranges, self_ref, mean_ref, tail_ref, own_ref):
    spare = jnp.zeros((sz.hold - sz.feat, LANES), F32)
    base = ranges[0][1]
    for i, (start, at, count) in enumerate(ranges):
        for tile in range(count // LANES):
            place = start + LANES * tile
            out_lanes = slice(at - base + LANES * tile, at - base + LANES * (tile + 1))
            own_ref[: sz.hold, out_lanes] = take_tile(self_ref, sz.hold, place, i == 1).astype(BF)
            average = [take_tile(mean_ref, sz.main, place, i == 1), take_tail(tail_ref, place, i == 1), spare]
            own_ref[sz.hold :, out_lanes] = jnp.concatenate(average, 0).astype(BF)


def mean_scratch(sz, tiles, slots):
    rows = -(-tiles // 8) * 8
    return [
        ((slots, LANES * tiles), jnp.int32),
        ((slots, LANES * tiles), jnp.int32),
        ((sz.hold, LANES * sz.tiles_all), BF),
        ((sz.tiles_all, LANES), F32),
        ((sz.main, LANES * sz.tiles_all), BF),
        ((max(rows + 8, sz.tiles_all), LANES), F32),
        ((2 * sz.main, LANES), F32),
        ((4 * rows + 16, LANES), F32),
        ((slots, rows, LANES), jnp.int32),
        ((rows, LANES), F32),
    ]


def unpack_tails(sz, message, lanes, turn_ref):
    for block in range(-(-lanes // LANES // sz.main)):
        at = lanes + LANES * block
        turn_ref[sz.main * block : sz.main * (block + 1), :] = message[:, at : at + LANES].astype(F32)
    return turn_ref[...]


def unpack_tiles(sz, message, tail, first, tiles, row, at, out_ref):
    for tile in range(tiles):
        lane = at + LANES * tile
        out_ref[row : row + sz.hold, lane : lane + LANES] = unpack_tile(sz, message, tail, first + tile)


def first_kernel(
    sz, features, neighbors, present, w1_in, w2_in, w3_in, wh_in, own_b, packed, mean_out, tail_out, m1, m2, m3,
    feat_ref, nbr_ref, pres_ref, w1, w2, w3, wh, own_ref,
    links_ref, present_ref, self_ref, self_tail, mean_ref, tail_ref, turn_ref, base_ref, code_ref, count_ref, one_ref, three_ref, pack, sems,
):
    part = lax.axis_index("col")
    rows = pl.ds(0, nbr_ref.shape[1])
    weights = start_copies(((w1_in, w1), (w2_in, w2), (w3_in, w3), (wh_in, wh)), sems)
    copies = start_copies(
        (
            (features.at[:, pl.ds(0, feat_ref.shape[1])], feat_ref),
            (neighbors.at[:, rows], nbr_ref),
            (present.at[:, rows], pres_ref),
        ),
        sems,
        4,
    )
    wait_all(weights)
    one_ref[...] = jnp.zeros_like(one_ref)
    three_ref[...] = jnp.zeros_like(three_ref)
    for s in range(2):
        for f in range(sz.feat):
            one_ref[s * sz.hold + f : s * sz.hold + f + 1, :] = w1[f, s : s + 1, :]
        for c in range(sz.classes):
            three_ref[c : c + 1, s * sz.group : (s + 1) * sz.group] = w3[c, s : s + 1, :]
    at = 0
    for half in range(sz.hid // LANES):
        pack[at : at + 2 * sz.hold, :] = one_ref[:, LANES * half : LANES * (half + 1)]
        at += 2 * sz.hold
    for half in range(sz.hid // LANES):
        for s in range(2):
            pack[at : at + sz.group, :] = w2[s, :, LANES * half : LANES * (half + 1)]
            at += sz.group
    pack[at : at + sz.head, :] = three_ref[...]
    row = jnp.concatenate([wh[0:1, :], wh[1:2, :]], 1)
    row_at = lax.broadcasted_iota(jnp.int32, (16, LANES), 0)
    misc = jnp.zeros((16, LANES), F32)
    for i, piece in enumerate(three_parts(row)):
        misc = jnp.where(row_at == i, piece, misc)
    pack[sz.misc : sz.pay, :] = misc
    pack[sz.pay :, :] = jnp.zeros((sz.main * sz.blocks - sz.pay, LANES), F32)
    store = start_copies(((pack, packed),), sems, 7)
    for block in range(sz.blocks):
        at = sz.message_b + LANES * block
        piece = pack[sz.main * block : sz.main * (block + 1), :].astype(BF)
        m1[:, at : at + LANES] = piece
        m2[:, at : at + LANES] = piece
    wait_all(copies)
    fill_own(sz, feat_ref, self_ref, self_tail, 48 * sz.own // LANES + EARLY)
    mean_ref[:, :FRONT] = jnp.zeros((sz.main, FRONT), BF)
    tail_ref[...] = jnp.zeros_like(tail_ref)
    mean_tiles(sz, 0, sz.tiles_b_all, feat_ref, nbr_ref, pres_ref, links_ref, present_ref, mean_ref, tail_ref, base_ref, code_ref, count_ref)
    done = pl.ds(0, LANES * (sz.tiles_b_all + 2))
    store += start_copies(((mean_ref.at[:, done], mean_out), (tail_ref, tail_out)), sems, 9)
    own_pair(sz, sz.ranges(part)[1:], self_ref, mean_ref, tail_ref, own_ref)
    store += start_copies(((own_ref, own_b),), sems, 8)
    for r, out in ((1, m1), (2, m2), (3, m3)):
        pack_pair(sz, sz.first_ranges(part ^ r), self_ref, self_tail, mean_ref, tail_ref, turn_ref, out)
    wait_all(store)


def first_messages(sz, features, neighbors, present, w1, w2, w3, hidden):
    rows = LANES * sz.tiles_b_all
    bases = min(4 * rows + LANES, sz.base)
    slots = neighbors.shape[0]
    return call(
        functools.partial(first_kernel, sz),
        [
            ((2 * sz.hold, sz.n_mid), BF),
            ((sz.main * sz.blocks, LANES), F32),
            ((sz.main, rows + 2 * LANES), BF),
            ((max(-(-sz.tiles_b_all // 8) * 8 + 8, sz.tiles_all), LANES), F32),
            ((sz.main, sz.full_b), BF),
            ((sz.main, sz.full_b), BF),
            ((sz.main, sz.message_b), BF),
        ],
        [
            ((sz.feat, bases), BF),
            ((slots, rows), jnp.int32),
            ((slots, rows), jnp.int32),
            (w1.shape, F32),
            (w2.shape, F32),
            (w3.shape, F32),
            (hidden.shape, F32),
            ((2 * sz.hold, sz.n_mid), BF),
            *mean_scratch(sz, sz.tiles_b_all, slots),
            ((2 * sz.hold, sz.hid), F32),
            ((sz.head, LANES), F32),
            ((sz.main * sz.blocks, LANES), F32),
        ],
        FIRST_MIB,
        features,
        neighbors,
        present,
        w1,
        w2,
        w3,
        hidden,
        far_in=range(7),
        far_out=(0, 1, 2, 3),
        copies=11,
        micros=4,
    )


def mean_kernel(
    sz, feat_ref, nbr_ref, pres_ref, mean_in, tail_in, nbr2, pres2, nbr3, pres3, own_a, counts_out, a1, a2, a3,
    links_ref, present_ref, self_ref, self_tail, mean_ref, tail_ref, turn_ref, base_ref, code_ref, count_ref, own_ref, kept_ref, counts, sems,
):
    part = lax.axis_index("col")
    tiles = sz.low // LANES + 1
    begin = sz.tiles_b_all
    loads = start_copies(((mean_in, mean_ref.at[:, pl.ds(0, LANES * (begin + 2))]), (tail_in, kept_ref)), sems, 1)
    fill_counts(sz, part, nbr2, pres2, nbr3, pres3, counts)
    store = start_copies(((counts, counts_out),), sems, 3)
    fill_own(sz, feat_ref, self_ref, self_tail, (48 * sz.own + sz.n_a) // LANES)
    last = LANES * (tiles + 2)
    mean_ref[:, last:] = jnp.zeros((sz.main, LANES * sz.tiles_all - last), BF)
    tail_ref[...] = jnp.zeros_like(tail_ref)
    mean_tiles(sz, begin, tiles, feat_ref, nbr_ref, pres_ref, links_ref, present_ref, mean_ref, tail_ref, base_ref, code_ref, count_ref)
    wait_all(loads)
    tail_ref[: begin + 2, :] = kept_ref[: begin + 2, :]
    own_pair(sz, sz.ranges(part)[:1], self_ref, mean_ref, tail_ref, own_ref)
    store += start_copies(((own_ref, own_a),), sems)
    for r, out in ((1, a1), (2, a2), (3, a3)):
        pack_pair(sz, sz.second_ranges(part ^ r), self_ref, self_tail, mean_ref, tail_ref, turn_ref, out)
    wait_all(store)


def mean_messages(sz, features, neighbors, present, mean, tail, links):
    counts = (sz.count_rows * (sz.tiles_b + 2 * (sz.own // LANES)), LANES)
    return call(
        functools.partial(mean_kernel, sz),
        [((2 * sz.hold, sz.n_a), BF), (counts, BF)] + [((sz.main, sz.message_a), BF)] * 3,
        mean_scratch(sz, sz.low // LANES + 1, neighbors.shape[0]) + [((2 * sz.hold, sz.n_a), BF), (tail.shape, F32), (counts, BF)],
        MEAN_MIB,
        features,
        neighbors,
        present,
        mean,
        tail,
        *links,
        far_in=(3, 4),
        far_out=(0, 1),
        copies=4,
        micros=6,
    )


def window_counts(local, rows):
    spots = lax.broadcasted_iota(jnp.int32, (256, LANES), 0).astype(F32).astype(BF)
    blocks = []
    for first in range(0, rows, 256):
        size = min(256, rows - first)
        place = local - first
        place = jnp.where((place >= 0) & (place < size), place, -1).astype(F32)
        counts = jnp.zeros((size, LANES), BF)
        for slot in range(local.shape[0]):
            row = jnp.broadcast_to(place[slot : slot + 1], (16, LANES)).astype(BF)
            row = jnp.concatenate([row] * (size // 16), 0)
            counts = counts + jnp.where(row == spots[:size], jnp.bfloat16(1.0), jnp.bfloat16(0.0))
        blocks.append(counts)
    return jnp.concatenate(blocks, 0)


def slot_totals(present):
    return jnp.maximum(jnp.sum(present.astype(F32), 0, keepdims=True), 1.0)


def counts_tile(sz, links, marks, start, at, counts):
    local = jnp.where(marks > 0, links - start, -1)
    counts[at : at + WINDOW, :] = window_counts(local, WINDOW)
    counts[at + WINDOW : at + sz.count_rows, :] = jnp.broadcast_to(slot_totals(marks), (16, LANES)).astype(BF)


def fill_counts(sz, part, nbr2, pres2, nbr3, pres3, counts):
    tiles = nbr2.shape[1] // LANES
    for tile in range(sz.tiles_b):
        column = 4 * sz.own // LANES * part + tile
        start = sz.a_row(part) + 4 * LANES * tile
        links, marks = half_columns(nbr2, column, tiles, 0), half_columns(pres2, column, tiles, 0)
        counts_tile(sz, links, marks, start, sz.count_rows * tile, counts)
    for tile in range(sz.own // LANES):
        columns = pl.ds(aligned(sz.own * part + LANES * tile), LANES)
        at = sz.count_rows * (sz.tiles_b + tile)
        counts_tile(sz, nbr3[:, columns], pres3[:, columns], sz.b_row(part), at, counts)
        at += sz.count_rows * (sz.own // LANES)
        counts_tile(sz, nbr2[:, columns], pres2[:, columns], sz.b_row(part), at, counts)


def tile_counts(sz, counts, tile):
    at = sz.count_rows * tile
    totals = counts[at + WINDOW : at + WINDOW + 16, :].astype(F32)[0:1]
    return counts[at : at + WINDOW, :], totals


def activate(result):
    active = result * sigmoid(result)
    scale = lax.rsqrt(jnp.sum(active * active, 0, keepdims=True) + ROW_EPS)
    return result, scale, active * scale


def first_layer(weight, inputs, bias):
    result = dot(weight, inputs, (1, 0)) + bias
    active = result * sigmoid(result)
    scale = lax.rsqrt(jnp.sum(active * active, 0, keepdims=True) + ROW_EPS)
    return result, scale, active * scale


def join_inputs(sz, own, average):
    pieces = []
    for c in range(4):
        pieces.append(own[sz.group * c : sz.group * (c + 1)])
        pieces.append(average[sz.group * c : sz.group * (c + 1)])
    return jnp.concatenate(pieces, 0)


def norm_backward(grad, result, scale):
    gate = sigmoid(result)
    active = result * gate
    inner = jnp.sum(grad * active, 0, keepdims=True)
    grad_active = scale * grad - active * (scale * scale * scale * inner)
    return (grad_active * gate * (1.0 + result * (1.0 - gate))).astype(BF)


def split_inputs(sz, grad):
    pieces = [grad[sz.group * c : sz.group * (c + 1)] for c in range(8)]
    return jnp.concatenate(pieces[0::2], 0), jnp.concatenate(pieces[1::2], 0)


def row_sums(grad):
    return dot(jnp.ones((16, grad.shape[1]), BF), grad, (1, 1))


def spread(sz, scaled, counts):
    return dot(scaled.astype(BF), counts, (1, 1))


def halves(ref, at, lanes):
    return jnp.concatenate([ref[:, at : at + lanes], ref[:, at + lanes : at + 2 * lanes]], 0)


def store_halves(ref, at, lanes, value):
    rows = value.shape[0] // 2
    ref[:rows, at : at + lanes] = value[:rows]
    ref[:rows, at + lanes : at + 2 * lanes] = value[rows:]


def slot_column(table):
    rows, slots = table.shape
    wide = jnp.broadcast_to(table.astype(F32)[:, None, :], (rows, slots, slots))
    hit = lax.broadcasted_iota(jnp.int32, wide.shape, 1) == lax.broadcasted_iota(jnp.int32, wide.shape, 2)
    return jnp.sum(jnp.where(hit, wide, 0.0), 2, keepdims=True).reshape(rows * slots, 1)


def alive_column(sz, live):
    shape = (sz.dp, sz.dp)
    hit = lax.broadcasted_iota(jnp.int32, shape, 0) == lax.broadcasted_iota(jnp.int32, shape, 1)
    counts = jnp.sum(jnp.where(hit, jnp.broadcast_to(live.astype(F32), shape), 0.0), 1, keepdims=True)
    slot = lax.broadcasted_iota(jnp.int32, (sz.dp, sz.slot), 1).astype(F32)
    return slot_column(jnp.where(slot < counts, 1.0, 0.0))


def seed_picks(sz, serve_rows, take_rows, part):
    spots = (lax.broadcasted_iota(jnp.int32, (sz.slots, sz.own), 1) + sz.own * part).astype(F32)
    serve = jnp.where(slot_column(serve_rows) == spots, 1.0, 0.0)
    take = jnp.where(slot_column(take_rows) == spots, 1.0, 0.0)
    return serve, take, jnp.sum(serve, 1, keepdims=True), jnp.sum(take, 1, keepdims=True)


def seeds_kernel(
    sz, own_b, packed, s1, s2, s3, passed, counts_in, serve_in, take_in, live_in,
    low_out, high_out, sent,
    xb, pack, m1, m2, m3, p3, window_ref, serve_rows, take_rows, live_rows, low, high, turn_ref, w1_ref, w2_ref, states, sems,
):
    part = lax.axis_index("col")
    own, hid, n_b, group, hold, at = sz.own, sz.hid, sz.n_b, sz.group, sz.hold, sz.at
    n_mid = sz.n_mid
    copies = start_copies(
        (
            (packed, pack),
            (passed.at[:, pl.ds(sz.message_b, LANES * sz.blocks)], p3),
            (s1, m1),
            (s2, m2),
            (s3, m3),
            (own_b, xb),
            (counts_in.at[sz.seed_window(), :], window_ref),
            (serve_in, serve_rows),
            (take_in, take_rows),
            (live_in, live_rows),
        ),
        sems,
    )
    wait_all(copies[:4])
    for r, (message, first_lane) in enumerate(((None, 0), (m1, sz.message_b), (m2, sz.message_b), (p3, 0))):
        for block in range(sz.blocks if r else 0):
            first = first_lane + LANES * block
            pack[sz.main * block : sz.main * (block + 1), :] = message[:, first : first + LANES].astype(F32)
        shard = part ^ r
        for half in range(hid // LANES):
            lanes = slice(LANES * half, LANES * (half + 1))
            for s in range(2):
                first = 2 * hold * half + hold * s
                w1_ref[4 * hold * s + hold * r : 4 * hold * s + hold * (r + 1), lanes] = pack[first : first + hold, :]
            first = sz.rows_one + 2 * group * half
            row = pl.multiple_of(2 * group * shard, 2 * group)
            w2_ref[pl.ds(row, 2 * group), lanes] = pack[first : first + 2 * group, :]
        low[: sz.head, pl.ds(aligned(at["turned3"] + 2 * group * shard), LANES)] = pack[sz.at_three : sz.misc, :].astype(BF)
        misc = pack[sz.misc : sz.misc + 8, :]
        column = jnp.broadcast_to(misc[0:1] + misc[1:2] + misc[2:3], (LANES, LANES)).T
        row = pl.multiple_of(group * shard, group)
        for layer in range(2):
            lanes = slice(at["bias"] + LANES * layer, at["bias"] + LANES * (layer + 1))
            high[pl.ds(row, group), lanes] = column[group * layer : group * (layer + 1)]
    turned1 = w1_ref[...].T.astype(BF)
    turned2 = w2_ref[...].T.astype(BF)
    low[:, at["turned1"] : at["turned1"] + hid] = turned1
    low[:, at["turned2"] : at["turned2"] + 2 * hid] = turned2
    store_halves(low, at["weight2"], hid, w2_ref[...].astype(BF))
    weight3 = low[: sz.head, at["turned3"] : at["turned3"] + 2 * hid].astype(F32).T
    weight3 = jnp.concatenate([weight3, jnp.zeros((2 * hid, LANES - sz.head), F32)], 1)
    store_halves(low, at["weight3"], LANES, weight3.astype(BF))

    def piece(lanes, count):
        return (low.at[:, pl.ds(lanes, count)], low_out.at[:, pl.ds(lanes, count)])

    stores = start_copies((piece(n_mid, at["states"] - n_mid),), sems, 11)
    wait_all(copies[4:])
    low[:hold, :n_mid] = xb[:hold, :]
    low[4 * hold : 5 * hold, :n_mid] = xb[hold:, :]
    for r, message in ((1, m1), (2, m2), (3, m3)):
        tail = unpack_tails(sz, message, 2 * n_mid + sz.early, turn_ref)
        unpack_tiles(sz, message, tail, 0, sz.tiles_mid, hold * r, 0, low)
        first = (n_mid + sz.early) // LANES
        unpack_tiles(sz, message, tail, first, sz.tiles_mid, hold * (4 + r), 0, low)
    stores += start_copies((piece(0, n_mid),), sems, 12)
    bias1 = high[:hid, at["bias"] : at["bias"] + LANES]
    bias2 = high[:hid, at["bias"] + LANES : at["bias"] + 2 * LANES]
    high[:hid, :n_mid] = dot(turned1, low[:, :n_mid], (1, 0))
    for tile in range(sz.tiles_mid):
        lanes = slice(LANES * tile, LANES * (tile + 1))
        result, scale, state = activate(high[:hid, lanes] + bias1)
        high[:hid, lanes] = result
        high[hid:, lanes] = jnp.broadcast_to(scale, (8, LANES))
        upper, lower = two_parts(state)
        states[:hid, lanes] = upper
        states[hid:, lanes] = lower
    low[:, at["states"] : at["states"] + n_b] = states[:hid, :n_b]
    rows = pl.ds(0, hid + 8)
    others = pl.ds(at["bias"], 2 * LANES)
    stores += start_copies(
        (
            piece(at["states"], n_b),
            (high.at[rows, pl.ds(0, n_mid)], high_out.at[rows, pl.ds(0, n_mid)]),
            (high.at[rows, others], high_out.at[rows, others]),
        ),
        sems,
        13,
    )
    for tile in range(own // LANES):
        window, totals = tile_counts(sz, window_ref, tile)
        total = dot(states[:, :n_b], window, (1, 0))
        average = ((total[:hid] + total[hid:]) / totals).astype(BF)
        x = join_inputs(sz, states[:hid, n_b + LANES * tile : n_b + LANES * (tile + 1)], average)
        first = at["inputs2"] + LANES * tile
        low[:, first : first + LANES] = x[:hid]
        low[:, first + own : first + own + LANES] = x[hid:]
        result, scale, state = first_layer(turned2, x, bias2)
        first = at["result2"] + LANES * tile
        high[:hid, first : first + LANES] = result
        high[hid:, first : first + LANES] = jnp.broadcast_to(scale, (8, LANES))
        upper, lower = two_parts(state)
        first = at["embed"] + LANES * tile
        low[:, first : first + LANES] = upper
        low[:, first + own : first + own + LANES] = lower
    last = pl.ds(at["result2"], own)
    tail = (piece(at["embed"], sz.low_lanes - at["embed"]), (high.at[rows, last], high_out.at[rows, last]))
    stores += start_copies(tail, sems, 16)
    serve, take, _, owned = seed_picks(sz, serve_rows[...], take_rows[...], part)
    embed_high = low[:, at["embed"] : at["embed"] + own]
    served = dot(serve.astype(BF), embed_high, (1, 1))
    taken = dot(take.astype(BF), embed_high, (1, 1))
    dead = (owned > 0.5) & (alive_column(sz, live_rows[...]) < 0.5)
    first = lax.broadcasted_iota(jnp.int32, (sz.slots, hid), 1) == 0
    value = jnp.concatenate([served, jnp.where(first & dead, SENTINEL, taken)], 1)
    value = value.reshape(sz.dp, 1, sz.slot, 2 * hid)
    value = jnp.broadcast_to(value, (sz.dp, 4, sz.slot, 2 * hid))
    sent[...] = value.reshape(4 * sz.slots, 2 * hid).astype(BF)
    wait_all(stores)


def sent_rows(sz, low, at, serve, take):
    embed_high = low[:, at : at + sz.own]
    embed_low = low[:, at + sz.own : at + 2 * sz.own]
    take = take.astype(BF)
    return jnp.concatenate(
        [dot(serve.astype(BF), embed_high, (1, 1)), dot(take, embed_high, (1, 1)), dot(take, embed_low, (1, 1))], 1
    )


def seeds_forward(sz, messages, counts, tables):
    hid = sz.hid
    tail = (sz.main, LANES * sz.blocks)
    return call(
        functools.partial(seeds_kernel, sz),
        [
            ((hid, sz.low_lanes), BF),
            ((hid + 8, sz.high_lanes), F32),
            ((4 * sz.slots, 2 * hid), BF),
        ],
        [
            ((2 * sz.hold, sz.n_mid), BF),
            ((sz.main * sz.blocks, LANES), F32),
            ((sz.main, sz.full_b), BF),
            ((sz.main, sz.full_b), BF),
            ((sz.main, sz.message_b), BF),
            (tail, BF),
            ((sz.count_rows * (sz.own // LANES), LANES), BF),
            *[(item.shape, jnp.int32) for item in tables],
            ((hid, sz.low_lanes), BF),
            ((hid + 8, sz.high_lanes), F32),
            ((2 * sz.main, LANES), F32),
            ((8 * sz.hold, hid), F32),
            ((2 * hid, hid), F32),
            ((2 * hid, sz.n_mid), BF),
        ],
        SEEDS_MIB,
        *messages,
        counts,
        *tables,
        far_in=(0, 1, 6, 7, 8, 9),
        loose=(2, 3, 4, 5),
        micros=4,
        far_out=(0, 1),
        copies=19,
    )


def rest_kernel(
    sz, low_in, high_in, counts_in, own_a, a1, a2, a3, e1, e2, e3, labels_in, weighting_in, head_in, part_out,
    labels, weighting, head_bias, low, xa, bias, counts, xo, c1, c2, c3, turn_ref,
    states, states2, result1, scale1, inputs2, result2, scale2, grad_a, low_grad, part_ref, sems,
):
    part = lax.axis_index("col")
    own, hid, n_a, n_b, hold = sz.own, sz.hid, sz.n_a, sz.n_b, sz.hold
    at = dict(sz.at)
    for name in ("turned1", "turned2", "weight2", "weight3", "turned3", "states", "embed"):
        at[name] -= sz.n_mid
    lanes = at["embed"] + own
    copies = start_copies(
        (
            (own_a, xo),
            *[(e.at[:, pl.ds(sz.n_mid, sz.early)], c.at[:, pl.ds(0, sz.early)]) for e, c in ((e1, c1), (e2, c2), (e3, c3))],
            *[
                (e.at[:, pl.ds(2 * sz.n_mid + sz.early, LANES)], c.at[:, pl.ds(sz.early, LANES)])
                for e, c in ((e1, c1), (e2, c2), (e3, c3))
            ],
            (low_in.at[:, pl.ds(sz.n_mid, hid)], low.at[:, pl.ds(0, hid)]),
            (high_in.at[:, pl.ds(sz.at["bias"], 2 * LANES)], bias),
            (low_in.at[:, pl.ds(sz.n_mid + hid, lanes - hid)], low.at[:, pl.ds(hid, lanes - hid)]),
            (counts_in, counts),
            (labels_in, labels),
            (weighting_in, weighting),
            (head_in, head_bias),
        ),
        sems,
    )
    late = (n_a - sz.early) // LANES
    for r, message in ((1, a1), (2, a2), (3, a3)):
        tail = unpack_tails(sz, message, 2 * n_a - sz.early, turn_ref)
        unpack_tiles(sz, message, tail, 0, late, hold * r, sz.early, xa)
        unpack_tiles(sz, message, tail, late, n_a // LANES, hold * (4 + r), 0, xa)
    wait_all(copies[:7])
    for r, before in ((1, c1), (2, c2), (3, c3)):
        tail = before[:, sz.early :].astype(F32)[sz.tiles_mid : sz.tiles_mid + EARLY]
        unpack_tiles(sz, before, tail, 0, EARLY, hold * r, 0, xa)
    xa[:hold, :] = xo[:hold, :]
    xa[4 * hold : 5 * hold, :] = xo[hold:, :]
    wait_all(copies[7:9])
    turned1 = low[:, at["turned1"] : at["turned1"] + hid]
    bias1 = bias[:hid, :LANES]
    bias2 = bias[:hid, LANES:]

    result1[...] = dot(turned1, xa[...], (1, 0))

    def forward_step(index, carry):
        lanes = pl.ds(aligned(index * LANES), LANES)
        result, scale, state = activate(result1[:, lanes] + bias1)
        result1[:, lanes] = result
        scale1[:, lanes] = scale
        upper, lower = two_parts(state)
        states[:hid, lanes] = upper
        states[hid:, lanes] = lower
        return carry

    lax.fori_loop(0, n_a // LANES, forward_step, 0, unroll=3)
    wait_all(copies[9:])
    turned2 = low[:, at["turned2"] : at["turned2"] + 2 * hid]
    for tile in range(sz.tiles_b):
        lanes = slice(LANES * tile, LANES * (tile + 1))
        window, totals = tile_counts(sz, counts, tile)
        total = dot(states[:, 4 * LANES * tile : 4 * LANES * tile + WINDOW], window, (1, 0))
        average = ((total[:hid] + total[hid:]) / totals).astype(BF)
        inputs2[:, lanes] = join_inputs(sz, low[:, at["states"] + LANES * tile : at["states"] + LANES * (tile + 1)], average)
    result2[...] = dot(turned2, inputs2[...], (1, 0))
    for tile in range(sz.tiles_b):
        lanes = slice(LANES * tile, LANES * (tile + 1))
        result, scale, state = activate(result2[:, lanes] + bias2)
        result2[:, lanes] = result
        scale2[:, lanes] = scale
        upper, lower = two_parts(state)
        states2[:hid, lanes] = upper
        states2[hid:, lanes] = lower
    counts3, totals3 = tile_counts(sz, counts, sz.tiles_b)
    total = dot(states2[...], counts3, (1, 0))
    average = ((total[:hid] + total[hid:]) / totals3).astype(BF)
    inputs3 = join_inputs(sz, low[:, at["embed"] : at["embed"] + own], average)

    columns = pl.ds(aligned(own * part), own)
    classes = lax.broadcasted_iota(jnp.int32, (sz.head, own), 0)
    head_row = jnp.concatenate([head_bias[...], jnp.zeros((1, LANES - sz.classes), F32)], 1)
    head_column = jnp.broadcast_to(head_row, (LANES, LANES)).T[: sz.head]
    logits = dot(low[: sz.head, at["turned3"] : at["turned3"] + 2 * hid], inputs3, (1, 0)) + head_column
    logits = jnp.where(classes < sz.classes, logits, -1e30)
    highest = jnp.max(logits, 0, keepdims=True)
    expo = jnp.exp(logits - highest)
    totals = jnp.sum(expo, 0, keepdims=True)
    hit = classes == labels[:, columns]
    weights = weighting[:, columns].astype(F32)
    target = jnp.sum(jnp.where(hit, logits, 0.0), 0, keepdims=True)
    ce_total = jnp.sum(weights * (highest + jnp.log(totals) - target), 1, keepdims=True)
    seed_count = jnp.sum(weights, 1, keepdims=True)
    grad_logits = (weights * (expo / totals - jnp.where(hit, 1.0, 0.0))).astype(BF)
    g3 = at["g3"]
    part_ref[: sz.head, g3 : g3 + 2 * hid] = dot(grad_logits, inputs3, (1, 1))
    head_sums = jnp.concatenate([row_sums(grad_logits), jnp.zeros((16, LANES - sz.head), F32)], 1)
    part_ref[sz.head + 16 : sz.head + 32, g3 : g3 + LANES] = head_sums
    lane_at = lax.broadcasted_iota(jnp.int32, (16, LANES), 1)
    sums = jnp.where(lane_at == 0, ce_total, jnp.where(lane_at == 1, seed_count, 0.0))
    part_ref[sz.head + 16 : sz.head + 32, g3 + LANES : g3 + 2 * LANES] = sums
    own_part, average_part = split_inputs(sz, dot(halves(low, at["weight3"], LANES)[:, : sz.head], grad_logits, (1, 0)))
    part_ref[:hid, at["grad_embed"] : at["grad_embed"] + own] = own_part
    grad_mid = spread(sz, average_part / totals3, counts3)
    low_grad2 = norm_backward(grad_mid, result2[...], scale2[...])
    g2 = dot(inputs2[...], low_grad2, (1, 1))
    part_ref[:hid, at["g2"] : at["g2"] + hid] = g2[:hid]
    part_ref[:hid, at["g2"] + hid : at["g2"] + 2 * hid] = g2[hid:]
    part_ref[sz.head : sz.head + 16, g3 + hid : g3 + 2 * hid] = row_sums(low_grad2)
    weight2 = halves(low, at["weight2"], hid)
    grad_a[...] = jnp.zeros_like(grad_a)
    own_part, average_part = split_inputs(sz, dot(weight2, low_grad2, (1, 0)))
    part_ref[:hid, at["grad_b"] : at["grad_b"] + n_b] = own_part
    for tile in range(sz.tiles_b):
        window, totals = tile_counts(sz, counts, tile)
        lanes = slice(4 * LANES * tile, 4 * LANES * tile + WINDOW)
        grad_a[:, lanes] = grad_a[:, lanes] + spread(sz, average_part[:, LANES * tile : LANES * (tile + 1)] / totals, window)
    rows, few = pl.ds(0, hid + 8), pl.ds(0, sz.head + 32)
    split = at["g2"]
    stores = start_copies(
        (
            (part_ref.at[rows, pl.ds(split, hid * 2)], part_out.at[rows, pl.ds(split, hid * 2)]),
            (
                part_ref.at[rows, pl.ds(at["grad_b"], n_b + own)],
                part_out.at[rows, pl.ds(at["grad_b"], n_b + own)],
            ),
        ),
        sems,
        14,
    )

    def backward_step(index, carry):
        lanes = pl.ds(aligned(index * LANES), LANES)
        low_grad[:, lanes] = norm_backward(grad_a[:, lanes], result1[:, lanes], scale1[:, lanes])
        return carry

    lax.fori_loop(0, n_a // LANES, backward_step, 0, unroll=3)
    part_ref[:hid, at["g1"] : at["g1"] + hid] = dot(xa[...], low_grad[...], (1, 1))
    part_ref[sz.head : sz.head + 16, g3 : g3 + hid] = row_sums(low_grad[...])
    stores += start_copies(
        (
            (part_ref.at[rows, pl.ds(0, hid)], part_out.at[rows, pl.ds(0, hid)]),
            (part_ref.at[few, pl.ds(g3, 2 * hid)], part_out.at[few, pl.ds(g3, 2 * hid)]),
        ),
        sems,
        16,
    )
    wait_all(stores)


def rest_step(sz, low, high, counts, means, labels, weighting, head_bias):
    hid = sz.hid
    return call(
        functools.partial(rest_kernel, sz),
        [((hid + 8, sz.part_lanes), F32)],
        [
            (labels.shape, jnp.int32),
            (weighting.shape, jnp.int32),
            (head_bias.shape, F32),
            ((hid, sz.at["embed"] + sz.own - sz.n_mid), BF),
            ((hid, sz.n_a), BF),
            ((hid + 8, 2 * LANES), F32),
            (counts.shape, BF),
            ((2 * sz.hold, sz.n_a), BF),
            *[((sz.main, sz.early + LANES), BF)] * 3,
            ((2 * sz.main, LANES), F32),
            ((2 * hid, sz.n_a), BF),
            ((2 * hid, sz.n_b), BF),
            ((hid, sz.n_a), F32),
            ((1, sz.n_a), F32),
            ((2 * hid, sz.n_b), BF),
            ((hid, sz.n_b), F32),
            ((1, sz.n_b), F32),
            ((hid, sz.n_a), F32),
            ((hid, sz.n_a), BF),
            ((hid + 8, sz.part_lanes), F32),
        ],
        REST_MIB,
        low,
        high,
        counts,
        *means,
        labels,
        weighting,
        head_bias,
        far_in=(0, 1, 2, 3, 10, 11, 12),
        loose=(7, 8, 9),
        micros=14,
        far_out=(0,),
        copies=18,
    )[0]


def seeds_back_kernel(
    sz, serve_in, take_in, live_in, received, low_in, high_in, counts_in, part_in, keep0, keep1, send,
    serve_rows, take_rows, live_rows, x_ref, weight_ref, low, high, window_ref, partial, g1_ref, g2_ref, gb_ref, sems,
):
    part = lax.axis_index("col")
    own, hid, group, n_b, n_mid = sz.own, sz.hid, sz.group, sz.n_b, sz.n_mid
    at = dict(sz.at)
    at["inputs2"] -= at["embed"]
    split = at["grad_b"]
    few = pl.ds(0, sz.head + 32)
    lanes = pl.ds(at["result2"], own)
    copies = start_copies(
        (
            (serve_in, serve_rows),
            (take_in, take_rows),
            (live_in, live_rows),
            (low_in.at[:, pl.ds(at["embed"], 4 * own)], low),
            (part_in.at[:, pl.ds(split + n_b, own)], partial.at[:, pl.ds(split + n_b, own)]),
            (high_in.at[:, lanes], high.at[:, lanes]),
            (low_in.at[:, pl.ds(at["weight2"], 2 * hid)], weight_ref),
            (counts_in.at[sz.seed_window(), :], window_ref),
            (part_in.at[:, pl.ds(split, n_b)], partial.at[:, pl.ds(split, n_b)]),
            (high_in.at[:, pl.ds(0, n_mid)], high.at[:, pl.ds(0, n_mid)]),
            (low_in.at[:, pl.ds(0, n_mid)], x_ref),
            (part_in.at[:, pl.ds(0, at["g3"])], partial.at[:, pl.ds(0, at["g3"])]),
            (part_in.at[few, pl.ds(at["g3"], 2 * hid)], partial.at[few, pl.ds(at["g3"], 2 * hid)]),
        ),
        sems,
    )
    arrived = received[...].astype(F32).reshape(sz.dp, 4, sz.slot, 2 * hid)
    arrived = jnp.sum(arrived, 1).reshape(sz.slots, 2 * hid)
    at["embed"] = 0
    wait_all(copies[:4])
    serve, take, served, taken = seed_picks(sz, serve_rows[...], take_rows[...], part)
    mine = sent_rows(sz, low, 0, serve, take)
    theirs = arrived[:, hid:]
    alive_there = theirs[:, 0:1] < 0.5 * SENTINEL
    differ = mine[:, hid : 2 * hid] + mine[:, 2 * hid :] - arrived[:, :hid]
    differ = jnp.where((taken > 0.5) & (alive_column(sz, live_rows[...]) > 0.5), differ, 0.0)
    dist_total = DIST_WEIGHT * jnp.sum(jnp.sum(differ * differ, 0, keepdims=True), 1, keepdims=True)
    local_high, local_low = two_parts(2.0 * DIST_WEIGHT * differ)
    back = jnp.where((served > 0.5) & alive_there, theirs - mine[:, :hid], 0.0)
    back = (-2.0 * DIST_WEIGHT * back).astype(BF)
    take = take.astype(BF)
    serve = serve.astype(BF)
    wait_all(copies[4:6])
    grad = partial[:hid, at["grad_embed"] : at["grad_embed"] + own]
    grad = grad + dot(local_high, take, (0, 0)) + dot(local_low, take, (0, 0)) + dot(back, serve, (0, 0))
    lanes = slice(at["result2"], at["result2"] + own)
    low_grad2 = norm_backward(grad, high[:hid, lanes], high[hid:, lanes][0:1])
    wait_all(copies[6:9])
    weight2 = halves(weight_ref, 0, hid)
    own_part, average_part = split_inputs(sz, dot(weight2, low_grad2, (1, 0)))
    total_b = partial[:hid, at["grad_b"] : at["grad_b"] + n_b]
    for tile in range(own // LANES):
        window, totals = tile_counts(sz, window_ref, tile)
        total_b = total_b + spread(sz, average_part[:, LANES * tile : LANES * (tile + 1)] / totals, window)
    wait_all(copies[9:10])
    low_grad = jnp.concatenate(
        [
            norm_backward(total_b, high[:hid, :n_b], high[hid:, :n_b][0:1]),
            norm_backward(own_part, high[:hid, n_b:n_mid], high[hid:, n_b:n_mid][0:1]),
        ],
        1,
    )
    wait_all(copies[10:])
    added = dot(halves(low, at["inputs2"], own), low_grad2, (1, 1))
    for half in range(2):
        lanes = slice(at["g2"] + hid * half, at["g2"] + hid * (half + 1))
        g2_ref[hid * half : hid * (half + 1), :] = partial[:hid, lanes] + added[hid * half : hid * (half + 1)]
    g3 = at["g3"]
    sums = partial[sz.head : sz.head + 16, g3 : g3 + 2 * hid]
    gb_ref[:, hid:] = sums[:, hid:] + row_sums(low_grad2)
    half = 4 * sz.hold
    g1_ref[...] = partial[:hid, at["g1"] : at["g1"] + hid] + dot(x_ref[...], low_grad, (1, 1))
    gb_ref[:, :hid] = sums[:, :hid] + row_sums(low_grad)
    head_row = partial[sz.head + 16 : sz.head + 32, g3 : g3 + LANES]
    totals = partial[sz.head + 16 : sz.head + 32, g3 + LANES : g3 + 2 * LANES]
    lane_at = lax.broadcasted_iota(jnp.int32, (16, LANES), 1)
    row_at = lax.broadcasted_iota(jnp.int32, (16, LANES), 0)
    fixed = ((totals[0:1, 0:1] + dist_total) * float(2**LOSS_BITS) + 0.5).astype(jnp.int32)
    count = totals[0:1, 1:2].astype(jnp.int32)
    whole = jnp.where(lane_at < 32, fixed, count)
    bits = (lax.shift_right_logical(whole, lane_at & 31) & 1).astype(F32)
    bits = jnp.where(lane_at < 64, bits, 0.0)
    for r, (target_ref, base) in enumerate(((keep0, 0), (send, 0), (keep1, 0), (send, sz.pay))):
        shard = part ^ r
        block2 = pl.ds(pl.multiple_of(2 * group * shard, 2 * group), 2 * group)
        row = base
        for h in range(hid // LANES):
            lanes = slice(LANES * h, LANES * (h + 1))
            for s in range(2):
                rows = slice(half * s + sz.hold * r, half * s + sz.hold * (r + 1))
                target_ref[row : row + sz.hold, :] = g1_ref[rows, lanes].astype(BF)
                row += sz.hold
        for h in range(hid // LANES):
            target_ref[row : row + 2 * group, :] = g2_ref[block2, LANES * h : LANES * (h + 1)].astype(BF)
            row += 2 * group
        third = partial[: sz.head, pl.ds(aligned(g3 + 2 * group * shard), LANES)]
        target_ref[row : row + sz.head, :] = third.astype(BF)
        row += sz.head
        odd = (shard % 2) == 1
        block = aligned((shard // 2) * LANES)
        one = gb_ref[:, pl.ds(block, LANES)]
        two = gb_ref[:, pl.ds(aligned(hid + block), LANES)]
        one = jnp.where(odd, pltpu.roll(one, group, 1), one)
        two = jnp.where(odd, two, pltpu.roll(two, group, 1))
        bias_row = jnp.where(lane_at < group, one, two)
        misc = jnp.where(row_at == 0, bias_row, jnp.where(row_at == 1, head_row, jnp.where(row_at == 2, bits, 0.0)))
        target_ref[row : row + 16, :] = misc.astype(BF)


def seeds_backward(sz, tables, received, low, high, counts, partial):
    hid = sz.hid
    return call(
        functools.partial(seeds_back_kernel, sz),
        [((sz.pay, LANES), BF), ((sz.pay, LANES), BF), ((2 * sz.pay, LANES), BF)],
        [
            *[(item.shape, jnp.int32) for item in tables],
            ((hid, sz.n_mid), BF),
            ((hid, 2 * hid), BF),
            ((hid, 4 * sz.own), BF),
            ((hid + 8, sz.high_lanes), F32),
            ((sz.count_rows * (sz.own // LANES), LANES), BF),
            ((hid + 8, sz.part_lanes), F32),
            ((8 * sz.hold, hid), F32),
            ((2 * hid, hid), F32),
            ((16, 2 * hid), F32),
        ],
        BACK_MIB,
        *tables,
        received,
        low,
        high,
        counts,
        partial,
        far_in=(0, 1, 2, 4, 5, 6, 7),
        micros=3,
        copies=13,
    )


def lamb_kernel(sz, grad, w1, w2, w3, wh, wb, f1, f2, f3, fh, fb, s1, s2, s3, sh, sb, *rest):
    params = (w1, w2, w3, wh, wb)
    firsts = (f1, f2, f3, fh, fb)
    seconds = (s1, s2, s3, sh, sb)
    moments, squares, updates = rest[:5], rest[5:10], rest[10:15]
    sums_ref, totals_ref, one_ref, three_ref = rest[15:]
    group, hold = sz.group, sz.hold

    def wide(at, rows):
        return jnp.concatenate([grad[at : at + rows, :], grad[at + rows : at + 2 * rows, :]], 1)

    one = wide(0, 2 * hold)
    three = grad[sz.at_three : sz.misc, :]
    turned = pltpu.roll(three, group, 1)
    for f in range(sz.feat):
        one_ref[f, 0:1, :] = one[f : f + 1]
        one_ref[f, 1:2, :] = one[hold + f : hold + f + 1]
    for c in range(sz.classes):
        three_ref[c, 0:1, :] = three[c : c + 1, :group]
        three_ref[c, 1:2, :] = turned[c : c + 1, :group]
    misc = grad[sz.misc : sz.misc + 8, :]
    hidden = jnp.concatenate([misc[0:1, :group], misc[0:1, group : 2 * group]], 0)
    two = wide(sz.rows_one, 2 * group).reshape(2, group, sz.hid)
    grads = (one_ref[...], two, three_ref[...], hidden, misc[1:2, : sz.classes])
    lane_at = lax.broadcasted_iota(jnp.int32, (8, LANES), 1)
    row_at = lax.broadcasted_iota(jnp.int32, (8, LANES), 0)
    sums = jnp.zeros((8, LANES), F32)
    for i in range(5):
        g = grads[i]
        w = params[i][...]
        m = BETA_ONE * firsts[i][...] + (1.0 - BETA_ONE) * g
        v = BETA_TWO * seconds[i][...] + (1.0 - BETA_TWO) * g * g
        u = (m / (1.0 - BETA_ONE**STEP)) / (jnp.sqrt(v / (1.0 - BETA_TWO**STEP)) + ADAM_EPS) + DECAY_RATE * w
        moments[i][...] = m
        squares[i][...] = v
        updates[i][...] = u
        for row, item in ((0, w), (1, u)):
            item = item * item
            if i < 3:
                item = jnp.sum(item, 0)
            total = jnp.sum(jnp.sum(item, 0, keepdims=True), 1, keepdims=True)
            if i == 4:
                total = 0.25 * total
            sums = jnp.where((lane_at == i) & (row_at == row), total, sums)
    sums_ref[...] = sums
    power = (1 << (lane_at & 15)).astype(F32)
    power = jnp.where((lane_at & 31) < 16, power, power * float(2**16))
    bits = jnp.broadcast_to(misc[2:3], (8, LANES)) * power
    loss = jnp.sum(jnp.where(lane_at < 32, bits, 0.0), 1, keepdims=True) * float(2.0**-LOSS_BITS)
    count = jnp.sum(jnp.where((lane_at >= 32) & (lane_at < 64), bits, 0.0), 1, keepdims=True)
    totals_ref[...] = jnp.where(lane_at == 0, loss, count)


def lamb(sz, grad, params, firsts, seconds):
    like = [(item.shape, F32) for item in params]
    return call(
        functools.partial(lamb_kernel, sz),
        like * 3 + [((8, LANES), F32)] * 2,
        [(params[0].shape, F32), (params[2].shape, F32)],
        6,
        grad,
        *params,
        *firsts,
        *seconds,
    )


def step_kernel(own, far, w1, w2, w3, wh, wb, u1, u2, u3, uh, ub, n1, n2, n3, nh, nb, norms_ref):
    norms = jnp.sqrt(own[...] + far[...])
    norms_ref[...] = norms[0:2, 0:5]
    for i, (w, u, n) in enumerate(
        ((w1, u1, n1), (w2, u2, n2), (w3, u3, n3), (wh, uh, nh), (wb, ub, nb))
    ):
        ratio = LEARN_RATE * (norms[0:1, i : i + 1] / norms[1:2, i : i + 1])
        n[...] = w[...] - ratio * u[...]


def take_step(sums, params, updates):
    return call(
        step_kernel,
        [(item.shape, F32) for item in params] + [((2, 5), F32)],
        [],
        3,
        *sums,
        *params,
        *updates,
    )


def swap(value, axis, count, bit):
    return lax.ppermute(value, axis, [(i, i ^ bit) for i in range(count)])


def merged(own, other):
    return lax.reduce_precision(own.astype(F32) + other.astype(F32), 8, 7)


def shards(
    features, neighbors_one, present_one, neighbors_two, present_two, neighbors_three, present_three,
    labels, seed_weight, serve_rows, take_seed, fetch_live,
    weight_one, weight_two, weight_three, hidden_bias, head_bias,
    first_one, first_two, first_three, first_hidden, first_head,
    second_one, second_two, second_three, second_hidden, second_head,
):
    sz = Sizes(features, neighbors_one, neighbors_two, neighbors_three, weight_two, weight_three, serve_rows)

    def tree(one, two, three, hidden, head):
        return (one.transpose(1, 0, 2), two, three.transpose(2, 0, 1), hidden, head[None, :])

    def back(one, two, three, hidden, head):
        return (one.transpose(1, 0, 2), two, three.transpose(1, 2, 0), hidden, head[0])

    params = tree(weight_one, weight_two, weight_three, hidden_bias, head_bias)
    firsts = tree(first_one, first_two, first_three, first_hidden, first_head)
    seconds = tree(second_one, second_two, second_three, second_hidden, second_head)

    own_b, packed, mean, tail, *sent = first_messages(sz, features, neighbors_one, present_one, *params[:4])
    s1, s2, s3 = [swap(sent[r - 1], "col", 4, r) for r in (1, 2, 3)]
    links = (neighbors_two, present_two, neighbors_three, present_three)
    own_a, counts, *means = mean_messages(sz, features, neighbors_one, present_one, mean, tail, links)
    s1, *means = lax.optimization_barrier((s1, *means))
    means = [swap(means[r - 1], "col", 4, r) for r in (1, 2, 3)]
    later, s3, counts = lax.optimization_barrier((s2, s3, counts))
    passed = swap(later, "col", 4, 1)
    tables = (serve_rows, take_seed, fetch_live[None, :])
    low, high, rows = seeds_forward(sz, (own_b, packed, s1, s2, s3, passed), counts, tables)
    received = lax.all_to_all(rows, ("dp", "col"), split_axis=0, concat_axis=0, tiled=True)
    partial = rest_step(sz, low, high, counts, (own_a, *means, s1, s2, s3), labels[None, :], seed_weight[None, :], head_bias[None, :])
    keep0, keep1, send = seeds_backward(sz, tables, received, low, high, counts, partial)
    other = swap(send, "col", 4, 1)
    own = merged(keep0, other[: sz.pay]).astype(BF)
    far = merged(keep1, other[sz.pay :]).astype(BF)
    pair = [[(d, c), (d ^ 1, c ^ 2)] for d in range(sz.dp) for c in range(4)]
    pair = [(a * 4 + b, c * 4 + d) for (a, b), (c, d) in pair]
    near = (swap(far, "col", 4, 2), swap(own, "dp", sz.dp, 1), lax.ppermute(far, ("dp", "col"), pair))
    near = [item.astype(F32) for item in (own, *near)]
    grad = lax.reduce_precision((near[0] + near[1]) + (near[2] + near[3]), 8, 7)
    bit = 2
    while bit < sz.dp:
        grad = merged(grad, swap(grad.astype(BF), "dp", sz.dp, bit))
        bit *= 2
    outs = lamb(sz, grad, params, firsts, seconds)
    moments, squares, updates = outs[:5], outs[5:10], outs[10:15]
    sums, totals = outs[15], outs[16]
    pair = sums + swap(sums, "col", 4, 1)
    fresh = take_step([pair, swap(pair, "col", 4, 2)], params, updates)
    return (*back(*fresh[:5]), *back(*moments), *back(*squares), fresh[5], totals[0, 0], totals[0, 1])


def solution(mesh):
    wide = P(None, "col", None)
    tree = [wide, wide, wide, P(None, "col"), P()]
    return jax.shard_map(
        shards,
        mesh=mesh,
        in_specs=(
            P("col", "dp"),
            *[P(None, "dp")] * 6,
            P("dp"),
            P("dp"),
            P("dp", None),
            P("dp", None),
            P("dp"),
            *tree,
            *tree,
            *tree,
        ),
        out_specs=(*tree, *tree, *tree, P(), P(), P()),
        check_vma=False,
    )
```

```python
import functools

import jax
import jax.numpy as jnp
from jax import lax
from jax.experimental import pallas as pl
from jax.experimental.pallas import tpu as pltpu
from jax.sharding import PartitionSpec as P

REACH = 64
STEP = 5
DIST_WEIGHT = 1.0
ROW_EPS = 1e-06
LEARN_RATE = 0.5
BETA_ONE = 0.9
BETA_TWO = 0.999
ADAM_EPS = 1e-06
DECAY_RATE = 0.01

BF = jnp.bfloat16
F32 = jnp.float32
LANES = 128
WINDOW = 640
HALF = 64
FRONT = 320
SENTINEL = 4.0
MIB = 2**20
LOSS_BITS = 14
EARLY = 4
FIRST_MIB = 8
MEAN_MIB = 8
SEEDS_MIB = 16
REST_MIB = 28
BACK_MIB = 12


def cost(micros):
    return pl.CostEstimate(flops=int(micros * 10**9), bytes_accessed=1, transcendentals=0)


def call(kernel, outs, scratch, mib, *args, far_in=(), far_out=(), copies=0, micros=1, loose=(), name=None):
    near = pl.BlockSpec(memory_space=pltpu.VMEM)
    far = pl.BlockSpec(memory_space=pltpu.HBM)
    free = pl.BlockSpec(memory_space=pl.ANY)
    scratch = [pltpu.VMEM(shape, kind) for shape, kind in scratch]
    args = [pltpu.with_memory_space_constraint(a, pltpu.HBM) if i in far_in else a for i, a in enumerate(args)]
    return pl.pallas_call(
        kernel,
        in_specs=[free if i in loose else far if i in far_in else near for i in range(len(args))],
        out_specs=tuple(far if i in far_out else near for i in range(len(outs))),
        out_shape=tuple(
            pltpu.HBM(shape, kind) if i in far_out else jax.ShapeDtypeStruct(shape, kind)
            for i, (shape, kind) in enumerate(outs)
        ),
        scratch_shapes=scratch + ([pltpu.SemaphoreType.DMA((copies,))] if copies else []),
        compiler_params=pltpu.CompilerParams(vmem_limit_bytes=mib * MIB),
        cost_estimate=cost(micros),
        name=name,
    )(*args)


def start_copies(pairs, sems, first=0):
    copies = [pltpu.make_async_copy(src, dst, sems.at[first + i]) for i, (src, dst) in enumerate(pairs)]
    for copy in copies:
        copy.start()
    return copies


def wait_all(copies):
    for copy in copies:
        copy.wait()


class Sizes:
    def __init__(self, features, neighbors_one, neighbors_two, neighbors_three, weight_two, weight_three, serve_rows):
        self.feat = features.shape[0]
        self.main = self.feat - 1
        self.hold = 32
        self.base = features.shape[1]
        self.low = neighbors_one.shape[1]
        self.mid = neighbors_two.shape[1]
        self.seeds = neighbors_three.shape[1]
        self.hid = weight_two.shape[2]
        self.group = weight_two.shape[1]
        self.classes = weight_three.shape[2]
        self.head = -(-self.classes // 16) * 16
        self.own = self.seeds // 4
        self.n_b = 4 * self.own + LANES
        self.n_a = 16 * self.own + 5 * LANES
        self.n_mid = self.n_b + self.own
        self.n_low = self.n_a + self.n_mid
        self.tiles_b = self.n_b // LANES
        self.tiles_mid = self.n_mid // LANES
        self.tiles_low = self.n_low // LANES
        self.slots = serve_rows.shape[0] * serve_rows.shape[1]
        self.slot = serve_rows.shape[1]
        self.dp = serve_rows.shape[0]
        self.rows_one = 2 * 2 * self.feat
        self.rows_two = 4 * self.group
        self.at_three = self.rows_one + self.rows_two
        self.misc = self.at_three + self.classes
        self.pay = -(-(self.misc + 5) // 16) * 16
        self.blocks = -(-(self.misc + 3) // self.main)
        self.early = EARLY * LANES
        self.message_a = self.pair_lanes(self.n_a, self.n_a - self.early)
        self.message_b = self.pair_lanes(self.n_mid, self.n_mid + self.early)
        self.full_b = self.message_b + LANES * self.blocks
        self.tiles_b_all = 16 * self.own // LANES + 1
        self.tiles_all = self.low // LANES + 8
        self.count_rows = WINDOW + 16
        hid, at = self.hid, self.n_mid
        places = {}
        for name, lanes in (
            ("turned1", hid), ("turned2", 2 * hid), ("weight2", 2 * hid), ("weight3", 2 * LANES), ("turned3", 2 * hid),
            ("states", self.n_b), ("embed", 2 * self.own), ("inputs2", 2 * self.own),
        ):
            places[name] = at
            at += lanes
        self.low_lanes = at
        at = 0
        for name, lanes in (("result1", self.n_mid), ("result2", self.own), ("bias", 2 * LANES)):
            places[name] = at
            at += lanes
        self.high_lanes = at
        at = 0
        for name, lanes in (("g1", hid), ("g2", 2 * hid), ("g3", 2 * hid), ("grad_b", self.n_b), ("grad_embed", self.own)):
            places[name] = at
            at += lanes
        self.part_lanes = at
        self.at = places

    def pair_lanes(self, means, own):
        lanes = means + own
        return lanes + LANES * -(-lanes // LANES // self.main)

    def first_ranges(self, part):
        a, b, c = self.ranges(part)
        b = (b[0], 0, b[2])
        c = (c[0], b[2], c[2])
        return [b, c, (a[0], self.n_mid, self.early)], [b, c]

    def second_ranges(self, part):
        first = 16 * self.own * part
        return [(first + self.early, 0, self.n_a - self.early)], [(first, 0, self.n_a)]

    def a_row(self, part):
        return 16 * self.own * part - FRONT

    def b_row(self, part):
        return 4 * self.own * part - HALF

    def seed_window(self):
        rows = self.count_rows * (self.own // LANES)
        return pl.ds(self.count_rows * self.tiles_b + rows, rows)

    def ranges(self, part):
        return (
            (16 * self.own * part, 0, self.n_a),
            (self.b_row(part) + FRONT, self.n_a, self.n_b),
            (self.own * part + FRONT, self.n_a + self.n_b, self.own),
        )


def dot(a, b, over):
    return lax.dot_general(a, b, (((over[0],), (over[1],)), ((), ())), preferred_element_type=F32)


def two_parts(value):
    high = value.astype(BF)
    return high, (value - high.astype(F32)).astype(BF)


def three_parts(value):
    high = value.astype(BF).astype(F32)
    rest = value - high
    middle = rest.astype(BF).astype(F32)
    return high, middle, (rest - middle).astype(BF).astype(F32)


def aligned(value):
    return pl.multiple_of(value, LANES)


def sigmoid(value):
    return 0.5 * jnp.tanh(0.5 * value) + 0.5


def unpack_tile(sz, message, tail, tile):
    spare = jnp.zeros((sz.hold - sz.feat, LANES), F32)
    main = message[:, LANES * tile : LANES * (tile + 1)].astype(F32)
    return jnp.concatenate([main, tail[tile : tile + 1, :], spare], 0).astype(BF)


def half_tiles(left, right):
    lane = lax.broadcasted_iota(jnp.int32, left.shape, 1)
    return jnp.where(lane < HALF, pltpu.roll(left, HALF, 1), pltpu.roll(right, HALF, 1))


def half_columns(ref, tile, tiles, spare):
    if isinstance(tile, int):
        left, right = max(tile - 1, 0), min(tile, tiles - 1)
        left, right = [ref[:, LANES * i : LANES * (i + 1)] for i in (left, right)]
        left = left if tile > 0 else jnp.full_like(left, spare)
        right = right if tile < tiles else jnp.full_like(right, spare)
        return half_tiles(left, right)
    left = ref[:, pl.ds(aligned(jnp.maximum(tile - 1, 0) * LANES), LANES)]
    right = ref[:, pl.ds(aligned(jnp.minimum(tile, tiles - 1) * LANES), LANES)]
    left = jnp.where(tile > 0, left, spare)
    right = jnp.where(tile < tiles, right, spare)
    return half_tiles(left, right)


def take_tile(ref, rows, first, half):
    if not half:
        return ref[:rows, pl.ds(aligned(first), LANES)].astype(F32)
    first = first - HALF
    left = ref[:rows, pl.ds(aligned(first), LANES)].astype(F32)
    return half_tiles(left, ref[:rows, pl.ds(aligned(first + LANES), LANES)].astype(F32))


def take_tail(ref, first, half):
    if not half:
        return ref[pl.ds(first // LANES, 1), :]
    row = (first - HALF) // LANES
    return half_tiles(ref[pl.ds(row, 1), :], ref[pl.ds(row + 1, 1), :])


def fill_own(sz, feat_ref, self_ref, self_tail, places):
    spare = jnp.zeros((sz.hold - sz.feat, LANES), F32)
    zeros = jnp.zeros((sz.feat, LANES), BF)
    count = min(sz.low, feat_ref.shape[1]) // LANES
    lane = lax.broadcasted_iota(jnp.int32, (sz.feat, LANES), 1)
    shift = FRONT // LANES
    before = zeros
    for place in range(places):
        tile = place - shift
        after = zeros
        if tile >= 0 and tile < count:
            after = pltpu.roll(feat_ref[:, LANES * tile : LANES * (tile + 1)], HALF, 1)
        value = jnp.where(lane < HALF, before.astype(F32), after.astype(F32))
        self_tail[place : place + 1, :] = value[sz.main : sz.feat]
        self_ref[:, LANES * place : LANES * (place + 1)] = jnp.concatenate([value, spare], 0).astype(BF)
        before = after


def mean_tiles(sz, begin, tiles, feat_ref, nbr_ref, pres_ref, links_ref, present_ref, mean_ref, tail_ref, base_ref, code_ref, count_ref):
    last = feat_ref.shape[1] // LANES - 6
    slots = nbr_ref.shape[0]
    base_ref[...] = jnp.zeros_like(base_ref)
    if begin % 8 or tiles % 8:
        code_ref[...] = jnp.full_like(code_ref, -1)
        count_ref[...] = jnp.ones_like(count_ref)
    for tile in range(feat_ref.shape[1] // LANES):
        row = feat_ref[:, LANES * tile : LANES * (tile + 1)].astype(F32)
        base_ref[8 + tile : 9 + tile, :] = row[sz.main : sz.feat]

    for table, shifted in ((nbr_ref, links_ref), (pres_ref, present_ref)):
        count = table.shape[1] // LANES
        for tile in range(begin, tiles):
            shifted[:, LANES * tile : LANES * (tile + 1)] = half_columns(table, tile, count, 0)

    def one_tile(step, carry):
        lanes = pl.ds(aligned(step * LANES), LANES)
        present = present_ref[:, lanes]
        valid = present.astype(F32)
        counts = jnp.maximum(jnp.sum(valid, 0, keepdims=True), 1.0)
        first = jnp.clip(4 * step - 3, 0, last)
        links = links_ref[:, lanes]
        code = jnp.where(present > 0, links, -1)
        count_ref[pl.ds(step, 1), :] = counts
        for slot in range(slots):
            code_ref[slot, pl.ds(step, 1), :] = code[slot : slot + 1]
        local = links - first * LANES
        piece = local >> 7
        spot = local & 127
        sources = [
            feat_ref[:, pl.ds(aligned((first + j) * LANES), LANES)].astype(F32) for j in range(6)
        ]
        totals = [jnp.zeros((8, LANES), F32) for _ in range(sz.main // 8)]
        for slot in range(slots):
            spots = jnp.broadcast_to(spot[slot : slot + 1], (8, LANES))
            pieces = jnp.broadcast_to(piece[slot : slot + 1], (8, LANES))
            marks = jnp.broadcast_to(valid[slot : slot + 1], (8, LANES))
            for h in range(sz.main // 8):
                taken = None
                for j in range(6):
                    found = jnp.take_along_axis(
                        sources[j][8 * h : 8 * h + 8], spots, axis=1, mode="promise_in_bounds"
                    )
                    taken = found if j == 0 else jnp.where(pieces == j, found, taken)
                totals[h] = totals[h] + taken * marks
        mean_ref[:, pl.ds(aligned((step + 2) * LANES), LANES)] = (jnp.concatenate(totals, 0) / counts).astype(BF)
        return carry

    even = begin + (tiles - begin) // 4 * 4
    lax.fori_loop(begin, even, one_tile, 0, unroll=4)
    for step in range(even, tiles):
        one_tile(step, 0)
    sub = lax.broadcasted_iota(jnp.int32, (8, LANES), 0)

    for block in range(begin // 8, -(-tiles // 8)):
        total = jnp.zeros((8, LANES), F32)
        for slot in range(slots):
            code = code_ref[slot, 8 * block : 8 * (block + 1), :]
            piece = (code >> 7) - (4 * (8 * block + sub) - 3)
            taken = None
            for j in range(6):
                source = base_ref[pl.ds(8 + 32 * block - 3 + j, 8, stride=4), :]
                found = jnp.take_along_axis(source, code & 127, axis=1, mode="promise_in_bounds")
                taken = found if j == 0 else jnp.where(piece == j, found, taken)
            total = total + jnp.where(code >= 0, taken, 0.0)
        tail_ref[8 * block + 2 : 8 * block + 10, :] = total / count_ref[8 * block : 8 * (block + 1), :]


def pack_pair(sz, ranges, self_ref, self_tail, mean_ref, tail_ref, turn_ref, out_ref):
    turn_ref[...] = jnp.zeros_like(turn_ref)
    lanes = 0
    for source_ref, rows_ref, group in zip((self_ref, mean_ref), (self_tail, tail_ref), ranges):
        for i, (first, at, count) in enumerate(group):
            at = at + lanes
            if i != 1:
                out_ref[:, at : at + count] = source_ref[: sz.main, pl.ds(aligned(first), count)]
                turn_ref[at // LANES : (at + count) // LANES, :] = rows_ref[pl.ds(first // LANES, count // LANES), :]
                continue
            for tile in range(count // LANES):
                place = first + LANES * tile
                piece = take_tile(source_ref, sz.main, place, True)
                out_ref[:, at + LANES * tile : at + LANES * (tile + 1)] = piece.astype(BF)
                turn_ref[at // LANES + tile : at // LANES + tile + 1, :] = take_tail(rows_ref, place, True)
        lanes += sum(count for _, _, count in group)
    for block in range(-(-lanes // LANES // sz.main)):
        at = lanes + LANES * block
        out_ref[:, at : at + LANES] = turn_ref[sz.main * block : sz.main * (block + 1), :].astype(BF)


def own_pair(sz, ranges, self_ref, mean_ref, tail_ref, own_ref):
    spare = jnp.zeros((sz.hold - sz.feat, LANES), F32)
    base = ranges[0][1]
    for i, (start, at, count) in enumerate(ranges):
        for tile in range(count // LANES):
            place = start + LANES * tile
            out_lanes = slice(at - base + LANES * tile, at - base + LANES * (tile + 1))
            own_ref[: sz.hold, out_lanes] = take_tile(self_ref, sz.hold, place, i == 1).astype(BF)
            average = [take_tile(mean_ref, sz.main, place, i == 1), take_tail(tail_ref, place, i == 1), spare]
            own_ref[sz.hold :, out_lanes] = jnp.concatenate(average, 0).astype(BF)


def mean_scratch(sz, tiles, slots):
    rows = -(-tiles // 8) * 8
    return [
        ((slots, LANES * tiles), jnp.int32),
        ((slots, LANES * tiles), jnp.int32),
        ((sz.hold, LANES * sz.tiles_all), BF),
        ((sz.tiles_all, LANES), F32),
        ((sz.main, LANES * sz.tiles_all), BF),
        ((max(rows + 8, sz.tiles_all), LANES), F32),
        ((2 * sz.main, LANES), F32),
        ((4 * rows + 16, LANES), F32),
        ((slots, rows, LANES), jnp.int32),
        ((rows, LANES), F32),
    ]


def unpack_tails(sz, message, lanes, turn_ref):
    for block in range(-(-lanes // LANES // sz.main)):
        at = lanes + LANES * block
        turn_ref[sz.main * block : sz.main * (block + 1), :] = message[:, at : at + LANES].astype(F32)
    return turn_ref[...]


def unpack_tiles(sz, message, tail, first, tiles, row, at, out_ref):
    for tile in range(tiles):
        lane = at + LANES * tile
        out_ref[row : row + sz.hold, lane : lane + LANES] = unpack_tile(sz, message, tail, first + tile)


def first_kernel(
    sz, features, neighbors, present, w1_in, w2_in, w3_in, wh_in, own_b, packed, mean_out, tail_out, m1, m2, m3,
    feat_ref, nbr_ref, pres_ref, w1, w2, w3, wh, own_ref,
    links_ref, present_ref, self_ref, self_tail, mean_ref, tail_ref, turn_ref, base_ref, code_ref, count_ref, pack, sems,
):
    part = lax.axis_index("col")
    rows = pl.ds(0, nbr_ref.shape[1])
    weights = start_copies(((w1_in, w1), (w2_in, w2), (w3_in, w3), (wh_in, wh)), sems)
    copies = start_copies(
        (
            (features.at[:, pl.ds(0, feat_ref.shape[1])], feat_ref),
            (neighbors.at[:, rows], nbr_ref),
            (present.at[:, rows], pres_ref),
        ),
        sems,
        4,
    )
    wait_all(weights)
    pack[sz.at_three :, :] = jnp.zeros((pack.shape[0] - sz.at_three, LANES), F32)
    for half in range(sz.hid // LANES):
        lanes = slice(LANES * half, LANES * (half + 1))
        for s in range(2):
            for f in range(sz.feat):
                at = sz.feat * (2 * half + s) + f
                pack[at : at + 1, :] = w1[f, s : s + 1, lanes]
            at = sz.rows_one + sz.group * (2 * half + s)
            pack[at : at + sz.group, :] = w2[s, :, lanes]
    for c in range(sz.classes):
        for s in range(2):
            at = sz.at_three + c
            pack[at : at + 1, sz.group * s : sz.group * (s + 1)] = w3[c, s : s + 1, :]
    row = jnp.concatenate([wh[0:1, :], wh[1:2, :]], 1)
    for i, piece in enumerate(three_parts(row)):
        pack[sz.misc + i : sz.misc + i + 1, :] = piece
    store = start_copies(((pack, packed),), sems, 7)
    for block in range(sz.blocks):
        at = sz.message_b + LANES * block
        piece = pack[sz.main * block : sz.main * (block + 1), :].astype(BF)
        m1[:, at : at + LANES] = piece
        m2[:, at : at + LANES] = piece
    wait_all(copies)
    fill_own(sz, feat_ref, self_ref, self_tail, 48 * sz.own // LANES + EARLY)
    mean_ref[:, :FRONT] = jnp.zeros((sz.main, FRONT), BF)
    tail_ref[...] = jnp.zeros_like(tail_ref)
    mean_tiles(sz, 0, sz.tiles_b_all, feat_ref, nbr_ref, pres_ref, links_ref, present_ref, mean_ref, tail_ref, base_ref, code_ref, count_ref)
    done = pl.ds(0, LANES * (sz.tiles_b_all + 2))
    store += start_copies(((mean_ref.at[:, done], mean_out), (tail_ref, tail_out)), sems, 9)
    own_pair(sz, sz.ranges(part)[1:], self_ref, mean_ref, tail_ref, own_ref)
    store += start_copies(((own_ref, own_b),), sems, 8)
    for r, out in ((1, m1), (2, m2), (3, m3)):
        pack_pair(sz, sz.first_ranges(part ^ r), self_ref, self_tail, mean_ref, tail_ref, turn_ref, out)
    wait_all(store)


def first_messages(sz, features, neighbors, present, w1, w2, w3, hidden):
    rows = LANES * sz.tiles_b_all
    bases = min(4 * rows + LANES, sz.base)
    slots = neighbors.shape[0]
    return call(
        functools.partial(first_kernel, sz),
        [
            ((2 * sz.hold, sz.n_mid), BF),
            ((sz.main * sz.blocks, LANES), F32),
            ((sz.main, rows + 2 * LANES), BF),
            ((max(-(-sz.tiles_b_all // 8) * 8 + 8, sz.tiles_all), LANES), F32),
            ((sz.main, sz.full_b), BF),
            ((sz.main, sz.full_b), BF),
            ((sz.main, sz.message_b), BF),
        ],
        [
            ((sz.feat, bases), BF),
            ((slots, rows), jnp.int32),
            ((slots, rows), jnp.int32),
            (w1.shape, F32),
            (w2.shape, F32),
            (w3.shape, F32),
            (hidden.shape, F32),
            ((2 * sz.hold, sz.n_mid), BF),
            *mean_scratch(sz, sz.tiles_b_all, slots),
            ((sz.main * sz.blocks, LANES), F32),
        ],
        FIRST_MIB,
        features,
        neighbors,
        present,
        w1,
        w2,
        w3,
        hidden,
        far_in=range(7),
        far_out=(0, 1, 2, 3),
        copies=11,
        micros=4,
    )


def mean_kernel(
    sz, feat_ref, nbr_ref, pres_ref, mean_in, tail_in, nbr2, pres2, nbr3, pres3, own_a, counts_out, a1, a2, a3,
    links_ref, present_ref, self_ref, self_tail, mean_ref, tail_ref, turn_ref, base_ref, code_ref, count_ref, own_ref, kept_ref, counts, sems,
):
    part = lax.axis_index("col")
    tiles = sz.low // LANES + 1
    begin = sz.tiles_b_all
    loads = start_copies(((mean_in, mean_ref.at[:, pl.ds(0, LANES * (begin + 2))]), (tail_in, kept_ref)), sems, 1)
    fill_counts(sz, part, nbr2, pres2, nbr3, pres3, counts)
    store = start_copies(((counts, counts_out),), sems, 3)
    fill_own(sz, feat_ref, self_ref, self_tail, (48 * sz.own + sz.n_a) // LANES)
    last = LANES * (tiles + 2)
    mean_ref[:, last:] = jnp.zeros((sz.main, LANES * sz.tiles_all - last), BF)
    tail_ref[...] = jnp.zeros_like(tail_ref)
    mean_tiles(sz, begin, tiles, feat_ref, nbr_ref, pres_ref, links_ref, present_ref, mean_ref, tail_ref, base_ref, code_ref, count_ref)
    wait_all(loads)
    tail_ref[: begin + 2, :] = kept_ref[: begin + 2, :]
    own_pair(sz, sz.ranges(part)[:1], self_ref, mean_ref, tail_ref, own_ref)
    store += start_copies(((own_ref, own_a),), sems)
    for r, out in ((1, a1), (2, a2), (3, a3)):
        pack_pair(sz, sz.second_ranges(part ^ r), self_ref, self_tail, mean_ref, tail_ref, turn_ref, out)
    wait_all(store)


def mean_messages(sz, features, neighbors, present, mean, tail, links):
    counts = (sz.count_rows * (sz.tiles_b + 2 * (sz.own // LANES)), LANES)
    return call(
        functools.partial(mean_kernel, sz),
        [((2 * sz.hold, sz.n_a), BF), (counts, BF)] + [((sz.main, sz.message_a), BF)] * 3,
        mean_scratch(sz, sz.low // LANES + 1, neighbors.shape[0]) + [((2 * sz.hold, sz.n_a), BF), (tail.shape, F32), (counts, BF)],
        MEAN_MIB,
        features,
        neighbors,
        present,
        mean,
        tail,
        *links,
        far_in=(3, 4),
        far_out=(0, 1),
        copies=4,
        micros=6,
    )


def window_counts(local, rows):
    spots = lax.broadcasted_iota(jnp.int32, (256, LANES), 0).astype(F32).astype(BF)
    blocks = []
    for first in range(0, rows, 256):
        size = min(256, rows - first)
        place = local - first
        place = jnp.where((place >= 0) & (place < size), place, -1).astype(F32)
        counts = jnp.zeros((size, LANES), BF)
        for slot in range(local.shape[0]):
            row = jnp.broadcast_to(place[slot : slot + 1], (16, LANES)).astype(BF)
            row = jnp.concatenate([row] * (size // 16), 0)
            counts = counts + jnp.where(row == spots[:size], jnp.bfloat16(1.0), jnp.bfloat16(0.0))
        blocks.append(counts)
    return jnp.concatenate(blocks, 0)


def slot_totals(present):
    return jnp.maximum(jnp.sum(present.astype(F32), 0, keepdims=True), 1.0)


def counts_tile(sz, links, marks, start, at, counts):
    local = jnp.where(marks > 0, links - start, -1)
    counts[at : at + WINDOW, :] = window_counts(local, WINDOW)
    counts[at + WINDOW : at + sz.count_rows, :] = jnp.broadcast_to(slot_totals(marks), (16, LANES)).astype(BF)


def fill_counts(sz, part, nbr2, pres2, nbr3, pres3, counts):
    tiles = nbr2.shape[1] // LANES
    for tile in range(sz.tiles_b):
        column = 4 * sz.own // LANES * part + tile
        start = sz.a_row(part) + 4 * LANES * tile
        links, marks = half_columns(nbr2, column, tiles, 0), half_columns(pres2, column, tiles, 0)
        counts_tile(sz, links, marks, start, sz.count_rows * tile, counts)
    for tile in range(sz.own // LANES):
        columns = pl.ds(aligned(sz.own * part + LANES * tile), LANES)
        at = sz.count_rows * (sz.tiles_b + tile)
        counts_tile(sz, nbr3[:, columns], pres3[:, columns], sz.b_row(part), at, counts)
        at += sz.count_rows * (sz.own // LANES)
        counts_tile(sz, nbr2[:, columns], pres2[:, columns], sz.b_row(part), at, counts)


def tile_counts(sz, counts, tile):
    at = sz.count_rows * tile
    totals = counts[at + WINDOW : at + WINDOW + 16, :].astype(F32)[0:1]
    return counts[at : at + WINDOW, :], totals


def activate(result):
    active = result * sigmoid(result)
    scale = lax.rsqrt(jnp.sum(active * active, 0, keepdims=True) + ROW_EPS)
    return result, scale, active * scale


def first_layer(weight, inputs, bias):
    result = dot(weight, inputs, (1, 0)) + bias
    active = result * sigmoid(result)
    scale = lax.rsqrt(jnp.sum(active * active, 0, keepdims=True) + ROW_EPS)
    return result, scale, active * scale


def join_inputs(sz, own, average):
    pieces = []
    for c in range(4):
        pieces.append(own[sz.group * c : sz.group * (c + 1)])
        pieces.append(average[sz.group * c : sz.group * (c + 1)])
    return jnp.concatenate(pieces, 0)


def norm_backward(grad, result, scale):
    gate = sigmoid(result)
    active = result * gate
    inner = jnp.sum(grad * active, 0, keepdims=True)
    grad_active = scale * grad - active * (scale * scale * scale * inner)
    return (grad_active * gate * (1.0 + result * (1.0 - gate))).astype(BF)


def split_inputs(sz, grad):
    pieces = [grad[sz.group * c : sz.group * (c + 1)] for c in range(8)]
    return jnp.concatenate(pieces[0::2], 0), jnp.concatenate(pieces[1::2], 0)


def row_sums(grad):
    return dot(jnp.ones((16, grad.shape[1]), BF), grad, (1, 1))


def spread(sz, scaled, counts):
    return dot(scaled.astype(BF), counts, (1, 1))


def halves(ref, at, lanes):
    return jnp.concatenate([ref[:, at : at + lanes], ref[:, at + lanes : at + 2 * lanes]], 0)


def store_halves(ref, at, lanes, value):
    rows = value.shape[0] // 2
    ref[:rows, at : at + lanes] = value[:rows]
    ref[:rows, at + lanes : at + 2 * lanes] = value[rows:]


def slot_column(table):
    rows, slots = table.shape
    wide = jnp.broadcast_to(table.astype(F32)[:, None, :], (rows, slots, slots))
    hit = lax.broadcasted_iota(jnp.int32, wide.shape, 1) == lax.broadcasted_iota(jnp.int32, wide.shape, 2)
    return jnp.sum(jnp.where(hit, wide, 0.0), 2, keepdims=True).reshape(rows * slots, 1)


def alive_column(sz, live):
    shape = (sz.dp, sz.dp)
    hit = lax.broadcasted_iota(jnp.int32, shape, 0) == lax.broadcasted_iota(jnp.int32, shape, 1)
    counts = jnp.sum(jnp.where(hit, jnp.broadcast_to(live.astype(F32), shape), 0.0), 1, keepdims=True)
    slot = lax.broadcasted_iota(jnp.int32, (sz.dp, sz.slot), 1).astype(F32)
    return slot_column(jnp.where(slot < counts, 1.0, 0.0))


def seed_picks(sz, serve_rows, take_rows, part):
    spots = (lax.broadcasted_iota(jnp.int32, (sz.slots, sz.own), 1) + sz.own * part).astype(F32)
    serve = jnp.where(slot_column(serve_rows) == spots, 1.0, 0.0)
    take = jnp.where(slot_column(take_rows) == spots, 1.0, 0.0)
    return serve, take, jnp.sum(serve, 1, keepdims=True), jnp.sum(take, 1, keepdims=True)


def seeds_kernel(
    sz, own_b, packed, s1, s2, s3, passed, counts_in, serve_in, take_in, live_in,
    low_out, high_out, sent,
    xb, pack, m1, m2, m3, p3, window_ref, serve_rows, take_rows, live_rows, low, high, turn_ref, w1_ref, w2_ref, states, sems,
):
    part = lax.axis_index("col")
    own, hid, n_b, group, hold, at = sz.own, sz.hid, sz.n_b, sz.group, sz.hold, sz.at
    n_mid = sz.n_mid
    copies = start_copies(
        (
            (packed, pack),
            (passed.at[:, pl.ds(sz.message_b, LANES * sz.blocks)], p3),
            (s1, m1),
            (s2, m2),
            (s3, m3),
            (own_b, xb),
            (counts_in.at[sz.seed_window(), :], window_ref),
            (serve_in, serve_rows),
            (take_in, take_rows),
            (live_in, live_rows),
        ),
        sems,
    )
    w1_ref[...] = jnp.zeros_like(w1_ref)
    wait_all(copies[:4])
    for r, (message, first_lane) in enumerate(((None, 0), (m1, sz.message_b), (m2, sz.message_b), (p3, 0))):
        for block in range(sz.blocks if r else 0):
            first = first_lane + LANES * block
            pack[sz.main * block : sz.main * (block + 1), :] = message[:, first : first + LANES].astype(F32)
        shard = part ^ r
        for half in range(hid // LANES):
            lanes = slice(LANES * half, LANES * (half + 1))
            for s in range(2):
                first = sz.feat * (2 * half + s)
                row = 4 * hold * s + hold * r
                w1_ref[row : row + sz.feat, lanes] = pack[first : first + sz.feat, :]
            first = sz.rows_one + 2 * group * half
            row = pl.multiple_of(2 * group * shard, 2 * group)
            w2_ref[pl.ds(row, 2 * group), lanes] = pack[first : first + 2 * group, :]
        third = jnp.concatenate([pack[sz.at_three : sz.misc, :], jnp.zeros((sz.head - sz.classes, LANES), F32)], 0)
        low[: sz.head, pl.ds(aligned(at["turned3"] + 2 * group * shard), LANES)] = third.astype(BF)
        misc = pack[sz.misc : sz.misc + 3, :]
        column = jnp.broadcast_to(misc[0:1] + misc[1:2] + misc[2:3], (LANES, LANES)).T
        row = pl.multiple_of(group * shard, group)
        for layer in range(2):
            lanes = slice(at["bias"] + LANES * layer, at["bias"] + LANES * (layer + 1))
            high[pl.ds(row, group), lanes] = column[group * layer : group * (layer + 1)]
    turned1 = w1_ref[...].T.astype(BF)
    turned2 = w2_ref[...].T.astype(BF)
    low[:, at["turned1"] : at["turned1"] + hid] = turned1
    low[:, at["turned2"] : at["turned2"] + 2 * hid] = turned2
    store_halves(low, at["weight2"], hid, w2_ref[...].astype(BF))
    weight3 = low[: sz.head, at["turned3"] : at["turned3"] + 2 * hid].astype(F32).T
    weight3 = jnp.concatenate([weight3, jnp.zeros((2 * hid, LANES - sz.head), F32)], 1)
    store_halves(low, at["weight3"], LANES, weight3.astype(BF))

    def piece(lanes, count):
        return (low.at[:, pl.ds(lanes, count)], low_out.at[:, pl.ds(lanes, count)])

    stores = start_copies((piece(n_mid, at["states"] - n_mid),), sems, 11)
    wait_all(copies[4:])
    low[:hold, :n_mid] = xb[:hold, :]
    low[4 * hold : 5 * hold, :n_mid] = xb[hold:, :]
    for r, message in ((1, m1), (2, m2), (3, m3)):
        tail = unpack_tails(sz, message, 2 * n_mid + sz.early, turn_ref)
        unpack_tiles(sz, message, tail, 0, sz.tiles_mid, hold * r, 0, low)
        first = (n_mid + sz.early) // LANES
        unpack_tiles(sz, message, tail, first, sz.tiles_mid, hold * (4 + r), 0, low)
    stores += start_copies((piece(0, n_mid),), sems, 12)
    bias1 = high[:hid, at["bias"] : at["bias"] + LANES]
    bias2 = high[:hid, at["bias"] + LANES : at["bias"] + 2 * LANES]
    high[:hid, :n_mid] = dot(turned1, low[:, :n_mid], (1, 0))
    for tile in range(sz.tiles_mid):
        lanes = slice(LANES * tile, LANES * (tile + 1))
        result, scale, state = activate(high[:hid, lanes] + bias1)
        high[:hid, lanes] = result
        high[hid:, lanes] = jnp.broadcast_to(scale, (8, LANES))
        upper, lower = two_parts(state)
        states[:hid, lanes] = upper
        states[hid:, lanes] = lower
    low[:, at["states"] : at["states"] + n_b] = states[:hid, :n_b]
    rows = pl.ds(0, hid + 8)
    others = pl.ds(at["bias"], 2 * LANES)
    stores += start_copies(
        (
            piece(at["states"], n_b),
            (high.at[rows, pl.ds(0, n_mid)], high_out.at[rows, pl.ds(0, n_mid)]),
            (high.at[rows, others], high_out.at[rows, others]),
        ),
        sems,
        13,
    )
    for tile in range(own // LANES):
        window, totals = tile_counts(sz, window_ref, tile)
        total = dot(states[:, :n_b], window, (1, 0))
        average = ((total[:hid] + total[hid:]) / totals).astype(BF)
        x = join_inputs(sz, states[:hid, n_b + LANES * tile : n_b + LANES * (tile + 1)], average)
        first = at["inputs2"] + LANES * tile
        low[:, first : first + LANES] = x[:hid]
        low[:, first + own : first + own + LANES] = x[hid:]
        result, scale, state = first_layer(turned2, x, bias2)
        first = at["result2"] + LANES * tile
        high[:hid, first : first + LANES] = result
        high[hid:, first : first + LANES] = jnp.broadcast_to(scale, (8, LANES))
        upper, lower = two_parts(state)
        first = at["embed"] + LANES * tile
        low[:, first : first + LANES] = upper
        low[:, first + own : first + own + LANES] = lower
    last = pl.ds(at["result2"], own)
    tail = (piece(at["embed"], sz.low_lanes - at["embed"]), (high.at[rows, last], high_out.at[rows, last]))
    stores += start_copies(tail, sems, 16)
    serve, take, _, owned = seed_picks(sz, serve_rows[...], take_rows[...], part)
    embed_high = low[:, at["embed"] : at["embed"] + own]
    served = dot(serve.astype(BF), embed_high, (1, 1))
    taken = dot(take.astype(BF), embed_high, (1, 1))
    dead = (owned > 0.5) & (alive_column(sz, live_rows[...]) < 0.5)
    first = lax.broadcasted_iota(jnp.int32, (sz.slots, hid), 1) == 0
    value = jnp.concatenate([served, jnp.where(first & dead, SENTINEL, taken)], 1)
    value = value.reshape(sz.dp, 1, sz.slot, 2 * hid)
    value = jnp.broadcast_to(value, (sz.dp, 4, sz.slot, 2 * hid))
    sent[...] = value.reshape(4 * sz.slots, 2 * hid).astype(BF)
    wait_all(stores)


def sent_rows(sz, low, at, serve, take):
    embed_high = low[:, at : at + sz.own]
    embed_low = low[:, at + sz.own : at + 2 * sz.own]
    take = take.astype(BF)
    return jnp.concatenate(
        [dot(serve.astype(BF), embed_high, (1, 1)), dot(take, embed_high, (1, 1)), dot(take, embed_low, (1, 1))], 1
    )


def seeds_forward(sz, messages, counts, tables):
    hid = sz.hid
    tail = (sz.main, LANES * sz.blocks)
    return call(
        functools.partial(seeds_kernel, sz),
        [
            ((hid, sz.low_lanes), BF),
            ((hid + 8, sz.high_lanes), F32),
            ((4 * sz.slots, 2 * hid), BF),
        ],
        [
            ((2 * sz.hold, sz.n_mid), BF),
            ((sz.main * sz.blocks, LANES), F32),
            ((sz.main, sz.full_b), BF),
            ((sz.main, sz.full_b), BF),
            ((sz.main, sz.message_b), BF),
            (tail, BF),
            ((sz.count_rows * (sz.own // LANES), LANES), BF),
            *[(item.shape, jnp.int32) for item in tables],
            ((hid, sz.low_lanes), BF),
            ((hid + 8, sz.high_lanes), F32),
            ((2 * sz.main, LANES), F32),
            ((8 * sz.hold, hid), F32),
            ((2 * hid, hid), F32),
            ((2 * hid, sz.n_mid), BF),
        ],
        SEEDS_MIB,
        *messages,
        counts,
        *tables,
        far_in=(0, 1, 6, 7, 8, 9),
        loose=(2, 3, 4, 5),
        micros=4,
        far_out=(0, 1),
        copies=19,
    )


def rest_kernel(
    sz, low_in, high_in, counts_in, own_a, a1, a2, a3, e1, e2, e3, labels_in, weighting_in, head_in, part_out,
    labels, weighting, head_bias, low, xa, bias, counts, xo, c1, c2, c3, turn_ref,
    states, states2, result1, slope1, scale1, inputs2, result2, scale2, grad_a, low_grad, part_ref, sems,
):
    part = lax.axis_index("col")
    own, hid, n_a, n_b, hold = sz.own, sz.hid, sz.n_a, sz.n_b, sz.hold
    at = dict(sz.at)
    for name in ("turned1", "turned2", "weight2", "weight3", "turned3", "states", "embed"):
        at[name] -= sz.n_mid
    lanes = at["embed"] + own
    copies = start_copies(
        (
            (own_a, xo),
            *[(e.at[:, pl.ds(sz.n_mid, sz.early)], c.at[:, pl.ds(0, sz.early)]) for e, c in ((e1, c1), (e2, c2), (e3, c3))],
            *[
                (e.at[:, pl.ds(2 * sz.n_mid + sz.early, LANES)], c.at[:, pl.ds(sz.early, LANES)])
                for e, c in ((e1, c1), (e2, c2), (e3, c3))
            ],
            (low_in.at[:, pl.ds(sz.n_mid, hid)], low.at[:, pl.ds(0, hid)]),
            (high_in.at[:, pl.ds(sz.at["bias"], 2 * LANES)], bias),
            (low_in.at[:, pl.ds(sz.n_mid + hid, lanes - hid)], low.at[:, pl.ds(hid, lanes - hid)]),
            (counts_in, counts),
            (labels_in, labels),
            (weighting_in, weighting),
            (head_in, head_bias),
        ),
        sems,
    )
    late = (n_a - sz.early) // LANES
    for r, message in ((1, a1), (2, a2), (3, a3)):
        tail = unpack_tails(sz, message, 2 * n_a - sz.early, turn_ref)
        unpack_tiles(sz, message, tail, 0, late, hold * r, sz.early, xa)
        unpack_tiles(sz, message, tail, late, n_a // LANES, hold * (4 + r), 0, xa)
    wait_all(copies[:7])
    for r, before in ((1, c1), (2, c2), (3, c3)):
        tail = before[:, sz.early :].astype(F32)[sz.tiles_mid : sz.tiles_mid + EARLY]
        unpack_tiles(sz, before, tail, 0, EARLY, hold * r, 0, xa)
    xa[:hold, :] = xo[:hold, :]
    xa[4 * hold : 5 * hold, :] = xo[hold:, :]
    wait_all(copies[7:9])
    turned1 = low[:, at["turned1"] : at["turned1"] + hid]
    bias1 = bias[:hid, :LANES]
    bias2 = bias[:hid, LANES:]

    result1[...] = dot(turned1, xa[...], (1, 0))

    def forward_step(index, carry):
        lanes = pl.ds(aligned(index * LANES), LANES)
        result = result1[:, lanes] + bias1
        gate = sigmoid(result)
        active = result * gate
        scale = lax.rsqrt(jnp.sum(active * active, 0, keepdims=True) + ROW_EPS)
        result1[:, lanes] = active
        slope1[:, lanes] = gate + active * (1.0 - gate)
        scale1[:, lanes] = scale
        upper, lower = two_parts(active * scale)
        states[:hid, lanes] = upper
        states[hid:, lanes] = lower
        return carry

    lax.fori_loop(0, n_a // LANES, forward_step, 0, unroll=7)
    wait_all(copies[9:])
    turned2 = low[:, at["turned2"] : at["turned2"] + 2 * hid]
    for tile in range(sz.tiles_b):
        lanes = slice(LANES * tile, LANES * (tile + 1))
        window, totals = tile_counts(sz, counts, tile)
        total = dot(states[:, 4 * LANES * tile : 4 * LANES * tile + WINDOW], window, (1, 0))
        average = ((total[:hid] + total[hid:]) / totals).astype(BF)
        inputs2[:, lanes] = join_inputs(sz, low[:, at["states"] + LANES * tile : at["states"] + LANES * (tile + 1)], average)
    result2[...] = dot(turned2, inputs2[...], (1, 0))
    for tile in range(sz.tiles_b):
        lanes = slice(LANES * tile, LANES * (tile + 1))
        result, scale, state = activate(result2[:, lanes] + bias2)
        result2[:, lanes] = result
        scale2[:, lanes] = scale
        upper, lower = two_parts(state)
        states2[:hid, lanes] = upper
        states2[hid:, lanes] = lower
    counts3, totals3 = tile_counts(sz, counts, sz.tiles_b)
    total = dot(states2[...], counts3, (1, 0))
    average = ((total[:hid] + total[hid:]) / totals3).astype(BF)
    inputs3 = join_inputs(sz, low[:, at["embed"] : at["embed"] + own], average)

    columns = pl.ds(aligned(own * part), own)
    classes = lax.broadcasted_iota(jnp.int32, (sz.head, own), 0)
    head_row = jnp.concatenate([head_bias[...], jnp.zeros((1, LANES - sz.classes), F32)], 1)
    head_column = jnp.broadcast_to(head_row, (LANES, LANES)).T[: sz.head]
    logits = dot(low[: sz.head, at["turned3"] : at["turned3"] + 2 * hid], inputs3, (1, 0)) + head_column
    logits = jnp.where(classes < sz.classes, logits, -1e30)
    highest = jnp.max(logits, 0, keepdims=True)
    expo = jnp.exp(logits - highest)
    totals = jnp.sum(expo, 0, keepdims=True)
    hit = classes == labels[:, columns]
    weights = weighting[:, columns].astype(F32)
    target = jnp.sum(jnp.where(hit, logits, 0.0), 0, keepdims=True)
    ce_total = jnp.sum(weights * (highest + jnp.log(totals) - target), 1, keepdims=True)
    seed_count = jnp.sum(weights, 1, keepdims=True)
    grad_logits = (weights * (expo / totals - jnp.where(hit, 1.0, 0.0))).astype(BF)
    g3 = at["g3"]
    part_ref[: sz.head, g3 : g3 + 2 * hid] = dot(grad_logits, inputs3, (1, 1))
    head_sums = jnp.concatenate([row_sums(grad_logits), jnp.zeros((16, LANES - sz.head), F32)], 1)
    part_ref[sz.head + 16 : sz.head + 32, g3 : g3 + LANES] = head_sums
    lane_at = lax.broadcasted_iota(jnp.int32, (16, LANES), 1)
    sums = jnp.where(lane_at == 0, ce_total, jnp.where(lane_at == 1, seed_count, 0.0))
    part_ref[sz.head + 16 : sz.head + 32, g3 + LANES : g3 + 2 * LANES] = sums
    own_part, average_part = split_inputs(sz, dot(halves(low, at["weight3"], LANES)[:, : sz.head], grad_logits, (1, 0)))
    part_ref[:hid, at["grad_embed"] : at["grad_embed"] + own] = own_part
    grad_mid = spread(sz, average_part / totals3, counts3)
    low_grad2 = norm_backward(grad_mid, result2[...], scale2[...])
    g2 = dot(inputs2[...], low_grad2, (1, 1))
    part_ref[:hid, at["g2"] : at["g2"] + hid] = g2[:hid]
    part_ref[:hid, at["g2"] + hid : at["g2"] + 2 * hid] = g2[hid:]
    part_ref[sz.head : sz.head + 16, g3 + hid : g3 + 2 * hid] = row_sums(low_grad2)
    weight2 = halves(low, at["weight2"], hid)
    own_part, average_part = split_inputs(sz, dot(weight2, low_grad2, (1, 0)))
    part_ref[:hid, at["grad_b"] : at["grad_b"] + n_b] = own_part
    for tile in range(sz.tiles_b):
        window, totals = tile_counts(sz, counts, tile)
        added = spread(sz, average_part[:, LANES * tile : LANES * (tile + 1)] / totals, window)
        first = 4 * LANES * tile
        shared = slice(first, first + LANES)
        grad_a[:, shared] = added[:, :LANES] + grad_a[:, shared] if tile else added[:, :LANES]
        grad_a[:, first + LANES : first + WINDOW] = added[:, LANES:]
    rows, few = pl.ds(0, hid + 8), pl.ds(0, sz.head + 32)
    split = at["g2"]
    stores = start_copies(
        (
            (part_ref.at[rows, pl.ds(split, hid * 2)], part_out.at[rows, pl.ds(split, hid * 2)]),
            (
                part_ref.at[rows, pl.ds(at["grad_b"], n_b + own)],
                part_out.at[rows, pl.ds(at["grad_b"], n_b + own)],
            ),
        ),
        sems,
        14,
    )

    def backward_step(index, carry):
        lanes = pl.ds(aligned(index * LANES), LANES)
        scale = scale1[:, lanes]
        inner = jnp.zeros((8, LANES), F32)
        for row in range(0, hid, 8):
            rows = slice(row, row + 8)
            inner = inner + grad_a[rows, lanes] * result1[rows, lanes]
        inner = scale * scale * scale * jnp.sum(inner, 0, keepdims=True)
        for row in range(0, hid, 16):
            rows = slice(row, row + 16)
            grad = scale * grad_a[rows, lanes] - inner * result1[rows, lanes]
            low_grad[rows, lanes] = (grad * slope1[rows, lanes]).astype(BF)
        return carry

    lax.fori_loop(0, n_a // LANES, backward_step, 0, unroll=7)
    part_ref[:hid, at["g1"] : at["g1"] + hid] = dot(xa[...], low_grad[...], (1, 1))
    part_ref[sz.head : sz.head + 16, g3 : g3 + hid] = row_sums(low_grad[...])
    stores += start_copies(
        (
            (part_ref.at[rows, pl.ds(0, hid)], part_out.at[rows, pl.ds(0, hid)]),
            (part_ref.at[few, pl.ds(g3, 2 * hid)], part_out.at[few, pl.ds(g3, 2 * hid)]),
        ),
        sems,
        16,
    )
    wait_all(stores)


def rest_step(sz, low, high, counts, means, labels, weighting, head_bias):
    hid = sz.hid
    return call(
        functools.partial(rest_kernel, sz),
        [((hid + 8, sz.part_lanes), F32)],
        [
            (labels.shape, jnp.int32),
            (weighting.shape, jnp.int32),
            (head_bias.shape, F32),
            ((hid, sz.at["embed"] + sz.own - sz.n_mid), BF),
            ((hid, sz.n_a), BF),
            ((hid + 8, 2 * LANES), F32),
            (counts.shape, BF),
            ((2 * sz.hold, sz.n_a), BF),
            *[((sz.main, sz.early + LANES), BF)] * 3,
            ((2 * sz.main, LANES), F32),
            ((2 * hid, sz.n_a), BF),
            ((2 * hid, sz.n_b), BF),
            ((hid, sz.n_a), F32),
            ((hid, sz.n_a), F32),
            ((1, sz.n_a), F32),
            ((2 * hid, sz.n_b), BF),
            ((hid, sz.n_b), F32),
            ((1, sz.n_b), F32),
            ((hid, sz.n_a), F32),
            ((hid, sz.n_a), BF),
            ((hid + 8, sz.part_lanes), F32),
        ],
        REST_MIB,
        low,
        high,
        counts,
        *means,
        labels,
        weighting,
        head_bias,
        far_in=(0, 1, 2, 3, 10, 11, 12),
        loose=(7, 8, 9),
        micros=14,
        far_out=(0,),
        copies=18,
    )[0]


def seeds_back_kernel(
    sz, serve_in, take_in, live_in, received, low_in, high_in, counts_in, part_in, keep0, keep1, send,
    serve_rows, take_rows, live_rows, x_ref, weight_ref, low, high, window_ref, partial, g1_ref, g2_ref, gb_ref, stage, sems,
):
    part = lax.axis_index("col")
    own, hid, group, n_b, n_mid = sz.own, sz.hid, sz.group, sz.n_b, sz.n_mid
    at = dict(sz.at)
    at["inputs2"] -= at["embed"]
    split = at["grad_b"]
    few = pl.ds(0, sz.head + 32)
    lanes = pl.ds(at["result2"], own)
    copies = start_copies(
        (
            (serve_in, serve_rows),
            (take_in, take_rows),
            (live_in, live_rows),
            (low_in.at[:, pl.ds(at["embed"], 4 * own)], low),
            (part_in.at[:, pl.ds(split + n_b, own)], partial.at[:, pl.ds(split + n_b, own)]),
            (high_in.at[:, lanes], high.at[:, lanes]),
            (low_in.at[:, pl.ds(at["weight2"], 2 * hid)], weight_ref),
            (counts_in.at[sz.seed_window(), :], window_ref),
            (part_in.at[:, pl.ds(split, n_b)], partial.at[:, pl.ds(split, n_b)]),
            (high_in.at[:, pl.ds(0, n_mid)], high.at[:, pl.ds(0, n_mid)]),
            (low_in.at[:, pl.ds(0, n_mid)], x_ref),
            (part_in.at[:, pl.ds(0, at["g3"])], partial.at[:, pl.ds(0, at["g3"])]),
            (part_in.at[few, pl.ds(at["g3"], 2 * hid)], partial.at[few, pl.ds(at["g3"], 2 * hid)]),
        ),
        sems,
    )
    arrived = received[...].astype(F32).reshape(sz.dp, 4, sz.slot, 2 * hid)
    arrived = jnp.sum(arrived, 1).reshape(sz.slots, 2 * hid)
    at["embed"] = 0
    wait_all(copies[:4])
    serve, take, served, taken = seed_picks(sz, serve_rows[...], take_rows[...], part)
    mine = sent_rows(sz, low, 0, serve, take)
    theirs = arrived[:, hid:]
    alive_there = theirs[:, 0:1] < 0.5 * SENTINEL
    differ = mine[:, hid : 2 * hid] + mine[:, 2 * hid :] - arrived[:, :hid]
    differ = jnp.where((taken > 0.5) & (alive_column(sz, live_rows[...]) > 0.5), differ, 0.0)
    dist_total = DIST_WEIGHT * jnp.sum(jnp.sum(differ * differ, 0, keepdims=True), 1, keepdims=True)
    local_high, local_low = two_parts(2.0 * DIST_WEIGHT * differ)
    back = jnp.where((served > 0.5) & alive_there, theirs - mine[:, :hid], 0.0)
    back = (-2.0 * DIST_WEIGHT * back).astype(BF)
    take = take.astype(BF)
    serve = serve.astype(BF)
    wait_all(copies[4:6])
    grad = partial[:hid, at["grad_embed"] : at["grad_embed"] + own]
    grad = grad + dot(local_high, take, (0, 0)) + dot(local_low, take, (0, 0)) + dot(back, serve, (0, 0))
    lanes = slice(at["result2"], at["result2"] + own)
    low_grad2 = norm_backward(grad, high[:hid, lanes], high[hid:, lanes][0:1])
    wait_all(copies[6:9])
    weight2 = halves(weight_ref, 0, hid)
    own_part, average_part = split_inputs(sz, dot(weight2, low_grad2, (1, 0)))
    total_b = partial[:hid, at["grad_b"] : at["grad_b"] + n_b]
    for tile in range(own // LANES):
        window, totals = tile_counts(sz, window_ref, tile)
        total_b = total_b + spread(sz, average_part[:, LANES * tile : LANES * (tile + 1)] / totals, window)
    wait_all(copies[9:10])
    low_grad = jnp.concatenate(
        [
            norm_backward(total_b, high[:hid, :n_b], high[hid:, :n_b][0:1]),
            norm_backward(own_part, high[:hid, n_b:n_mid], high[hid:, n_b:n_mid][0:1]),
        ],
        1,
    )
    wait_all(copies[10:])
    added = dot(halves(low, at["inputs2"], own), low_grad2, (1, 1))
    for half in range(2):
        lanes = slice(at["g2"] + hid * half, at["g2"] + hid * (half + 1))
        g2_ref[hid * half : hid * (half + 1), :] = partial[:hid, lanes] + added[hid * half : hid * (half + 1)]
    g3 = at["g3"]
    sums = partial[sz.head : sz.head + 16, g3 : g3 + 2 * hid]
    gb_ref[:, hid:] = sums[:, hid:] + row_sums(low_grad2)
    half = 4 * sz.hold
    g1_ref[...] = partial[:hid, at["g1"] : at["g1"] + hid] + dot(x_ref[...], low_grad, (1, 1))
    gb_ref[:, :hid] = sums[:, :hid] + row_sums(low_grad)
    head_row = partial[sz.head + 16 : sz.head + 32, g3 : g3 + LANES]
    totals = partial[sz.head + 16 : sz.head + 32, g3 + LANES : g3 + 2 * LANES]
    lane_at = lax.broadcasted_iota(jnp.int32, (16, LANES), 1)
    fixed = ((totals[0:1, 0:1] + dist_total) * float(2**LOSS_BITS) + 0.5).astype(jnp.int32)
    count = totals[0:1, 1:2].astype(jnp.int32)
    whole = jnp.where(lane_at < 32, fixed, count)
    bits = (lax.shift_right_logical(whole, lane_at & 31) & 1).astype(F32)
    bits = jnp.where(lane_at < 64, bits, 0.0)
    stage[sz.misc :, :] = jnp.zeros((sz.pay - sz.misc, LANES), F32)
    for r, (target_ref, base) in enumerate(((keep0, 0), (send, 0), (keep1, 0), (send, sz.pay))):
        shard = part ^ r
        block2 = pl.ds(pl.multiple_of(2 * group * shard, 2 * group), 2 * group)
        for h in range(hid // LANES):
            lanes = slice(LANES * h, LANES * (h + 1))
            for s in range(2):
                first, row = half * s + sz.hold * r, sz.feat * (2 * h + s)
                stage[row : row + sz.feat, :] = g1_ref[first : first + sz.feat, lanes]
            row = sz.rows_one + 2 * group * h
            stage[row : row + 2 * group, :] = g2_ref[block2, lanes]
        third = partial[: sz.head, pl.ds(aligned(g3 + 2 * group * shard), LANES)]
        stage[sz.at_three : sz.misc, :] = third[: sz.classes]
        odd = (shard % 2) == 1
        block = aligned((shard // 2) * LANES)
        one = gb_ref[:, pl.ds(block, LANES)]
        two = gb_ref[:, pl.ds(aligned(hid + block), LANES)]
        one = jnp.where(odd, pltpu.roll(one, group, 1), one)
        two = jnp.where(odd, two, pltpu.roll(two, group, 1))
        bias_row = jnp.where(lane_at < group, one, two)[0:1]
        rows = [bias_row, head_row[0:1], bits[0:1]]
        rows += [item - item.astype(BF).astype(F32) for item in rows[:2]]
        for i, item in enumerate(rows):
            stage[sz.misc + i : sz.misc + i + 1, :] = item
        target_ref[base : base + sz.pay, :] = stage[...].astype(BF)


def seeds_backward(sz, tables, received, low, high, counts, partial):
    hid = sz.hid
    return call(
        functools.partial(seeds_back_kernel, sz),
        [((sz.pay, LANES), BF), ((sz.pay, LANES), BF), ((2 * sz.pay, LANES), BF)],
        [
            *[(item.shape, jnp.int32) for item in tables],
            ((hid, sz.n_mid), BF),
            ((hid, 2 * hid), BF),
            ((hid, 4 * sz.own), BF),
            ((hid + 8, sz.high_lanes), F32),
            ((sz.count_rows * (sz.own // LANES), LANES), BF),
            ((hid + 8, sz.part_lanes), F32),
            ((8 * sz.hold, hid), F32),
            ((2 * hid, hid), F32),
            ((16, 2 * hid), F32),
            ((sz.pay, LANES), F32),
        ],
        BACK_MIB,
        *tables,
        received,
        low,
        high,
        counts,
        partial,
        far_in=(0, 1, 2, 4, 5, 6, 7),
        micros=3,
        copies=13,
    )


def lamb_kernel(sz, grad, w1, w2, w3, wh, wb, f1, f2, f3, fh, fb, s1, s2, s3, sh, sb, *rest):
    params = (w1, w2, w3, wh, wb)
    firsts = (f1, f2, f3, fh, fb)
    seconds = (s1, s2, s3, sh, sb)
    moments, squares, updates = rest[:5], rest[5:10], rest[10:15]
    sums_ref, totals_ref, one_ref, three_ref = rest[15:]
    group = sz.group

    def wide(at, rows):
        return jnp.concatenate([grad[at : at + rows, :], grad[at + rows : at + 2 * rows, :]], 1)

    one = wide(0, 2 * sz.feat)
    three = grad[sz.at_three : sz.misc, :]
    turned = pltpu.roll(three, group, 1)
    for f in range(sz.feat):
        one_ref[f, 0:1, :] = one[f : f + 1]
        one_ref[f, 1:2, :] = one[sz.feat + f : sz.feat + f + 1]
    for c in range(sz.classes):
        three_ref[c, 0:1, :] = three[c : c + 1, :group]
        three_ref[c, 1:2, :] = turned[c : c + 1, :group]
    misc = grad[sz.misc : sz.misc + 5, :]
    fine = misc[0:2] + misc[3:5]
    hidden = jnp.concatenate([fine[0:1, :group], fine[0:1, group : 2 * group]], 0)
    two = wide(sz.rows_one, 2 * group).reshape(2, group, sz.hid)
    grads = (one_ref[...], two, three_ref[...], hidden, fine[1:2, : sz.classes])
    lane_at = lax.broadcasted_iota(jnp.int32, (8, LANES), 1)
    row_at = lax.broadcasted_iota(jnp.int32, (8, LANES), 0)
    sums = jnp.zeros((8, LANES), F32)
    for i in range(5):
        g = grads[i]
        w = params[i][...]
        m = BETA_ONE * firsts[i][...] + (1.0 - BETA_ONE) * g
        v = BETA_TWO * seconds[i][...] + (1.0 - BETA_TWO) * g * g
        u = (m / (1.0 - BETA_ONE**STEP)) / (jnp.sqrt(v / (1.0 - BETA_TWO**STEP)) + ADAM_EPS) + DECAY_RATE * w
        moments[i][...] = m
        squares[i][...] = v
        updates[i][...] = u
        for row, item in ((0, w), (1, u)):
            item = item * item
            if i < 3:
                item = jnp.sum(item, 0)
            total = jnp.sum(jnp.sum(item, 0, keepdims=True), 1, keepdims=True)
            if i == 4:
                total = 0.25 * total
            sums = jnp.where((lane_at == i) & (row_at == row), total, sums)
    sums_ref[...] = sums
    power = (1 << (lane_at & 15)).astype(F32)
    power = jnp.where((lane_at & 31) < 16, power, power * float(2**16))
    bits = jnp.broadcast_to(misc[2:3], (8, LANES)) * power
    loss = jnp.sum(jnp.where(lane_at < 32, bits, 0.0), 1, keepdims=True) * float(2.0**-LOSS_BITS)
    count = jnp.sum(jnp.where((lane_at >= 32) & (lane_at < 64), bits, 0.0), 1, keepdims=True)
    totals_ref[...] = jnp.where(lane_at == 0, loss, count)


def lamb(sz, grad, params, firsts, seconds):
    like = [(item.shape, F32) for item in params]
    return call(
        functools.partial(lamb_kernel, sz),
        like * 3 + [((8, LANES), F32)] * 2,
        [(params[0].shape, F32), (params[2].shape, F32)],
        6,
        grad,
        *params,
        *firsts,
        *seconds,
    )


def step_kernel(own, far, w1, w2, w3, wh, wb, u1, u2, u3, uh, ub, n1, n2, n3, nh, nb, norms_ref):
    norms = jnp.sqrt(own[...] + far[...])
    norms_ref[...] = norms[0:2, 0:5]
    for i, (w, u, n) in enumerate(
        ((w1, u1, n1), (w2, u2, n2), (w3, u3, n3), (wh, uh, nh), (wb, ub, nb))
    ):
        ratio = LEARN_RATE * (norms[0:1, i : i + 1] / norms[1:2, i : i + 1])
        n[...] = w[...] - ratio * u[...]


def take_step(sums, params, updates):
    return call(
        step_kernel,
        [(item.shape, F32) for item in params] + [((2, 5), F32)],
        [],
        3,
        *sums,
        *params,
        *updates,
    )


def swap(value, axis, count, bit):
    return lax.ppermute(value, axis, [(i, i ^ bit) for i in range(count)])


def merged(own, other):
    return lax.reduce_precision(own.astype(F32) + other.astype(F32), 8, 7)


def shards(
    features, neighbors_one, present_one, neighbors_two, present_two, neighbors_three, present_three,
    labels, seed_weight, serve_rows, take_seed, fetch_live,
    weight_one, weight_two, weight_three, hidden_bias, head_bias,
    first_one, first_two, first_three, first_hidden, first_head,
    second_one, second_two, second_three, second_hidden, second_head,
):
    sz = Sizes(features, neighbors_one, neighbors_two, neighbors_three, weight_two, weight_three, serve_rows)

    def tree(one, two, three, hidden, head):
        return (one.transpose(1, 0, 2), two, three.transpose(2, 0, 1), hidden, head[None, :])

    def back(one, two, three, hidden, head):
        return (one.transpose(1, 0, 2), two, three.transpose(1, 2, 0), hidden, head[0])

    params = tree(weight_one, weight_two, weight_three, hidden_bias, head_bias)
    firsts = tree(first_one, first_two, first_three, first_hidden, first_head)
    seconds = tree(second_one, second_two, second_three, second_hidden, second_head)

    own_b, packed, mean, tail, *sent = first_messages(sz, features, neighbors_one, present_one, *params[:4])
    s1, s2, s3 = [swap(sent[r - 1], "col", 4, r) for r in (1, 2, 3)]
    links = (neighbors_two, present_two, neighbors_three, present_three)
    own_a, counts, *means = mean_messages(sz, features, neighbors_one, present_one, mean, tail, links)
    s1, *means = lax.optimization_barrier((s1, *means))
    means = [swap(means[r - 1], "col", 4, r) for r in (1, 2, 3)]
    later, s3, counts = lax.optimization_barrier((s2, s3, counts))
    passed = swap(later, "col", 4, 1)
    tables = (serve_rows, take_seed, fetch_live[None, :])
    low, high, rows = seeds_forward(sz, (own_b, packed, s1, s2, s3, passed), counts, tables)
    received = lax.all_to_all(rows, ("dp", "col"), split_axis=0, concat_axis=0, tiled=True)
    partial = rest_step(sz, low, high, counts, (own_a, *means, s1, s2, s3), labels[None, :], seed_weight[None, :], head_bias[None, :])
    keep0, keep1, send = seeds_backward(sz, tables, received, low, high, counts, partial)
    other = swap(send, "col", 4, 1)
    own = merged(keep0, other[: sz.pay]).astype(BF)
    far = merged(keep1, other[sz.pay :]).astype(BF)
    pair = [[(d, c), (d ^ 1, c ^ 2)] for d in range(sz.dp) for c in range(4)]
    pair = [(a * 4 + b, c * 4 + d) for (a, b), (c, d) in pair]
    near = (swap(far, "col", 4, 2), swap(own, "dp", sz.dp, 1), lax.ppermute(far, ("dp", "col"), pair))
    near = [item.astype(F32) for item in (own, *near)]
    grad = lax.reduce_precision((near[0] + near[1]) + (near[2] + near[3]), 8, 7)
    bit = 2
    while bit < sz.dp:
        grad = merged(grad, swap(grad.astype(BF), "dp", sz.dp, bit))
        bit *= 2
    outs = lamb(sz, grad, params, firsts, seconds)
    moments, squares, updates = outs[:5], outs[5:10], outs[10:15]
    sums, totals = outs[15], outs[16]
    pair = sums + swap(sums, "col", 4, 1)
    fresh = take_step([pair, swap(pair, "col", 4, 2)], params, updates)
    return (*back(*fresh[:5]), *back(*moments), *back(*squares), fresh[5], totals[0, 0], totals[0, 1])


def solution(mesh):
    wide = P(None, "col", None)
    tree = [wide, wide, wide, P(None, "col"), P()]
    return jax.shard_map(
        shards,
        mesh=mesh,
        in_specs=(
            P("col", "dp"),
            *[P(None, "dp")] * 6,
            P("dp"),
            P("dp"),
            P("dp", None),
            P("dp", None),
            P("dp"),
            *tree,
            *tree,
            *tree,
        ),
        out_specs=(*tree, *tree, *tree, P(), P(), P()),
        check_vma=False,
    )
```

```python
import functools

import jax
import jax.numpy as jnp
from jax import lax
from jax.experimental import pallas as pl
from jax.experimental.pallas import tpu as pltpu
from jax.sharding import PartitionSpec as P

REACH = 64
STEP = 5
DIST_WEIGHT = 1.0
ROW_EPS = 1e-06
LEARN_RATE = 0.5
BETA_ONE = 0.9
BETA_TWO = 0.999
ADAM_EPS = 1e-06
DECAY_RATE = 0.01

BF = jnp.bfloat16
F32 = jnp.float32
LANES = 128
WINDOW = 640
HALF = 64
FRONT = 320
SENTINEL = 4.0
MIB = 2**20
LOSS_BITS = 14
EARLY = 4
FIRST_MIB = 8
MEAN_MIB = 8
SEEDS_MIB = 16
REST_MIB = 28
BACK_MIB = 12


def cost(micros):
    return pl.CostEstimate(flops=int(micros * 10**9), bytes_accessed=1, transcendentals=0)


def call(kernel, outs, scratch, mib, *args, far_in=(), far_out=(), copies=0, micros=1, loose=(), name=None):
    near = pl.BlockSpec(memory_space=pltpu.VMEM)
    far = pl.BlockSpec(memory_space=pltpu.HBM)
    free = pl.BlockSpec(memory_space=pl.ANY)
    scratch = [pltpu.VMEM(shape, kind) for shape, kind in scratch]
    args = [pltpu.with_memory_space_constraint(a, pltpu.HBM) if i in far_in else a for i, a in enumerate(args)]
    return pl.pallas_call(
        kernel,
        in_specs=[free if i in loose else far if i in far_in else near for i in range(len(args))],
        out_specs=tuple(far if i in far_out else near for i in range(len(outs))),
        out_shape=tuple(
            pltpu.HBM(shape, kind) if i in far_out else jax.ShapeDtypeStruct(shape, kind)
            for i, (shape, kind) in enumerate(outs)
        ),
        scratch_shapes=scratch + ([pltpu.SemaphoreType.DMA((copies,))] if copies else []),
        compiler_params=pltpu.CompilerParams(vmem_limit_bytes=mib * MIB),
        cost_estimate=cost(micros),
        name=name,
    )(*args)


def start_copies(pairs, sems, first=0):
    copies = [pltpu.make_async_copy(src, dst, sems.at[first + i]) for i, (src, dst) in enumerate(pairs)]
    for copy in copies:
        copy.start()
    return copies


def wait_all(copies):
    for copy in copies:
        copy.wait()


class Sizes:
    def __init__(self, features, neighbors_one, neighbors_two, neighbors_three, weight_two, weight_three, serve_rows):
        self.feat = features.shape[0]
        self.main = self.feat - 1
        self.hold = 32
        self.base = features.shape[1]
        self.low = neighbors_one.shape[1]
        self.mid = neighbors_two.shape[1]
        self.seeds = neighbors_three.shape[1]
        self.hid = weight_two.shape[2]
        self.group = weight_two.shape[1]
        self.classes = weight_three.shape[2]
        self.head = -(-self.classes // 16) * 16
        self.own = self.seeds // 4
        self.n_b = 4 * self.own + LANES
        self.n_a = 16 * self.own + 5 * LANES
        self.n_mid = self.n_b + self.own
        self.n_low = self.n_a + self.n_mid
        self.tiles_b = self.n_b // LANES
        self.tiles_mid = self.n_mid // LANES
        self.tiles_low = self.n_low // LANES
        self.slots = serve_rows.shape[0] * serve_rows.shape[1]
        self.slot = serve_rows.shape[1]
        self.dp = serve_rows.shape[0]
        self.rows_one = 2 * 2 * self.feat
        self.rows_two = 4 * self.group
        self.at_three = self.rows_one + self.rows_two
        self.misc = self.at_three + self.classes
        self.pay = -(-(self.misc + 5) // 16) * 16
        self.blocks = -(-(self.misc + 3) // self.main)
        self.early = EARLY * LANES
        self.message_a = self.pair_lanes(self.n_a, self.n_a - self.early)
        self.message_b = self.pair_lanes(self.n_mid, self.n_mid + self.early)
        self.full_b = self.message_b + LANES * self.blocks
        self.tiles_b_all = 16 * self.own // LANES + 1
        self.tiles_all = self.low // LANES + 8
        self.count_rows = WINDOW + 16
        hid, at = self.hid, self.n_mid
        places = {}
        for name, lanes in (
            ("turned1", hid), ("turned2", 2 * hid), ("weight2", 2 * hid), ("weight3", 2 * LANES), ("turned3", 2 * hid),
            ("states", self.n_b), ("embed", 2 * self.own), ("inputs2", 2 * self.own),
        ):
            places[name] = at
            at += lanes
        self.low_lanes = at
        at = 0
        for name, lanes in (("result1", self.n_mid), ("result2", self.own), ("bias", 2 * LANES)):
            places[name] = at
            at += lanes
        self.high_lanes = at
        at = 0
        for name, lanes in (("g1", hid), ("g2", 2 * hid), ("g3", 2 * hid), ("grad_b", self.n_b), ("grad_embed", self.own)):
            places[name] = at
            at += lanes
        self.part_lanes = at
        self.at = places

    def pair_lanes(self, means, own):
        lanes = means + own
        return lanes + LANES * -(-lanes // LANES // self.main)

    def first_ranges(self, part):
        a, b, c = self.ranges(part)
        b = (b[0], 0, b[2])
        c = (c[0], b[2], c[2])
        return [b, c, (a[0], self.n_mid, self.early)], [b, c]

    def second_ranges(self, part):
        first = 16 * self.own * part
        return [(first + self.early, 0, self.n_a - self.early)], [(first, 0, self.n_a)]

    def a_row(self, part):
        return 16 * self.own * part - FRONT

    def b_row(self, part):
        return 4 * self.own * part - HALF

    def seed_window(self):
        rows = self.count_rows * (self.own // LANES)
        return pl.ds(self.count_rows * self.tiles_b + rows, rows)

    def ranges(self, part):
        return (
            (16 * self.own * part, 0, self.n_a),
            (self.b_row(part) + FRONT, self.n_a, self.n_b),
            (self.own * part + FRONT, self.n_a + self.n_b, self.own),
        )


def dot(a, b, over):
    return lax.dot_general(a, b, (((over[0],), (over[1],)), ((), ())), preferred_element_type=F32)


def two_parts(value):
    high = value.astype(BF)
    return high, (value - high.astype(F32)).astype(BF)


def three_parts(value):
    high = value.astype(BF).astype(F32)
    rest = value - high
    middle = rest.astype(BF).astype(F32)
    return high, middle, (rest - middle).astype(BF).astype(F32)


def aligned(value):
    return pl.multiple_of(value, LANES)


def sigmoid(value):
    return 0.5 * jnp.tanh(0.5 * value) + 0.5


def unpack_tile(sz, message, tail, tile):
    spare = jnp.zeros((sz.hold - sz.feat, LANES), F32)
    main = message[:, LANES * tile : LANES * (tile + 1)].astype(F32)
    return jnp.concatenate([main, tail[tile : tile + 1, :], spare], 0).astype(BF)


def half_tiles(left, right):
    lane = lax.broadcasted_iota(jnp.int32, left.shape, 1)
    return jnp.where(lane < HALF, pltpu.roll(left, HALF, 1), pltpu.roll(right, HALF, 1))


def half_columns(ref, tile, tiles, spare):
    if isinstance(tile, int):
        left, right = max(tile - 1, 0), min(tile, tiles - 1)
        left, right = [ref[:, LANES * i : LANES * (i + 1)] for i in (left, right)]
        left = left if tile > 0 else jnp.full_like(left, spare)
        right = right if tile < tiles else jnp.full_like(right, spare)
        return half_tiles(left, right)
    left = ref[:, pl.ds(aligned(jnp.maximum(tile - 1, 0) * LANES), LANES)]
    right = ref[:, pl.ds(aligned(jnp.minimum(tile, tiles - 1) * LANES), LANES)]
    left = jnp.where(tile > 0, left, spare)
    right = jnp.where(tile < tiles, right, spare)
    return half_tiles(left, right)


def take_tile(ref, rows, first, half):
    if not half:
        return ref[:rows, pl.ds(aligned(first), LANES)].astype(F32)
    first = first - HALF
    left = ref[:rows, pl.ds(aligned(first), LANES)].astype(F32)
    return half_tiles(left, ref[:rows, pl.ds(aligned(first + LANES), LANES)].astype(F32))


def take_tail(ref, first, half):
    if not half:
        return ref[pl.ds(first // LANES, 1), :]
    row = (first - HALF) // LANES
    return half_tiles(ref[pl.ds(row, 1), :], ref[pl.ds(row + 1, 1), :])


def fill_own(sz, feat_ref, self_ref, self_tail, places):
    spare = jnp.zeros((sz.hold - sz.feat, LANES), F32)
    zeros = jnp.zeros((sz.feat, LANES), BF)
    count = min(sz.low, feat_ref.shape[1]) // LANES
    lane = lax.broadcasted_iota(jnp.int32, (sz.feat, LANES), 1)
    shift = FRONT // LANES
    before = zeros
    for place in range(places):
        tile = place - shift
        after = zeros
        if tile >= 0 and tile < count:
            after = pltpu.roll(feat_ref[:, LANES * tile : LANES * (tile + 1)], HALF, 1)
        value = jnp.where(lane < HALF, before.astype(F32), after.astype(F32))
        self_tail[place : place + 1, :] = value[sz.main : sz.feat]
        self_ref[:, LANES * place : LANES * (place + 1)] = jnp.concatenate([value, spare], 0).astype(BF)
        before = after


def mean_tiles(sz, begin, tiles, feat_ref, nbr_ref, pres_ref, links_ref, present_ref, mean_ref, tail_ref, base_ref, code_ref, count_ref):
    last = feat_ref.shape[1] // LANES - 6
    slots = nbr_ref.shape[0]
    base_ref[...] = jnp.zeros_like(base_ref)
    if begin % 8 or tiles % 8:
        code_ref[...] = jnp.full_like(code_ref, -1)
        count_ref[...] = jnp.ones_like(count_ref)
    for tile in range(feat_ref.shape[1] // LANES):
        row = feat_ref[:, LANES * tile : LANES * (tile + 1)].astype(F32)
        base_ref[8 + tile : 9 + tile, :] = row[sz.main : sz.feat]

    for table, shifted in ((nbr_ref, links_ref), (pres_ref, present_ref)):
        count = table.shape[1] // LANES
        for tile in range(begin, tiles):
            shifted[:, LANES * tile : LANES * (tile + 1)] = half_columns(table, tile, count, 0)

    def one_tile(step, carry):
        lanes = pl.ds(aligned(step * LANES), LANES)
        present = present_ref[:, lanes]
        valid = present.astype(F32)
        counts = jnp.maximum(jnp.sum(valid, 0, keepdims=True), 1.0)
        first = jnp.clip(4 * step - 3, 0, last)
        links = links_ref[:, lanes]
        code = jnp.where(present > 0, links, -1)
        count_ref[pl.ds(step, 1), :] = counts
        for slot in range(slots):
            code_ref[slot, pl.ds(step, 1), :] = code[slot : slot + 1]
        local = links - first * LANES
        piece = local >> 7
        spot = local & 127
        sources = [
            feat_ref[:, pl.ds(aligned((first + j) * LANES), LANES)].astype(F32) for j in range(6)
        ]
        totals = [jnp.zeros((8, LANES), F32) for _ in range(sz.main // 8)]
        for slot in range(slots):
            spots = jnp.broadcast_to(spot[slot : slot + 1], (8, LANES))
            pieces = jnp.broadcast_to(piece[slot : slot + 1], (8, LANES))
            marks = jnp.broadcast_to(valid[slot : slot + 1], (8, LANES))
            for h in range(sz.main // 8):
                taken = None
                for j in range(6):
                    found = jnp.take_along_axis(
                        sources[j][8 * h : 8 * h + 8], spots, axis=1, mode="promise_in_bounds"
                    )
                    taken = found if j == 0 else jnp.where(pieces == j, found, taken)
                totals[h] = totals[h] + taken * marks
        mean_ref[:, pl.ds(aligned((step + 2) * LANES), LANES)] = (jnp.concatenate(totals, 0) / counts).astype(BF)
        return carry

    even = begin + (tiles - begin) // 4 * 4
    lax.fori_loop(begin, even, one_tile, 0, unroll=4)
    for step in range(even, tiles):
        one_tile(step, 0)
    sub = lax.broadcasted_iota(jnp.int32, (8, LANES), 0)

    for block in range(begin // 8, -(-tiles // 8)):
        total = jnp.zeros((8, LANES), F32)
        for slot in range(slots):
            code = code_ref[slot, 8 * block : 8 * (block + 1), :]
            piece = (code >> 7) - (4 * (8 * block + sub) - 3)
            taken = None
            for j in range(6):
                source = base_ref[pl.ds(8 + 32 * block - 3 + j, 8, stride=4), :]
                found = jnp.take_along_axis(source, code & 127, axis=1, mode="promise_in_bounds")
                taken = found if j == 0 else jnp.where(piece == j, found, taken)
            total = total + jnp.where(code >= 0, taken, 0.0)
        tail_ref[8 * block + 2 : 8 * block + 10, :] = total / count_ref[8 * block : 8 * (block + 1), :]


def pack_pair(sz, ranges, self_ref, self_tail, mean_ref, tail_ref, turn_ref, out_ref):
    turn_ref[...] = jnp.zeros_like(turn_ref)
    lanes = 0
    for source_ref, rows_ref, group in zip((self_ref, mean_ref), (self_tail, tail_ref), ranges):
        for i, (first, at, count) in enumerate(group):
            at = at + lanes
            if i != 1:
                out_ref[:, at : at + count] = source_ref[: sz.main, pl.ds(aligned(first), count)]
                turn_ref[at // LANES : (at + count) // LANES, :] = rows_ref[pl.ds(first // LANES, count // LANES), :]
                continue
            for tile in range(count // LANES):
                place = first + LANES * tile
                piece = take_tile(source_ref, sz.main, place, True)
                out_ref[:, at + LANES * tile : at + LANES * (tile + 1)] = piece.astype(BF)
                turn_ref[at // LANES + tile : at // LANES + tile + 1, :] = take_tail(rows_ref, place, True)
        lanes += sum(count for _, _, count in group)
    for block in range(-(-lanes // LANES // sz.main)):
        at = lanes + LANES * block
        out_ref[:, at : at + LANES] = turn_ref[sz.main * block : sz.main * (block + 1), :].astype(BF)


def own_pair(sz, ranges, self_ref, mean_ref, tail_ref, own_ref):
    spare = jnp.zeros((sz.hold - sz.feat, LANES), F32)
    base = ranges[0][1]
    for i, (start, at, count) in enumerate(ranges):
        for tile in range(count // LANES):
            place = start + LANES * tile
            out_lanes = slice(at - base + LANES * tile, at - base + LANES * (tile + 1))
            own_ref[: sz.hold, out_lanes] = take_tile(self_ref, sz.hold, place, i == 1).astype(BF)
            average = [take_tile(mean_ref, sz.main, place, i == 1), take_tail(tail_ref, place, i == 1), spare]
            own_ref[sz.hold :, out_lanes] = jnp.concatenate(average, 0).astype(BF)


def mean_scratch(sz, tiles, slots):
    rows = -(-tiles // 8) * 8
    return [
        ((slots, LANES * tiles), jnp.int32),
        ((slots, LANES * tiles), jnp.int32),
        ((sz.hold, LANES * sz.tiles_all), BF),
        ((sz.tiles_all, LANES), F32),
        ((sz.main, LANES * sz.tiles_all), BF),
        ((max(rows + 8, sz.tiles_all), LANES), F32),
        ((2 * sz.main, LANES), F32),
        ((4 * rows + 16, LANES), F32),
        ((slots, rows, LANES), jnp.int32),
        ((rows, LANES), F32),
    ]


def unpack_tails(sz, message, lanes, turn_ref):
    for block in range(-(-lanes // LANES // sz.main)):
        at = lanes + LANES * block
        turn_ref[sz.main * block : sz.main * (block + 1), :] = message[:, at : at + LANES].astype(F32)
    return turn_ref[...]


def unpack_tiles(sz, message, tail, first, tiles, row, at, out_ref):
    for tile in range(tiles):
        lane = at + LANES * tile
        out_ref[row : row + sz.hold, lane : lane + LANES] = unpack_tile(sz, message, tail, first + tile)


def first_kernel(
    sz, features, neighbors, present, w1_in, w2_in, w3_in, wh_in, own_b, packed, mean_out, tail_out, m1, m2, m3,
    feat_ref, nbr_ref, pres_ref, w1, w2, w3, wh, own_ref,
    links_ref, present_ref, self_ref, self_tail, mean_ref, tail_ref, turn_ref, base_ref, code_ref, count_ref, pack, sems,
):
    part = lax.axis_index("col")
    rows = pl.ds(0, nbr_ref.shape[1])
    weights = start_copies(((w1_in, w1), (w2_in, w2), (w3_in, w3), (wh_in, wh)), sems)
    copies = start_copies(
        (
            (features.at[:, pl.ds(0, feat_ref.shape[1])], feat_ref),
            (neighbors.at[:, rows], nbr_ref),
            (present.at[:, rows], pres_ref),
        ),
        sems,
        4,
    )
    wait_all(weights)
    pack[sz.at_three :, :] = jnp.zeros((pack.shape[0] - sz.at_three, LANES), F32)
    for half in range(sz.hid // LANES):
        lanes = slice(LANES * half, LANES * (half + 1))
        for s in range(2):
            for f in range(sz.feat):
                at = sz.feat * (2 * half + s) + f
                pack[at : at + 1, :] = w1[f, s : s + 1, lanes]
            at = sz.rows_one + sz.group * (2 * half + s)
            pack[at : at + sz.group, :] = w2[s, :, lanes]
    for c in range(sz.classes):
        for s in range(2):
            at = sz.at_three + c
            pack[at : at + 1, sz.group * s : sz.group * (s + 1)] = w3[c, s : s + 1, :]
    row = jnp.concatenate([wh[0:1, :], wh[1:2, :]], 1)
    for i, piece in enumerate(three_parts(row)):
        pack[sz.misc + i : sz.misc + i + 1, :] = piece
    store = start_copies(((pack, packed),), sems, 7)
    for block in range(sz.blocks):
        at = sz.message_b + LANES * block
        piece = pack[sz.main * block : sz.main * (block + 1), :].astype(BF)
        m1[:, at : at + LANES] = piece
        m2[:, at : at + LANES] = piece
    wait_all(copies)
    fill_own(sz, feat_ref, self_ref, self_tail, 48 * sz.own // LANES + EARLY)
    mean_ref[:, :FRONT] = jnp.zeros((sz.main, FRONT), BF)
    tail_ref[...] = jnp.zeros_like(tail_ref)
    mean_tiles(sz, 0, sz.tiles_b_all, feat_ref, nbr_ref, pres_ref, links_ref, present_ref, mean_ref, tail_ref, base_ref, code_ref, count_ref)
    done = pl.ds(0, LANES * (sz.tiles_b_all + 2))
    store += start_copies(((mean_ref.at[:, done], mean_out), (tail_ref, tail_out)), sems, 9)
    own_pair(sz, sz.ranges(part)[1:], self_ref, mean_ref, tail_ref, own_ref)
    store += start_copies(((own_ref, own_b),), sems, 8)
    for r, out in ((1, m1), (2, m2), (3, m3)):
        pack_pair(sz, sz.first_ranges(part ^ r), self_ref, self_tail, mean_ref, tail_ref, turn_ref, out)
    wait_all(store)


def first_messages(sz, features, neighbors, present, w1, w2, w3, hidden):
    rows = LANES * sz.tiles_b_all
    bases = min(4 * rows + LANES, sz.base)
    slots = neighbors.shape[0]
    return call(
        functools.partial(first_kernel, sz),
        [
            ((2 * sz.hold, sz.n_mid), BF),
            ((sz.main * sz.blocks, LANES), F32),
            ((sz.main, rows + 2 * LANES), BF),
            ((max(-(-sz.tiles_b_all // 8) * 8 + 8, sz.tiles_all), LANES), F32),
            ((sz.main, sz.full_b), BF),
            ((sz.main, sz.full_b), BF),
            ((sz.main, sz.message_b), BF),
        ],
        [
            ((sz.feat, bases), BF),
            ((slots, rows), jnp.int32),
            ((slots, rows), jnp.int32),
            (w1.shape, F32),
            (w2.shape, F32),
            (w3.shape, F32),
            (hidden.shape, F32),
            ((2 * sz.hold, sz.n_mid), BF),
            *mean_scratch(sz, sz.tiles_b_all, slots),
            ((sz.main * sz.blocks, LANES), F32),
        ],
        FIRST_MIB,
        features,
        neighbors,
        present,
        w1,
        w2,
        w3,
        hidden,
        far_in=range(7),
        far_out=(0, 1, 2, 3),
        copies=11,
        micros=4,
    )


def mean_kernel(
    sz, feat_ref, nbr_ref, pres_ref, mean_in, tail_in, nbr2, pres2, nbr3, pres3, own_a, counts_out, a1, a2, a3,
    links_ref, present_ref, self_ref, self_tail, mean_ref, tail_ref, turn_ref, base_ref, code_ref, count_ref, own_ref, kept_ref, counts, sems,
):
    part = lax.axis_index("col")
    tiles = sz.low // LANES + 1
    begin = sz.tiles_b_all
    loads = start_copies(((mean_in, mean_ref.at[:, pl.ds(0, LANES * (begin + 2))]), (tail_in, kept_ref)), sems, 1)
    fill_counts(sz, part, nbr2, pres2, nbr3, pres3, counts)
    store = start_copies(((counts, counts_out),), sems, 3)
    fill_own(sz, feat_ref, self_ref, self_tail, (48 * sz.own + sz.n_a) // LANES)
    last = LANES * (tiles + 2)
    mean_ref[:, last:] = jnp.zeros((sz.main, LANES * sz.tiles_all - last), BF)
    tail_ref[...] = jnp.zeros_like(tail_ref)
    mean_tiles(sz, begin, tiles, feat_ref, nbr_ref, pres_ref, links_ref, present_ref, mean_ref, tail_ref, base_ref, code_ref, count_ref)
    wait_all(loads)
    tail_ref[: begin + 2, :] = kept_ref[: begin + 2, :]
    own_pair(sz, sz.ranges(part)[:1], self_ref, mean_ref, tail_ref, own_ref)
    store += start_copies(((own_ref, own_a),), sems)
    for r, out in ((1, a1), (2, a2), (3, a3)):
        pack_pair(sz, sz.second_ranges(part ^ r), self_ref, self_tail, mean_ref, tail_ref, turn_ref, out)
    wait_all(store)


def mean_messages(sz, features, neighbors, present, mean, tail, links):
    counts = (sz.count_rows * (sz.tiles_b + 2 * (sz.own // LANES)), LANES)
    return call(
        functools.partial(mean_kernel, sz),
        [((2 * sz.hold, sz.n_a), BF), (counts, BF)] + [((sz.main, sz.message_a), BF)] * 3,
        mean_scratch(sz, sz.low // LANES + 1, neighbors.shape[0]) + [((2 * sz.hold, sz.n_a), BF), (tail.shape, F32), (counts, BF)],
        MEAN_MIB,
        features,
        neighbors,
        present,
        mean,
        tail,
        *links,
        far_in=(3, 4),
        far_out=(0, 1),
        copies=4,
        micros=6,
    )


def window_counts(local, rows):
    spots = lax.broadcasted_iota(jnp.int32, (256, LANES), 0).astype(F32).astype(BF)
    blocks = []
    for first in range(0, rows, 256):
        size = min(256, rows - first)
        place = local - first
        place = jnp.where((place >= 0) & (place < size), place, -1).astype(F32)
        counts = jnp.zeros((size, LANES), BF)
        for slot in range(local.shape[0]):
            row = jnp.broadcast_to(place[slot : slot + 1], (16, LANES)).astype(BF)
            row = jnp.concatenate([row] * (size // 16), 0)
            counts = counts + jnp.where(row == spots[:size], jnp.bfloat16(1.0), jnp.bfloat16(0.0))
        blocks.append(counts)
    return jnp.concatenate(blocks, 0)


def slot_totals(present):
    return jnp.maximum(jnp.sum(present.astype(F32), 0, keepdims=True), 1.0)


def counts_tile(sz, links, marks, start, at, counts):
    local = jnp.where(marks > 0, links - start, -1)
    counts[at : at + WINDOW, :] = window_counts(local, WINDOW)
    counts[at + WINDOW : at + sz.count_rows, :] = jnp.broadcast_to(slot_totals(marks), (16, LANES)).astype(BF)


def fill_counts(sz, part, nbr2, pres2, nbr3, pres3, counts):
    tiles = nbr2.shape[1] // LANES
    for tile in range(sz.tiles_b):
        column = 4 * sz.own // LANES * part + tile
        start = sz.a_row(part) + 4 * LANES * tile
        links, marks = half_columns(nbr2, column, tiles, 0), half_columns(pres2, column, tiles, 0)
        counts_tile(sz, links, marks, start, sz.count_rows * tile, counts)
    for tile in range(sz.own // LANES):
        columns = pl.ds(aligned(sz.own * part + LANES * tile), LANES)
        at = sz.count_rows * (sz.tiles_b + tile)
        counts_tile(sz, nbr3[:, columns], pres3[:, columns], sz.b_row(part), at, counts)
        at += sz.count_rows * (sz.own // LANES)
        counts_tile(sz, nbr2[:, columns], pres2[:, columns], sz.b_row(part), at, counts)


def tile_counts(sz, counts, tile):
    at = sz.count_rows * tile
    totals = counts[at + WINDOW : at + WINDOW + 16, :].astype(F32)[0:1]
    return counts[at : at + WINDOW, :], totals


def activate(result):
    active = result * sigmoid(result)
    scale = lax.rsqrt(jnp.sum(active * active, 0, keepdims=True) + ROW_EPS)
    return result, scale, active * scale


def first_layer(weight, inputs, bias):
    result = dot(weight, inputs, (1, 0)) + bias
    active = result * sigmoid(result)
    scale = lax.rsqrt(jnp.sum(active * active, 0, keepdims=True) + ROW_EPS)
    return result, scale, active * scale


def join_inputs(sz, own, average):
    pieces = []
    for c in range(4):
        pieces.append(own[sz.group * c : sz.group * (c + 1)])
        pieces.append(average[sz.group * c : sz.group * (c + 1)])
    return jnp.concatenate(pieces, 0)


def norm_backward(grad, result, scale):
    gate = sigmoid(result)
    active = result * gate
    inner = jnp.sum(grad * active, 0, keepdims=True)
    grad_active = scale * grad - active * (scale * scale * scale * inner)
    return (grad_active * gate * (1.0 + result * (1.0 - gate))).astype(BF)


def split_inputs(sz, grad):
    pieces = [grad[sz.group * c : sz.group * (c + 1)] for c in range(8)]
    return jnp.concatenate(pieces[0::2], 0), jnp.concatenate(pieces[1::2], 0)


def row_sums(grad):
    return dot(jnp.ones((16, grad.shape[1]), BF), grad, (1, 1))


def spread(sz, scaled, counts):
    return dot(scaled.astype(BF), counts, (1, 1))


def halves(ref, at, lanes):
    return jnp.concatenate([ref[:, at : at + lanes], ref[:, at + lanes : at + 2 * lanes]], 0)


def store_halves(ref, at, lanes, value):
    rows = value.shape[0] // 2
    ref[:rows, at : at + lanes] = value[:rows]
    ref[:rows, at + lanes : at + 2 * lanes] = value[rows:]


def slot_column(table):
    rows, slots = table.shape
    wide = jnp.broadcast_to(table.astype(F32)[:, None, :], (rows, slots, slots))
    hit = lax.broadcasted_iota(jnp.int32, wide.shape, 1) == lax.broadcasted_iota(jnp.int32, wide.shape, 2)
    return jnp.sum(jnp.where(hit, wide, 0.0), 2, keepdims=True).reshape(rows * slots, 1)


def alive_column(sz, live):
    shape = (sz.dp, sz.dp)
    hit = lax.broadcasted_iota(jnp.int32, shape, 0) == lax.broadcasted_iota(jnp.int32, shape, 1)
    counts = jnp.sum(jnp.where(hit, jnp.broadcast_to(live.astype(F32), shape), 0.0), 1, keepdims=True)
    slot = lax.broadcasted_iota(jnp.int32, (sz.dp, sz.slot), 1).astype(F32)
    return slot_column(jnp.where(slot < counts, 1.0, 0.0))


def seed_picks(sz, serve_rows, take_rows, part):
    spots = (lax.broadcasted_iota(jnp.int32, (sz.slots, sz.own), 1) + sz.own * part).astype(F32)
    serve = jnp.where(slot_column(serve_rows) == spots, 1.0, 0.0)
    take = jnp.where(slot_column(take_rows) == spots, 1.0, 0.0)
    return serve, take, jnp.sum(serve, 1, keepdims=True), jnp.sum(take, 1, keepdims=True)


def seeds_kernel(
    sz, own_b, packed, s1, s2, s3, passed, counts_in, serve_in, take_in, live_in,
    low_out, high_out, sent,
    xb, pack, m1, m2, m3, p3, window_ref, serve_rows, take_rows, live_rows, low, high, turn_ref, w1_ref, w2_ref, states, sems,
):
    part = lax.axis_index("col")
    own, hid, n_b, group, hold, at = sz.own, sz.hid, sz.n_b, sz.group, sz.hold, sz.at
    n_mid = sz.n_mid
    copies = start_copies(
        (
            (packed, pack),
            (passed.at[:, pl.ds(sz.message_b, LANES * sz.blocks)], p3),
            (s1, m1),
            (s2, m2),
            (s3, m3),
            (own_b, xb),
            (counts_in.at[sz.seed_window(), :], window_ref),
            (serve_in, serve_rows),
            (take_in, take_rows),
            (live_in, live_rows),
        ),
        sems,
    )
    w1_ref[...] = jnp.zeros_like(w1_ref)
    wait_all(copies[:4])
    for r, (message, first_lane) in enumerate(((None, 0), (m1, sz.message_b), (m2, sz.message_b), (p3, 0))):
        for block in range(sz.blocks if r else 0):
            first = first_lane + LANES * block
            pack[sz.main * block : sz.main * (block + 1), :] = message[:, first : first + LANES].astype(F32)
        shard = part ^ r
        for half in range(hid // LANES):
            lanes = slice(LANES * half, LANES * (half + 1))
            for s in range(2):
                first = sz.feat * (2 * half + s)
                row = 4 * hold * s + hold * r
                w1_ref[row : row + sz.feat, lanes] = pack[first : first + sz.feat, :]
            first = sz.rows_one + 2 * group * half
            row = pl.multiple_of(2 * group * shard, 2 * group)
            w2_ref[pl.ds(row, 2 * group), lanes] = pack[first : first + 2 * group, :]
        third = jnp.concatenate([pack[sz.at_three : sz.misc, :], jnp.zeros((sz.head - sz.classes, LANES), F32)], 0)
        low[: sz.head, pl.ds(aligned(at["turned3"] + 2 * group * shard), LANES)] = third.astype(BF)
        misc = pack[sz.misc : sz.misc + 3, :]
        column = jnp.broadcast_to(misc[0:1] + misc[1:2] + misc[2:3], (LANES, LANES)).T
        row = pl.multiple_of(group * shard, group)
        for layer in range(2):
            lanes = slice(at["bias"] + LANES * layer, at["bias"] + LANES * (layer + 1))
            high[pl.ds(row, group), lanes] = column[group * layer : group * (layer + 1)]
    turned1 = w1_ref[...].T.astype(BF)
    turned2 = w2_ref[...].T.astype(BF)
    low[:, at["turned1"] : at["turned1"] + hid] = turned1
    low[:, at["turned2"] : at["turned2"] + 2 * hid] = turned2
    store_halves(low, at["weight2"], hid, w2_ref[...].astype(BF))
    weight3 = low[: sz.head, at["turned3"] : at["turned3"] + 2 * hid].astype(F32).T
    weight3 = jnp.concatenate([weight3, jnp.zeros((2 * hid, LANES - sz.head), F32)], 1)
    store_halves(low, at["weight3"], LANES, weight3.astype(BF))

    def piece(lanes, count):
        return (low.at[:, pl.ds(lanes, count)], low_out.at[:, pl.ds(lanes, count)])

    stores = start_copies((piece(n_mid, at["states"] - n_mid),), sems, 11)
    wait_all(copies[4:])
    low[:hold, :n_mid] = xb[:hold, :]
    low[4 * hold : 5 * hold, :n_mid] = xb[hold:, :]
    for r, message in ((1, m1), (2, m2), (3, m3)):
        tail = unpack_tails(sz, message, 2 * n_mid + sz.early, turn_ref)
        unpack_tiles(sz, message, tail, 0, sz.tiles_mid, hold * r, 0, low)
        first = (n_mid + sz.early) // LANES
        unpack_tiles(sz, message, tail, first, sz.tiles_mid, hold * (4 + r), 0, low)
    stores += start_copies((piece(0, n_mid),), sems, 12)
    bias1 = high[:hid, at["bias"] : at["bias"] + LANES]
    bias2 = high[:hid, at["bias"] + LANES : at["bias"] + 2 * LANES]
    high[:hid, :n_mid] = dot(turned1, low[:, :n_mid], (1, 0))
    for tile in range(sz.tiles_mid):
        lanes = slice(LANES * tile, LANES * (tile + 1))
        result, scale, state = activate(high[:hid, lanes] + bias1)
        high[:hid, lanes] = result
        high[hid:, lanes] = jnp.broadcast_to(scale, (8, LANES))
        upper, lower = two_parts(state)
        states[:hid, lanes] = upper
        states[hid:, lanes] = lower
    low[:, at["states"] : at["states"] + n_b] = states[:hid, :n_b]
    rows = pl.ds(0, hid + 8)
    others = pl.ds(at["bias"], 2 * LANES)
    stores += start_copies(
        (
            piece(at["states"], n_b),
            (high.at[rows, pl.ds(0, n_mid)], high_out.at[rows, pl.ds(0, n_mid)]),
            (high.at[rows, others], high_out.at[rows, others]),
        ),
        sems,
        13,
    )
    for tile in range(own // LANES):
        window, totals = tile_counts(sz, window_ref, tile)
        total = dot(states[:, :n_b], window, (1, 0))
        average = ((total[:hid] + total[hid:]) / totals).astype(BF)
        x = join_inputs(sz, states[:hid, n_b + LANES * tile : n_b + LANES * (tile + 1)], average)
        first = at["inputs2"] + LANES * tile
        low[:, first : first + LANES] = x[:hid]
        low[:, first + own : first + own + LANES] = x[hid:]
        result, scale, state = first_layer(turned2, x, bias2)
        first = at["result2"] + LANES * tile
        high[:hid, first : first + LANES] = result
        high[hid:, first : first + LANES] = jnp.broadcast_to(scale, (8, LANES))
        upper, lower = two_parts(state)
        first = at["embed"] + LANES * tile
        low[:, first : first + LANES] = upper
        low[:, first + own : first + own + LANES] = lower
    last = pl.ds(at["result2"], own)
    tail = (piece(at["embed"], sz.low_lanes - at["embed"]), (high.at[rows, last], high_out.at[rows, last]))
    stores += start_copies(tail, sems, 16)
    serve, take, _, owned = seed_picks(sz, serve_rows[...], take_rows[...], part)
    embed_high = low[:, at["embed"] : at["embed"] + own]
    served = dot(serve.astype(BF), embed_high, (1, 1))
    taken = dot(take.astype(BF), embed_high, (1, 1))
    dead = (owned > 0.5) & (alive_column(sz, live_rows[...]) < 0.5)
    first = lax.broadcasted_iota(jnp.int32, (sz.slots, hid), 1) == 0
    value = jnp.concatenate([served, jnp.where(first & dead, SENTINEL, taken)], 1)
    value = value.reshape(sz.dp, 1, sz.slot, 2 * hid)
    value = jnp.broadcast_to(value, (sz.dp, 4, sz.slot, 2 * hid))
    sent[...] = value.reshape(4 * sz.slots, 2 * hid).astype(BF)
    wait_all(stores)


def sent_rows(sz, low, at, serve, take):
    embed_high = low[:, at : at + sz.own]
    embed_low = low[:, at + sz.own : at + 2 * sz.own]
    take = take.astype(BF)
    return jnp.concatenate(
        [dot(serve.astype(BF), embed_high, (1, 1)), dot(take, embed_high, (1, 1)), dot(take, embed_low, (1, 1))], 1
    )


def seeds_forward(sz, messages, counts, tables):
    hid = sz.hid
    tail = (sz.main, LANES * sz.blocks)
    return call(
        functools.partial(seeds_kernel, sz),
        [
            ((hid, sz.low_lanes), BF),
            ((hid + 8, sz.high_lanes), F32),
            ((4 * sz.slots, 2 * hid), BF),
        ],
        [
            ((2 * sz.hold, sz.n_mid), BF),
            ((sz.main * sz.blocks, LANES), F32),
            ((sz.main, sz.full_b), BF),
            ((sz.main, sz.full_b), BF),
            ((sz.main, sz.message_b), BF),
            (tail, BF),
            ((sz.count_rows * (sz.own // LANES), LANES), BF),
            *[(item.shape, jnp.int32) for item in tables],
            ((hid, sz.low_lanes), BF),
            ((hid + 8, sz.high_lanes), F32),
            ((2 * sz.main, LANES), F32),
            ((8 * sz.hold, hid), F32),
            ((2 * hid, hid), F32),
            ((2 * hid, sz.n_mid), BF),
        ],
        SEEDS_MIB,
        *messages,
        counts,
        *tables,
        far_in=(0, 1, 6, 7, 8, 9),
        loose=(2, 3, 4, 5),
        micros=4,
        far_out=(0, 1),
        copies=19,
    )


def rest_kernel(
    sz, low_in, high_in, counts_in, own_a, a1, a2, a3, e1, e2, e3, labels_in, weighting_in, head_in, part_out,
    labels, weighting, head_bias, low, xa, bias, counts, xo, c1, c2, c3, turn_ref,
    states, states2, result1, slope1, scale1, inputs2, result2, scale2, grad_a, low_grad, part_ref, sems,
):
    part = lax.axis_index("col")
    own, hid, n_a, n_b, hold = sz.own, sz.hid, sz.n_a, sz.n_b, sz.hold
    at = dict(sz.at)
    for name in ("turned1", "turned2", "weight2", "weight3", "turned3", "states", "embed"):
        at[name] -= sz.n_mid
    lanes = at["embed"] + own
    copies = start_copies(
        (
            (own_a, xo),
            *[(e.at[:, pl.ds(sz.n_mid, sz.early)], c.at[:, pl.ds(0, sz.early)]) for e, c in ((e1, c1), (e2, c2), (e3, c3))],
            *[
                (e.at[:, pl.ds(2 * sz.n_mid + sz.early, LANES)], c.at[:, pl.ds(sz.early, LANES)])
                for e, c in ((e1, c1), (e2, c2), (e3, c3))
            ],
            (low_in.at[:, pl.ds(sz.n_mid, hid)], low.at[:, pl.ds(0, hid)]),
            (high_in.at[:, pl.ds(sz.at["bias"], 2 * LANES)], bias),
            (low_in.at[:, pl.ds(sz.n_mid + hid, lanes - hid)], low.at[:, pl.ds(hid, lanes - hid)]),
            (counts_in, counts),
            (labels_in, labels),
            (weighting_in, weighting),
            (head_in, head_bias),
        ),
        sems,
    )
    late = (n_a - sz.early) // LANES
    for r, message in ((1, a1), (2, a2), (3, a3)):
        tail = unpack_tails(sz, message, 2 * n_a - sz.early, turn_ref)
        unpack_tiles(sz, message, tail, 0, late, hold * r, sz.early, xa)
        unpack_tiles(sz, message, tail, late, n_a // LANES, hold * (4 + r), 0, xa)
    wait_all(copies[:7])
    for r, before in ((1, c1), (2, c2), (3, c3)):
        tail = before[:, sz.early :].astype(F32)[sz.tiles_mid : sz.tiles_mid + EARLY]
        unpack_tiles(sz, before, tail, 0, EARLY, hold * r, 0, xa)
    xa[:hold, :] = xo[:hold, :]
    xa[4 * hold : 5 * hold, :] = xo[hold:, :]
    wait_all(copies[7:9])
    turned1 = low[:, at["turned1"] : at["turned1"] + hid]
    bias1 = bias[:hid, :LANES]
    bias2 = bias[:hid, LANES:]

    result1[...] = dot(turned1, xa[...], (1, 0))

    def forward_step(index, carry):
        lanes = pl.ds(aligned(index * LANES), LANES)
        result = result1[:, lanes] + bias1
        gate = sigmoid(result)
        active = result * gate
        scale = lax.rsqrt(jnp.sum(active * active, 0, keepdims=True) + ROW_EPS)
        result1[:, lanes] = active
        slope1[:, lanes] = gate + active * (1.0 - gate)
        scale1[:, lanes] = scale
        upper, lower = two_parts(active * scale)
        states[:hid, lanes] = upper
        states[hid:, lanes] = lower
        return carry

    lax.fori_loop(0, n_a // LANES, forward_step, 0, unroll=7)
    wait_all(copies[9:])
    turned2 = low[:, at["turned2"] : at["turned2"] + 2 * hid]
    for tile in range(sz.tiles_b):
        lanes = slice(LANES * tile, LANES * (tile + 1))
        window, totals = tile_counts(sz, counts, tile)
        total = dot(states[:, 4 * LANES * tile : 4 * LANES * tile + WINDOW], window, (1, 0))
        average = ((total[:hid] + total[hid:]) / totals).astype(BF)
        inputs2[:, lanes] = join_inputs(sz, low[:, at["states"] + LANES * tile : at["states"] + LANES * (tile + 1)], average)
    result2[...] = dot(turned2, inputs2[...], (1, 0))
    for tile in range(sz.tiles_b):
        lanes = slice(LANES * tile, LANES * (tile + 1))
        result, scale, state = activate(result2[:, lanes] + bias2)
        result2[:, lanes] = result
        scale2[:, lanes] = scale
        upper, lower = two_parts(state)
        states2[:hid, lanes] = upper
        states2[hid:, lanes] = lower
    counts3, totals3 = tile_counts(sz, counts, sz.tiles_b)
    total = dot(states2[...], counts3, (1, 0))
    average = ((total[:hid] + total[hid:]) / totals3).astype(BF)
    inputs3 = join_inputs(sz, low[:, at["embed"] : at["embed"] + own], average)

    columns = pl.ds(aligned(own * part), own)
    classes = lax.broadcasted_iota(jnp.int32, (sz.head, own), 0)
    head_row = jnp.concatenate([head_bias[...], jnp.zeros((1, LANES - sz.classes), F32)], 1)
    head_column = jnp.broadcast_to(head_row, (LANES, LANES)).T[: sz.head]
    logits = dot(low[: sz.head, at["turned3"] : at["turned3"] + 2 * hid], inputs3, (1, 0)) + head_column
    logits = jnp.where(classes < sz.classes, logits, -1e30)
    highest = jnp.max(logits, 0, keepdims=True)
    expo = jnp.exp(logits - highest)
    totals = jnp.sum(expo, 0, keepdims=True)
    hit = classes == labels[:, columns]
    weights = weighting[:, columns].astype(F32)
    target = jnp.sum(jnp.where(hit, logits, 0.0), 0, keepdims=True)
    ce_total = jnp.sum(weights * (highest + jnp.log(totals) - target), 1, keepdims=True)
    seed_count = jnp.sum(weights, 1, keepdims=True)
    grad_logits = (weights * (expo / totals - jnp.where(hit, 1.0, 0.0))).astype(BF)
    g3 = at["g3"]
    part_ref[: sz.head, g3 : g3 + 2 * hid] = dot(grad_logits, inputs3, (1, 1))
    head_sums = jnp.concatenate([row_sums(grad_logits), jnp.zeros((16, LANES - sz.head), F32)], 1)
    part_ref[sz.head + 16 : sz.head + 32, g3 : g3 + LANES] = head_sums
    lane_at = lax.broadcasted_iota(jnp.int32, (16, LANES), 1)
    sums = jnp.where(lane_at == 0, ce_total, jnp.where(lane_at == 1, seed_count, 0.0))
    part_ref[sz.head + 16 : sz.head + 32, g3 + LANES : g3 + 2 * LANES] = sums
    own_part, average_part = split_inputs(sz, dot(halves(low, at["weight3"], LANES)[:, : sz.head], grad_logits, (1, 0)))
    part_ref[:hid, at["grad_embed"] : at["grad_embed"] + own] = own_part
    grad_mid = spread(sz, average_part / totals3, counts3)
    low_grad2 = norm_backward(grad_mid, result2[...], scale2[...])
    g2 = dot(inputs2[...], low_grad2, (1, 1))
    part_ref[:hid, at["g2"] : at["g2"] + hid] = g2[:hid]
    part_ref[:hid, at["g2"] + hid : at["g2"] + 2 * hid] = g2[hid:]
    part_ref[sz.head : sz.head + 16, g3 + hid : g3 + 2 * hid] = row_sums(low_grad2)
    weight2 = halves(low, at["weight2"], hid)
    own_part, average_part = split_inputs(sz, dot(weight2, low_grad2, (1, 0)))
    part_ref[:hid, at["grad_b"] : at["grad_b"] + n_b] = own_part
    for tile in range(sz.tiles_b):
        window, totals = tile_counts(sz, counts, tile)
        added = spread(sz, average_part[:, LANES * tile : LANES * (tile + 1)] / totals, window)
        first = 4 * LANES * tile
        shared = slice(first, first + LANES)
        grad_a[:, shared] = added[:, :LANES] + grad_a[:, shared] if tile else added[:, :LANES]
        grad_a[:, first + LANES : first + WINDOW] = added[:, LANES:]
    rows, few = pl.ds(0, hid + 8), pl.ds(0, sz.head + 32)
    split = at["g2"]
    stores = start_copies(
        (
            (part_ref.at[rows, pl.ds(split, hid * 2)], part_out.at[rows, pl.ds(split, hid * 2)]),
            (
                part_ref.at[rows, pl.ds(at["grad_b"], n_b + own)],
                part_out.at[rows, pl.ds(at["grad_b"], n_b + own)],
            ),
        ),
        sems,
        14,
    )

    def backward_step(index, carry):
        lanes = pl.ds(aligned(index * LANES), LANES)
        scale = scale1[:, lanes]
        inner = jnp.zeros((8, LANES), F32)
        for row in range(0, hid, 8):
            rows = slice(row, row + 8)
            inner = inner + grad_a[rows, lanes] * result1[rows, lanes]
        inner = scale * scale * scale * jnp.sum(inner, 0, keepdims=True)
        for row in range(0, hid, 16):
            rows = slice(row, row + 16)
            grad = scale * grad_a[rows, lanes] - inner * result1[rows, lanes]
            low_grad[rows, lanes] = (grad * slope1[rows, lanes]).astype(BF)
        return carry

    lax.fori_loop(0, n_a // LANES, backward_step, 0, unroll=7)
    part_ref[:hid, at["g1"] : at["g1"] + hid] = dot(xa[...], low_grad[...], (1, 1))
    part_ref[sz.head : sz.head + 16, g3 : g3 + hid] = row_sums(low_grad[...])
    stores += start_copies(
        (
            (part_ref.at[rows, pl.ds(0, hid)], part_out.at[rows, pl.ds(0, hid)]),
            (part_ref.at[few, pl.ds(g3, 2 * hid)], part_out.at[few, pl.ds(g3, 2 * hid)]),
        ),
        sems,
        16,
    )
    wait_all(stores)


def rest_step(sz, low, high, counts, means, labels, weighting, head_bias):
    hid = sz.hid
    return call(
        functools.partial(rest_kernel, sz),
        [((hid + 8, sz.part_lanes), F32)],
        [
            (labels.shape, jnp.int32),
            (weighting.shape, jnp.int32),
            (head_bias.shape, F32),
            ((hid, sz.at["embed"] + sz.own - sz.n_mid), BF),
            ((hid, sz.n_a), BF),
            ((hid + 8, 2 * LANES), F32),
            (counts.shape, BF),
            ((2 * sz.hold, sz.n_a), BF),
            *[((sz.main, sz.early + LANES), BF)] * 3,
            ((2 * sz.main, LANES), F32),
            ((2 * hid, sz.n_a), BF),
            ((2 * hid, sz.n_b), BF),
            ((hid, sz.n_a), F32),
            ((hid, sz.n_a), F32),
            ((1, sz.n_a), F32),
            ((2 * hid, sz.n_b), BF),
            ((hid, sz.n_b), F32),
            ((1, sz.n_b), F32),
            ((hid, sz.n_a), F32),
            ((hid, sz.n_a), BF),
            ((hid + 8, sz.part_lanes), F32),
        ],
        REST_MIB,
        low,
        high,
        counts,
        *means,
        labels,
        weighting,
        head_bias,
        far_in=(0, 1, 2, 3, 10, 11, 12),
        loose=(7, 8, 9),
        micros=14,
        far_out=(0,),
        copies=18,
    )[0]


def seeds_back_kernel(
    sz, serve_in, take_in, live_in, received, low_in, high_in, counts_in, part_in, keep0, keep1, send,
    serve_rows, take_rows, live_rows, x_ref, weight_ref, low, high, window_ref, partial, g1_ref, g2_ref, gb_ref, stage, sems,
):
    part = lax.axis_index("col")
    own, hid, group, n_b, n_mid = sz.own, sz.hid, sz.group, sz.n_b, sz.n_mid
    at = dict(sz.at)
    at["inputs2"] -= at["embed"]
    split = at["grad_b"]
    few = pl.ds(0, sz.head + 32)
    lanes = pl.ds(at["result2"], own)
    copies = start_copies(
        (
            (serve_in, serve_rows),
            (take_in, take_rows),
            (live_in, live_rows),
            (low_in.at[:, pl.ds(at["embed"], 4 * own)], low),
            (part_in.at[:, pl.ds(split + n_b, own)], partial.at[:, pl.ds(split + n_b, own)]),
            (high_in.at[:, lanes], high.at[:, lanes]),
            (low_in.at[:, pl.ds(at["weight2"], 2 * hid)], weight_ref),
            (counts_in.at[sz.seed_window(), :], window_ref),
            (part_in.at[:, pl.ds(split, n_b)], partial.at[:, pl.ds(split, n_b)]),
            (high_in.at[:, pl.ds(0, n_mid)], high.at[:, pl.ds(0, n_mid)]),
            (low_in.at[:, pl.ds(0, n_mid)], x_ref),
            (part_in.at[:, pl.ds(0, at["g3"])], partial.at[:, pl.ds(0, at["g3"])]),
            (part_in.at[few, pl.ds(at["g3"], 2 * hid)], partial.at[few, pl.ds(at["g3"], 2 * hid)]),
        ),
        sems,
    )
    arrived = received[...].astype(F32).reshape(sz.dp, 4, sz.slot, 2 * hid)
    arrived = jnp.sum(arrived, 1).reshape(sz.slots, 2 * hid)
    at["embed"] = 0
    wait_all(copies[:4])
    serve, take, served, taken = seed_picks(sz, serve_rows[...], take_rows[...], part)
    mine = sent_rows(sz, low, 0, serve, take)
    theirs = arrived[:, hid:]
    alive_there = theirs[:, 0:1] < 0.5 * SENTINEL
    differ = mine[:, hid : 2 * hid] + mine[:, 2 * hid :] - arrived[:, :hid]
    differ = jnp.where((taken > 0.5) & (alive_column(sz, live_rows[...]) > 0.5), differ, 0.0)
    dist_total = DIST_WEIGHT * jnp.sum(jnp.sum(differ * differ, 0, keepdims=True), 1, keepdims=True)
    local_high, local_low = two_parts(2.0 * DIST_WEIGHT * differ)
    back = jnp.where((served > 0.5) & alive_there, theirs - mine[:, :hid], 0.0)
    back = (-2.0 * DIST_WEIGHT * back).astype(BF)
    take = take.astype(BF)
    serve = serve.astype(BF)
    wait_all(copies[4:6])
    grad = partial[:hid, at["grad_embed"] : at["grad_embed"] + own]
    grad = grad + dot(local_high, take, (0, 0)) + dot(local_low, take, (0, 0)) + dot(back, serve, (0, 0))
    lanes = slice(at["result2"], at["result2"] + own)
    low_grad2 = norm_backward(grad, high[:hid, lanes], high[hid:, lanes][0:1])
    wait_all(copies[6:9])
    weight2 = halves(weight_ref, 0, hid)
    own_part, average_part = split_inputs(sz, dot(weight2, low_grad2, (1, 0)))
    total_b = partial[:hid, at["grad_b"] : at["grad_b"] + n_b]
    for tile in range(own // LANES):
        window, totals = tile_counts(sz, window_ref, tile)
        total_b = total_b + spread(sz, average_part[:, LANES * tile : LANES * (tile + 1)] / totals, window)
    wait_all(copies[9:10])
    low_grad = jnp.concatenate(
        [
            norm_backward(total_b, high[:hid, :n_b], high[hid:, :n_b][0:1]),
            norm_backward(own_part, high[:hid, n_b:n_mid], high[hid:, n_b:n_mid][0:1]),
        ],
        1,
    )
    wait_all(copies[10:])
    added = dot(halves(low, at["inputs2"], own), low_grad2, (1, 1))
    for half in range(2):
        lanes = slice(at["g2"] + hid * half, at["g2"] + hid * (half + 1))
        g2_ref[hid * half : hid * (half + 1), :] = partial[:hid, lanes] + added[hid * half : hid * (half + 1)]
    g3 = at["g3"]
    sums = partial[sz.head : sz.head + 16, g3 : g3 + 2 * hid]
    gb_ref[:, hid:] = sums[:, hid:] + row_sums(low_grad2)
    half = 4 * sz.hold
    g1_ref[...] = partial[:hid, at["g1"] : at["g1"] + hid] + dot(x_ref[...], low_grad, (1, 1))
    gb_ref[:, :hid] = sums[:, :hid] + row_sums(low_grad)
    head_row = partial[sz.head + 16 : sz.head + 32, g3 : g3 + LANES]
    totals = partial[sz.head + 16 : sz.head + 32, g3 + LANES : g3 + 2 * LANES]
    lane_at = lax.broadcasted_iota(jnp.int32, (16, LANES), 1)
    fixed = ((totals[0:1, 0:1] + dist_total) * float(2**LOSS_BITS) + 0.5).astype(jnp.int32)
    count = totals[0:1, 1:2].astype(jnp.int32)
    whole = jnp.where(lane_at < 32, fixed, count)
    bits = (lax.shift_right_logical(whole, lane_at & 31) & 1).astype(F32)
    bits = jnp.where(lane_at < 64, bits, 0.0)
    stage[sz.misc :, :] = jnp.zeros((sz.pay - sz.misc, LANES), F32)
    for r, (target_ref, base) in enumerate(((keep0, 0), (send, 0), (keep1, 0), (send, sz.pay))):
        shard = part ^ r
        block2 = pl.ds(pl.multiple_of(2 * group * shard, 2 * group), 2 * group)
        for h in range(hid // LANES):
            lanes = slice(LANES * h, LANES * (h + 1))
            for s in range(2):
                first, row = half * s + sz.hold * r, sz.feat * (2 * h + s)
                stage[row : row + sz.feat, :] = g1_ref[first : first + sz.feat, lanes]
            row = sz.rows_one + 2 * group * h
            stage[row : row + 2 * group, :] = g2_ref[block2, lanes]
        third = partial[: sz.head, pl.ds(aligned(g3 + 2 * group * shard), LANES)]
        stage[sz.at_three : sz.misc, :] = third[: sz.classes]
        odd = (shard % 2) == 1
        block = aligned((shard // 2) * LANES)
        one = gb_ref[:, pl.ds(block, LANES)]
        two = gb_ref[:, pl.ds(aligned(hid + block), LANES)]
        one = jnp.where(odd, pltpu.roll(one, group, 1), one)
        two = jnp.where(odd, two, pltpu.roll(two, group, 1))
        bias_row = jnp.where(lane_at < group, one, two)[0:1]
        rows = [bias_row, head_row[0:1], bits[0:1]]
        rows += [item - item.astype(BF).astype(F32) for item in rows[:2]]
        for i, item in enumerate(rows):
            stage[sz.misc + i : sz.misc + i + 1, :] = item
        target_ref[base : base + sz.pay, :] = stage[...].astype(BF)


def seeds_backward(sz, tables, received, low, high, counts, partial):
    hid = sz.hid
    return call(
        functools.partial(seeds_back_kernel, sz),
        [((sz.pay, LANES), BF), ((sz.pay, LANES), BF), ((2 * sz.pay, LANES), BF)],
        [
            *[(item.shape, jnp.int32) for item in tables],
            ((hid, sz.n_mid), BF),
            ((hid, 2 * hid), BF),
            ((hid, 4 * sz.own), BF),
            ((hid + 8, sz.high_lanes), F32),
            ((sz.count_rows * (sz.own // LANES), LANES), BF),
            ((hid + 8, sz.part_lanes), F32),
            ((8 * sz.hold, hid), F32),
            ((2 * hid, hid), F32),
            ((16, 2 * hid), F32),
            ((sz.pay, LANES), F32),
        ],
        BACK_MIB,
        *tables,
        received,
        low,
        high,
        counts,
        partial,
        far_in=(0, 1, 2, 4, 5, 6, 7),
        micros=3,
        copies=13,
    )


def unpacked(sz, grad, one_ref, three_ref):
    group = sz.group

    def wide(at, rows):
        return jnp.concatenate([grad[at : at + rows, :], grad[at + rows : at + 2 * rows, :]], 1)

    one = wide(0, 2 * sz.feat)
    three = grad[sz.at_three : sz.misc, :]
    turned = pltpu.roll(three, group, 1)
    for f in range(sz.feat):
        one_ref[f, 0:1, :] = one[f : f + 1]
        one_ref[f, 1:2, :] = one[sz.feat + f : sz.feat + f + 1]
    for c in range(sz.classes):
        three_ref[c, 0:1, :] = three[c : c + 1, :group]
        three_ref[c, 1:2, :] = turned[c : c + 1, :group]
    misc = grad[sz.misc : sz.misc + 5, :]
    fine = misc[0:2] + misc[3:5]
    hidden = jnp.concatenate([fine[0:1, :group], fine[0:1, group : 2 * group]], 0)
    two = wide(sz.rows_one, 2 * group).reshape(2, group, sz.hid)
    return (one_ref[...], two, three_ref[...], hidden, fine[1:2, : sz.classes]), misc[2:3]


def new_moments(first, second, g):
    return BETA_ONE * first + (1.0 - BETA_ONE) * g, BETA_TWO * second + (1.0 - BETA_TWO) * g * g


def lamb_kernel(sz, grad, *rest):
    params, firsts, seconds, updates = rest[:5], rest[5:10], rest[10:15], rest[15:20]
    sums_ref, totals_ref, one_ref, three_ref = rest[20:]
    grads, bits_row = unpacked(sz, grad, one_ref, three_ref)
    lane_at = lax.broadcasted_iota(jnp.int32, (8, LANES), 1)
    row_at = lax.broadcasted_iota(jnp.int32, (8, LANES), 0)
    sums = jnp.zeros((8, LANES), F32)
    for i in range(5):
        w = params[i][...]
        m, v = new_moments(firsts[i][...], seconds[i][...], grads[i])
        u = (m / (1.0 - BETA_ONE**STEP)) / (jnp.sqrt(v / (1.0 - BETA_TWO**STEP)) + ADAM_EPS) + DECAY_RATE * w
        updates[i][...] = u
        for row, item in ((0, w), (1, u)):
            item = item * item
            if i < 3:
                item = jnp.sum(item, 0)
            total = jnp.sum(jnp.sum(item, 0, keepdims=True), 1, keepdims=True)
            if i == 4:
                total = 0.25 * total
            sums = jnp.where((lane_at == i) & (row_at == row), total, sums)
    sums_ref[...] = sums
    power = (1 << (lane_at & 15)).astype(F32)
    power = jnp.where((lane_at & 31) < 16, power, power * float(2**16))
    bits = jnp.broadcast_to(bits_row, (8, LANES)) * power
    loss = jnp.sum(jnp.where(lane_at < 32, bits, 0.0), 1, keepdims=True) * float(2.0**-LOSS_BITS)
    count = jnp.sum(jnp.where((lane_at >= 32) & (lane_at < 64), bits, 0.0), 1, keepdims=True)
    totals_ref[...] = jnp.where(lane_at == 0, loss, count)


def moments_kernel(sz, grad, *rest):
    firsts, seconds, moments, squares = rest[:5], rest[5:10], rest[10:15], rest[15:20]
    grads, _ = unpacked(sz, grad, *rest[20:])
    for i in range(5):
        moments[i][...], squares[i][...] = new_moments(firsts[i][...], seconds[i][...], grads[i])


def lamb(sz, grad, params, firsts, seconds):
    like = [(item.shape, F32) for item in params]
    scratch = [(params[0].shape, F32), (params[2].shape, F32)]
    outs = call(
        functools.partial(lamb_kernel, sz),
        like + [((8, LANES), F32)] * 2,
        scratch,
        6,
        grad,
        *params,
        *firsts,
        *seconds,
        micros=1,
    )
    moments = call(functools.partial(moments_kernel, sz), like * 2, scratch, 6, grad, *firsts, *seconds, micros=2)
    return outs, moments


def step_kernel(own, far, w1, w2, w3, wh, wb, u1, u2, u3, uh, ub, n1, n2, n3, nh, nb, norms_ref):
    norms = jnp.sqrt(own[...] + far[...])
    norms_ref[...] = norms[0:2, 0:5]
    for i, (w, u, n) in enumerate(
        ((w1, u1, n1), (w2, u2, n2), (w3, u3, n3), (wh, uh, nh), (wb, ub, nb))
    ):
        ratio = LEARN_RATE * (norms[0:1, i : i + 1] / norms[1:2, i : i + 1])
        n[...] = w[...] - ratio * u[...]


def take_step(sums, params, updates):
    return call(
        step_kernel,
        [(item.shape, F32) for item in params] + [((2, 5), F32)],
        [],
        3,
        *sums,
        *params,
        *updates,
    )


def swap(value, axis, count, bit):
    return lax.ppermute(value, axis, [(i, i ^ bit) for i in range(count)])


def merged(own, other):
    return lax.reduce_precision(own.astype(F32) + other.astype(F32), 8, 7)


def shards(
    features, neighbors_one, present_one, neighbors_two, present_two, neighbors_three, present_three,
    labels, seed_weight, serve_rows, take_seed, fetch_live,
    weight_one, weight_two, weight_three, hidden_bias, head_bias,
    first_one, first_two, first_three, first_hidden, first_head,
    second_one, second_two, second_three, second_hidden, second_head,
):
    sz = Sizes(features, neighbors_one, neighbors_two, neighbors_three, weight_two, weight_three, serve_rows)

    def tree(one, two, three, hidden, head):
        return (one.transpose(1, 0, 2), two, three.transpose(2, 0, 1), hidden, head[None, :])

    def back(one, two, three, hidden, head):
        return (one.transpose(1, 0, 2), two, three.transpose(1, 2, 0), hidden, head[0])

    params = tree(weight_one, weight_two, weight_three, hidden_bias, head_bias)
    firsts = tree(first_one, first_two, first_three, first_hidden, first_head)
    seconds = tree(second_one, second_two, second_three, second_hidden, second_head)

    own_b, packed, mean, tail, *sent = first_messages(sz, features, neighbors_one, present_one, *params[:4])
    s1, s2, s3 = [swap(sent[r - 1], "col", 4, r) for r in (1, 2, 3)]
    links = (neighbors_two, present_two, neighbors_three, present_three)
    own_a, counts, *means = mean_messages(sz, features, neighbors_one, present_one, mean, tail, links)
    s1, *means = lax.optimization_barrier((s1, *means))
    means = [swap(means[r - 1], "col", 4, r) for r in (1, 2, 3)]
    later, s3, counts = lax.optimization_barrier((s2, s3, counts))
    passed = swap(later, "col", 4, 1)
    tables = (serve_rows, take_seed, fetch_live[None, :])
    low, high, rows = seeds_forward(sz, (own_b, packed, s1, s2, s3, passed), counts, tables)
    received = lax.all_to_all(rows, ("dp", "col"), split_axis=0, concat_axis=0, tiled=True)
    partial = rest_step(sz, low, high, counts, (own_a, *means, s1, s2, s3), labels[None, :], seed_weight[None, :], head_bias[None, :])
    keep0, keep1, send = seeds_backward(sz, tables, received, low, high, counts, partial)
    other = swap(send, "col", 4, 1)
    own = merged(keep0, other[: sz.pay]).astype(BF)
    far = merged(keep1, other[sz.pay :]).astype(BF)
    pair = [[(d, c), (d ^ 1, c ^ 2)] for d in range(sz.dp) for c in range(4)]
    pair = [(a * 4 + b, c * 4 + d) for (a, b), (c, d) in pair]
    near = (swap(far, "col", 4, 2), swap(own, "dp", sz.dp, 1), lax.ppermute(far, ("dp", "col"), pair))
    near = [item.astype(F32) for item in (own, *near)]
    grad = lax.reduce_precision((near[0] + near[1]) + (near[2] + near[3]), 8, 7)
    bit = 2
    while bit < sz.dp:
        grad = merged(grad, swap(grad.astype(BF), "dp", sz.dp, bit))
        bit *= 2
    outs, moments = lamb(sz, grad, params, firsts, seconds)
    moments, squares, updates = moments[:5], moments[5:], outs[:5]
    sums, totals = outs[5], outs[6]
    pair = sums + swap(sums, "col", 4, 1)
    fresh = take_step([pair, swap(pair, "col", 4, 2)], params, updates)
    return (*back(*fresh[:5]), *back(*moments), *back(*squares), fresh[5], totals[0, 0], totals[0, 1])


def solution(mesh):
    wide = P(None, "col", None)
    tree = [wide, wide, wide, P(None, "col"), P()]
    return jax.shard_map(
        shards,
        mesh=mesh,
        in_specs=(
            P("col", "dp"),
            *[P(None, "dp")] * 6,
            P("dp"),
            P("dp"),
            P("dp", None),
            P("dp", None),
            P("dp"),
            *tree,
            *tree,
            *tree,
        ),
        out_specs=(*tree, *tree, *tree, P(), P(), P()),
        check_vma=False,
    )
```

```python
import functools

import jax
import jax.numpy as jnp
from jax import lax
from jax.experimental import pallas as pl
from jax.experimental.pallas import tpu as pltpu
from jax.sharding import PartitionSpec as P

REACH = 64
STEP = 5
DIST_WEIGHT = 1.0
ROW_EPS = 1e-06
LEARN_RATE = 0.5
BETA_ONE = 0.9
BETA_TWO = 0.999
ADAM_EPS = 1e-06
DECAY_RATE = 0.01

BF = jnp.bfloat16
F32 = jnp.float32
LANES = 128
WINDOW = 640
HALF = 64
FRONT = 320
SENTINEL = 4.0
MIB = 2**20
LOSS_BITS = 14
EARLY = 4
FIRST_MIB = 8
MEAN_MIB = 8
SEEDS_MIB = 16
REST_MIB = 28
BACK_MIB = 12


def cost(micros):
    return pl.CostEstimate(flops=int(micros * 10**9), bytes_accessed=1, transcendentals=0)


def call(kernel, outs, scratch, mib, *args, far_in=(), far_out=(), copies=0, micros=1, loose=(), name=None):
    near = pl.BlockSpec(memory_space=pltpu.VMEM)
    far = pl.BlockSpec(memory_space=pltpu.HBM)
    free = pl.BlockSpec(memory_space=pl.ANY)
    scratch = [pltpu.VMEM(shape, kind) for shape, kind in scratch]
    args = [pltpu.with_memory_space_constraint(a, pltpu.HBM) if i in far_in else a for i, a in enumerate(args)]
    return pl.pallas_call(
        kernel,
        in_specs=[free if i in loose else far if i in far_in else near for i in range(len(args))],
        out_specs=tuple(far if i in far_out else near for i in range(len(outs))),
        out_shape=tuple(
            pltpu.HBM(shape, kind) if i in far_out else jax.ShapeDtypeStruct(shape, kind)
            for i, (shape, kind) in enumerate(outs)
        ),
        scratch_shapes=scratch + ([pltpu.SemaphoreType.DMA((copies,))] if copies else []),
        compiler_params=pltpu.CompilerParams(vmem_limit_bytes=mib * MIB),
        cost_estimate=cost(micros),
        name=name,
    )(*args)


def start_copies(pairs, sems, first=0):
    copies = [pltpu.make_async_copy(src, dst, sems.at[first + i]) for i, (src, dst) in enumerate(pairs)]
    for copy in copies:
        copy.start()
    return copies


def wait_all(copies):
    for copy in copies:
        copy.wait()


class Sizes:
    def __init__(self, features, neighbors_one, neighbors_two, neighbors_three, weight_two, weight_three, serve_rows):
        self.feat = features.shape[0]
        self.main = self.feat - 1
        self.hold = 32
        self.base = features.shape[1]
        self.low = neighbors_one.shape[1]
        self.mid = neighbors_two.shape[1]
        self.seeds = neighbors_three.shape[1]
        self.hid = weight_two.shape[2]
        self.group = weight_two.shape[1]
        self.classes = weight_three.shape[2]
        self.head = -(-self.classes // 16) * 16
        self.own = self.seeds // 4
        self.n_b = 4 * self.own + LANES
        self.n_a = 16 * self.own + 5 * LANES
        self.n_mid = self.n_b + self.own
        self.n_low = self.n_a + self.n_mid
        self.tiles_b = self.n_b // LANES
        self.tiles_mid = self.n_mid // LANES
        self.tiles_low = self.n_low // LANES
        self.slots = serve_rows.shape[0] * serve_rows.shape[1]
        self.slot = serve_rows.shape[1]
        self.dp = serve_rows.shape[0]
        self.rows_one = 2 * 2 * self.feat
        self.rows_two = 4 * self.group
        self.at_three = self.rows_one + self.rows_two
        self.misc = self.at_three + self.classes
        self.pay = -(-(self.misc + 5) // 16) * 16
        self.blocks = -(-(self.misc + 3) // self.main)
        self.early = EARLY * LANES
        self.message_a = self.pair_lanes(self.n_a, self.n_a - self.early)
        self.message_b = self.pair_lanes(self.n_mid, self.n_mid + self.early)
        self.full_b = self.message_b + LANES * self.blocks
        self.tiles_b_all = 16 * self.own // LANES + 1
        self.tiles_all = self.low // LANES + 8
        self.count_rows = WINDOW + 16
        hid, at = self.hid, self.n_mid
        places = {}
        for name, lanes in (
            ("turned1", hid), ("turned2", 2 * hid), ("weight2", 2 * hid), ("weight3", 2 * LANES), ("turned3", 2 * hid),
            ("states", self.n_b), ("embed", 2 * self.own), ("inputs2", 2 * self.own),
        ):
            places[name] = at
            at += lanes
        self.low_lanes = at
        at = 0
        for name, lanes in (("result1", self.n_mid), ("result2", self.own), ("bias", 2 * LANES)):
            places[name] = at
            at += lanes
        self.high_lanes = at
        at = 0
        for name, lanes in (("g1", hid), ("g2", 2 * hid), ("g3", 2 * hid), ("grad_b", self.n_b), ("grad_embed", self.own)):
            places[name] = at
            at += lanes
        self.part_lanes = at
        self.at = places

    def pair_lanes(self, means, own):
        lanes = means + own
        return lanes + LANES * -(-lanes // LANES // self.main)

    def first_ranges(self, part):
        a, b, c = self.ranges(part)
        b = (b[0], 0, b[2])
        c = (c[0], b[2], c[2])
        return [b, c, (a[0], self.n_mid, self.early)], [b, c]

    def second_ranges(self, part):
        first = 16 * self.own * part
        return [(first + self.early, 0, self.n_a - self.early)], [(first, 0, self.n_a)]

    def a_row(self, part):
        return 16 * self.own * part - FRONT

    def b_row(self, part):
        return 4 * self.own * part - HALF

    def seed_window(self):
        rows = self.count_rows * (self.own // LANES)
        return pl.ds(self.count_rows * self.tiles_b + rows, rows)

    def ranges(self, part):
        return (
            (16 * self.own * part, 0, self.n_a),
            (self.b_row(part) + FRONT, self.n_a, self.n_b),
            (self.own * part + FRONT, self.n_a + self.n_b, self.own),
        )


def dot(a, b, over):
    return lax.dot_general(a, b, (((over[0],), (over[1],)), ((), ())), preferred_element_type=F32)


def two_parts(value):
    high = value.astype(BF)
    return high, (value - high.astype(F32)).astype(BF)


def three_parts(value):
    high = value.astype(BF).astype(F32)
    rest = value - high
    middle = rest.astype(BF).astype(F32)
    return high, middle, (rest - middle).astype(BF).astype(F32)


def aligned(value):
    return pl.multiple_of(value, LANES)


def sigmoid(value):
    return 0.5 * jnp.tanh(0.5 * value) + 0.5


def unpack_tile(sz, message, tail, tile):
    spare = jnp.zeros((sz.hold - sz.feat, LANES), F32)
    main = message[:, LANES * tile : LANES * (tile + 1)].astype(F32)
    return jnp.concatenate([main, tail[tile : tile + 1, :], spare], 0).astype(BF)


def half_tiles(left, right):
    lane = lax.broadcasted_iota(jnp.int32, left.shape, 1)
    return jnp.where(lane < HALF, pltpu.roll(left, HALF, 1), pltpu.roll(right, HALF, 1))


def half_columns(ref, tile, tiles, spare):
    if isinstance(tile, int):
        left, right = max(tile - 1, 0), min(tile, tiles - 1)
        left, right = [ref[:, LANES * i : LANES * (i + 1)] for i in (left, right)]
        left = left if tile > 0 else jnp.full_like(left, spare)
        right = right if tile < tiles else jnp.full_like(right, spare)
        return half_tiles(left, right)
    left = ref[:, pl.ds(aligned(jnp.maximum(tile - 1, 0) * LANES), LANES)]
    right = ref[:, pl.ds(aligned(jnp.minimum(tile, tiles - 1) * LANES), LANES)]
    left = jnp.where(tile > 0, left, spare)
    right = jnp.where(tile < tiles, right, spare)
    return half_tiles(left, right)


def take_tile(ref, rows, first, half):
    if not half:
        return ref[:rows, pl.ds(aligned(first), LANES)].astype(F32)
    first = first - HALF
    left = ref[:rows, pl.ds(aligned(first), LANES)].astype(F32)
    return half_tiles(left, ref[:rows, pl.ds(aligned(first + LANES), LANES)].astype(F32))


def take_tail(ref, first, half):
    if not half:
        return ref[pl.ds(first // LANES, 1), :]
    row = (first - HALF) // LANES
    return half_tiles(ref[pl.ds(row, 1), :], ref[pl.ds(row + 1, 1), :])


def fill_own(sz, feat_ref, self_ref, self_tail, places):
    spare = jnp.zeros((sz.hold - sz.feat, LANES), F32)
    zeros = jnp.zeros((sz.feat, LANES), BF)
    count = min(sz.low, feat_ref.shape[1]) // LANES
    lane = lax.broadcasted_iota(jnp.int32, (sz.feat, LANES), 1)
    shift = FRONT // LANES
    before = zeros
    for place in range(places):
        tile = place - shift
        after = zeros
        if tile >= 0 and tile < count:
            after = pltpu.roll(feat_ref[:, LANES * tile : LANES * (tile + 1)], HALF, 1)
        value = jnp.where(lane < HALF, before.astype(F32), after.astype(F32))
        self_tail[place : place + 1, :] = value[sz.main : sz.feat]
        self_ref[:, LANES * place : LANES * (place + 1)] = jnp.concatenate([value, spare], 0).astype(BF)
        before = after


def mean_tiles(sz, begin, tiles, feat_ref, nbr_ref, pres_ref, links_ref, present_ref, mean_ref, tail_ref, base_ref, code_ref, count_ref):
    last = feat_ref.shape[1] // LANES - 6
    slots = nbr_ref.shape[0]
    base_ref[...] = jnp.zeros_like(base_ref)
    if begin % 8 or tiles % 8:
        code_ref[...] = jnp.full_like(code_ref, -1)
        count_ref[...] = jnp.ones_like(count_ref)
    for tile in range(feat_ref.shape[1] // LANES):
        row = feat_ref[:, LANES * tile : LANES * (tile + 1)].astype(F32)
        base_ref[8 + tile : 9 + tile, :] = row[sz.main : sz.feat]

    for table, shifted in ((nbr_ref, links_ref), (pres_ref, present_ref)):
        count = table.shape[1] // LANES
        for tile in range(begin, tiles):
            shifted[:, LANES * tile : LANES * (tile + 1)] = half_columns(table, tile, count, 0)

    def one_tile(step, carry):
        lanes = pl.ds(aligned(step * LANES), LANES)
        present = present_ref[:, lanes]
        valid = present.astype(F32)
        counts = jnp.maximum(jnp.sum(valid, 0, keepdims=True), 1.0)
        first = jnp.clip(4 * step - 3, 0, last)
        links = links_ref[:, lanes]
        code = jnp.where(present > 0, links, -1)
        count_ref[pl.ds(step, 1), :] = counts
        for slot in range(slots):
            code_ref[slot, pl.ds(step, 1), :] = code[slot : slot + 1]
        local = links - first * LANES
        piece = local >> 7
        spot = local & 127
        sources = [
            feat_ref[:, pl.ds(aligned((first + j) * LANES), LANES)].astype(F32) for j in range(6)
        ]
        totals = [jnp.zeros((8, LANES), F32) for _ in range(sz.main // 8)]
        for slot in range(slots):
            spots = jnp.broadcast_to(spot[slot : slot + 1], (8, LANES))
            pieces = jnp.broadcast_to(piece[slot : slot + 1], (8, LANES))
            marks = jnp.broadcast_to(valid[slot : slot + 1], (8, LANES))
            for h in range(sz.main // 8):
                taken = None
                for j in range(6):
                    found = jnp.take_along_axis(
                        sources[j][8 * h : 8 * h + 8], spots, axis=1, mode="promise_in_bounds"
                    )
                    taken = found if j == 0 else jnp.where(pieces == j, found, taken)
                totals[h] = totals[h] + taken * marks
        mean_ref[:, pl.ds(aligned((step + 2) * LANES), LANES)] = (jnp.concatenate(totals, 0) / counts).astype(BF)
        return carry

    even = begin + (tiles - begin) // 8 * 8
    lax.fori_loop(begin, even, one_tile, 0, unroll=8)
    for step in range(even, tiles):
        one_tile(step, 0)
    sub = lax.broadcasted_iota(jnp.int32, (8, LANES), 0)

    for block in range(begin // 8, -(-tiles // 8)):
        total = jnp.zeros((8, LANES), F32)
        for slot in range(slots):
            code = code_ref[slot, 8 * block : 8 * (block + 1), :]
            piece = (code >> 7) - (4 * (8 * block + sub) - 3)
            taken = None
            for j in range(6):
                source = base_ref[pl.ds(8 + 32 * block - 3 + j, 8, stride=4), :]
                found = jnp.take_along_axis(source, code & 127, axis=1, mode="promise_in_bounds")
                taken = found if j == 0 else jnp.where(piece == j, found, taken)
            total = total + jnp.where(code >= 0, taken, 0.0)
        tail_ref[8 * block + 2 : 8 * block + 10, :] = total / count_ref[8 * block : 8 * (block + 1), :]


def pack_pair(sz, ranges, self_ref, self_tail, mean_ref, tail_ref, turn_ref, out_ref):
    turn_ref[...] = jnp.zeros_like(turn_ref)
    lanes = 0
    for source_ref, rows_ref, group in zip((self_ref, mean_ref), (self_tail, tail_ref), ranges):
        for i, (first, at, count) in enumerate(group):
            at = at + lanes
            if i != 1:
                out_ref[:, at : at + count] = source_ref[: sz.main, pl.ds(aligned(first), count)]
                turn_ref[at // LANES : (at + count) // LANES, :] = rows_ref[pl.ds(first // LANES, count // LANES), :]
                continue
            for tile in range(count // LANES):
                place = first + LANES * tile
                piece = take_tile(source_ref, sz.main, place, True)
                out_ref[:, at + LANES * tile : at + LANES * (tile + 1)] = piece.astype(BF)
                turn_ref[at // LANES + tile : at // LANES + tile + 1, :] = take_tail(rows_ref, place, True)
        lanes += sum(count for _, _, count in group)
    for block in range(-(-lanes // LANES // sz.main)):
        at = lanes + LANES * block
        out_ref[:, at : at + LANES] = turn_ref[sz.main * block : sz.main * (block + 1), :].astype(BF)


def own_pair(sz, ranges, self_ref, mean_ref, tail_ref, own_ref):
    spare = jnp.zeros((sz.hold - sz.feat, LANES), F32)
    base = ranges[0][1]
    for i, (start, at, count) in enumerate(ranges):
        for tile in range(count // LANES):
            place = start + LANES * tile
            out_lanes = slice(at - base + LANES * tile, at - base + LANES * (tile + 1))
            own_ref[: sz.hold, out_lanes] = take_tile(self_ref, sz.hold, place, i == 1).astype(BF)
            average = [take_tile(mean_ref, sz.main, place, i == 1), take_tail(tail_ref, place, i == 1), spare]
            own_ref[sz.hold :, out_lanes] = jnp.concatenate(average, 0).astype(BF)


def mean_scratch(sz, tiles, slots):
    rows = -(-tiles // 8) * 8
    return [
        ((slots, LANES * tiles), jnp.int32),
        ((slots, LANES * tiles), jnp.int32),
        ((sz.hold, LANES * sz.tiles_all), BF),
        ((sz.tiles_all, LANES), F32),
        ((sz.main, LANES * sz.tiles_all), BF),
        ((max(rows + 8, sz.tiles_all), LANES), F32),
        ((2 * sz.main, LANES), F32),
        ((4 * rows + 16, LANES), F32),
        ((slots, rows, LANES), jnp.int32),
        ((rows, LANES), F32),
    ]


def unpack_tails(sz, message, lanes, turn_ref):
    for block in range(-(-lanes // LANES // sz.main)):
        at = lanes + LANES * block
        turn_ref[sz.main * block : sz.main * (block + 1), :] = message[:, at : at + LANES].astype(F32)
    return turn_ref[...]


def unpack_tiles(sz, message, tail, first, tiles, row, at, out_ref):
    for tile in range(tiles):
        lane = at + LANES * tile
        out_ref[row : row + sz.hold, lane : lane + LANES] = unpack_tile(sz, message, tail, first + tile)


def first_kernel(
    sz, features, neighbors, present, w1_in, w2_in, w3_in, wh_in, own_b, packed, mean_out, tail_out, m1, m2, m3,
    feat_ref, nbr_ref, pres_ref, w1, w2, w3, wh, own_ref,
    links_ref, present_ref, self_ref, self_tail, mean_ref, tail_ref, turn_ref, base_ref, code_ref, count_ref, pack, sems,
):
    part = lax.axis_index("col")
    rows = pl.ds(0, nbr_ref.shape[1])
    weights = start_copies(((w1_in, w1), (w2_in, w2), (w3_in, w3), (wh_in, wh)), sems)
    copies = start_copies(
        (
            (features.at[:, pl.ds(0, feat_ref.shape[1])], feat_ref),
            (neighbors.at[:, rows], nbr_ref),
            (present.at[:, rows], pres_ref),
        ),
        sems,
        4,
    )
    wait_all(weights)
    pack[sz.at_three :, :] = jnp.zeros((pack.shape[0] - sz.at_three, LANES), F32)
    for half in range(sz.hid // LANES):
        lanes = slice(LANES * half, LANES * (half + 1))
        for s in range(2):
            for f in range(sz.feat):
                at = sz.feat * (2 * half + s) + f
                pack[at : at + 1, :] = w1[f, s : s + 1, lanes]
            at = sz.rows_one + sz.group * (2 * half + s)
            pack[at : at + sz.group, :] = w2[s, :, lanes]
    for c in range(sz.classes):
        for s in range(2):
            at = sz.at_three + c
            pack[at : at + 1, sz.group * s : sz.group * (s + 1)] = w3[c, s : s + 1, :]
    row = jnp.concatenate([wh[0:1, :], wh[1:2, :]], 1)
    for i, piece in enumerate(three_parts(row)):
        pack[sz.misc + i : sz.misc + i + 1, :] = piece
    store = start_copies(((pack, packed),), sems, 7)
    for block in range(sz.blocks):
        at = sz.message_b + LANES * block
        piece = pack[sz.main * block : sz.main * (block + 1), :].astype(BF)
        m1[:, at : at + LANES] = piece
        m2[:, at : at + LANES] = piece
    wait_all(copies)
    fill_own(sz, feat_ref, self_ref, self_tail, 48 * sz.own // LANES + EARLY)
    mean_ref[:, :FRONT] = jnp.zeros((sz.main, FRONT), BF)
    tail_ref[...] = jnp.zeros_like(tail_ref)
    mean_tiles(sz, 0, sz.tiles_b_all, feat_ref, nbr_ref, pres_ref, links_ref, present_ref, mean_ref, tail_ref, base_ref, code_ref, count_ref)
    done = pl.ds(0, LANES * (sz.tiles_b_all + 2))
    store += start_copies(((mean_ref.at[:, done], mean_out), (tail_ref, tail_out)), sems, 9)
    own_pair(sz, sz.ranges(part)[1:], self_ref, mean_ref, tail_ref, own_ref)
    store += start_copies(((own_ref, own_b),), sems, 8)
    for r, out in ((1, m1), (2, m2), (3, m3)):
        pack_pair(sz, sz.first_ranges(part ^ r), self_ref, self_tail, mean_ref, tail_ref, turn_ref, out)
    wait_all(store)


def first_messages(sz, features, neighbors, present, w1, w2, w3, hidden):
    rows = LANES * sz.tiles_b_all
    bases = min(4 * rows + LANES, sz.base)
    slots = neighbors.shape[0]
    return call(
        functools.partial(first_kernel, sz),
        [
            ((2 * sz.hold, sz.n_mid), BF),
            ((sz.main * sz.blocks, LANES), F32),
            ((sz.main, rows + 2 * LANES), BF),
            ((max(-(-sz.tiles_b_all // 8) * 8 + 8, sz.tiles_all), LANES), F32),
            ((sz.main, sz.full_b), BF),
            ((sz.main, sz.full_b), BF),
            ((sz.main, sz.message_b), BF),
        ],
        [
            ((sz.feat, bases), BF),
            ((slots, rows), jnp.int32),
            ((slots, rows), jnp.int32),
            (w1.shape, F32),
            (w2.shape, F32),
            (w3.shape, F32),
            (hidden.shape, F32),
            ((2 * sz.hold, sz.n_mid), BF),
            *mean_scratch(sz, sz.tiles_b_all, slots),
            ((sz.main * sz.blocks, LANES), F32),
        ],
        FIRST_MIB,
        features,
        neighbors,
        present,
        w1,
        w2,
        w3,
        hidden,
        far_in=range(7),
        far_out=(0, 1, 2, 3),
        copies=11,
        micros=4,
    )


def mean_kernel(
    sz, feat_ref, nbr_ref, pres_ref, mean_in, tail_in, nbr2, pres2, nbr3, pres3, own_a, counts_out, a1, a2, a3,
    links_ref, present_ref, self_ref, self_tail, mean_ref, tail_ref, turn_ref, base_ref, code_ref, count_ref, own_ref, kept_ref, counts, sems,
):
    part = lax.axis_index("col")
    tiles = sz.low // LANES + 1
    begin = sz.tiles_b_all
    loads = start_copies(((mean_in, mean_ref.at[:, pl.ds(0, LANES * (begin + 2))]), (tail_in, kept_ref)), sems, 1)
    fill_counts(sz, part, nbr2, pres2, nbr3, pres3, counts)
    store = start_copies(((counts, counts_out),), sems, 3)
    fill_own(sz, feat_ref, self_ref, self_tail, (48 * sz.own + sz.n_a) // LANES)
    last = LANES * (tiles + 2)
    mean_ref[:, last:] = jnp.zeros((sz.main, LANES * sz.tiles_all - last), BF)
    tail_ref[...] = jnp.zeros_like(tail_ref)
    mean_tiles(sz, begin, tiles, feat_ref, nbr_ref, pres_ref, links_ref, present_ref, mean_ref, tail_ref, base_ref, code_ref, count_ref)
    wait_all(loads)
    tail_ref[: begin + 2, :] = kept_ref[: begin + 2, :]
    own_pair(sz, sz.ranges(part)[:1], self_ref, mean_ref, tail_ref, own_ref)
    store += start_copies(((own_ref, own_a),), sems)
    for r, out in ((1, a1), (2, a2), (3, a3)):
        pack_pair(sz, sz.second_ranges(part ^ r), self_ref, self_tail, mean_ref, tail_ref, turn_ref, out)
    wait_all(store)


def mean_messages(sz, features, neighbors, present, mean, tail, links):
    counts = (sz.count_rows * (sz.tiles_b + 2 * (sz.own // LANES)), LANES)
    return call(
        functools.partial(mean_kernel, sz),
        [((2 * sz.hold, sz.n_a), BF), (counts, BF)] + [((sz.main, sz.message_a), BF)] * 3,
        mean_scratch(sz, sz.low // LANES + 1, neighbors.shape[0]) + [((2 * sz.hold, sz.n_a), BF), (tail.shape, F32), (counts, BF)],
        MEAN_MIB,
        features,
        neighbors,
        present,
        mean,
        tail,
        *links,
        far_in=(3, 4),
        far_out=(0, 1),
        copies=4,
        micros=6,
    )


def window_counts(local, rows):
    spots = lax.broadcasted_iota(jnp.int32, (256, LANES), 0).astype(F32).astype(BF)
    blocks = []
    for first in range(0, rows, 256):
        size = min(256, rows - first)
        place = local - first
        place = jnp.where((place >= 0) & (place < size), place, -1).astype(F32)
        counts = jnp.zeros((size, LANES), BF)
        for slot in range(local.shape[0]):
            row = jnp.broadcast_to(place[slot : slot + 1], (16, LANES)).astype(BF)
            row = jnp.concatenate([row] * (size // 16), 0)
            counts = counts + jnp.where(row == spots[:size], jnp.bfloat16(1.0), jnp.bfloat16(0.0))
        blocks.append(counts)
    return jnp.concatenate(blocks, 0)


def slot_totals(present):
    return jnp.maximum(jnp.sum(present.astype(F32), 0, keepdims=True), 1.0)


def counts_tile(sz, links, marks, start, at, counts):
    local = jnp.where(marks > 0, links - start, -1)
    counts[at : at + WINDOW, :] = window_counts(local, WINDOW)
    counts[at + WINDOW : at + sz.count_rows, :] = jnp.broadcast_to(slot_totals(marks), (16, LANES)).astype(BF)


def fill_counts(sz, part, nbr2, pres2, nbr3, pres3, counts):
    tiles = nbr2.shape[1] // LANES
    for tile in range(sz.tiles_b):
        column = 4 * sz.own // LANES * part + tile
        start = sz.a_row(part) + 4 * LANES * tile
        links, marks = half_columns(nbr2, column, tiles, 0), half_columns(pres2, column, tiles, 0)
        counts_tile(sz, links, marks, start, sz.count_rows * tile, counts)
    for tile in range(sz.own // LANES):
        columns = pl.ds(aligned(sz.own * part + LANES * tile), LANES)
        at = sz.count_rows * (sz.tiles_b + tile)
        counts_tile(sz, nbr3[:, columns], pres3[:, columns], sz.b_row(part), at, counts)
        at += sz.count_rows * (sz.own // LANES)
        counts_tile(sz, nbr2[:, columns], pres2[:, columns], sz.b_row(part), at, counts)


def tile_counts(sz, counts, tile):
    at = sz.count_rows * tile
    totals = counts[at + WINDOW : at + WINDOW + 16, :].astype(F32)[0:1]
    return counts[at : at + WINDOW, :], totals


def activate(result):
    active = result * sigmoid(result)
    scale = lax.rsqrt(jnp.sum(active * active, 0, keepdims=True) + ROW_EPS)
    return result, scale, active * scale


def first_layer(weight, inputs, bias):
    result = dot(weight, inputs, (1, 0)) + bias
    active = result * sigmoid(result)
    scale = lax.rsqrt(jnp.sum(active * active, 0, keepdims=True) + ROW_EPS)
    return result, scale, active * scale


def join_inputs(sz, own, average):
    pieces = []
    for c in range(4):
        pieces.append(own[sz.group * c : sz.group * (c + 1)])
        pieces.append(average[sz.group * c : sz.group * (c + 1)])
    return jnp.concatenate(pieces, 0)


def norm_backward(grad, result, scale):
    gate = sigmoid(result)
    active = result * gate
    inner = jnp.sum(grad * active, 0, keepdims=True)
    grad_active = scale * grad - active * (scale * scale * scale * inner)
    return (grad_active * gate * (1.0 + result * (1.0 - gate))).astype(BF)


def split_inputs(sz, grad):
    pieces = [grad[sz.group * c : sz.group * (c + 1)] for c in range(8)]
    return jnp.concatenate(pieces[0::2], 0), jnp.concatenate(pieces[1::2], 0)


def row_sums(grad):
    return dot(jnp.ones((16, grad.shape[1]), BF), grad, (1, 1))


def spread(sz, scaled, counts):
    return dot(scaled.astype(BF), counts, (1, 1))


def halves(ref, at, lanes):
    return jnp.concatenate([ref[:, at : at + lanes], ref[:, at + lanes : at + 2 * lanes]], 0)


def store_halves(ref, at, lanes, value):
    rows = value.shape[0] // 2
    ref[:rows, at : at + lanes] = value[:rows]
    ref[:rows, at + lanes : at + 2 * lanes] = value[rows:]


def slot_column(table):
    rows, slots = table.shape
    wide = jnp.broadcast_to(table.astype(F32)[:, None, :], (rows, slots, slots))
    hit = lax.broadcasted_iota(jnp.int32, wide.shape, 1) == lax.broadcasted_iota(jnp.int32, wide.shape, 2)
    return jnp.sum(jnp.where(hit, wide, 0.0), 2, keepdims=True).reshape(rows * slots, 1)


def alive_column(sz, live):
    shape = (sz.dp, sz.dp)
    hit = lax.broadcasted_iota(jnp.int32, shape, 0) == lax.broadcasted_iota(jnp.int32, shape, 1)
    counts = jnp.sum(jnp.where(hit, jnp.broadcast_to(live.astype(F32), shape), 0.0), 1, keepdims=True)
    slot = lax.broadcasted_iota(jnp.int32, (sz.dp, sz.slot), 1).astype(F32)
    return slot_column(jnp.where(slot < counts, 1.0, 0.0))


def seed_picks(sz, serve_rows, take_rows, part):
    spots = (lax.broadcasted_iota(jnp.int32, (sz.slots, sz.own), 1) + sz.own * part).astype(F32)
    serve = jnp.where(slot_column(serve_rows) == spots, 1.0, 0.0)
    take = jnp.where(slot_column(take_rows) == spots, 1.0, 0.0)
    return serve, take, jnp.sum(serve, 1, keepdims=True), jnp.sum(take, 1, keepdims=True)


def seeds_kernel(
    sz, own_b, packed, s1, s2, s3, passed, counts_in, serve_in, take_in, live_in,
    low_out, high_out, sent,
    xb, pack, m1, m2, m3, p3, window_ref, serve_rows, take_rows, live_rows, low, high, turn_ref, w1_ref, w2_ref, states, sems,
):
    part = lax.axis_index("col")
    own, hid, n_b, group, hold, at = sz.own, sz.hid, sz.n_b, sz.group, sz.hold, sz.at
    n_mid = sz.n_mid
    copies = start_copies(
        (
            (packed, pack),
            (passed.at[:, pl.ds(sz.message_b, LANES * sz.blocks)], p3),
            (s1, m1),
            (s2, m2),
            (s3, m3),
            (own_b, xb),
            (counts_in.at[sz.seed_window(), :], window_ref),
            (serve_in, serve_rows),
            (take_in, take_rows),
            (live_in, live_rows),
        ),
        sems,
    )
    w1_ref[...] = jnp.zeros_like(w1_ref)
    wait_all(copies[:4])
    for r, (message, first_lane) in enumerate(((None, 0), (m1, sz.message_b), (m2, sz.message_b), (p3, 0))):
        for block in range(sz.blocks if r else 0):
            first = first_lane + LANES * block
            pack[sz.main * block : sz.main * (block + 1), :] = message[:, first : first + LANES].astype(F32)
        shard = part ^ r
        for half in range(hid // LANES):
            lanes = slice(LANES * half, LANES * (half + 1))
            for s in range(2):
                first = sz.feat * (2 * half + s)
                row = 4 * hold * s + hold * r
                w1_ref[row : row + sz.feat, lanes] = pack[first : first + sz.feat, :]
            first = sz.rows_one + 2 * group * half
            row = pl.multiple_of(2 * group * shard, 2 * group)
            w2_ref[pl.ds(row, 2 * group), lanes] = pack[first : first + 2 * group, :]
        third = jnp.concatenate([pack[sz.at_three : sz.misc, :], jnp.zeros((sz.head - sz.classes, LANES), F32)], 0)
        low[: sz.head, pl.ds(aligned(at["turned3"] + 2 * group * shard), LANES)] = third.astype(BF)
        misc = pack[sz.misc : sz.misc + 3, :]
        column = jnp.broadcast_to(misc[0:1] + misc[1:2] + misc[2:3], (LANES, LANES)).T
        row = pl.multiple_of(group * shard, group)
        for layer in range(2):
            lanes = slice(at["bias"] + LANES * layer, at["bias"] + LANES * (layer + 1))
            high[pl.ds(row, group), lanes] = column[group * layer : group * (layer + 1)]
    turned1 = w1_ref[...].T.astype(BF)
    turned2 = w2_ref[...].T.astype(BF)
    low[:, at["turned1"] : at["turned1"] + hid] = turned1
    low[:, at["turned2"] : at["turned2"] + 2 * hid] = turned2
    store_halves(low, at["weight2"], hid, w2_ref[...].astype(BF))
    weight3 = low[: sz.head, at["turned3"] : at["turned3"] + 2 * hid].astype(F32).T
    weight3 = jnp.concatenate([weight3, jnp.zeros((2 * hid, LANES - sz.head), F32)], 1)
    store_halves(low, at["weight3"], LANES, weight3.astype(BF))

    def piece(lanes, count):
        return (low.at[:, pl.ds(lanes, count)], low_out.at[:, pl.ds(lanes, count)])

    stores = start_copies((piece(n_mid, at["states"] - n_mid),), sems, 11)
    wait_all(copies[4:])
    low[:hold, :n_mid] = xb[:hold, :]
    low[4 * hold : 5 * hold, :n_mid] = xb[hold:, :]
    for r, message in ((1, m1), (2, m2), (3, m3)):
        tail = unpack_tails(sz, message, 2 * n_mid + sz.early, turn_ref)
        unpack_tiles(sz, message, tail, 0, sz.tiles_mid, hold * r, 0, low)
        first = (n_mid + sz.early) // LANES
        unpack_tiles(sz, message, tail, first, sz.tiles_mid, hold * (4 + r), 0, low)
    stores += start_copies((piece(0, n_mid),), sems, 12)
    bias1 = high[:hid, at["bias"] : at["bias"] + LANES]
    bias2 = high[:hid, at["bias"] + LANES : at["bias"] + 2 * LANES]
    high[:hid, :n_mid] = dot(turned1, low[:, :n_mid], (1, 0))
    for tile in range(sz.tiles_mid):
        lanes = slice(LANES * tile, LANES * (tile + 1))
        result, scale, state = activate(high[:hid, lanes] + bias1)
        high[:hid, lanes] = result
        high[hid:, lanes] = jnp.broadcast_to(scale, (8, LANES))
        upper, lower = two_parts(state)
        states[:hid, lanes] = upper
        states[hid:, lanes] = lower
    low[:, at["states"] : at["states"] + n_b] = states[:hid, :n_b]
    rows = pl.ds(0, hid + 8)
    others = pl.ds(at["bias"], 2 * LANES)
    stores += start_copies(
        (
            piece(at["states"], n_b),
            (high.at[rows, pl.ds(0, n_mid)], high_out.at[rows, pl.ds(0, n_mid)]),
            (high.at[rows, others], high_out.at[rows, others]),
        ),
        sems,
        13,
    )
    for tile in range(own // LANES):
        window, totals = tile_counts(sz, window_ref, tile)
        total = dot(states[:, :n_b], window, (1, 0))
        average = ((total[:hid] + total[hid:]) / totals).astype(BF)
        x = join_inputs(sz, states[:hid, n_b + LANES * tile : n_b + LANES * (tile + 1)], average)
        first = at["inputs2"] + LANES * tile
        low[:, first : first + LANES] = x[:hid]
        low[:, first + own : first + own + LANES] = x[hid:]
        result, scale, state = first_layer(turned2, x, bias2)
        first = at["result2"] + LANES * tile
        high[:hid, first : first + LANES] = result
        high[hid:, first : first + LANES] = jnp.broadcast_to(scale, (8, LANES))
        upper, lower = two_parts(state)
        first = at["embed"] + LANES * tile
        low[:, first : first + LANES] = upper
        low[:, first + own : first + own + LANES] = lower
    last = pl.ds(at["result2"], own)
    tail = (piece(at["embed"], sz.low_lanes - at["embed"]), (high.at[rows, last], high_out.at[rows, last]))
    stores += start_copies(tail, sems, 16)
    serve, take, _, owned = seed_picks(sz, serve_rows[...], take_rows[...], part)
    embed_high = low[:, at["embed"] : at["embed"] + own]
    served = dot(serve.astype(BF), embed_high, (1, 1))
    taken = dot(take.astype(BF), embed_high, (1, 1))
    dead = (owned > 0.5) & (alive_column(sz, live_rows[...]) < 0.5)
    first = lax.broadcasted_iota(jnp.int32, (sz.slots, hid), 1) == 0
    value = jnp.concatenate([served, jnp.where(first & dead, SENTINEL, taken)], 1)
    value = value.reshape(sz.dp, 1, sz.slot, 2 * hid)
    value = jnp.broadcast_to(value, (sz.dp, 4, sz.slot, 2 * hid))
    sent[...] = value.reshape(4 * sz.slots, 2 * hid).astype(BF)
    wait_all(stores)


def sent_rows(sz, low, at, serve, take):
    embed_high = low[:, at : at + sz.own]
    embed_low = low[:, at + sz.own : at + 2 * sz.own]
    take = take.astype(BF)
    return jnp.concatenate(
        [dot(serve.astype(BF), embed_high, (1, 1)), dot(take, embed_high, (1, 1)), dot(take, embed_low, (1, 1))], 1
    )


def seeds_forward(sz, messages, counts, tables):
    hid = sz.hid
    tail = (sz.main, LANES * sz.blocks)
    return call(
        functools.partial(seeds_kernel, sz),
        [
            ((hid, sz.low_lanes), BF),
            ((hid + 8, sz.high_lanes), F32),
            ((4 * sz.slots, 2 * hid), BF),
        ],
        [
            ((2 * sz.hold, sz.n_mid), BF),
            ((sz.main * sz.blocks, LANES), F32),
            ((sz.main, sz.full_b), BF),
            ((sz.main, sz.full_b), BF),
            ((sz.main, sz.message_b), BF),
            (tail, BF),
            ((sz.count_rows * (sz.own // LANES), LANES), BF),
            *[(item.shape, jnp.int32) for item in tables],
            ((hid, sz.low_lanes), BF),
            ((hid + 8, sz.high_lanes), F32),
            ((2 * sz.main, LANES), F32),
            ((8 * sz.hold, hid), F32),
            ((2 * hid, hid), F32),
            ((2 * hid, sz.n_mid), BF),
        ],
        SEEDS_MIB,
        *messages,
        counts,
        *tables,
        far_in=(0, 1, 6, 7, 8, 9),
        loose=(2, 3, 4, 5),
        micros=4,
        far_out=(0, 1),
        copies=19,
    )


def rest_kernel(
    sz, low_in, high_in, counts_in, own_a, a1, a2, a3, e1, e2, e3, labels_in, weighting_in, head_in, part_out,
    labels, weighting, head_bias, low, xa, bias, counts, xo, c1, c2, c3, turn_ref,
    states, states2, result1, slope1, scale1, inputs2, result2, scale2, grad_a, low_grad, part_ref, sems,
):
    part = lax.axis_index("col")
    own, hid, n_a, n_b, hold = sz.own, sz.hid, sz.n_a, sz.n_b, sz.hold
    at = dict(sz.at)
    for name in ("turned1", "turned2", "weight2", "weight3", "turned3", "states", "embed"):
        at[name] -= sz.n_mid
    lanes = at["embed"] + own
    copies = start_copies(
        (
            (own_a, xo),
            *[(e.at[:, pl.ds(sz.n_mid, sz.early)], c.at[:, pl.ds(0, sz.early)]) for e, c in ((e1, c1), (e2, c2), (e3, c3))],
            *[
                (e.at[:, pl.ds(2 * sz.n_mid + sz.early, LANES)], c.at[:, pl.ds(sz.early, LANES)])
                for e, c in ((e1, c1), (e2, c2), (e3, c3))
            ],
            (low_in.at[:, pl.ds(sz.n_mid, hid)], low.at[:, pl.ds(0, hid)]),
            (high_in.at[:, pl.ds(sz.at["bias"], 2 * LANES)], bias),
            (low_in.at[:, pl.ds(sz.n_mid + hid, lanes - hid)], low.at[:, pl.ds(hid, lanes - hid)]),
            (counts_in, counts),
            (labels_in, labels),
            (weighting_in, weighting),
            (head_in, head_bias),
        ),
        sems,
    )
    late = (n_a - sz.early) // LANES
    for r, message in ((1, a1), (2, a2), (3, a3)):
        tail = unpack_tails(sz, message, 2 * n_a - sz.early, turn_ref)
        unpack_tiles(sz, message, tail, 0, late, hold * r, sz.early, xa)
        unpack_tiles(sz, message, tail, late, n_a // LANES, hold * (4 + r), 0, xa)
    wait_all(copies[:7])
    for r, before in ((1, c1), (2, c2), (3, c3)):
        tail = before[:, sz.early :].astype(F32)[sz.tiles_mid : sz.tiles_mid + EARLY]
        unpack_tiles(sz, before, tail, 0, EARLY, hold * r, 0, xa)
    xa[:hold, :] = xo[:hold, :]
    xa[4 * hold : 5 * hold, :] = xo[hold:, :]
    wait_all(copies[7:9])
    turned1 = low[:, at["turned1"] : at["turned1"] + hid]
    bias1 = bias[:hid, :LANES]
    bias2 = bias[:hid, LANES:]

    result1[...] = dot(turned1, xa[...], (1, 0))

    def forward_step(index, carry):
        lanes = pl.ds(aligned(index * LANES), LANES)
        result = result1[:, lanes] + bias1
        gate = sigmoid(result)
        active = result * gate
        scale = lax.rsqrt(jnp.sum(active * active, 0, keepdims=True) + ROW_EPS)
        result1[:, lanes] = active
        slope1[:, lanes] = gate + active * (1.0 - gate)
        scale1[:, lanes] = scale
        upper, lower = two_parts(active * scale)
        states[:hid, lanes] = upper
        states[hid:, lanes] = lower
        return carry

    lax.fori_loop(0, n_a // LANES, forward_step, 0, unroll=7)
    wait_all(copies[9:])
    turned2 = low[:, at["turned2"] : at["turned2"] + 2 * hid]
    for tile in range(sz.tiles_b):
        lanes = slice(LANES * tile, LANES * (tile + 1))
        window, totals = tile_counts(sz, counts, tile)
        total = dot(states[:, 4 * LANES * tile : 4 * LANES * tile + WINDOW], window, (1, 0))
        average = ((total[:hid] + total[hid:]) / totals).astype(BF)
        inputs2[:, lanes] = join_inputs(sz, low[:, at["states"] + LANES * tile : at["states"] + LANES * (tile + 1)], average)
    result2[...] = dot(turned2, inputs2[...], (1, 0))
    for tile in range(sz.tiles_b):
        lanes = slice(LANES * tile, LANES * (tile + 1))
        result, scale, state = activate(result2[:, lanes] + bias2)
        result2[:, lanes] = result
        scale2[:, lanes] = scale
        upper, lower = two_parts(state)
        states2[:hid, lanes] = upper
        states2[hid:, lanes] = lower
    counts3, totals3 = tile_counts(sz, counts, sz.tiles_b)
    total = dot(states2[...], counts3, (1, 0))
    average = ((total[:hid] + total[hid:]) / totals3).astype(BF)
    inputs3 = join_inputs(sz, low[:, at["embed"] : at["embed"] + own], average)

    columns = pl.ds(aligned(own * part), own)
    classes = lax.broadcasted_iota(jnp.int32, (sz.head, own), 0)
    head_row = jnp.concatenate([head_bias[...], jnp.zeros((1, LANES - sz.classes), F32)], 1)
    head_column = jnp.broadcast_to(head_row, (LANES, LANES)).T[: sz.head]
    logits = dot(low[: sz.head, at["turned3"] : at["turned3"] + 2 * hid], inputs3, (1, 0)) + head_column
    logits = jnp.where(classes < sz.classes, logits, -1e30)
    highest = jnp.max(logits, 0, keepdims=True)
    expo = jnp.exp(logits - highest)
    totals = jnp.sum(expo, 0, keepdims=True)
    hit = classes == labels[:, columns]
    weights = weighting[:, columns].astype(F32)
    target = jnp.sum(jnp.where(hit, logits, 0.0), 0, keepdims=True)
    ce_total = jnp.sum(weights * (highest + jnp.log(totals) - target), 1, keepdims=True)
    seed_count = jnp.sum(weights, 1, keepdims=True)
    grad_logits = (weights * (expo / totals - jnp.where(hit, 1.0, 0.0))).astype(BF)
    g3 = at["g3"]
    part_ref[: sz.head, g3 : g3 + 2 * hid] = dot(grad_logits, inputs3, (1, 1))
    head_sums = jnp.concatenate([row_sums(grad_logits), jnp.zeros((16, LANES - sz.head), F32)], 1)
    part_ref[sz.head + 16 : sz.head + 32, g3 : g3 + LANES] = head_sums
    lane_at = lax.broadcasted_iota(jnp.int32, (16, LANES), 1)
    sums = jnp.where(lane_at == 0, ce_total, jnp.where(lane_at == 1, seed_count, 0.0))
    part_ref[sz.head + 16 : sz.head + 32, g3 + LANES : g3 + 2 * LANES] = sums
    own_part, average_part = split_inputs(sz, dot(halves(low, at["weight3"], LANES)[:, : sz.head], grad_logits, (1, 0)))
    part_ref[:hid, at["grad_embed"] : at["grad_embed"] + own] = own_part
    grad_mid = spread(sz, average_part / totals3, counts3)
    low_grad2 = norm_backward(grad_mid, result2[...], scale2[...])
    g2 = dot(inputs2[...], low_grad2, (1, 1))
    part_ref[:hid, at["g2"] : at["g2"] + hid] = g2[:hid]
    part_ref[:hid, at["g2"] + hid : at["g2"] + 2 * hid] = g2[hid:]
    part_ref[sz.head : sz.head + 16, g3 + hid : g3 + 2 * hid] = row_sums(low_grad2)
    weight2 = halves(low, at["weight2"], hid)
    own_part, average_part = split_inputs(sz, dot(weight2, low_grad2, (1, 0)))
    part_ref[:hid, at["grad_b"] : at["grad_b"] + n_b] = own_part
    for tile in range(sz.tiles_b):
        window, totals = tile_counts(sz, counts, tile)
        added = spread(sz, average_part[:, LANES * tile : LANES * (tile + 1)] / totals, window)
        first = 4 * LANES * tile
        shared = slice(first, first + LANES)
        grad_a[:, shared] = added[:, :LANES] + grad_a[:, shared] if tile else added[:, :LANES]
        grad_a[:, first + LANES : first + WINDOW] = added[:, LANES:]
    rows, few = pl.ds(0, hid + 8), pl.ds(0, sz.head + 32)
    split = at["g2"]
    stores = start_copies(
        (
            (part_ref.at[rows, pl.ds(split, hid * 2)], part_out.at[rows, pl.ds(split, hid * 2)]),
            (
                part_ref.at[rows, pl.ds(at["grad_b"], n_b + own)],
                part_out.at[rows, pl.ds(at["grad_b"], n_b + own)],
            ),
        ),
        sems,
        14,
    )

    def backward_step(index, carry):
        lanes = pl.ds(aligned(index * LANES), LANES)
        scale = scale1[:, lanes]
        inner = jnp.zeros((8, LANES), F32)
        for row in range(0, hid, 8):
            rows = slice(row, row + 8)
            inner = inner + grad_a[rows, lanes] * result1[rows, lanes]
        inner = scale * scale * scale * jnp.sum(inner, 0, keepdims=True)
        for row in range(0, hid, 16):
            rows = slice(row, row + 16)
            grad = scale * grad_a[rows, lanes] - inner * result1[rows, lanes]
            low_grad[rows, lanes] = (grad * slope1[rows, lanes]).astype(BF)
        return carry

    lax.fori_loop(0, n_a // LANES, backward_step, 0, unroll=7)
    part_ref[:hid, at["g1"] : at["g1"] + hid] = dot(xa[...], low_grad[...], (1, 1))
    part_ref[sz.head : sz.head + 16, g3 : g3 + hid] = row_sums(low_grad[...])
    stores += start_copies(
        (
            (part_ref.at[rows, pl.ds(0, hid)], part_out.at[rows, pl.ds(0, hid)]),
            (part_ref.at[few, pl.ds(g3, 2 * hid)], part_out.at[few, pl.ds(g3, 2 * hid)]),
        ),
        sems,
        16,
    )
    wait_all(stores)


def rest_step(sz, low, high, counts, means, labels, weighting, head_bias):
    hid = sz.hid
    return call(
        functools.partial(rest_kernel, sz),
        [((hid + 8, sz.part_lanes), F32)],
        [
            (labels.shape, jnp.int32),
            (weighting.shape, jnp.int32),
            (head_bias.shape, F32),
            ((hid, sz.at["embed"] + sz.own - sz.n_mid), BF),
            ((hid, sz.n_a), BF),
            ((hid + 8, 2 * LANES), F32),
            (counts.shape, BF),
            ((2 * sz.hold, sz.n_a), BF),
            *[((sz.main, sz.early + LANES), BF)] * 3,
            ((2 * sz.main, LANES), F32),
            ((2 * hid, sz.n_a), BF),
            ((2 * hid, sz.n_b), BF),
            ((hid, sz.n_a), F32),
            ((hid, sz.n_a), F32),
            ((1, sz.n_a), F32),
            ((2 * hid, sz.n_b), BF),
            ((hid, sz.n_b), F32),
            ((1, sz.n_b), F32),
            ((hid, sz.n_a), F32),
            ((hid, sz.n_a), BF),
            ((hid + 8, sz.part_lanes), F32),
        ],
        REST_MIB,
        low,
        high,
        counts,
        *means,
        labels,
        weighting,
        head_bias,
        far_in=(0, 1, 2, 3, 10, 11, 12),
        loose=(7, 8, 9),
        micros=14,
        far_out=(0,),
        copies=18,
    )[0]


def seeds_back_kernel(
    sz, serve_in, take_in, live_in, received, low_in, high_in, counts_in, part_in, keep0, keep1, send,
    serve_rows, take_rows, live_rows, x_ref, weight_ref, low, high, window_ref, partial, g1_ref, g2_ref, gb_ref, stage, sems,
):
    part = lax.axis_index("col")
    own, hid, group, n_b, n_mid = sz.own, sz.hid, sz.group, sz.n_b, sz.n_mid
    at = dict(sz.at)
    at["inputs2"] -= at["embed"]
    split = at["grad_b"]
    few = pl.ds(0, sz.head + 32)
    lanes = pl.ds(at["result2"], own)
    copies = start_copies(
        (
            (serve_in, serve_rows),
            (take_in, take_rows),
            (live_in, live_rows),
            (low_in.at[:, pl.ds(at["embed"], 4 * own)], low),
            (part_in.at[:, pl.ds(split + n_b, own)], partial.at[:, pl.ds(split + n_b, own)]),
            (high_in.at[:, lanes], high.at[:, lanes]),
            (low_in.at[:, pl.ds(at["weight2"], 2 * hid)], weight_ref),
            (counts_in.at[sz.seed_window(), :], window_ref),
            (part_in.at[:, pl.ds(split, n_b)], partial.at[:, pl.ds(split, n_b)]),
            (high_in.at[:, pl.ds(0, n_mid)], high.at[:, pl.ds(0, n_mid)]),
            (low_in.at[:, pl.ds(0, n_mid)], x_ref),
            (part_in.at[:, pl.ds(0, at["g3"])], partial.at[:, pl.ds(0, at["g3"])]),
            (part_in.at[few, pl.ds(at["g3"], 2 * hid)], partial.at[few, pl.ds(at["g3"], 2 * hid)]),
        ),
        sems,
    )
    arrived = received[...].astype(F32).reshape(sz.dp, 4, sz.slot, 2 * hid)
    arrived = jnp.sum(arrived, 1).reshape(sz.slots, 2 * hid)
    at["embed"] = 0
    wait_all(copies[:4])
    serve, take, served, taken = seed_picks(sz, serve_rows[...], take_rows[...], part)
    mine = sent_rows(sz, low, 0, serve, take)
    theirs = arrived[:, hid:]
    alive_there = theirs[:, 0:1] < 0.5 * SENTINEL
    differ = mine[:, hid : 2 * hid] + mine[:, 2 * hid :] - arrived[:, :hid]
    differ = jnp.where((taken > 0.5) & (alive_column(sz, live_rows[...]) > 0.5), differ, 0.0)
    dist_total = DIST_WEIGHT * jnp.sum(jnp.sum(differ * differ, 0, keepdims=True), 1, keepdims=True)
    local_high, local_low = two_parts(2.0 * DIST_WEIGHT * differ)
    back = jnp.where((served > 0.5) & alive_there, theirs - mine[:, :hid], 0.0)
    back = (-2.0 * DIST_WEIGHT * back).astype(BF)
    take = take.astype(BF)
    serve = serve.astype(BF)
    wait_all(copies[4:6])
    grad = partial[:hid, at["grad_embed"] : at["grad_embed"] + own]
    grad = grad + dot(local_high, take, (0, 0)) + dot(local_low, take, (0, 0)) + dot(back, serve, (0, 0))
    lanes = slice(at["result2"], at["result2"] + own)
    low_grad2 = norm_backward(grad, high[:hid, lanes], high[hid:, lanes][0:1])
    wait_all(copies[6:9])
    weight2 = halves(weight_ref, 0, hid)
    own_part, average_part = split_inputs(sz, dot(weight2, low_grad2, (1, 0)))
    total_b = partial[:hid, at["grad_b"] : at["grad_b"] + n_b]
    for tile in range(own // LANES):
        window, totals = tile_counts(sz, window_ref, tile)
        total_b = total_b + spread(sz, average_part[:, LANES * tile : LANES * (tile + 1)] / totals, window)
    wait_all(copies[9:10])
    low_grad = jnp.concatenate(
        [
            norm_backward(total_b, high[:hid, :n_b], high[hid:, :n_b][0:1]),
            norm_backward(own_part, high[:hid, n_b:n_mid], high[hid:, n_b:n_mid][0:1]),
        ],
        1,
    )
    wait_all(copies[10:])
    added = dot(halves(low, at["inputs2"], own), low_grad2, (1, 1))
    for half in range(2):
        lanes = slice(at["g2"] + hid * half, at["g2"] + hid * (half + 1))
        g2_ref[hid * half : hid * (half + 1), :] = partial[:hid, lanes] + added[hid * half : hid * (half + 1)]
    g3 = at["g3"]
    sums = partial[sz.head : sz.head + 16, g3 : g3 + 2 * hid]
    gb_ref[:, hid:] = sums[:, hid:] + row_sums(low_grad2)
    half = 4 * sz.hold
    g1_ref[...] = partial[:hid, at["g1"] : at["g1"] + hid] + dot(x_ref[...], low_grad, (1, 1))
    gb_ref[:, :hid] = sums[:, :hid] + row_sums(low_grad)
    head_row = partial[sz.head + 16 : sz.head + 32, g3 : g3 + LANES]
    totals = partial[sz.head + 16 : sz.head + 32, g3 + LANES : g3 + 2 * LANES]
    lane_at = lax.broadcasted_iota(jnp.int32, (16, LANES), 1)
    fixed = ((totals[0:1, 0:1] + dist_total) * float(2**LOSS_BITS) + 0.5).astype(jnp.int32)
    count = totals[0:1, 1:2].astype(jnp.int32)
    whole = jnp.where(lane_at < 32, fixed, count)
    bits = (lax.shift_right_logical(whole, lane_at & 31) & 1).astype(F32)
    bits = jnp.where(lane_at < 64, bits, 0.0)
    stage[sz.misc :, :] = jnp.zeros((sz.pay - sz.misc, LANES), F32)
    for r, (target_ref, base) in enumerate(((keep0, 0), (send, 0), (keep1, 0), (send, sz.pay))):
        shard = part ^ r
        block2 = pl.ds(pl.multiple_of(2 * group * shard, 2 * group), 2 * group)
        for h in range(hid // LANES):
            lanes = slice(LANES * h, LANES * (h + 1))
            for s in range(2):
                first, row = half * s + sz.hold * r, sz.feat * (2 * h + s)
                stage[row : row + sz.feat, :] = g1_ref[first : first + sz.feat, lanes]
            row = sz.rows_one + 2 * group * h
            stage[row : row + 2 * group, :] = g2_ref[block2, lanes]
        third = partial[: sz.head, pl.ds(aligned(g3 + 2 * group * shard), LANES)]
        stage[sz.at_three : sz.misc, :] = third[: sz.classes]
        odd = (shard % 2) == 1
        block = aligned((shard // 2) * LANES)
        one = gb_ref[:, pl.ds(block, LANES)]
        two = gb_ref[:, pl.ds(aligned(hid + block), LANES)]
        one = jnp.where(odd, pltpu.roll(one, group, 1), one)
        two = jnp.where(odd, two, pltpu.roll(two, group, 1))
        bias_row = jnp.where(lane_at < group, one, two)[0:1]
        rows = [bias_row, head_row[0:1], bits[0:1]]
        rows += [item - item.astype(BF).astype(F32) for item in rows[:2]]
        for i, item in enumerate(rows):
            stage[sz.misc + i : sz.misc + i + 1, :] = item
        target_ref[base : base + sz.pay, :] = stage[...].astype(BF)


def seeds_backward(sz, tables, received, low, high, counts, partial):
    hid = sz.hid
    return call(
        functools.partial(seeds_back_kernel, sz),
        [((sz.pay, LANES), BF), ((sz.pay, LANES), BF), ((2 * sz.pay, LANES), BF)],
        [
            *[(item.shape, jnp.int32) for item in tables],
            ((hid, sz.n_mid), BF),
            ((hid, 2 * hid), BF),
            ((hid, 4 * sz.own), BF),
            ((hid + 8, sz.high_lanes), F32),
            ((sz.count_rows * (sz.own // LANES), LANES), BF),
            ((hid + 8, sz.part_lanes), F32),
            ((8 * sz.hold, hid), F32),
            ((2 * hid, hid), F32),
            ((16, 2 * hid), F32),
            ((sz.pay, LANES), F32),
        ],
        BACK_MIB,
        *tables,
        received,
        low,
        high,
        counts,
        partial,
        far_in=(0, 1, 2, 4, 5, 6, 7),
        micros=3,
        copies=13,
    )


def unpacked(sz, grad, one_ref, three_ref):
    group = sz.group

    def wide(at, rows):
        return jnp.concatenate([grad[at : at + rows, :], grad[at + rows : at + 2 * rows, :]], 1)

    one = wide(0, 2 * sz.feat)
    three = grad[sz.at_three : sz.misc, :]
    turned = pltpu.roll(three, group, 1)
    for f in range(sz.feat):
        one_ref[f, 0:1, :] = one[f : f + 1]
        one_ref[f, 1:2, :] = one[sz.feat + f : sz.feat + f + 1]
    for c in range(sz.classes):
        three_ref[c, 0:1, :] = three[c : c + 1, :group]
        three_ref[c, 1:2, :] = turned[c : c + 1, :group]
    misc = grad[sz.misc : sz.misc + 5, :]
    fine = misc[0:2] + misc[3:5]
    hidden = jnp.concatenate([fine[0:1, :group], fine[0:1, group : 2 * group]], 0)
    two = wide(sz.rows_one, 2 * group).reshape(2, group, sz.hid)
    return (one_ref[...], two, three_ref[...], hidden, fine[1:2, : sz.classes]), misc[2:3]


def new_moments(first, second, g):
    return BETA_ONE * first + (1.0 - BETA_ONE) * g, BETA_TWO * second + (1.0 - BETA_TWO) * g * g


def lamb_kernel(sz, grad, *rest):
    params, firsts, seconds, updates = rest[:5], rest[5:10], rest[10:15], rest[15:20]
    sums_ref, totals_ref, one_ref, three_ref = rest[20:]
    grads, bits_row = unpacked(sz, grad, one_ref, three_ref)
    lane_at = lax.broadcasted_iota(jnp.int32, (8, LANES), 1)
    row_at = lax.broadcasted_iota(jnp.int32, (8, LANES), 0)
    sums = jnp.zeros((8, LANES), F32)
    for i in range(5):
        w = params[i][...]
        m, v = new_moments(firsts[i][...], seconds[i][...], grads[i])
        u = (m / (1.0 - BETA_ONE**STEP)) / (jnp.sqrt(v / (1.0 - BETA_TWO**STEP)) + ADAM_EPS) + DECAY_RATE * w
        updates[i][...] = u
        for row, item in ((0, w), (1, u)):
            item = item * item
            if i < 3:
                item = jnp.sum(item, 0)
            total = jnp.sum(jnp.sum(item, 0, keepdims=True), 1, keepdims=True)
            if i == 4:
                total = 0.25 * total
            sums = jnp.where((lane_at == i) & (row_at == row), total, sums)
    sums_ref[...] = sums
    power = (1 << (lane_at & 15)).astype(F32)
    power = jnp.where((lane_at & 31) < 16, power, power * float(2**16))
    bits = jnp.broadcast_to(bits_row, (8, LANES)) * power
    loss = jnp.sum(jnp.where(lane_at < 32, bits, 0.0), 1, keepdims=True) * float(2.0**-LOSS_BITS)
    count = jnp.sum(jnp.where((lane_at >= 32) & (lane_at < 64), bits, 0.0), 1, keepdims=True)
    totals_ref[...] = jnp.where(lane_at == 0, loss, count)


def moments_kernel(sz, grad, *rest):
    firsts, seconds, moments, squares = rest[:5], rest[5:10], rest[10:15], rest[15:20]
    grads, _ = unpacked(sz, grad, *rest[20:])
    for i in range(5):
        moments[i][...], squares[i][...] = new_moments(firsts[i][...], seconds[i][...], grads[i])


def lamb(sz, grad, params, firsts, seconds):
    like = [(item.shape, F32) for item in params]
    scratch = [(params[0].shape, F32), (params[2].shape, F32)]
    outs = call(
        functools.partial(lamb_kernel, sz),
        like + [((8, LANES), F32)] * 2,
        scratch,
        6,
        grad,
        *params,
        *firsts,
        *seconds,
        micros=1,
    )
    moments = call(functools.partial(moments_kernel, sz), like * 2, scratch, 6, grad, *firsts, *seconds, micros=2)
    return outs, moments


def step_kernel(own, far, w1, w2, w3, wh, wb, u1, u2, u3, uh, ub, n1, n2, n3, nh, nb, norms_ref):
    norms = jnp.sqrt(own[...] + far[...])
    norms_ref[...] = norms[0:2, 0:5]
    for i, (w, u, n) in enumerate(
        ((w1, u1, n1), (w2, u2, n2), (w3, u3, n3), (wh, uh, nh), (wb, ub, nb))
    ):
        ratio = LEARN_RATE * (norms[0:1, i : i + 1] / norms[1:2, i : i + 1])
        n[...] = w[...] - ratio * u[...]


def take_step(sums, params, updates):
    return call(
        step_kernel,
        [(item.shape, F32) for item in params] + [((2, 5), F32)],
        [],
        3,
        *sums,
        *params,
        *updates,
    )


def swap(value, axis, count, bit):
    return lax.ppermute(value, axis, [(i, i ^ bit) for i in range(count)])


def merged(own, other):
    return lax.reduce_precision(own.astype(F32) + other.astype(F32), 8, 7)


def shards(
    features, neighbors_one, present_one, neighbors_two, present_two, neighbors_three, present_three,
    labels, seed_weight, serve_rows, take_seed, fetch_live,
    weight_one, weight_two, weight_three, hidden_bias, head_bias,
    first_one, first_two, first_three, first_hidden, first_head,
    second_one, second_two, second_three, second_hidden, second_head,
):
    sz = Sizes(features, neighbors_one, neighbors_two, neighbors_three, weight_two, weight_three, serve_rows)

    def tree(one, two, three, hidden, head):
        return (one.transpose(1, 0, 2), two, three.transpose(2, 0, 1), hidden, head[None, :])

    def back(one, two, three, hidden, head):
        return (one.transpose(1, 0, 2), two, three.transpose(1, 2, 0), hidden, head[0])

    params = tree(weight_one, weight_two, weight_three, hidden_bias, head_bias)
    firsts = tree(first_one, first_two, first_three, first_hidden, first_head)
    seconds = tree(second_one, second_two, second_three, second_hidden, second_head)

    own_b, packed, mean, tail, *sent = first_messages(sz, features, neighbors_one, present_one, *params[:4])
    s1, s2, s3 = [swap(sent[r - 1], "col", 4, r) for r in (1, 2, 3)]
    links = (neighbors_two, present_two, neighbors_three, present_three)
    own_a, counts, *means = mean_messages(sz, features, neighbors_one, present_one, mean, tail, links)
    s1, *means = lax.optimization_barrier((s1, *means))
    means = [swap(means[r - 1], "col", 4, r) for r in (1, 2, 3)]
    later, s3, counts = lax.optimization_barrier((s2, s3, counts))
    passed = swap(later, "col", 4, 1)
    tables = (serve_rows, take_seed, fetch_live[None, :])
    low, high, rows = seeds_forward(sz, (own_b, packed, s1, s2, s3, passed), counts, tables)
    received = lax.all_to_all(rows, ("dp", "col"), split_axis=0, concat_axis=0, tiled=True)
    partial = rest_step(sz, low, high, counts, (own_a, *means, s1, s2, s3), labels[None, :], seed_weight[None, :], head_bias[None, :])
    keep0, keep1, send = seeds_backward(sz, tables, received, low, high, counts, partial)
    other = swap(send, "col", 4, 1)
    own = merged(keep0, other[: sz.pay]).astype(BF)
    far = merged(keep1, other[sz.pay :]).astype(BF)
    pair = [[(d, c), (d ^ 1, c ^ 2)] for d in range(sz.dp) for c in range(4)]
    pair = [(a * 4 + b, c * 4 + d) for (a, b), (c, d) in pair]
    near = (swap(far, "col", 4, 2), swap(own, "dp", sz.dp, 1), lax.ppermute(far, ("dp", "col"), pair))
    near = [item.astype(F32) for item in (own, *near)]
    grad = lax.reduce_precision((near[0] + near[1]) + (near[2] + near[3]), 8, 7)
    bit = 2
    while bit < sz.dp:
        grad = merged(grad, swap(grad.astype(BF), "dp", sz.dp, bit))
        bit *= 2
    outs, moments = lamb(sz, grad, params, firsts, seconds)
    moments, squares, updates = moments[:5], moments[5:], outs[:5]
    sums, totals = outs[5], outs[6]
    pair = sums + swap(sums, "col", 4, 1)
    fresh = take_step([pair, swap(pair, "col", 4, 2)], params, updates)
    return (*back(*fresh[:5]), *back(*moments), *back(*squares), fresh[5], totals[0, 0], totals[0, 1])


def solution(mesh):
    wide = P(None, "col", None)
    tree = [wide, wide, wide, P(None, "col"), P()]
    return jax.shard_map(
        shards,
        mesh=mesh,
        in_specs=(
            P("col", "dp"),
            *[P(None, "dp")] * 6,
            P("dp"),
            P("dp"),
            P("dp", None),
            P("dp", None),
            P("dp"),
            *tree,
            *tree,
            *tree,
        ),
        out_specs=(*tree, *tree, *tree, P(), P(), P()),
        check_vma=False,
    )
```
